32 devices in a mesh: row: 8 (over z, y), col: 4 (over x, core).
Axes of the slice: x: 2, y: 2, z: 4, core: 2. Of those that a mesh axis runs over, the one named last changes fastest.
Arguments:
- tokens: bfloat16 [16384, 768], P(('row', 'col')), may hold values from -12 to 12
- cotangent: bfloat16 [16384, 768], P(('row', 'col')), may hold values from -6 to 6
- w_qkv: float32 [768, 3, 768], P('row', None, 'col'), may hold values from -0.21875 to 0.21875
- w_out: float32 [768, 768], P('col', 'row'), may hold values from -0.625 to 0.625
- w_up: float32 [768, 3072], P('row', 'col'), may hold values from -0.21875 to 0.21875
- w_down: float32 [3072, 768], P('col', 'row'), may hold values from -0.109375 to 0.109375
- vectors: float32 [12, 768], P(None, 'row'), may hold values from -0.4 to 1.5
- first_qkv: float32 [768, 3, 768], P('row', None, 'col'), may hold values from -24 to 24
- first_out: float32 [768, 768], P('col', 'row'), may hold values from -32 to 32
- first_up: float32 [768, 3072], P('row', 'col'), may hold values from -20 to 20
- first_down: float32 [3072, 768], P('col', 'row'), may hold values from -48 to 48
- first_vectors: float32 [12, 768], P(None, 'row'), may hold values from -80 to 80
- second_qkv: float32 [768, 3, 768], P('row', None, 'col'), may hold values from 1.47456 to 5.89824
- second_out: float32 [768, 768], P('col', 'row'), may hold values from 2.62144 to 10.48576
- second_up: float32 [768, 3072], P('row', 'col'), may hold values from 1.024 to 4.096
- second_down: float32 [3072, 768], P('col', 'row'), may hold values from 5.89824 to 23.59296
- second_vectors: float32 [12, 768], P(None, 'row'), may hold values from 16.384 to 65.536
Outputs:
- mixed_out: float32 [16384, 768], P(('row', 'col'))
- token_grad: float32 [16384, 768], P(('row', 'col'))
- new_qkv: float32 [768, 3, 768], P('row', None, 'col')
- new_out: float32 [768, 768], P('col', 'row')
- new_up: float32 [768, 3072], P('row', 'col')
- new_down: float32 [3072, 768], P('col', 'row')
- new_vectors: float32 [12, 768], P(None, 'row')
- new_first_qkv: float32 [768, 3, 768], P('row', None, 'col')
- new_first_out: float32 [768, 768], P('col', 'row')
- new_first_up: float32 [768, 3072], P('row', 'col')
- new_first_down: float32 [3072, 768], P('col', 'row')
- new_first_vectors: float32 [12, 768], P(None, 'row')
- new_second_qkv: float32 [768, 3, 768], P('row', None, 'col')
- new_second_out: float32 [768, 768], P('col', 'row')
- new_second_up: float32 [768, 3072], P('row', 'col')
- new_second_down: float32 [3072, 768], P('col', 'row')
- new_second_vectors: float32 [12, 768], P(None, 'row')
The draws below stay inside these ranges and needn't reach their ends.
All inputs are finite; a program needn't handle non-finite values.
Results may differ from the reference program's by a relative error of at most 0.008.
The reference program's roundings to bfloat16 on the way count: a program that leaves them out, or rounds other values in their place, can miss the bound.
Values may be sent and summed in bfloat16 or wider, within the bound.
No kernel may reach another device: no remote copies, remote signals or barrier semaphores. Data moves between devices by JAX's collectives and lax.ppermute only.
A program may use at most 128 MiB of HBM per device.

```python
import math
import jax
import jax.numpy as jnp
from jax import lax

D = 768
HEADS = 12
HEAD_DIM = 64
FF = 3072
LENGTH = 1024
STEP_NUMBER = 10
VECTORS = 12
SEQS = 16
TOKENS = 16384


def draw_tokens(key, part):
    key = jax.random.fold_in(key, 11)
    position = jnp.arange(D, dtype=jnp.float32) / (D - 1)
    base = jnp.clip(jax.random.normal(key, (TOKENS, D), jnp.float32), -4.0, 4.0)
    rising = 1.0 + 2.0 * position
    return (base * rising[None, :]).astype(jnp.bfloat16)


def draw_vectors(key, part):
    key = jax.random.fold_in(key, 23)
    key_gain, key_bias = jax.random.split(key)
    gains = jax.random.uniform(key_gain, (VECTORS, D), jnp.float32, 0.5, 1.5)
    biases = jax.random.uniform(key_bias, (VECTORS, D), jnp.float32, -0.4, 0.4)
    row_ids = jnp.arange(VECTORS)[:, None]
    picked = (row_ids == 0) | (row_ids == 5)
    return jnp.where(picked, gains, biases)


def level_of(own_key, shape, cuts, low, high):
    factor_of, own = 1.0, jax.random.fold_in(own_key, 6)
    for axis_at, shards_of in cuts:
        heights = jnp.exp(jax.random.uniform(jax.random.fold_in(own, axis_at), (shards_of,), jnp.float32, low / len(cuts), high / len(cuts)))
        factor_of = factor_of * jnp.repeat(heights, shape[axis_at] // shards_of).reshape([-1 if axis == axis_at else 1 for axis in range(len(shape))])
    return factor_of


def bell_draw(key, dims, width, bound, shards=(), held_as=jnp.bfloat16):
    drawn = jax.random.normal(key, dims, jnp.float32) * width
    if len(shards) > 0:
        drawn = level_of(key, dims, shards, -0.22, 0.18) * drawn
    return jnp.clip(drawn, min=-bound, max=bound).astype(held_as)


def setup_inputs(seed: int = 0) -> dict:
    seeds = jax.random.split(jax.random.key(seed), 18)
    tokens = draw_tokens(jax.random.fold_in(seeds[17], 71), 0)
    cotangent = bell_draw(seeds[1], (TOKENS, D), 1.0, 6.0, ((0, 32),))
    w_qkv = bell_draw(seeds[2], (D, 3, D), D ** -0.5, 0.21875, ((0, 8), (2, 4)), jnp.float32)
    w_out = bell_draw(seeds[3], (D, D), (D // 8) ** -0.5, 0.625, ((0, 4), (1, 8)), jnp.float32)
    w_up = bell_draw(seeds[4], (D, FF), D ** -0.5, 0.21875, ((0, 8), (1, 4)), jnp.float32)
    w_down = bell_draw(seeds[5], (FF, D), FF ** -0.5, 0.109375, ((0, 4), (1, 8)), jnp.float32)
    vectors = draw_vectors(jax.random.fold_in(seeds[17], 71), 0)
    first_qkv = bell_draw(seeds[7], (D, 3, D), (0.033 * TOKENS ** 0.5), 24.0, ((0, 8), (2, 4)), jnp.float32)
    first_out = bell_draw(seeds[8], (D, D), (0.044 * TOKENS ** 0.5), 32.0, ((0, 4), (1, 8)), jnp.float32)
    first_up = bell_draw(seeds[9], (D, FF), (0.028 * TOKENS ** 0.5), 20.0, ((0, 8), (1, 4)), jnp.float32)
    first_down = bell_draw(seeds[10], (FF, D), (0.066 * TOKENS ** 0.5), 48.0, ((0, 4), (1, 8)), jnp.float32)
    first_vectors = bell_draw(seeds[11], (VECTORS, D), (0.11 * TOKENS ** 0.5), 80.0, ((1, 8),), jnp.float32)
    second_qkv = jnp.clip(jnp.exp(math.log(5.89824) - 1.3862944 * jax.random.uniform(seeds[12], (D, 3, D), jnp.float32) ** level_of(seeds[12], (D, 3, D), ((0, 8), (2, 4)), -0.2, 0.2)), 1.47456, 5.89824)
    second_out = jnp.clip(jnp.exp(math.log(10.48576) - 1.3862944 * jax.random.uniform(seeds[13], (D, D), jnp.float32) ** level_of(seeds[13], (D, D), ((0, 4), (1, 8)), -0.2, 0.2)), 2.62144, 10.48576)
    second_up = jnp.clip(jnp.exp(math.log(4.096) - 1.3862944 * jax.random.uniform(seeds[14], (D, FF), jnp.float32) ** level_of(seeds[14], (D, FF), ((0, 8), (1, 4)), -0.2, 0.2)), 1.024, 4.096)
    second_down = jnp.clip(jnp.exp(math.log(23.59296) - 1.3862944 * jax.random.uniform(seeds[15], (FF, D), jnp.float32) ** level_of(seeds[15], (FF, D), ((0, 4), (1, 8)), -0.2, 0.2)), 5.89824, 23.59296)
    second_vectors = jnp.clip(jnp.exp(math.log(65.536) - 1.3862944 * jax.random.uniform(seeds[16], (VECTORS, D), jnp.float32) ** level_of(seeds[16], (VECTORS, D), ((1, 8),), -0.2, 0.2)), 16.384, 65.536)
    return {"tokens": tokens, "cotangent": cotangent, "w_qkv": w_qkv, "w_out": w_out, "w_up": w_up, "w_down": w_down, "vectors": vectors, "first_qkv": first_qkv, "first_out": first_out, "first_up": first_up, "first_down": first_down, "first_vectors": first_vectors, "second_qkv": second_qkv, "second_out": second_out, "second_up": second_up, "second_down": second_down, "second_vectors": second_vectors}


EPS = 1e-05
BETA_ONE = 0.9
BETA_TWO = 0.999
ADAM_EPS = 1e-08
DECAY = 0.1
RATE_MATRIX = 0.04
RATE_VECTOR = 0.3
HIGHEST = lax.Precision.HIGHEST

@jax.custom_vjp
def low(v):
    return lax.optimization_barrier(v.astype(jnp.bfloat16)).astype(jnp.float32)

@jax.custom_vjp
def low_back(v):
    return v

def low_keep(v):
    return (low(v), None)

def low_pass(kept, grad):
    return (grad,)

def back_keep(v):
    return (v, None)

def back_low(kept, grad):
    return (low(grad),)
low.defvjp(low_keep, low_pass)
low_back.defvjp(back_keep, back_low)

def normalize(values_in, gain_row, bias_row):
    row_mean = lax.optimization_barrier(jnp.mean(values_in, axis=-1, keepdims=True))
    centred = values_in - row_mean
    row_var = lax.optimization_barrier(jnp.mean(centred * centred, axis=-1, keepdims=True))
    return centred * lax.rsqrt(row_var + EPS) * gain_row + bias_row

def layer(inputs, params):
    w_qkv, w_out, w_up, w_down, vec_all = [low(weight) for weight in params]
    first_in = low(normalize(inputs, vec_all[0], vec_all[1]))
    qkv = jnp.einsum('td,dkc->tkc', first_in, w_qkv, precision=HIGHEST)
    queries = qkv[:, 0] + vec_all[2]
    keys_in = qkv[:, 1]
    values_in = qkv[:, 2] + vec_all[3]
    stacked = low(low_back(jnp.stack([queries, keys_in, values_in])))
    heads = stacked.reshape(3, LENGTH, HEADS, HEAD_DIM)
    scores = jnp.einsum('qhe,khe->hqk', heads[0], heads[1], precision=HIGHEST) * HEAD_DIM ** (-0.5)
    scores = low_back(scores)
    causal = jnp.arange(LENGTH)[None, :] <= jnp.arange(LENGTH)[:, None]
    scores = jnp.where(causal[None], scores, -1e+30)
    attend_prob = jax.nn.softmax(scores, axis=-1)
    mixture = jnp.einsum('hqk,khe->qhe', low(attend_prob), heads[2], precision=HIGHEST).reshape(LENGTH, D)
    mixture = low(low_back(mixture))
    attended = low_back(jnp.dot(mixture, w_out, precision=HIGHEST))
    hidden_state = inputs + attended + vec_all[4]
    second_in = low(normalize(hidden_state, vec_all[5], vec_all[6]))
    up_proj = low_back(jnp.dot(second_in, w_up, precision=HIGHEST) + vec_all[8:].reshape(FF))
    activated = low(jax.nn.gelu(up_proj, approximate=True))
    down_proj = low_back(jnp.dot(activated, w_down, precision=HIGHEST))
    return hidden_state + down_proj + vec_all[7]

def adamw(weight, moment_one, moment_two, gradient, rate):
    first = BETA_ONE * moment_one + (1 - BETA_ONE) * gradient
    second = BETA_TWO * moment_two + (1 - BETA_TWO) * gradient * gradient
    first_hat = first / (1 - BETA_ONE ** STEP_NUMBER)
    second_hat = second / (1 - BETA_TWO ** STEP_NUMBER)
    updated = weight - rate * (first_hat / (jnp.sqrt(second_hat) + ADAM_EPS) + DECAY * weight)
    return (updated, first, second)

def reference(tokens, cotangent, w_qkv, w_out, w_up, w_down, vectors, first_qkv, first_out, first_up, first_down, first_vectors, second_qkv, second_out, second_up, second_down, second_vectors):
    inputs = tokens.astype(jnp.float32).reshape(SEQS, LENGTH, D)
    grads_in = cotangent.astype(jnp.float32).reshape(SEQS, LENGTH, D)
    params = (w_qkv, w_out, w_up, w_down, vectors)

    def one_sequence(totals, pair):
        seq_in, seq_grad = pair
        outputs, backward = jax.vjp(layer, seq_in, params)
        input_grad, param_grads = backward(seq_grad)
        totals = jax.tree.map(jnp.add, totals, param_grads)
        return (totals, (outputs, input_grad))
    zeros = jax.tree.map(jnp.zeros_like, params)
    grads, (outputs, input_grads) = lax.scan(one_sequence, zeros, (inputs, grads_in))
    rates = (RATE_MATRIX, RATE_MATRIX, RATE_MATRIX, RATE_MATRIX, RATE_VECTOR)
    firsts = (first_qkv, first_out, first_up, first_down, first_vectors)
    seconds = (second_qkv, second_out, second_up, second_down, second_vectors)
    results = [adamw(params[number], firsts[number], seconds[number], grads[number], rates[number]) for number in range(5)]
    return (outputs.reshape(TOKENS, D), input_grads.reshape(TOKENS, D), results[0][0], results[1][0], results[2][0], results[3][0], results[4][0], results[0][1], results[1][1], results[2][1], results[3][1], results[4][1], results[0][2], results[1][2], results[2][2], results[3][2], results[4][2])
```

```python
import jax
import jax.numpy as jnp
from jax import lax
from jax.experimental import pallas as pl
from jax.experimental.pallas import tpu as pltpu
from jax.sharding import PartitionSpec as P

HEAD_DIM = 64
LENGTH = 1024
STEP_NUMBER = 10
VEC_ROWS = 12
PAIR = 2 * HEAD_DIM
QUERY_BLOCK = 256


EPS = 1e-05
BETA_ONE = 0.9
BETA_TWO = 0.999
ADAM_EPS = 1e-08
DECAY = 0.1
RATE_MATRIX = 0.04
RATE_VECTOR = 0.3

F32 = jnp.float32
BF16 = jnp.bfloat16


def normalize_rows(values_in):
    row_mean = jnp.mean(values_in, axis=-1, keepdims=True)
    centred = values_in - row_mean
    row_var = jnp.mean(centred * centred, axis=-1, keepdims=True)
    inv_std = lax.rsqrt(row_var + EPS)
    return (centred * inv_std, inv_std)


def norm_back(grad_in, normed, inv_std):
    mean_grad = jnp.mean(grad_in, axis=-1, keepdims=True)
    mean_cross = jnp.mean(grad_in * normed, axis=-1, keepdims=True)
    return inv_std * (grad_in - mean_grad - normed * mean_cross)


def adamw(weight, moment_one, moment_two, gradient, rate):
    first = BETA_ONE * moment_one + (1 - BETA_ONE) * gradient
    second = BETA_TWO * moment_two + (1 - BETA_TWO) * gradient * gradient
    first_hat = first / (1 - BETA_ONE**STEP_NUMBER)
    second_hat = second / (1 - BETA_TWO**STEP_NUMBER)
    updated = weight - rate * (first_hat / (jnp.sqrt(second_hat) + ADAM_EPS) + DECAY * weight)
    return (updated, first, second)


def gelu_value(value_up):
    return jax.nn.gelu(value_up, approximate=True)


def row_lines(count):
    factors = {8: (4, 2), 64: (2, 8, 4)}.get(count, (count,))
    lines = []
    stride = count
    for size in factors:
        stride //= size
        lines.append(("row", count, size, stride))
    return lines


def place_on(line):
    name, _, size, stride = line
    return lax.axis_index(name) // stride % size


def hop_pairs(line, hop, keep):
    _, count, size, stride = line
    pairs = []
    for index in range(count):
        place = index // stride % size
        if 0 <= place + hop < size and keep(place):
            pairs.append((index, index + hop * stride))
    return pairs


def swap_over(value, line):
    name, count, _, stride = line
    pairs = [(index, index ^ stride) for index in range(count)]
    return lax.ppermute(value, name, pairs)


def gather_line(block, line, dim):
    name, _, size, _ = line
    if size == 1:
        return jnp.expand_dims(block, dim)
    place = place_on(line)
    below, above = [block], [block]
    if size == 2:
        other = swap_over(block, line)
        below.append(other)
        above.append(other)
    else:
        for step in range(1, size):
            below.append(
                lax.ppermute(below[-1], name, hop_pairs(line, 1, lambda at: at >= step - 1))
            )
            above.append(
                lax.ppermute(above[-1], name, hop_pairs(line, -1, lambda at: at <= size - step))
            )
    shape = block.shape[:dim] + (size,) + block.shape[dim:]
    gathered = jnp.broadcast_to(jnp.expand_dims(block, dim), shape)
    for ahead in range(1, size):
        if size == 2:
            piece = above[1]
        else:
            piece = jnp.where(place + ahead < size, above[ahead], below[size - ahead])
        gathered = lax.dynamic_update_slice_in_dim(
            gathered, jnp.expand_dims(piece, dim), (place + ahead) % size, dim
        )
    return gathered


def reduce_line(parts, line, dim):
    name, _, size, _ = line
    place = place_on(line)

    def part(index):
        return lax.dynamic_index_in_dim(parts, index % size, dim, keepdims=False)

    if size == 1:
        return part(0)
    if size == 2:
        return part(place) + swap_over(part(1 - place).astype(BF16), line).astype(F32)
    up_sum = down_sum = None
    for step in range(1, size):
        far = size - step
        up_send, down_send = part(place + far), part(place - far + size)
        if up_sum is not None:
            up_send, down_send = up_send + up_sum, down_send + down_sum
        up_sum = lax.ppermute(
            up_send.astype(BF16), name, hop_pairs(line, 1, lambda at: at + far < size)
        ).astype(F32)
        down_sum = lax.ppermute(
            down_send.astype(BF16), name, hop_pairs(line, -1, lambda at: at - far >= 0)
        ).astype(F32)
    return part(place) + up_sum + down_sum


def gather_far(block, lines):
    for line in reversed(lines[:-1]):
        block = gather_line(block, line, 0)
        if block.ndim > 3:
            block = block.reshape((-1,) + block.shape[2:])
    if len(lines) == 1:
        block = block[None]
    return block


def gather_near(stacked, near, x_line):
    far, rows, cols = stacked.shape
    half = rows // 2
    front, back = stacked[:, :half], stacked[:, half:]
    front_own = gather_line(front, near, 1)
    front_other = swap_over(front_own, x_line)
    back_pair = jnp.stack([back, swap_over(back, x_line)])
    back_pair = gather_line(back_pair, near, 2)

    def joined(front_part, back_part):
        return jnp.stack([front_part, back_part], axis=2).reshape(-1, cols)

    return joined(front_own, back_pair[0]), joined(front_other, back_pair[1])


def reduce_all(own, other, lines, x_line):
    near = lines[-1]
    cols = own.shape[1]
    count, near_size = near[1], near[2]
    rows = own.shape[0] // count
    shape = (count // near_size, near_size, 2, rows // 2, cols)
    own, other = own.reshape(shape), other.reshape(shape)
    front = own[:, :, 0] + swap_over(other[:, :, 0].astype(BF16), x_line).astype(F32)
    front = reduce_line(front, near, 1)
    back_pair = jnp.stack([own[:, :, 1], other[:, :, 1]])
    back_pair = reduce_line(back_pair, near, 2)
    back = back_pair[0] + swap_over(back_pair[1].astype(BF16), x_line).astype(F32)
    total = jnp.concatenate([front, back], axis=1)
    for line in lines[:-1]:
        total = total.reshape((line[2], -1) + total.shape[1:])
        total = reduce_line(total, line, 0)
    return total.reshape(rows, cols)


def sum_everywhere(value):
    for name in ("col", "row"):
        count = lax.axis_size(name)
        stride = 1
        while stride < count:
            value = value + swap_over(value, (name, count, 2, stride))
            stride *= 2
    return value


def dot_nt(left, right):
    return lax.dot_general(left, right, (((1,), (1,)), ((), ())), preferred_element_type=F32)


def dot_nn(left, right):
    return lax.dot_general(left, right, (((1,), (0,)), ((), ())), preferred_element_type=F32)


def lane_pick(half):
    lanes = lax.broadcasted_iota(jnp.int32, (1, PAIR), 1)
    return jnp.where((lanes // HEAD_DIM) == half, 1.0, 0.0).astype(BF16)


def causal_block(size):
    key_at = lax.broadcasted_iota(jnp.int32, (size, size), 0)
    query_at = lax.broadcasted_iota(jnp.int32, (size, size), 1)
    return key_at <= query_at


def attend_kernel(q_ref, k_ref, v_ref, out_ref, lse_ref):
    length = q_ref.shape[0]
    block = min(QUERY_BLOCK, length)
    allowed = causal_block(block)
    values_t = v_ref[...].T
    scaling = jnp.asarray(HEAD_DIM**-0.5, BF16)
    for first in range(0, length, block):
        last = first + block
        query = q_ref[first:last, :] * scaling
        outs = []
        for half in range(2):
            rows = slice(half * HEAD_DIM, (half + 1) * HEAD_DIM)
            query_half = query * lane_pick(half)
            diag = dot_nt(k_ref[first:last, :], query_half)
            diag = jnp.where(allowed, diag, -1e30)
            top = jnp.max(diag, axis=0, keepdims=True)
            if first:
                rest = dot_nt(k_ref[0:first, :], query_half)
                top = jnp.maximum(top, jnp.max(rest, axis=0, keepdims=True))
            diag = jnp.exp(diag - top)
            total = jnp.sum(diag, axis=0, keepdims=True)
            if first:
                rest = jnp.exp(rest - top)
                total = total + jnp.sum(rest, axis=0, keepdims=True)
            inverse = 1.0 / total
            result = dot_nn(values_t[rows, first:last], (diag * inverse).astype(BF16))
            if first:
                result = result + dot_nn(values_t[rows, 0:first], (rest * inverse).astype(BF16))
            outs.append(result)
            lse_ref[0, half : half + 1, first:last] = top + jnp.log(total)
        out_ref[first:last, :] = jnp.concatenate(outs, axis=0).T.astype(BF16)


def attend_forward(qkv):
    length, width = qkv.shape
    pairs = width // (3 * PAIR)

    def lanes(part):
        return pl.BlockSpec((length, PAIR), lambda pair: (0, part * pairs + pair))

    return pl.pallas_call(
        attend_kernel,
        grid=(pairs,),
        in_specs=[lanes(0), lanes(1), lanes(2)],
        out_specs=[lanes(0), pl.BlockSpec((1, 8, length), lambda pair: (pair, 0, 0))],
        out_shape=[
            jax.ShapeDtypeStruct((length, pairs * PAIR), BF16),
            jax.ShapeDtypeStruct((pairs, 8, length), F32),
        ],
        compiler_params=pltpu.CompilerParams(vmem_limit_bytes=40 * 2**20),
        cost_estimate=pl.CostEstimate(
            flops=pairs * 2 * 4 * length * length * HEAD_DIM,
            bytes_accessed=4 * length * pairs * PAIR * 2,
            transcendentals=pairs * length * length,
        ),
        name="attend_forward",
    )(qkv, qkv, qkv)


def attend_back_kernel(q_ref, k_ref, v_ref, go_ref, lse_ref, grad_ref, gk_sum, gv_sum):
    length = q_ref.shape[0]
    pairs = grad_ref.shape[1] // (3 * PAIR)
    block = min(QUERY_BLOCK, length)
    allowed = causal_block(block)
    keys_t = k_ref[...].T
    scaling = jnp.asarray(HEAD_DIM**-0.5, BF16)
    pair = pl.program_id(0)

    def lanes(part):
        return pl.ds(pl.multiple_of((part * pairs + pair) * PAIR, PAIR), PAIR)

    gk_sum[...] = jnp.zeros_like(gk_sum)
    gv_sum[...] = jnp.zeros_like(gv_sum)
    for first in range(0, length, block):
        last = first + block
        query = q_ref[first:last, :] * scaling
        grad_out = go_ref[first:last, :]
        outs = []
        for half in range(2):
            rows = slice(half * HEAD_DIM, (half + 1) * HEAD_DIM)
            pick = lane_pick(half)
            query_half = query * pick
            grad_half = grad_out * pick
            lse = lse_ref[0, half : half + 1, first:last]
            spans = [(first, last)] if first == 0 else [(0, first), (first, last)]
            probs, grads, inner = [], [], None
            for low, high in spans:
                scores = dot_nt(k_ref[low:high, :], query_half)
                if low == first:
                    scores = jnp.where(allowed, scores, -1e30)
                prob = jnp.exp(scores - lse)
                grad_prob = dot_nt(v_ref[low:high, :], grad_half)
                part = jnp.sum(prob * grad_prob, axis=0, keepdims=True)
                inner = part if inner is None else inner + part
                probs.append(prob)
                grads.append(grad_prob)
            result = None
            for (low, high), prob, grad_prob in zip(spans, probs, grads):
                grad_score = (prob * (grad_prob - inner)).astype(BF16)
                gk_sum[low:high, :] += dot_nn(grad_score, query_half)
                gv_sum[low:high, :] += dot_nn(prob.astype(BF16), grad_half)
                part = dot_nn(keys_t[rows, low:high], grad_score)
                result = part if result is None else result + part
            outs.append(result)
        grad_query = jnp.concatenate(outs, axis=0).T * (HEAD_DIM**-0.5)
        grad_ref[first:last, lanes(0)] = grad_query.astype(BF16)
    grad_ref[:, lanes(1)] = gk_sum[...].astype(BF16)
    grad_ref[:, lanes(2)] = gv_sum[...].astype(BF16)


def attend_backward(qkv, grad_heads, lse):
    length, width = qkv.shape
    pairs = width // (3 * PAIR)

    def lanes(part):
        return pl.BlockSpec((length, PAIR), lambda pair: (0, part * pairs + pair))

    return pl.pallas_call(
        attend_back_kernel,
        grid=(pairs,),
        in_specs=[
            lanes(0),
            lanes(1),
            lanes(2),
            lanes(0),
            pl.BlockSpec((1, 8, length), lambda pair: (pair, 0, 0)),
        ],
        out_specs=pl.BlockSpec((length, width), lambda pair: (0, 0)),
        out_shape=jax.ShapeDtypeStruct((length, width), BF16),
        scratch_shapes=[pltpu.VMEM((length, PAIR), F32), pltpu.VMEM((length, PAIR), F32)],
        compiler_params=pltpu.CompilerParams(vmem_limit_bytes=40 * 2**20),
        cost_estimate=pl.CostEstimate(
            flops=pairs * 2 * 10 * length * length * HEAD_DIM,
            bytes_accessed=7 * length * pairs * PAIR * 2,
            transcendentals=pairs * length * length,
        ),
        name="attend_backward",
    )(qkv, qkv, qkv, grad_heads, lse)


def shards(
    tokens,
    cotangent,
    w_qkv,
    w_out,
    w_up,
    w_down,
    vectors,
    first_qkv,
    first_out,
    first_up,
    first_down,
    first_vectors,
    second_qkv,
    second_out,
    second_up,
    second_down,
    second_vectors,
):
    row_index = lax.axis_index("row")
    row_count = lax.axis_size("row")
    col_index = lax.axis_index("col")
    col_count = lax.axis_size("col")
    lines = row_lines(row_count)
    near = lines[-1]
    x_line = ("col", col_count, col_count // 2, 2)
    core_line = ("col", col_count, 2, 1)
    core = col_index % 2
    other_col = col_index ^ 2
    rows_loc, width = tokens.shape
    width_loc = w_qkv.shape[2]
    hidden_loc = w_up.shape[1]
    shard_rows = w_up.shape[0]

    pad = -(3 * width_loc + VEC_ROWS) % 128
    pack_qkv = jnp.concatenate(
        [
            w_qkv.reshape(shard_rows, 3 * width_loc).astype(BF16),
            vectors.T.astype(BF16),
            jnp.zeros((shard_rows, pad), BF16),
        ],
        axis=1,
    )
    pack_up = jnp.concatenate([w_up.astype(BF16), w_out.T.astype(BF16)], axis=1)
    pack_down = w_down.T.astype(BF16)

    def both_halves(mine):
        other = swap_over(mine, core_line)
        return jnp.where(
            core == 0,
            jnp.concatenate([mine, other], axis=0),
            jnp.concatenate([other, mine], axis=0),
        )

    def own_rows(value):
        return lax.dynamic_slice_in_dim(value, core * rows_loc, rows_loc, 0)

    def partner_rows(value):
        return lax.dynamic_slice_in_dim(value, (1 - core) * rows_loc, rows_loc, 0)

    far_qkv = gather_far(pack_qkv, lines)
    pack_up, far_qkv = lax.optimization_barrier((pack_up, far_qkv))
    own_qkv, other_qkv = gather_near(far_qkv, near, x_line)
    far_up = gather_far(pack_up, lines)
    pack_down, far_up = lax.optimization_barrier((pack_down, far_up))
    own_up, other_up = gather_near(far_up, near, x_line)
    far_down = gather_far(pack_down, lines)
    own_down, other_down = gather_near(far_down, near, x_line)

    all_tokens = both_halves(tokens)
    all_cot = both_halves(cotangent)

    vec_all = own_qkv[:, 3 * width_loc : 3 * width_loc + VEC_ROWS].T.astype(F32)

    def cat_blocks(vec_row, size):
        return jnp.concatenate(
            [
                lax.dynamic_slice_in_dim(vec_row, col_index * size, size, 0),
                lax.dynamic_slice_in_dim(vec_row, other_col * size, size, 0),
            ]
        )

    full_qkv = jnp.concatenate(
        [
            block[:, part * width_loc : (part + 1) * width_loc]
            for part in range(3)
            for block in (own_qkv, other_qkv)
        ],
        axis=1,
    )
    full_up = jnp.concatenate([own_up[:, :hidden_loc], other_up[:, :hidden_loc]], axis=1)
    full_out = jnp.concatenate([own_up[:, hidden_loc:], other_up[:, hidden_loc:]], axis=1)
    full_down = jnp.concatenate([own_down, other_down], axis=1)
    partner_out = swap_over(full_out, core_line)
    width_core = 2 * width_loc

    inputs_all = all_tokens.astype(F32)
    normed_one, inv_one = normalize_rows(inputs_all)
    first_in = (normed_one * vec_all[0] + vec_all[1]).astype(BF16)
    bias_qkv = jnp.concatenate(
        [
            cat_blocks(vec_all[2], width_loc),
            jnp.zeros((width_core,), F32),
            cat_blocks(vec_all[3], width_loc),
        ]
    )
    qkv = (dot_nn(first_in, full_qkv) + bias_qkv).astype(BF16)
    heads_low, lse = attend_forward(qkv)
    partner_heads = swap_over(heads_low, core_line)
    attended = dot_nt(heads_low, full_out) + dot_nt(partner_heads, partner_out)
    hidden_state = inputs_all + attended + vec_all[4]
    normed_two, inv_two = normalize_rows(hidden_state)
    second_in = (normed_two * vec_all[5] + vec_all[6]).astype(BF16)
    bias_up = cat_blocks(vec_all[8:].reshape(-1), hidden_loc)
    up_proj = dot_nn(second_in, full_up) + bias_up
    gelu_out, gelu_back = jax.vjp(gelu_value, up_proj)
    activated = gelu_out.astype(BF16)
    down_part = dot_nt(activated, full_down)
    down_other = swap_over(partner_rows(down_part).astype(BF16), core_line).astype(F32)
    mixed_out = own_rows(hidden_state) + own_rows(down_part) + down_other + vec_all[7]

    def tokens_dot(left, right):
        return lax.dot_general(left, right, (((0,), (0,)), ((), ())), preferred_element_type=F32)

    grad_act = dot_nn(all_cot, full_down)
    grad_upper = gelu_back(grad_act)[0].astype(BF16)
    grad_second_part = dot_nt(grad_upper, full_up)
    grad_second_other = swap_over(grad_second_part.astype(BF16), core_line).astype(F32)
    grad_second = grad_second_part + grad_second_other
    grad_hidden = all_cot.astype(F32) + norm_back(grad_second * vec_all[5], normed_two, inv_two)
    grad_hidden_low = grad_hidden.astype(BF16)
    grad_heads = dot_nn(grad_hidden_low, full_out).astype(BF16)
    grad_qkv_low = attend_backward(qkv, grad_heads, lse)
    grad_first_part = dot_nt(grad_qkv_low, full_qkv)
    grad_first_other = swap_over(partner_rows(grad_first_part).astype(BF16), core_line).astype(F32)
    grad_first = own_rows(grad_first_part) + grad_first_other
    token_grad = own_rows(grad_hidden) + norm_back(
        grad_first * vec_all[0], own_rows(normed_one), own_rows(inv_one)
    )

    grad_down = tokens_dot(all_cot, activated)
    grad_up = tokens_dot(second_in, grad_upper)
    grad_out = tokens_dot(grad_hidden_low, heads_low)
    grad_qkv = tokens_dot(first_in, grad_qkv_low)
    owned_down = reduce_all(grad_down[:, :hidden_loc], grad_down[:, hidden_loc:], lines, x_line)
    owned_up = reduce_all(grad_up[:, :hidden_loc], grad_up[:, hidden_loc:], lines, x_line)
    owned_out = reduce_all(grad_out[:, :width_loc], grad_out[:, width_loc:], lines, x_line)
    by_block = grad_qkv.reshape(width, 3, 2, width_loc)
    owned_qkv = reduce_all(
        by_block[:, :, 0].reshape(width, -1), by_block[:, :, 1].reshape(width, -1), lines, x_line
    )

    def placed(part_row, length):
        size = part_row.shape[0] // 2
        start = jnp.zeros((length,), F32)
        start = lax.dynamic_update_slice_in_dim(start, part_row[:size], col_index * size, 0)
        return lax.dynamic_update_slice_in_dim(start, part_row[size:], other_col * size, 0)

    bias_sums = jnp.sum(grad_qkv_low.astype(F32), axis=0)
    front_rows = jnp.stack(
        [
            jnp.sum(grad_first_part * normed_one, axis=0),
            jnp.sum(grad_first_part, axis=0),
            placed(bias_sums[:width_core], width),
            placed(bias_sums[2 * width_core :], width),
            0.5 * jnp.sum(grad_hidden, axis=0),
            jnp.sum(grad_second_part * normed_two, axis=0),
            jnp.sum(grad_second_part, axis=0),
            jnp.sum(cotangent.astype(F32), axis=0),
        ]
    )
    grad_bias_up = jnp.sum(grad_upper.astype(F32), axis=0)
    up_rows = placed(grad_bias_up, hidden_loc * col_count).reshape(-1, width)
    grad_vec = sum_everywhere(jnp.concatenate([front_rows, up_rows], axis=0))
    owned_vec = lax.dynamic_slice_in_dim(grad_vec, row_index * shard_rows, shard_rows, 1)

    new_qkv, new_first_qkv, new_second_qkv = adamw(
        w_qkv, first_qkv, second_qkv, owned_qkv.reshape(w_qkv.shape), RATE_MATRIX
    )
    new_out, new_first_out, new_second_out = adamw(
        w_out, first_out, second_out, owned_out.T, RATE_MATRIX
    )
    new_up, new_first_up, new_second_up = adamw(w_up, first_up, second_up, owned_up, RATE_MATRIX)
    new_down, new_first_down, new_second_down = adamw(
        w_down, first_down, second_down, owned_down.T, RATE_MATRIX
    )
    new_vectors, new_first_vectors, new_second_vectors = adamw(
        vectors, first_vectors, second_vectors, owned_vec, RATE_VECTOR
    )
    return (
        mixed_out,
        token_grad,
        new_qkv,
        new_out,
        new_up,
        new_down,
        new_vectors,
        new_first_qkv,
        new_first_out,
        new_first_up,
        new_first_down,
        new_first_vectors,
        new_second_qkv,
        new_second_out,
        new_second_up,
        new_second_down,
        new_second_vectors,
    )


def solution(mesh):
    by_token = P(("row", "col"), None)
    weights = (
        P("row", None, "col"),
        P("col", "row"),
        P("row", "col"),
        P("col", "row"),
        P(None, "row"),
    )
    return jax.shard_map(
        shards,
        mesh=mesh,
        in_specs=(by_token, by_token) + weights * 3,
        out_specs=(by_token, by_token) + weights * 3,
        check_vma=False,
    )
```

```python
import math

import jax
import jax.numpy as jnp
from jax import lax
from jax.experimental import pallas as pl
from jax.experimental.pallas import tpu as pltpu
from jax.sharding import PartitionSpec as P

HEAD_DIM = 64
LENGTH = 1024
STEP_NUMBER = 10
VEC_ROWS = 12
PAIR = 2 * HEAD_DIM
QUERY_BLOCK = 256
ROW_BLOCK = 256


EPS = 1e-05
BETA_ONE = 0.9
BETA_TWO = 0.999
ADAM_EPS = 1e-08
DECAY = 0.1
RATE_MATRIX = 0.04
RATE_VECTOR = 0.3

F32 = jnp.float32
BF16 = jnp.bfloat16


def normalize_rows(values_in):
    row_mean = jnp.mean(values_in, axis=-1, keepdims=True)
    centred = values_in - row_mean
    row_var = jnp.mean(centred * centred, axis=-1, keepdims=True)
    inv_std = lax.rsqrt(row_var + EPS)
    return (centred * inv_std, inv_std)


def norm_back(grad_in, normed, inv_std):
    mean_grad = jnp.mean(grad_in, axis=-1, keepdims=True)
    mean_cross = jnp.mean(grad_in * normed, axis=-1, keepdims=True)
    return inv_std * (grad_in - mean_grad - normed * mean_cross)


def adamw(weight, moment_one, moment_two, gradient, rate):
    first = BETA_ONE * moment_one + (1 - BETA_ONE) * gradient
    second = BETA_TWO * moment_two + (1 - BETA_TWO) * gradient * gradient
    first_hat = first / (1 - BETA_ONE**STEP_NUMBER)
    second_hat = second / (1 - BETA_TWO**STEP_NUMBER)
    updated = weight - rate * (first_hat / (jnp.sqrt(second_hat) + ADAM_EPS) + DECAY * weight)
    return (updated, first, second)


def bit_strides(high, low):
    strides = []
    while high > low:
        high //= 2
        strides.append(high)
    return strides


def place_on(line):
    name, stride = line
    return lax.axis_index(name) // stride % 2


def swap_over(value, line):
    name, stride = line
    pairs = [(index, index ^ stride) for index in range(lax.axis_size(name))]
    return lax.ppermute(value, name, pairs)


def gather_bit(block, line, dim):
    other = jnp.expand_dims(swap_over(block, line), dim)
    shape = block.shape[:dim] + (2,) + block.shape[dim:]
    both = jnp.broadcast_to(jnp.expand_dims(block, dim), shape)
    return lax.dynamic_update_slice_in_dim(both, other, 1 - place_on(line), dim)


def gather_bits(block, lines, dim):
    for line in lines:
        block = gather_bit(block, line, dim)
        dim += 1
    return block


def reduce_bit(parts, line, dim):
    place = place_on(line)

    def part(index):
        return lax.dynamic_index_in_dim(parts, index, dim, keepdims=False)

    sent = swap_over(part(1 - place).astype(BF16), line)
    return part(place).astype(F32) + sent.astype(F32)


def reduce_bits(parts, lines, dim):
    for line in reversed(lines):
        parts = reduce_bit(parts, line, dim + len(lines) - 1)
        lines = lines[:-1]
    return parts


class Grid:
    def __init__(self, row_count):
        near_size = {8: 2, 64: 4}.get(row_count, 1)
        self.row_count = row_count
        self.far = [("row", stride) for stride in bit_strides(row_count, near_size)]
        self.near = [("row", stride) for stride in bit_strides(near_size, 1)]
        self.x_line = ("col", 2)

    def gather_far(self, block):
        rows, cols = block.shape
        return gather_bits(block, self.far, 0).reshape(-1, rows, cols)

    def gather_near(self, stacked, keep_cols):
        far, _, cols = stacked.shape
        front, back = stacked[: far // 2], stacked[far // 2 :]
        front_own = gather_bits(front, self.near, 1).reshape(-1, cols)
        front_other = swap_over(front_own[:, :keep_cols], self.x_line)
        back_other = swap_over(back[:, :, :keep_cols], self.x_line)
        back_pair = gather_bits(jnp.concatenate([back, back_other], axis=2), self.near, 1)
        back_pair = back_pair.reshape(-1, cols + keep_cols)
        own = jnp.concatenate([front_own, back_pair[:, :cols]], axis=0)
        other = jnp.concatenate([front_other, back_pair[:, cols:]], axis=0)
        return own, other

    def reduce_all(self, pair):
        _, all_rows, cols = pair.shape
        rows = all_rows // self.row_count
        middle = all_rows // 2
        bits = (2,) * len(self.near)
        front = pair[0, :middle].astype(F32) + swap_over(pair[1, :middle], self.x_line).astype(F32)
        front = reduce_bits(front.reshape((-1,) + bits + (rows, cols)), self.near, 1)
        back = pair[:, middle:].reshape((2, -1) + bits + (rows, cols))
        back = reduce_bits(back, self.near, 2)
        back = back[0].astype(F32) + swap_over(back[1].astype(BF16), self.x_line).astype(F32)
        total = jnp.concatenate([front, back], axis=0)
        total = total.reshape((2,) * len(self.far) + (rows, cols))
        return reduce_bits(total, self.far, 0)


def sum_everywhere(value):
    for name in ("col", "row"):
        for stride in bit_strides(lax.axis_size(name), 1):
            value = value + swap_over(value, (name, stride))
    return value


def dot_nt(left, right):
    return lax.dot_general(left, right, (((1,), (1,)), ((), ())), preferred_element_type=F32)


def dot_nn(left, right):
    return lax.dot_general(left, right, (((1,), (0,)), ((), ())), preferred_element_type=F32)


def lane_pick(half):
    lanes = lax.broadcasted_iota(jnp.int32, (1, PAIR), 1)
    return jnp.where((lanes // HEAD_DIM) == half, 1.0, 0.0).astype(BF16)


def causal_block(size):
    key_at = lax.broadcasted_iota(jnp.int32, (size, size), 0)
    query_at = lax.broadcasted_iota(jnp.int32, (size, size), 1)
    return key_at <= query_at


def attend_kernel(q_ref, k_ref, v_ref, out_ref, lse_ref):
    length = q_ref.shape[0]
    block = min(QUERY_BLOCK, length)
    allowed = causal_block(block)
    values_t = v_ref[...].T
    scaling = jnp.asarray(HEAD_DIM**-0.5, BF16)
    for first in range(0, length, block):
        last = first + block
        query = q_ref[first:last, :] * scaling
        outs = []
        for half in range(2):
            rows = slice(half * HEAD_DIM, (half + 1) * HEAD_DIM)
            query_half = query * lane_pick(half)
            diag = dot_nt(k_ref[first:last, :], query_half)
            diag = jnp.where(allowed, diag, -1e30)
            top = jnp.max(diag, axis=0, keepdims=True)
            if first:
                rest = dot_nt(k_ref[0:first, :], query_half)
                top = jnp.maximum(top, jnp.max(rest, axis=0, keepdims=True))
            diag = jnp.exp(diag - top)
            total = jnp.sum(diag, axis=0, keepdims=True)
            if first:
                rest = jnp.exp(rest - top)
                total = total + jnp.sum(rest, axis=0, keepdims=True)
            inverse = 1.0 / total
            result = dot_nn(values_t[rows, first:last], (diag * inverse).astype(BF16))
            if first:
                result = result + dot_nn(values_t[rows, 0:first], (rest * inverse).astype(BF16))
            outs.append(result)
            lse_ref[0, half : half + 1, first:last] = top + jnp.log(total)
        out_ref[first:last, :] = jnp.concatenate(outs, axis=0).T.astype(BF16)


def attend_forward(qkv):
    length, width = qkv.shape
    pairs = width // (3 * PAIR)

    def lanes(part):
        return pl.BlockSpec((length, PAIR), lambda pair: (0, part * pairs + pair))

    return pl.pallas_call(
        attend_kernel,
        grid=(pairs,),
        in_specs=[lanes(0), lanes(1), lanes(2)],
        out_specs=[lanes(0), pl.BlockSpec((1, 8, length), lambda pair: (pair, 0, 0))],
        out_shape=[
            jax.ShapeDtypeStruct((length, pairs * PAIR), BF16),
            jax.ShapeDtypeStruct((pairs, 8, length), F32),
        ],
        compiler_params=pltpu.CompilerParams(vmem_limit_bytes=40 * 2**20),
        cost_estimate=pl.CostEstimate(
            flops=pairs * 2 * 4 * length * length * HEAD_DIM,
            bytes_accessed=4 * length * pairs * PAIR * 2,
            transcendentals=pairs * length * length,
        ),
        name="attend_forward",
    )(qkv, qkv, qkv)


def attend_back_kernel(q_ref, k_ref, v_ref, go_ref, lse_ref, grad_ref, gk_sum, gv_sum):
    length = q_ref.shape[0]
    pairs = grad_ref.shape[1] // (3 * PAIR)
    block = min(QUERY_BLOCK, length)
    allowed = causal_block(block)
    keys_t = k_ref[...].T
    scaling = jnp.asarray(HEAD_DIM**-0.5, BF16)
    pair = pl.program_id(0)

    def lanes(part):
        return pl.ds(pl.multiple_of((part * pairs + pair) * PAIR, PAIR), PAIR)

    gk_sum[...] = jnp.zeros_like(gk_sum)
    gv_sum[...] = jnp.zeros_like(gv_sum)
    for first in range(0, length, block):
        last = first + block
        query = q_ref[first:last, :] * scaling
        grad_out = go_ref[first:last, :]
        outs = []
        for half in range(2):
            rows = slice(half * HEAD_DIM, (half + 1) * HEAD_DIM)
            pick = lane_pick(half)
            query_half = query * pick
            grad_half = grad_out * pick
            lse = lse_ref[0, half : half + 1, first:last]
            spans = [(first, last)] if first == 0 else [(0, first), (first, last)]
            probs, grads, inner = [], [], None
            for low, high in spans:
                scores = dot_nt(k_ref[low:high, :], query_half)
                if low == first:
                    scores = jnp.where(allowed, scores, -1e30)
                prob = jnp.exp(scores - lse)
                grad_prob = dot_nt(v_ref[low:high, :], grad_half)
                part = jnp.sum(prob * grad_prob, axis=0, keepdims=True)
                inner = part if inner is None else inner + part
                probs.append(prob)
                grads.append(grad_prob)
            result = None
            for (low, high), prob, grad_prob in zip(spans, probs, grads):
                grad_score = (prob * (grad_prob - inner)).astype(BF16)
                gk_sum[low:high, :] += dot_nn(grad_score, query_half)
                gv_sum[low:high, :] += dot_nn(prob.astype(BF16), grad_half)
                part = dot_nn(keys_t[rows, low:high], grad_score)
                result = part if result is None else result + part
            outs.append(result)
        grad_query = jnp.concatenate(outs, axis=0).T * (HEAD_DIM**-0.5)
        grad_ref[first:last, lanes(0)] = grad_query.astype(BF16)
    grad_ref[:, lanes(1)] = gk_sum[...].astype(BF16)
    grad_ref[:, lanes(2)] = gv_sum[...].astype(BF16)


def attend_backward(qkv, grad_heads, lse):
    length, width = qkv.shape
    pairs = width // (3 * PAIR)

    def lanes(part):
        return pl.BlockSpec((length, PAIR), lambda pair: (0, part * pairs + pair))

    return pl.pallas_call(
        attend_back_kernel,
        grid=(pairs,),
        in_specs=[
            lanes(0),
            lanes(1),
            lanes(2),
            lanes(0),
            pl.BlockSpec((1, 8, length), lambda pair: (pair, 0, 0)),
        ],
        out_specs=pl.BlockSpec((length, width), lambda pair: (0, 0)),
        out_shape=jax.ShapeDtypeStruct((length, width), BF16),
        scratch_shapes=[pltpu.VMEM((length, PAIR), F32), pltpu.VMEM((length, PAIR), F32)],
        compiler_params=pltpu.CompilerParams(vmem_limit_bytes=40 * 2**20),
        cost_estimate=pl.CostEstimate(
            flops=pairs * 2 * 10 * length * length * HEAD_DIM,
            bytes_accessed=7 * length * pairs * PAIR * 2,
            transcendentals=pairs * length * length,
        ),
        name="attend_backward",
    )(qkv, qkv, qkv, grad_heads, lse)


def rows_of(block, width):
    return pl.BlockSpec((block, width), lambda step: (step, 0))


def whole(shape):
    return pl.BlockSpec(shape, lambda *step: (0,) * len(shape))


def shaped(shape, dtype):
    return jax.ShapeDtypeStruct(shape, dtype)


def cost(flops, arrays):
    return pl.CostEstimate(flops=flops, bytes_accessed=arrays, transcendentals=0)


PARAMS = pltpu.CompilerParams(vmem_limit_bytes=48 * 2**20)


def first_norm_kernel(tokens_ref, vec_ref, weight_ref, bias_ref, norm_ref, qkv_ref):
    normed, _ = normalize_rows(tokens_ref[...].astype(F32))
    first_in = (normed * vec_ref[0:1, :] + vec_ref[1:2, :]).astype(BF16)
    norm_ref[...] = first_in
    qkv_ref[...] = (dot_nn(first_in, weight_ref[...]) + bias_ref[...]).astype(BF16)


def first_norm(tokens, vec_all, weight, bias):
    length, width = tokens.shape
    cols = weight.shape[1]
    return pl.pallas_call(
        first_norm_kernel,
        grid=(length // ROW_BLOCK,),
        in_specs=[
            rows_of(ROW_BLOCK, width),
            whole(vec_all.shape),
            whole(weight.shape),
            whole(bias.shape),
        ],
        out_specs=[rows_of(ROW_BLOCK, width), rows_of(ROW_BLOCK, cols)],
        out_shape=[shaped((length, width), BF16), shaped((length, cols), BF16)],
        compiler_params=PARAMS,
        cost_estimate=cost(2 * length * width * cols, 2 * length * (2 * width + cols)),
        name="first_norm",
    )(tokens, vec_all, weight, bias)


def attended_kernel(
    heads_ref, partner_ref, own_ref, other_ref, tokens_ref, vec_ref, hidden_ref, norm_ref
):
    attended = dot_nt(heads_ref[...], own_ref[...]) + dot_nt(partner_ref[...], other_ref[...])
    hidden = tokens_ref[...].astype(F32) + attended + vec_ref[4:5, :]
    hidden_ref[...] = hidden
    normed, _ = normalize_rows(hidden)
    norm_ref[...] = (normed * vec_ref[5:6, :] + vec_ref[6:7, :]).astype(BF16)


def attended_norm(heads, partner_heads, own_out, partner_out, tokens, vec_all):
    length, width = tokens.shape
    cols = heads.shape[1]
    return pl.pallas_call(
        attended_kernel,
        grid=(length // ROW_BLOCK,),
        in_specs=[
            rows_of(ROW_BLOCK, cols),
            rows_of(ROW_BLOCK, cols),
            whole(own_out.shape),
            whole(partner_out.shape),
            rows_of(ROW_BLOCK, width),
            whole(vec_all.shape),
        ],
        out_specs=[rows_of(ROW_BLOCK, width), rows_of(ROW_BLOCK, width)],
        out_shape=[shaped((length, width), F32), shaped((length, width), BF16)],
        compiler_params=PARAMS,
        cost_estimate=cost(4 * length * width * cols, length * width * 10),
        name="attended_norm",
    )(heads, partner_heads, own_out, partner_out, tokens, vec_all)


def feed_kernel(
    norm_ref, cot_ref, up_ref, down_ref, bias_ref, act_ref, gup_ref, bias_sum_ref, out_ref, back_ref,
    back_low_ref,
):
    step = pl.program_id(0)
    length = norm_ref.shape[0]
    curve, cubic = math.sqrt(2 / math.pi), 0.044715

    @pl.when(step == 0)
    def _():
        out_ref[...] = jnp.zeros_like(out_ref)
        back_ref[...] = jnp.zeros_like(back_ref)

    bias_sum = jnp.zeros(bias_ref.shape, F32)
    for first in range(0, length, ROW_BLOCK):
        rows = slice(first, first + ROW_BLOCK)
        up = dot_nn(norm_ref[rows, :], up_ref[...]) + bias_ref[...]
        square = up * up
        tanh = jnp.tanh(curve * up * (1.0 + cubic * square))
        act = (0.5 * up * (1.0 + tanh)).astype(BF16)
        act_ref[rows, :] = act
        slope = 0.5 * (1.0 + tanh) + 0.5 * up * (1.0 - tanh * tanh) * (
            curve * (1.0 + 3.0 * cubic * square)
        )
        grad_up = (dot_nn(cot_ref[rows, :], down_ref[...]) * slope).astype(BF16)
        gup_ref[rows, :] = grad_up
        bias_sum = bias_sum + jnp.sum(grad_up.astype(F32), axis=0, keepdims=True)
        out_ref[rows, :] += dot_nt(act, down_ref[...])
        back_ref[rows, :] += dot_nt(grad_up, up_ref[...])
    bias_sum_ref[...] = bias_sum

    @pl.when(step == pl.num_programs(0) - 1)
    def _():
        back_low_ref[...] = back_ref[...].astype(BF16)


def feed(norm, cot, up, down, bias):
    length, width = norm.shape
    hidden = up.shape[1]
    block = 512
    cols = pl.BlockSpec((width, block), lambda step: (0, step))
    tall = pl.BlockSpec((length, block), lambda step: (0, step))
    flat = pl.BlockSpec((1, block), lambda step: (0, step))
    full = whole((length, width))
    return pl.pallas_call(
        feed_kernel,
        grid=(hidden // block,),
        in_specs=[full, full, cols, cols, flat],
        out_specs=[tall, tall, flat, full, full, full],
        out_shape=[
            shaped((length, hidden), BF16),
            shaped((length, hidden), BF16),
            shaped((1, hidden), F32),
            shaped((length, width), F32),
            shaped((length, width), F32),
            shaped((length, width), BF16),
        ],
        compiler_params=PARAMS,
        cost_estimate=cost(8 * length * width * hidden, 4 * length * (width + hidden)),
        name="feed",
    )(norm, cot, up, down, bias)


def feed_grads_kernel(cot_ref, norm_ref, act_ref, gup_ref, out_ref, turned):
    kind = pl.program_id(0)
    first = (pl.program_id(1) == 0) & (pl.program_id(2) == 0)

    @pl.when(first & (kind == 0))
    def _():
        turned[...] = cot_ref[...].T

    @pl.when(first & (kind == 1))
    def _():
        turned[...] = norm_ref[...].T

    @pl.when(kind == 0)
    def _():
        out_ref[0] = dot_nn(turned[...], act_ref[...]).astype(BF16)

    @pl.when(kind == 1)
    def _():
        out_ref[0] = dot_nn(turned[...], gup_ref[...]).astype(BF16)


def feed_grads(cot, norm, act, grad_up):
    length, width = norm.shape
    hidden = act.shape[1]
    block = hidden // 4
    return pl.pallas_call(
        feed_grads_kernel,
        grid=(2, 2, 2),
        in_specs=[
            whole((length, width)),
            whole((length, width)),
            pl.BlockSpec((length, block), lambda kind, x, n: (0, jnp.where(kind == 0, 2 * x + n, 3))),
            pl.BlockSpec((length, block), lambda kind, x, n: (0, jnp.where(kind == 1, 2 * x + n, 0))),
        ],
        out_specs=pl.BlockSpec((1, width, block), lambda kind, x, n: (x, 0, 2 * kind + n)),
        out_shape=shaped((2, width, hidden), BF16),
        scratch_shapes=[pltpu.VMEM((width, length), BF16)],
        compiler_params=PARAMS,
        cost_estimate=cost(4 * length * width * hidden, 4 * length * (width + hidden)),
        name="feed_grads",
    )(cot, norm, act, grad_up)


def second_back_kernel(
    part_ref, other_ref, hidden_ref, cot_ref, vec_ref, out_w_ref, grad_ref, low_ref, heads_ref, sum_ref
):
    normed, inv_std = normalize_rows(hidden_ref[...])
    part = part_ref[...]
    cot = cot_ref[...].astype(F32)
    grad_second = part + other_ref[...].astype(F32)
    grad = cot + norm_back(grad_second * vec_ref[5:6, :], normed, inv_std)
    grad_ref[...] = grad
    low = grad.astype(BF16)
    low_ref[...] = low
    heads_ref[...] = dot_nn(low, out_w_ref[...]).astype(BF16)

    @pl.when(pl.program_id(0) == 0)
    def _():
        sum_ref[...] = jnp.zeros_like(sum_ref)

    for row, value in enumerate((grad, part * normed, part, cot)):
        sum_ref[row : row + 1, :] += jnp.sum(value, axis=0, keepdims=True)


def second_back(part, other, hidden, cot, vec_all, out_w):
    length, width = part.shape
    cols = out_w.shape[1]
    full = rows_of(ROW_BLOCK, width)
    return pl.pallas_call(
        second_back_kernel,
        grid=(length // ROW_BLOCK,),
        in_specs=[full, full, full, full, whole(vec_all.shape), whole(out_w.shape)],
        out_specs=[full, full, rows_of(ROW_BLOCK, cols), whole((8, width))],
        out_shape=[
            shaped((length, width), F32),
            shaped((length, width), BF16),
            shaped((length, cols), BF16),
            shaped((8, width), F32),
        ],
        compiler_params=PARAMS,
        cost_estimate=cost(2 * length * width * cols, length * width * 20),
        name="second_back",
    )(part, other, hidden, cot, vec_all, out_w)


def qkv_grads_kernel(norm_ref, low_ref, grad_ref, heads_ref, out_ref, turned):
    part = pl.program_id(0)
    cols = heads_ref.shape[1]
    half = cols // 2

    @pl.when(part == 0)
    def _():
        turned[...] = norm_ref[...].T

    @pl.when(part == 3)
    def _():
        turned[...] = low_ref[...].T

    for index in range(4):

        @pl.when(part == index)
        def _():
            right = heads_ref if index == 3 else grad_ref
            grads = dot_nn(turned[...], right[...]).astype(BF16)
            for x in range(2):
                out_ref[x, :, index * half : (index + 1) * half] = grads[:, x * half : (x + 1) * half]


def qkv_grads(norm, low, grad_qkv, heads):
    length, width = norm.shape
    cols = heads.shape[1]
    return pl.pallas_call(
        qkv_grads_kernel,
        grid=(4,),
        in_specs=[
            whole((length, width)),
            whole((length, width)),
            pl.BlockSpec((length, cols), lambda part: (0, jnp.minimum(part, 2))),
            whole((length, cols)),
        ],
        out_specs=whole((2, width, 2 * cols)),
        out_shape=shaped((2, width, 2 * cols), BF16),
        scratch_shapes=[pltpu.VMEM((width, length), BF16)],
        compiler_params=PARAMS,
        cost_estimate=cost(8 * length * width * cols, 4 * length * (2 * width + 2 * cols)),
        name="qkv_grads",
    )(norm, low, grad_qkv, heads)


def first_back_kernel(grad_ref, weight_ref, tokens_ref, part_ref, sum_ref, bias_ref):
    part = dot_nt(grad_ref[...], weight_ref[...])
    part_ref[...] = part
    normed, _ = normalize_rows(tokens_ref[...].astype(F32))

    @pl.when(pl.program_id(0) == 0)
    def _():
        sum_ref[...] = jnp.zeros_like(sum_ref)
        bias_ref[...] = jnp.zeros_like(bias_ref)

    for row, value in enumerate((part * normed, part)):
        sum_ref[row : row + 1, :] += jnp.sum(value, axis=0, keepdims=True)
    bias_ref[0:1, :] += jnp.sum(grad_ref[...].astype(F32), axis=0, keepdims=True)


def first_back(grad_qkv, weight, tokens):
    length, width = tokens.shape
    cols = grad_qkv.shape[1]
    return pl.pallas_call(
        first_back_kernel,
        grid=(length // ROW_BLOCK,),
        in_specs=[rows_of(ROW_BLOCK, cols), whole(weight.shape), rows_of(ROW_BLOCK, width)],
        out_specs=[rows_of(ROW_BLOCK, width), whole((8, width)), whole((8, cols))],
        out_shape=[
            shaped((length, width), F32),
            shaped((8, width), F32),
            shaped((8, cols), F32),
        ],
        compiler_params=PARAMS,
        cost_estimate=cost(2 * length * width * cols, length * (6 * width + 2 * cols)),
        name="first_back",
    )(grad_qkv, weight, tokens)


def token_back_kernel(core_ref, part_ref, other_ref, tokens_ref, grad_ref, vec_ref, out_ref):
    normed, inv_std = normalize_rows(tokens_ref[...].astype(F32))
    grad_first = part_ref[...] + other_ref[...].astype(F32)
    out_ref[...] = grad_ref[...] + norm_back(grad_first * vec_ref[0:1, :], normed, inv_std)


def token_back(core, part, other, tokens, grad_hidden, vec_all):
    rows, width = tokens.shape
    steps = rows // ROW_BLOCK
    own = pl.BlockSpec((ROW_BLOCK, width), lambda step, core_ref: (core_ref[0] * steps + step, 0))
    here = pl.BlockSpec((ROW_BLOCK, width), lambda step, core_ref: (step, 0))
    return pl.pallas_call(
        token_back_kernel,
        grid_spec=pltpu.PrefetchScalarGridSpec(
            num_scalar_prefetch=1,
            grid=(steps,),
            in_specs=[own, here, here, own, whole(vec_all.shape)],
            out_specs=here,
        ),
        out_shape=shaped((rows, width), F32),
        compiler_params=PARAMS,
        cost_estimate=cost(rows * width * 20, rows * width * 16),
        name="token_back",
    )(core.reshape(1), part, other, tokens, grad_hidden, vec_all)


def shards(
    tokens,
    cotangent,
    w_qkv,
    w_out,
    w_up,
    w_down,
    vectors,
    first_qkv,
    first_out,
    first_up,
    first_down,
    first_vectors,
    second_qkv,
    second_out,
    second_up,
    second_down,
    second_vectors,
):
    row_index = lax.axis_index("row")
    col_index = lax.axis_index("col")
    col_count = lax.axis_size("col")
    grid = Grid(lax.axis_size("row"))
    core_line = ("col", 1)
    core = col_index % 2
    other_col = col_index ^ 2
    rows_loc, width = tokens.shape
    width_loc = w_qkv.shape[2]
    width_core = 2 * width_loc
    hidden_loc = w_up.shape[1]
    shard_rows = w_up.shape[0]

    pad = -VEC_ROWS % 128
    pack_qkv = jnp.concatenate(
        [w_qkv[:, part].astype(BF16) for part in range(3)]
        + [w_out.T.astype(BF16), vectors.T.astype(BF16), jnp.zeros((shard_rows, pad), BF16)],
        axis=1,
    )
    pack_feed = jnp.concatenate([w_up.astype(BF16), w_down.T.astype(BF16)], axis=1)

    def both_halves(mine):
        return gather_bit(mine, core_line, 0).reshape(-1, width)

    def own_rows(value):
        return lax.dynamic_slice_in_dim(value, core * rows_loc, rows_loc, 0)

    def partner_rows(value):
        return lax.dynamic_slice_in_dim(value, (1 - core) * rows_loc, rows_loc, 0)

    far_qkv = grid.gather_far(pack_qkv)
    pack_feed, far_qkv = lax.optimization_barrier((pack_feed, far_qkv))
    own_qkv, other_qkv = grid.gather_near(far_qkv, 4 * width_loc)
    far_feed = grid.gather_far(pack_feed)
    own_feed, other_feed = grid.gather_near(far_feed, 2 * hidden_loc)

    all_tokens = both_halves(tokens)
    all_cot = both_halves(cotangent)

    vec_all = own_qkv[:, 4 * width_loc : 4 * width_loc + VEC_ROWS].T.astype(F32)

    def cat_blocks(vec_row, size):
        return jnp.concatenate(
            [
                lax.dynamic_slice_in_dim(vec_row, col_index * size, size, 0),
                lax.dynamic_slice_in_dim(vec_row, other_col * size, size, 0),
            ]
        )

    def joined(own, other, size, parts):
        return jnp.concatenate(
            [
                block[:, part * size : (part + 1) * size]
                for part in parts
                for block in (own, other)
            ],
            axis=1,
        )

    full_qkv = joined(own_qkv, other_qkv, width_loc, range(3))
    full_out = joined(own_qkv, other_qkv, width_loc, (3,))
    full_up = joined(own_feed, other_feed, hidden_loc, (0,))
    full_down = joined(own_feed, other_feed, hidden_loc, (1,))
    partner_out = swap_over(full_out, core_line)

    bias_qkv = jnp.concatenate(
        [
            cat_blocks(vec_all[2], width_loc),
            jnp.zeros((width_core,), F32),
            cat_blocks(vec_all[3], width_loc),
        ]
    )
    first_in, qkv = first_norm(all_tokens, vec_all, full_qkv, bias_qkv[None])
    heads_low, lse = attend_forward(qkv)
    partner_heads = swap_over(heads_low, core_line)
    hidden_state, second_in = attended_norm(
        heads_low, partner_heads, full_out, partner_out, all_tokens, vec_all
    )
    bias_up = cat_blocks(vec_all[8:].reshape(-1), hidden_loc)
    activated, grad_upper, grad_bias_up, down_part, second_part, second_low = feed(
        second_in, all_cot, full_up, full_down, bias_up[None]
    )

    second_other = swap_over(second_low, core_line)
    pair_feed = feed_grads(all_cot, second_in, activated, grad_upper)
    grad_hidden, grad_hidden_low, grad_heads, second_sums = second_back(
        second_part, second_other, hidden_state, all_cot, vec_all, full_out
    )
    down_other = swap_over(partner_rows(down_part).astype(BF16), core_line).astype(F32)
    mixed_out = own_rows(hidden_state) + own_rows(down_part) + down_other + vec_all[7]
    grad_qkv_low = attend_backward(qkv, grad_heads, lse)
    pair_qkv = qkv_grads(first_in, grad_hidden_low, grad_qkv_low, heads_low)
    first_part, first_sums, bias_sums = first_back(grad_qkv_low, full_qkv, all_tokens)
    first_other = swap_over(partner_rows(first_part).astype(BF16), core_line)
    token_grad = token_back(core, first_part, first_other, tokens, grad_hidden, vec_all)

    owned_feed = grid.reduce_all(pair_feed)
    owned_down, owned_up = owned_feed[:, :hidden_loc], owned_feed[:, hidden_loc:]
    owned_pack = grid.reduce_all(pair_qkv)
    owned_qkv = jnp.stack(
        [owned_pack[:, part * width_loc : (part + 1) * width_loc] for part in range(3)], axis=1
    )
    owned_out = owned_pack[:, 3 * width_loc :]

    def placed(part_row, length):
        size = part_row.shape[0] // 2
        start = jnp.zeros((length,), F32)
        start = lax.dynamic_update_slice_in_dim(start, part_row[:size], col_index * size, 0)
        return lax.dynamic_update_slice_in_dim(start, part_row[size:], other_col * size, 0)

    front_rows = jnp.stack(
        [
            first_sums[0],
            first_sums[1],
            placed(bias_sums[0, :width_core], width),
            placed(bias_sums[0, 2 * width_core :], width),
            0.5 * second_sums[0],
            second_sums[1],
            second_sums[2],
            0.5 * second_sums[3],
        ]
    )
    up_rows = placed(grad_bias_up[0], hidden_loc * col_count).reshape(-1, width)
    grad_vec = sum_everywhere(jnp.concatenate([front_rows, up_rows], axis=0))
    owned_vec = lax.dynamic_slice_in_dim(grad_vec, row_index * shard_rows, shard_rows, 1)

    new_qkv, new_first_qkv, new_second_qkv = adamw(
        w_qkv, first_qkv, second_qkv, owned_qkv, RATE_MATRIX
    )
    new_out, new_first_out, new_second_out = adamw(
        w_out, first_out, second_out, owned_out.T, RATE_MATRIX
    )
    new_up, new_first_up, new_second_up = adamw(w_up, first_up, second_up, owned_up, RATE_MATRIX)
    new_down, new_first_down, new_second_down = adamw(
        w_down, first_down, second_down, owned_down.T, RATE_MATRIX
    )
    new_vectors, new_first_vectors, new_second_vectors = adamw(
        vectors, first_vectors, second_vectors, owned_vec, RATE_VECTOR
    )
    return (
        mixed_out,
        token_grad,
        new_qkv,
        new_out,
        new_up,
        new_down,
        new_vectors,
        new_first_qkv,
        new_first_out,
        new_first_up,
        new_first_down,
        new_first_vectors,
        new_second_qkv,
        new_second_out,
        new_second_up,
        new_second_down,
        new_second_vectors,
    )


def solution(mesh):
    by_token = P(("row", "col"), None)
    weights = (
        P("row", None, "col"),
        P("col", "row"),
        P("row", "col"),
        P("col", "row"),
        P(None, "row"),
    )
    return jax.shard_map(
        shards,
        mesh=mesh,
        in_specs=(by_token, by_token) + weights * 3,
        out_specs=(by_token, by_token) + weights * 3,
        check_vma=False,
    )
```

```python
import functools
import math

import jax
import jax.numpy as jnp
from jax import lax
from jax.experimental import pallas as pl
from jax.experimental.pallas import tpu as pltpu
from jax.sharding import PartitionSpec as P

HEAD_DIM = 64
LENGTH = 1024
STEP_NUMBER = 10
VEC_ROWS = 12
PAIR = 2 * HEAD_DIM
QUERY_BLOCK = 256
ROW_BLOCK = 256


EPS = 1e-05
BETA_ONE = 0.9
BETA_TWO = 0.999
ADAM_EPS = 1e-08
DECAY = 0.1
RATE_MATRIX = 0.04
RATE_VECTOR = 0.3

F32 = jnp.float32
BF16 = jnp.bfloat16


def normalize_rows(values_in):
    row_mean = jnp.mean(values_in, axis=-1, keepdims=True)
    centred = values_in - row_mean
    row_var = jnp.mean(centred * centred, axis=-1, keepdims=True)
    inv_std = lax.rsqrt(row_var + EPS)
    return (centred * inv_std, inv_std)


def norm_back(grad_in, normed, inv_std):
    mean_grad = jnp.mean(grad_in, axis=-1, keepdims=True)
    mean_cross = jnp.mean(grad_in * normed, axis=-1, keepdims=True)
    return inv_std * (grad_in - mean_grad - normed * mean_cross)


def adamw(weight, moment_one, moment_two, gradient, rate):
    first = BETA_ONE * moment_one + (1 - BETA_ONE) * gradient
    second = BETA_TWO * moment_two + (1 - BETA_TWO) * gradient * gradient
    first_hat = first / (1 - BETA_ONE**STEP_NUMBER)
    second_hat = second / (1 - BETA_TWO**STEP_NUMBER)
    updated = weight - rate * (first_hat / (jnp.sqrt(second_hat) + ADAM_EPS) + DECAY * weight)
    return (updated, first, second)


def swap_over(value, line):
    name, offset = line
    pairs = [(index, index ^ offset) for index in range(lax.axis_size(name))]
    return lax.ppermute(value, name, pairs)


def bit_offsets(low, high):
    offsets = []
    while low < high:
        offsets.append(low)
        low *= 2
    return offsets


def flip_order(blocks):
    count = blocks.shape[0]
    row = lax.axis_index("row")
    for offset in bit_offsets(1, count):
        cut = blocks.reshape((-1, 2, offset) + blocks.shape[1:])
        turned = jnp.where((row // offset) % 2 == 1, cut[:, ::-1], cut)
        blocks = turned.reshape(blocks.shape)
    return blocks


def gather_small(block):
    blocks = block[None]
    for offset in bit_offsets(1, lax.axis_size("row")):
        blocks = jnp.concatenate([blocks, swap_over(blocks, ("row", offset))], axis=0)
    return flip_order(blocks)


class Gathered:
    def __init__(self, arrays, table):
        self.arrays = arrays
        self.table = table
        self.rows = arrays[0].shape[1]
        self.cols = arrays[0].shape[2]
        if self.rows % 16:
            total = []
            for x in range(2):
                found = sorted((offset, array, at) for x_at, array, at, offset in table if x_at == x)
                blocks = jnp.stack([arrays[array][at] for _, array, at in found])
                total.append(flip_order(blocks).reshape(-1, self.cols))
            self.arrays = [jnp.stack(total)]
            self.table = [(0, 0, 0, 0), (1, 0, 1, 0)]
            self.rows = self.arrays[0].shape[1]


class Grid:
    def __init__(self, row_count):
        self.near_size = {8: 2, 64: 4}.get(row_count, 1)
        self.row_count = row_count
        self.far_count = row_count // self.near_size
        self.near = bit_offsets(1, self.near_size)
        self.x_line = ("col", 2)

    def gather_far(self, block):
        blocks = [block]
        for index in range(1, self.far_count):
            blocks.append(swap_over(block, ("row", index * self.near_size)))
        return blocks

    def gather_near(self, blocks):
        half = self.far_count // 2
        front, back = jnp.stack(blocks[:half]), jnp.stack(blocks[half:])
        front_at = [index * self.near_size for index in range(half)]
        back_at = [(index + half) * self.near_size for index in range(half)]
        back_x = swap_over(back, self.x_line)
        for offset in self.near:
            front = jnp.concatenate([front, swap_over(front, ("row", offset))], axis=0)
            front_at = front_at + [at ^ offset for at in front_at]
        back = jnp.concatenate([back, back_x], axis=0)
        back_at = [(x, at) for x in range(2) for at in back_at]
        arrays = [front, swap_over(front, self.x_line), back]
        table = [(x, x, index, at) for x in range(2) for index, at in enumerate(front_at)]
        table += [(x, 2, index, at) for index, (x, at) in enumerate(back_at)]
        for offset in self.near:
            sent = back if len(arrays) == 3 else jnp.concatenate(arrays[2:], axis=0)
            arrays.append(swap_over(sent, ("row", offset)))
            moved = [(x, at ^ offset) for x, at in back_at]
            table += [(x, len(arrays) - 1, index, at) for index, (x, at) in enumerate(moved)]
            back_at = back_at + moved
        return Gathered(arrays, table)

    def reduce_near(self, pair, hold=None):
        _, all_rows, cols = pair.shape
        rows = all_rows // self.row_count
        half = self.far_count // 2
        pair = pair.reshape((2, 2, half, self.near_size, rows, cols))
        front_x = swap_over(pair[1, 0], self.x_line)
        back = pair[:, 1]
        step = self.near_size // 2
        sent = swap_over(back[:, :, step:], ("row", step)) if step else None
        if hold is not None:
            front_x, sent, _ = lax.optimization_barrier((front_x, sent, hold))
        back = back.astype(F32)
        if step:
            back = back[:, :, :step] + sent.astype(F32)
        front = pair[0, 0].astype(F32) + front_x.astype(F32)
        back = self.reduce_bits(back, 2)
        back = back[0] + swap_over(back[1].astype(BF16), self.x_line).astype(F32)
        front = self.reduce_bits(front, 1)
        return jnp.concatenate([front, back], axis=0).reshape(self.far_count, rows, cols)

    def reduce_bits(self, parts, dim):
        while parts.shape[dim] > 1:
            step = parts.shape[dim] // 2
            kept = lax.slice_in_dim(parts, 0, step, axis=dim)
            sent = lax.slice_in_dim(parts, step, 2 * step, axis=dim).astype(BF16)
            parts = kept + swap_over(sent, ("row", step)).astype(F32)
        return parts

    def reduce_far(self, parts):
        low = parts.astype(BF16)
        arrived = [
            swap_over(low[index], ("row", index * self.near_size))
            for index in range(1, self.far_count)
        ]
        total = parts[0]
        for part in arrived:
            total = total + part.astype(F32)
        return total


def sum_everywhere(value):
    for name in ("col", "row"):
        for offset in bit_offsets(1, lax.axis_size(name)):
            value = value + swap_over(value, (name, offset))
    return value


def dot_nt(left, right):
    return lax.dot_general(left, right, (((1,), (1,)), ((), ())), preferred_element_type=F32)


def dot_nn(left, right):
    return lax.dot_general(left, right, (((1,), (0,)), ((), ())), preferred_element_type=F32)


def lane_pick(half):
    lanes = lax.broadcasted_iota(jnp.int32, (1, PAIR), 1)
    return jnp.where((lanes // HEAD_DIM) == half, 1.0, 0.0).astype(BF16)


def causal_block(size):
    key_at = lax.broadcasted_iota(jnp.int32, (size, size), 0)
    query_at = lax.broadcasted_iota(jnp.int32, (size, size), 1)
    return key_at <= query_at


def attend_kernel(q_ref, k_ref, v_ref, out_ref, turned_ref, lse_ref):
    length = q_ref.shape[0]
    block = min(QUERY_BLOCK, length)
    allowed = causal_block(block)
    values_t = v_ref[...].T
    scaling = jnp.asarray(HEAD_DIM**-0.5, BF16)
    for first in range(0, length, block):
        last = first + block
        query = q_ref[first:last, :] * scaling
        outs = []
        for half in range(2):
            rows = slice(half * HEAD_DIM, (half + 1) * HEAD_DIM)
            query_half = query * lane_pick(half)
            diag = dot_nt(k_ref[first:last, :], query_half)
            diag = jnp.where(allowed, diag, -1e30)
            top = jnp.max(diag, axis=0, keepdims=True)
            if first:
                rest = dot_nt(k_ref[0:first, :], query_half)
                top = jnp.maximum(top, jnp.max(rest, axis=0, keepdims=True))
            diag = jnp.exp(diag - top)
            total = jnp.sum(diag, axis=0, keepdims=True)
            if first:
                rest = jnp.exp(rest - top)
                total = total + jnp.sum(rest, axis=0, keepdims=True)
            inverse = 1.0 / total
            result = dot_nn(values_t[rows, first:last], (diag * inverse).astype(BF16))
            if first:
                result = result + dot_nn(values_t[rows, 0:first], (rest * inverse).astype(BF16))
            outs.append(result)
            lse_ref[0, half : half + 1, first:last] = top + jnp.log(total)
        turned = jnp.concatenate(outs, axis=0)
        out_ref[first:last, :] = turned.T.astype(BF16)
        turned_ref[:, first:last] = turned.astype(BF16)


def attend_forward(qkv):
    length, width = qkv.shape
    pairs = width // (3 * PAIR)

    def lanes(part):
        return pl.BlockSpec((length, PAIR), lambda pair: (0, part * pairs + pair))

    return pl.pallas_call(
        attend_kernel,
        grid=(pairs,),
        in_specs=[lanes(0), lanes(1), lanes(2)],
        out_specs=[
            lanes(0),
            pl.BlockSpec((PAIR, length), lambda pair: (pair, 0)),
            pl.BlockSpec((1, 8, length), lambda pair: (pair, 0, 0)),
        ],
        out_shape=[
            jax.ShapeDtypeStruct((length, pairs * PAIR), BF16),
            jax.ShapeDtypeStruct((pairs * PAIR, length), BF16),
            jax.ShapeDtypeStruct((pairs, 8, length), F32),
        ],
        compiler_params=pltpu.CompilerParams(vmem_limit_bytes=40 * 2**20),
        cost_estimate=pl.CostEstimate(
            flops=pairs * 2 * 4 * length * length * HEAD_DIM,
            bytes_accessed=4 * length * pairs * PAIR * 2,
            transcendentals=pairs * length * length,
        ),
        name="attend_forward",
    )(qkv, qkv, qkv)


def attend_back_kernel(q_ref, k_ref, v_ref, go_ref, lse_ref, grad_ref, gk_sum, gv_sum):
    length = q_ref.shape[0]
    pairs = grad_ref.shape[1] // (3 * PAIR)
    block = min(QUERY_BLOCK, length)
    allowed = causal_block(block)
    keys_t = k_ref[...].T
    scaling = jnp.asarray(HEAD_DIM**-0.5, BF16)
    pair = pl.program_id(0)

    def lanes(part):
        return pl.ds(pl.multiple_of((part * pairs + pair) * PAIR, PAIR), PAIR)

    gk_sum[...] = jnp.zeros_like(gk_sum)
    gv_sum[...] = jnp.zeros_like(gv_sum)
    for first in range(0, length, block):
        last = first + block
        query = q_ref[first:last, :] * scaling
        grad_out = go_ref[first:last, :]
        outs = []
        for half in range(2):
            rows = slice(half * HEAD_DIM, (half + 1) * HEAD_DIM)
            pick = lane_pick(half)
            query_half = query * pick
            grad_half = grad_out * pick
            lse = lse_ref[0, half : half + 1, first:last]
            spans = [(first, last)] if first == 0 else [(0, first), (first, last)]
            probs, grads, inner = [], [], None
            for low, high in spans:
                scores = dot_nt(k_ref[low:high, :], query_half)
                if low == first:
                    scores = jnp.where(allowed, scores, -1e30)
                prob = jnp.exp(scores - lse)
                grad_prob = dot_nt(v_ref[low:high, :], grad_half)
                part = jnp.sum(prob * grad_prob, axis=0, keepdims=True)
                inner = part if inner is None else inner + part
                probs.append(prob)
                grads.append(grad_prob)
            result = None
            for (low, high), prob, grad_prob in zip(spans, probs, grads):
                grad_score = (prob * (grad_prob - inner)).astype(BF16)
                gk_sum[low:high, :] += dot_nn(grad_score, query_half)
                gv_sum[low:high, :] += dot_nn(prob.astype(BF16), grad_half)
                part = dot_nn(keys_t[rows, low:high], grad_score)
                result = part if result is None else result + part
            outs.append(result)
        grad_query = jnp.concatenate(outs, axis=0).T * (HEAD_DIM**-0.5)
        grad_ref[first:last, lanes(0)] = grad_query.astype(BF16)
    grad_ref[:, lanes(1)] = gk_sum[...].astype(BF16)
    grad_ref[:, lanes(2)] = gv_sum[...].astype(BF16)


def attend_backward(qkv, grad_heads, lse):
    length, width = qkv.shape
    pairs = width // (3 * PAIR)

    def lanes(part):
        return pl.BlockSpec((length, PAIR), lambda pair: (0, part * pairs + pair))

    return pl.pallas_call(
        attend_back_kernel,
        grid=(pairs,),
        in_specs=[
            lanes(0),
            lanes(1),
            lanes(2),
            lanes(0),
            pl.BlockSpec((1, 8, length), lambda pair: (pair, 0, 0)),
        ],
        out_specs=pl.BlockSpec((length, width), lambda pair: (0, 0)),
        out_shape=jax.ShapeDtypeStruct((length, width), BF16),
        scratch_shapes=[pltpu.VMEM((length, PAIR), F32), pltpu.VMEM((length, PAIR), F32)],
        compiler_params=pltpu.CompilerParams(vmem_limit_bytes=40 * 2**20),
        cost_estimate=pl.CostEstimate(
            flops=pairs * 2 * 10 * length * length * HEAD_DIM,
            bytes_accessed=7 * length * pairs * PAIR * 2,
            transcendentals=pairs * length * length,
        ),
        name="attend_backward",
    )(qkv, qkv, qkv, grad_heads, lse)


def rows_of(block, width):
    return pl.BlockSpec((block, width), lambda step: (step, 0))


def whole(shape):
    return pl.BlockSpec(shape, lambda *step: (0,) * len(shape))


def shaped(shape, dtype):
    return jax.ShapeDtypeStruct(shape, dtype)


def cost(flops, arrays):
    return pl.CostEstimate(flops=flops, bytes_accessed=arrays, transcendentals=0)


PARAMS = pltpu.CompilerParams(vmem_limit_bytes=48 * 2**20)


ANYWHERE = pl.BlockSpec(memory_space=pl.ANY)


def weight_copies(gathered, refs, held, sems):
    row = lax.axis_index("row")
    copies = ([], [])
    for number, (x, array, at, offset) in enumerate(gathered.table):
        if len(gathered.table) > 2:
            start = pl.multiple_of((row ^ offset) * gathered.rows, 16)
        else:
            start = 0
        target = held.at[x, pl.ds(start, gathered.rows), :]
        copies[x].append(
            pltpu.make_async_copy(refs[array].at[at], target, sems.at[number])
        )
    return copies


def weight_scratch(gathered):
    all_rows = len(gathered.table) // 2 * gathered.rows
    return [
        pltpu.VMEM((2, all_rows, gathered.cols), BF16),
        pltpu.SemaphoreType.DMA((len(gathered.table),)),
    ]


def start_all(copies):
    for copy in copies:
        copy.start()


def wait_all(copies):
    for copy in copies:
        copy.wait()


def store_rows(value, out_ref, x, lanes, count):
    rows = value.shape[0] // count
    if rows % 16:
        out_ref[x, :, lanes] = value
        return
    row = lax.axis_index("row")
    for index in range(count):
        start = pl.multiple_of((row ^ index) * rows, 16)
        out_ref[x, pl.ds(start, rows), lanes] = value[index * rows : (index + 1) * rows]


def relative_rows(pair, count):
    _, all_rows, cols = pair.shape
    if all_rows // count % 16 == 0:
        return pair
    blocks = jnp.moveaxis(pair.reshape(2, count, -1, cols), 1, 0)
    return jnp.moveaxis(flip_order(blocks), 0, 1).reshape(pair.shape)


def turn(value):
    return value.T


def first_norm_kernel(gathered, cols, tokens_ref, vec_ref, bias_ref, *refs):
    count = len(gathered.arrays)
    norm_ref, qkv_ref, out_w_ref, held, sems = refs[count:]
    copies = weight_copies(gathered, refs[:count], held, sems)
    third = cols // 3

    @pl.when(pl.program_id(0) == 0)
    def _():
        start_all(copies[0] + copies[1])

    normed, _ = normalize_rows(tokens_ref[...].astype(F32))
    first_in = (normed * vec_ref[0:1, :] + vec_ref[1:2, :]).astype(BF16)
    norm_ref[...] = first_in

    @pl.when(pl.program_id(0) == 0)
    def _():
        wait_all(copies[0] + copies[1])
        for x in range(2):
            out_w_ref[:, x * third : (x + 1) * third] = held[x, :, held.shape[2] - third :]

    for x in range(2):
        result = dot_nn(first_in, held[x, :, :cols])
        for part in range(3):
            lanes = slice((2 * part + x) * third, (2 * part + x + 1) * third)
            value = result[:, part * third : (part + 1) * third] + bias_ref[0:1, lanes]
            qkv_ref[:, lanes] = value.astype(BF16)


def first_norm(tokens, vec_all, bias, gathered, width_loc):
    length, width = tokens.shape
    cols = 3 * width_loc
    return pl.pallas_call(
        functools.partial(first_norm_kernel, gathered, cols),
        grid=(length // ROW_BLOCK,),
        in_specs=[rows_of(ROW_BLOCK, width), whole(vec_all.shape), whole(bias.shape)]
        + [ANYWHERE] * len(gathered.arrays),
        out_specs=[
            rows_of(ROW_BLOCK, width),
            rows_of(ROW_BLOCK, 2 * cols),
            whole((width, 2 * width_loc)),
        ],
        out_shape=[
            shaped((length, width), BF16),
            shaped((length, 2 * cols), BF16),
            shaped((width, 2 * width_loc), BF16),
        ],
        scratch_shapes=weight_scratch(gathered),
        compiler_params=PARAMS,
        cost_estimate=cost(4 * length * width * cols, 2 * length * (2 * width + cols)),
        name="first_norm",
    )(tokens, vec_all, bias, *gathered.arrays)


def attended_kernel(
    heads_ref, partner_ref, own_ref, other_ref, tokens_ref, vec_ref, first_ref, cot_ref,
    hidden_ref, norm_ref, norm_turned_ref, first_turned_ref, cot_turned_ref,
):
    attended = dot_nt(heads_ref[...], own_ref[...]) + dot_nt(partner_ref[...], other_ref[...])
    hidden = tokens_ref[...].astype(F32) + attended + vec_ref[4:5, :]
    hidden_ref[...] = hidden
    normed, _ = normalize_rows(hidden)
    second_in = (normed * vec_ref[5:6, :] + vec_ref[6:7, :]).astype(BF16)
    norm_ref[...] = second_in
    norm_turned_ref[...] = turn(second_in)
    first_turned_ref[...] = turn(first_ref[...])
    cot_turned_ref[...] = turn(cot_ref[...])


def attended_norm(heads, partner_heads, own_out, partner_out, tokens, vec_all, first_in, cot):
    length, width = tokens.shape
    cols = heads.shape[1]
    full = rows_of(ROW_BLOCK, width)
    turned = pl.BlockSpec((width, ROW_BLOCK), lambda step: (0, step))
    return pl.pallas_call(
        attended_kernel,
        grid=(length // ROW_BLOCK,),
        in_specs=[
            rows_of(ROW_BLOCK, cols),
            rows_of(ROW_BLOCK, cols),
            whole(own_out.shape),
            whole(partner_out.shape),
            full,
            whole(vec_all.shape),
            full,
            full,
        ],
        out_specs=[full, full, turned, turned, turned],
        out_shape=[shaped((length, width), F32), shaped((length, width), BF16)]
        + [shaped((width, length), BF16)] * 3,
        compiler_params=PARAMS,
        cost_estimate=cost(4 * length * width * cols, length * width * 20),
        name="attended_norm",
    )(heads, partner_heads, own_out, partner_out, tokens, vec_all, first_in, cot)


def feed_kernel(gathered, norm_ref, cot_ref, bias_ref, *refs):
    count = len(gathered.arrays)
    act_ref, gup_ref, bias_sum_ref, out_ref, back_ref, back_low_ref, held, sems = refs[count:]
    copies = weight_copies(gathered, refs[:count], held, sems)
    step = pl.program_id(0)
    length = norm_ref.shape[0]
    curve, cubic = math.sqrt(2 / math.pi), 0.044715
    cols = held.shape[2] // 2
    block = act_ref.shape[1]
    per_x = cols // block
    x = step // per_x
    up_lanes = pl.ds(pl.multiple_of(step % per_x * block, 128), block)
    down_lanes = pl.ds(pl.multiple_of(cols + step % per_x * block, 128), block)

    @pl.when(step == 0)
    def _():
        start_all(copies[0] + copies[1])
        out_ref[...] = jnp.zeros_like(out_ref)
        back_ref[...] = jnp.zeros_like(back_ref)
        wait_all(copies[0])

    @pl.when(step == per_x)
    def _():
        wait_all(copies[1])

    bias_sum = jnp.zeros(bias_ref.shape, F32)
    for first in range(0, length, ROW_BLOCK):
        rows = slice(first, first + ROW_BLOCK)
        up = dot_nn(norm_ref[rows, :], held[x, :, up_lanes]) + bias_ref[...]
        square = up * up
        tanh = jnp.tanh(curve * up * (1.0 + cubic * square))
        act = (0.5 * up * (1.0 + tanh)).astype(BF16)
        act_ref[rows, :] = act
        slope = 0.5 * (1.0 + tanh) + 0.5 * up * (1.0 - tanh * tanh) * (
            curve * (1.0 + 3.0 * cubic * square)
        )
        grad_up = (dot_nn(cot_ref[rows, :], held[x, :, down_lanes]) * slope).astype(BF16)
        gup_ref[rows, :] = grad_up
        bias_sum = bias_sum + jnp.sum(grad_up.astype(F32), axis=0, keepdims=True)
        out_ref[rows, :] += dot_nt(act, held[x, :, down_lanes])
        back_ref[rows, :] += dot_nt(grad_up, held[x, :, up_lanes])
    bias_sum_ref[...] = bias_sum

    @pl.when(step == pl.num_programs(0) - 1)
    def _():
        back_low_ref[...] = back_ref[...].astype(BF16)


def feed(norm, cot, bias, gathered):
    length, width = norm.shape
    hidden = bias.shape[1]
    block = hidden // 4
    tall = pl.BlockSpec((length, block), lambda step: (0, step))
    flat = pl.BlockSpec((1, block), lambda step: (0, step))
    full = whole((length, width))
    return pl.pallas_call(
        functools.partial(feed_kernel, gathered),
        grid=(hidden // block,),
        in_specs=[full, full, flat] + [ANYWHERE] * len(gathered.arrays),
        out_specs=[tall, tall, flat, full, full, full],
        out_shape=[
            shaped((length, hidden), BF16),
            shaped((length, hidden), BF16),
            shaped((1, hidden), F32),
            shaped((length, width), F32),
            shaped((length, width), F32),
            shaped((length, width), BF16),
        ],
        scratch_shapes=weight_scratch(gathered),
        compiler_params=PARAMS,
        cost_estimate=cost(8 * length * width * hidden, 4 * length * (width + hidden)),
        name="feed",
    )(norm, cot, bias, *gathered.arrays)


def feed_grads_kernel(row_count, cot_ref, norm_ref, act_ref, gup_ref, out_ref):
    kind = pl.program_id(0)

    @pl.when(kind == 0)
    def _():
        value = dot_nn(cot_ref[...], act_ref[...]).astype(BF16)
        store_rows(value, out_ref, 0, slice(None), row_count)

    @pl.when(kind == 1)
    def _():
        value = dot_nn(norm_ref[...], gup_ref[...]).astype(BF16)
        store_rows(value, out_ref, 0, slice(None), row_count)


def feed_grads(cot_turned, norm_turned, act, grad_up, row_count):
    width, length = cot_turned.shape
    hidden = act.shape[1]
    block = hidden // 2
    return pl.pallas_call(
        functools.partial(feed_grads_kernel, row_count),
        grid=(2, 2),
        in_specs=[
            whole((width, length)),
            whole((width, length)),
            pl.BlockSpec((length, block), lambda kind, x: (0, jnp.where(kind == 0, x, 1))),
            pl.BlockSpec((length, block), lambda kind, x: (0, jnp.where(kind == 1, x, 0))),
        ],
        out_specs=pl.BlockSpec((1, width, block), lambda kind, x: (x, 0, 1 - kind)),
        out_shape=shaped((2, width, hidden), BF16),
        compiler_params=PARAMS,
        cost_estimate=cost(4 * length * width * hidden, 4 * length * (width + hidden)),
        name="feed_grads",
    )(cot_turned, norm_turned, act, grad_up)


def second_back_kernel(
    part_ref, other_ref, hidden_ref, cot_ref, vec_ref, out_w_ref, turned_ref,
    grad_ref, heads_ref, sum_ref, out_grad_ref, total,
):
    step = pl.program_id(0)
    normed, inv_std = normalize_rows(hidden_ref[...])
    part = part_ref[...]
    cot = cot_ref[...].astype(F32)
    grad_second = part + other_ref[...].astype(F32)
    grad = cot + norm_back(grad_second * vec_ref[5:6, :], normed, inv_std)
    grad_ref[...] = grad
    low = grad.astype(BF16)
    heads_ref[...] = dot_nn(low, out_w_ref[...]).astype(BF16)

    @pl.when(step == 0)
    def _():
        sum_ref[...] = jnp.zeros_like(sum_ref)
        total[...] = jnp.zeros_like(total)

    total[...] += dot_nn(turned_ref[...], low)
    for row, value in enumerate((grad, part * normed, part, cot)):
        sum_ref[row : row + 1, :] += jnp.sum(value, axis=0, keepdims=True)

    @pl.when(step == pl.num_programs(0) - 1)
    def _():
        out_grad_ref[...] = total[...].T.astype(BF16)


def second_back(part, other, hidden, cot, vec_all, out_w, heads_turned):
    length, width = part.shape
    cols = out_w.shape[1]
    full = rows_of(ROW_BLOCK, width)
    return pl.pallas_call(
        second_back_kernel,
        grid=(length // ROW_BLOCK,),
        in_specs=[full, full, full, full, whole(vec_all.shape), whole(out_w.shape)]
        + [pl.BlockSpec((cols, ROW_BLOCK), lambda step: (0, step))],
        out_specs=[full, rows_of(ROW_BLOCK, cols), whole((8, width)), whole((width, cols))],
        out_shape=[
            shaped((length, width), F32),
            shaped((length, cols), BF16),
            shaped((8, width), F32),
            shaped((width, cols), BF16),
        ],
        scratch_shapes=[pltpu.VMEM((cols, width), F32)],
        compiler_params=PARAMS,
        cost_estimate=cost(4 * length * width * cols, length * width * 20),
        name="second_back",
    )(part, other, hidden, cot, vec_all, out_w, heads_turned)


def qkv_grads_kernel(row_count, norm_ref, grad_ref, out_grad_ref, out_ref):
    part = pl.program_id(0)
    half = grad_ref.shape[1] // 2
    for index in range(4):

        @pl.when(part == index)
        def _():
            if index == 3:
                grads = out_grad_ref[...]
            else:
                grads = dot_nn(norm_ref[...], grad_ref[...]).astype(BF16)
            lanes = slice(index * half, (index + 1) * half)
            for x in range(2):
                store_rows(grads[:, x * half : (x + 1) * half], out_ref, x, lanes, row_count)


def qkv_grads(norm_turned, grad_qkv, out_grad, row_count):
    width, length = norm_turned.shape
    cols = out_grad.shape[1]
    return pl.pallas_call(
        functools.partial(qkv_grads_kernel, row_count),
        grid=(4,),
        in_specs=[
            whole((width, length)),
            pl.BlockSpec((length, cols), lambda part: (0, jnp.minimum(part, 2))),
            whole((width, cols)),
        ],
        out_specs=whole((2, width, 2 * cols)),
        out_shape=shaped((2, width, 2 * cols), BF16),
        compiler_params=PARAMS,
        cost_estimate=cost(6 * length * width * cols, 4 * length * (2 * width + 2 * cols)),
        name="qkv_grads",
    )(norm_turned, grad_qkv, out_grad)


def first_back_kernel(gathered, cols, grad_ref, tokens_ref, after_ref, *refs):
    count = len(gathered.arrays)
    part_ref, sum_ref, bias_ref, held, sems = refs[count:]
    copies = weight_copies(gathered, refs[:count], held, sems)
    third = cols // 3

    @pl.when(pl.program_id(0) == 0)
    def _():
        start_all(copies[0] + copies[1])
        sum_ref[...] = jnp.zeros_like(sum_ref)
        bias_ref[...] = jnp.zeros_like(bias_ref)
        wait_all(copies[0] + copies[1])

    part = None
    for x in range(2):
        grads = jnp.concatenate(
            [grad_ref[:, (2 * at + x) * third : (2 * at + x + 1) * third] for at in range(3)], axis=1
        )
        product = dot_nt(grads, held[x, :, :cols])
        part = product if part is None else part + product
    part_ref[...] = part
    normed, _ = normalize_rows(tokens_ref[...].astype(F32))
    for row, value in enumerate((part * normed, part)):
        sum_ref[row : row + 1, :] += jnp.sum(value, axis=0, keepdims=True)
    bias_ref[0:1, :] += jnp.sum(grad_ref[...].astype(F32), axis=0, keepdims=True)


def first_back(grad_qkv, tokens, gathered, width_loc, after):
    length, width = tokens.shape
    cols = grad_qkv.shape[1]
    return pl.pallas_call(
        functools.partial(first_back_kernel, gathered, 3 * width_loc),
        grid=(length // ROW_BLOCK,),
        in_specs=[rows_of(ROW_BLOCK, cols), rows_of(ROW_BLOCK, width), ANYWHERE]
        + [ANYWHERE] * len(gathered.arrays),
        out_specs=[rows_of(ROW_BLOCK, width), whole((8, width)), whole((8, cols))],
        out_shape=[
            shaped((length, width), F32),
            shaped((8, width), F32),
            shaped((8, cols), F32),
        ],
        scratch_shapes=weight_scratch(gathered),
        compiler_params=PARAMS,
        cost_estimate=cost(2 * length * width * cols, length * (6 * width + 2 * cols)),
        name="first_back",
    )(grad_qkv, tokens, after, *gathered.arrays)


def token_back_kernel(core_ref, part_ref, other_ref, tokens_ref, grad_ref, vec_ref, out_ref):
    normed, inv_std = normalize_rows(tokens_ref[...].astype(F32))
    grad_first = part_ref[...] + other_ref[...].astype(F32)
    out_ref[...] = grad_ref[...] + norm_back(grad_first * vec_ref[0:1, :], normed, inv_std)


def token_back(core, part, other, tokens, grad_hidden, vec_all):
    rows, width = tokens.shape
    steps = rows // ROW_BLOCK
    own = pl.BlockSpec((ROW_BLOCK, width), lambda step, core_ref: (core_ref[0] * steps + step, 0))
    here = pl.BlockSpec((ROW_BLOCK, width), lambda step, core_ref: (step, 0))
    return pl.pallas_call(
        token_back_kernel,
        grid_spec=pltpu.PrefetchScalarGridSpec(
            num_scalar_prefetch=1,
            grid=(steps,),
            in_specs=[own, here, here, own, whole(vec_all.shape)],
            out_specs=here,
        ),
        out_shape=shaped((rows, width), F32),
        compiler_params=PARAMS,
        cost_estimate=cost(rows * width * 20, rows * width * 16),
        name="token_back",
    )(core.reshape(1), part, other, tokens, grad_hidden, vec_all)


def shards(
    tokens,
    cotangent,
    w_qkv,
    w_out,
    w_up,
    w_down,
    vectors,
    first_qkv,
    first_out,
    first_up,
    first_down,
    first_vectors,
    second_qkv,
    second_out,
    second_up,
    second_down,
    second_vectors,
):
    row_index = lax.axis_index("row")
    col_index = lax.axis_index("col")
    col_count = lax.axis_size("col")
    grid = Grid(lax.axis_size("row"))
    core_line = ("col", 1)
    core = col_index % 2
    other_col = col_index ^ 2
    rows_loc, width = tokens.shape
    width_loc = w_qkv.shape[2]
    width_core = 2 * width_loc
    hidden_loc = w_up.shape[1]
    shard_rows = w_up.shape[0]

    pad = -3 * width_loc % 128
    pack_qkv = jnp.concatenate(
        [w_qkv[:, part].astype(BF16) for part in range(3)]
        + [jnp.zeros((shard_rows, pad), BF16), w_out.T.astype(BF16)],
        axis=1,
    )
    pack_feed = jnp.concatenate([w_up.astype(BF16), w_down.T.astype(BF16)], axis=1)

    def both_halves(mine):
        other = swap_over(mine, core_line)
        return jnp.where(
            core == 0,
            jnp.concatenate([mine, other], axis=0),
            jnp.concatenate([other, mine], axis=0),
        )

    def own_rows(value):
        return lax.dynamic_slice_in_dim(value, core * rows_loc, rows_loc, 0)

    def partner_rows(value):
        return lax.dynamic_slice_in_dim(value, (1 - core) * rows_loc, rows_loc, 0)

    far_qkv = grid.gather_far(pack_qkv)
    vec_blocks = gather_small(vectors.astype(BF16))
    pack_feed, *far_qkv = lax.optimization_barrier((pack_feed, *far_qkv))
    near_qkv = grid.gather_near(far_qkv)
    far_feed = grid.gather_far(pack_feed)
    *far_feed, _ = lax.optimization_barrier((*far_feed, near_qkv.arrays[-1]))
    near_feed = grid.gather_near(far_feed)

    all_tokens = both_halves(tokens)
    all_cot = both_halves(cotangent)
    vec_all = jnp.swapaxes(vec_blocks, 0, 1).reshape(VEC_ROWS, width).astype(F32)

    def cat_blocks(vec_row, size):
        return jnp.concatenate(
            [
                lax.dynamic_slice_in_dim(vec_row, col_index * size, size, 0),
                lax.dynamic_slice_in_dim(vec_row, other_col * size, size, 0),
            ]
        )

    bias_qkv = jnp.concatenate(
        [
            cat_blocks(vec_all[2], width_loc),
            jnp.zeros((width_core,), F32),
            cat_blocks(vec_all[3], width_loc),
        ]
    )
    bias_up = cat_blocks(vec_all[8:].reshape(-1), hidden_loc)
    first_in, qkv, full_out = first_norm(
        all_tokens, vec_all, bias_qkv[None], near_qkv, width_loc
    )
    partner_out = swap_over(full_out, core_line)
    heads_low, heads_turned, lse = attend_forward(qkv)
    partner_heads = swap_over(heads_low, core_line)
    hidden_state, second_in, second_turned, first_turned, cot_turned = attended_norm(
        heads_low, partner_heads, full_out, partner_out, all_tokens, vec_all, first_in, all_cot
    )
    activated, grad_upper, grad_bias_up, down_part, second_part, second_low = feed(
        second_in, all_cot, bias_up[None], near_feed
    )

    second_other = swap_over(second_low, core_line)
    pair_feed = feed_grads(cot_turned, second_turned, activated, grad_upper, grid.row_count)
    pair_feed = relative_rows(pair_feed, grid.row_count)
    grad_hidden, grad_heads, second_sums, out_grad = second_back(
        second_part, second_other, hidden_state, all_cot, vec_all, full_out, heads_turned
    )
    down_other = swap_over(partner_rows(down_part).astype(BF16), core_line).astype(F32)
    mixed_out = own_rows(hidden_state) + own_rows(down_part) + down_other + vec_all[7]
    grad_qkv_low = attend_backward(qkv, grad_heads, lse)
    pair_qkv = qkv_grads(first_turned, grad_qkv_low, out_grad, grid.row_count)
    first_part, first_sums, bias_sums = first_back(
        grad_qkv_low, all_tokens, near_qkv, width_loc, pair_qkv
    )
    pair_qkv = relative_rows(pair_qkv, grid.row_count)
    first_other = swap_over(partner_rows(first_part).astype(BF16), core_line)
    token_grad = token_back(core, first_part, first_other, tokens, grad_hidden, vec_all)

    owned_feed = grid.reduce_far(grid.reduce_near(pair_feed, grad_qkv_low))
    owned_up, owned_down = owned_feed[:, :hidden_loc], owned_feed[:, hidden_loc:]
    owned_pack = grid.reduce_far(grid.reduce_near(pair_qkv))
    owned_qkv = jnp.stack(
        [owned_pack[:, part * width_loc : (part + 1) * width_loc] for part in range(3)], axis=1
    )
    owned_out = owned_pack[:, 3 * width_loc :]

    def placed(part_row, length):
        size = part_row.shape[0] // 2
        start = jnp.zeros((length,), F32)
        start = lax.dynamic_update_slice_in_dim(start, part_row[:size], col_index * size, 0)
        return lax.dynamic_update_slice_in_dim(start, part_row[size:], other_col * size, 0)

    front_rows = jnp.stack(
        [
            first_sums[0],
            first_sums[1],
            placed(bias_sums[0, :width_core], width),
            placed(bias_sums[0, 2 * width_core :], width),
            0.5 * second_sums[0],
            second_sums[1],
            second_sums[2],
            0.5 * second_sums[3],
        ]
    )
    up_rows = placed(grad_bias_up[0], hidden_loc * col_count).reshape(-1, width)
    grad_vec = sum_everywhere(jnp.concatenate([front_rows, up_rows], axis=0))
    owned_vec = lax.dynamic_slice_in_dim(grad_vec, row_index * shard_rows, shard_rows, 1)

    new_qkv, new_first_qkv, new_second_qkv = adamw(
        w_qkv, first_qkv, second_qkv, owned_qkv, RATE_MATRIX
    )
    new_out, new_first_out, new_second_out = adamw(
        w_out, first_out, second_out, owned_out.T, RATE_MATRIX
    )
    new_up, new_first_up, new_second_up = adamw(w_up, first_up, second_up, owned_up, RATE_MATRIX)
    new_down, new_first_down, new_second_down = adamw(
        w_down, first_down, second_down, owned_down.T, RATE_MATRIX
    )
    new_vectors, new_first_vectors, new_second_vectors = adamw(
        vectors, first_vectors, second_vectors, owned_vec, RATE_VECTOR
    )
    return (
        mixed_out,
        token_grad,
        new_qkv,
        new_out,
        new_up,
        new_down,
        new_vectors,
        new_first_qkv,
        new_first_out,
        new_first_up,
        new_first_down,
        new_first_vectors,
        new_second_qkv,
        new_second_out,
        new_second_up,
        new_second_down,
        new_second_vectors,
    )


def solution(mesh):
    by_token = P(("row", "col"), None)
    weights = (
        P("row", None, "col"),
        P("col", "row"),
        P("row", "col"),
        P("col", "row"),
        P(None, "row"),
    )
    return jax.shard_map(
        shards,
        mesh=mesh,
        in_specs=(by_token, by_token) + weights * 3,
        out_specs=(by_token, by_token) + weights * 3,
        check_vma=False,
    )
```

```python
import functools
import math

import jax
import jax.numpy as jnp
from jax import lax
from jax.experimental import pallas as pl
from jax.experimental.pallas import tpu as pltpu
from jax.sharding import PartitionSpec as P

HEAD_DIM = 64
LENGTH = 1024
STEP_NUMBER = 10
VEC_ROWS = 12
PAIR = 2 * HEAD_DIM
QUERY_BLOCK = 256
ROW_BLOCK = 256


EPS = 1e-05
BETA_ONE = 0.9
BETA_TWO = 0.999
ADAM_EPS = 1e-08
DECAY = 0.1
RATE_MATRIX = 0.04
RATE_VECTOR = 0.3

F32 = jnp.float32
BF16 = jnp.bfloat16


def normalize_rows(values_in):
    row_mean = jnp.mean(values_in, axis=-1, keepdims=True)
    centred = values_in - row_mean
    row_var = jnp.mean(centred * centred, axis=-1, keepdims=True)
    inv_std = lax.rsqrt(row_var + EPS)
    return (centred * inv_std, inv_std)


def norm_back(grad_in, normed, inv_std):
    mean_grad = jnp.mean(grad_in, axis=-1, keepdims=True)
    mean_cross = jnp.mean(grad_in * normed, axis=-1, keepdims=True)
    return inv_std * (grad_in - mean_grad - normed * mean_cross)


def adamw(weight, moment_one, moment_two, gradient, rate):
    first = BETA_ONE * moment_one + (1 - BETA_ONE) * gradient
    second = BETA_TWO * moment_two + (1 - BETA_TWO) * gradient * gradient
    first_hat = first / (1 - BETA_ONE**STEP_NUMBER)
    second_hat = second / (1 - BETA_TWO**STEP_NUMBER)
    updated = weight - rate * (first_hat / (jnp.sqrt(second_hat) + ADAM_EPS) + DECAY * weight)
    return (updated, first, second)


def swap_over(value, line):
    name, offset = line
    pairs = [(index, index ^ offset) for index in range(lax.axis_size(name))]
    return lax.ppermute(value, name, pairs)


def bit_offsets(low, high):
    offsets = []
    while low < high:
        offsets.append(low)
        low *= 2
    return offsets


def flip_order(blocks):
    count = blocks.shape[0]
    row = lax.axis_index("row")
    for offset in bit_offsets(1, count):
        cut = blocks.reshape((-1, 2, offset) + blocks.shape[1:])
        turned = jnp.where((row // offset) % 2 == 1, cut[:, ::-1], cut)
        blocks = turned.reshape(blocks.shape)
    return blocks


class Gathered:
    def __init__(self, arrays, table):
        self.arrays = arrays
        self.table = table
        self.rows = arrays[0].shape[1]
        self.cols = arrays[0].shape[2]
        if self.rows % 16:
            total = []
            for x in range(2):
                found = sorted((offset, array, at) for x_at, array, at, offset in table if x_at == x)
                blocks = jnp.stack([arrays[array][at] for _, array, at in found])
                total.append(flip_order(blocks).reshape(-1, self.cols))
            self.arrays = [jnp.stack(total)]
            self.table = [(0, 0, 0, 0), (1, 0, 1, 0)]
            self.rows = self.arrays[0].shape[1]


class Grid:
    def __init__(self, row_count):
        self.near_size = {8: 2, 64: 4}.get(row_count, 1)
        self.row_count = row_count
        self.far_count = row_count // self.near_size
        self.near = bit_offsets(1, self.near_size)
        self.x_line = ("col", 2)

    def gather_far(self, block):
        blocks = [block]
        for index in range(1, self.far_count):
            blocks.append(swap_over(block, ("row", index * self.near_size)))
        return blocks

    def gather_near(self, blocks):
        half = self.far_count // 2
        front, back = jnp.stack(blocks[:half]), jnp.stack(blocks[half:])
        front_at = [index * self.near_size for index in range(half)]
        back_at = [(index + half) * self.near_size for index in range(half)]
        back_x = swap_over(back, self.x_line)
        for offset in self.near:
            front = jnp.concatenate([front, swap_over(front, ("row", offset))], axis=0)
            front_at = front_at + [at ^ offset for at in front_at]
        back = jnp.concatenate([back, back_x], axis=0)
        back_at = [(x, at) for x in range(2) for at in back_at]
        arrays = [front, swap_over(front, self.x_line), back]
        table = [(x, x, index, at) for x in range(2) for index, at in enumerate(front_at)]
        table += [(x, 2, index, at) for index, (x, at) in enumerate(back_at)]
        for offset in self.near:
            sent = back if len(arrays) == 3 else jnp.concatenate(arrays[2:], axis=0)
            arrays.append(swap_over(sent, ("row", offset)))
            moved = [(x, at ^ offset) for x, at in back_at]
            table += [(x, len(arrays) - 1, index, at) for index, (x, at) in enumerate(moved)]
            back_at = back_at + moved
        return Gathered(arrays, table)

    def split(self, pair):
        _, all_rows, cols = pair.shape
        blocks = jnp.moveaxis(pair.reshape(2, self.row_count, -1, cols), 1, 0)
        blocks = jnp.moveaxis(flip_order(blocks), 0, 1)
        rows = blocks.shape[2]
        half = self.row_count // 2
        back = blocks[:, half:].reshape(2, self.far_count // 2, 2, -1, rows, cols)
        return (
            blocks[0, :half],
            blocks[1, :half],
            back[:, :, 0].reshape(2, -1, rows, cols),
            back[:, :, 1].reshape(2, -1, rows, cols),
        )

    def part_of(self, x, index):
        far, near = index // self.near_size, index % self.near_size
        half, step = self.far_count // 2, self.near_size // 2
        if far < half:
            return x, (index,)
        if near < step:
            return 2, (x, (far - half) * step + near)
        return 3, (x, (far - half) * step + near - step)

    def part_shapes(self, rows, cols):
        count = self.row_count
        return [(count // 2, rows, cols)] * 2 + [(2, count // 4, rows, cols)] * 2

    def reduce_near(self, parts, hold=None):
        front, other, back, sent = parts
        step = self.near_size // 2
        front_x = swap_over(other, self.x_line)
        back_y = swap_over(sent, ("row", step))
        if hold is not None:
            front_x, back_y, _ = lax.optimization_barrier((front_x, back_y, hold))
        rows, cols = front.shape[1:]
        half = self.far_count // 2
        back = back.astype(F32) + back_y.astype(F32)
        back = self.reduce_bits(back.reshape(2, half, step, rows, cols), 2)
        back = back[0] + swap_over(back[1].astype(BF16), self.x_line).astype(F32)
        front = front.astype(F32) + front_x.astype(F32)
        front = self.reduce_bits(front.reshape(half, self.near_size, rows, cols), 1)
        total = jnp.concatenate([front, back], axis=0).reshape(self.far_count, rows, cols)
        return total, front_x

    def reduce_bits(self, parts, dim):
        while parts.shape[dim] > 1:
            step = parts.shape[dim] // 2
            kept = lax.slice_in_dim(parts, 0, step, axis=dim)
            sent = lax.slice_in_dim(parts, step, 2 * step, axis=dim).astype(BF16)
            parts = kept + swap_over(sent, ("row", step)).astype(F32)
        return parts

    def reduce_far(self, parts):
        low = parts.astype(BF16)
        arrived = [
            swap_over(low[index], ("row", index * self.near_size))
            for index in range(1, self.far_count)
        ]
        total = parts[0]
        for part in arrived:
            total = total + part.astype(F32)
        return total


def sum_everywhere(value):
    for name in ("col", "row"):
        for offset in bit_offsets(1, lax.axis_size(name)):
            value = value + swap_over(value, (name, offset))
    return value


def dot_nt(left, right):
    return lax.dot_general(left, right, (((1,), (1,)), ((), ())), preferred_element_type=F32)


def dot_nn(left, right):
    return lax.dot_general(left, right, (((1,), (0,)), ((), ())), preferred_element_type=F32)


def lane_pick(half):
    lanes = lax.broadcasted_iota(jnp.int32, (1, PAIR), 1)
    return jnp.where((lanes // HEAD_DIM) == half, 1.0, 0.0).astype(BF16)


def causal_block(size):
    key_at = lax.broadcasted_iota(jnp.int32, (size, size), 0)
    query_at = lax.broadcasted_iota(jnp.int32, (size, size), 1)
    return key_at <= query_at


def attend_kernel(q_ref, k_ref, v_ref, out_ref, turned_ref, lse_ref):
    length = q_ref.shape[0]
    block = min(QUERY_BLOCK, length)
    allowed = causal_block(block)
    values_t = v_ref[...].T
    scaling = jnp.asarray(HEAD_DIM**-0.5, BF16)
    for first in range(0, length, block):
        last = first + block
        query = q_ref[first:last, :] * scaling
        outs = []
        for half in range(2):
            rows = slice(half * HEAD_DIM, (half + 1) * HEAD_DIM)
            query_half = query * lane_pick(half)
            diag = dot_nt(k_ref[first:last, :], query_half)
            diag = jnp.where(allowed, diag, -1e30)
            top = jnp.max(diag, axis=0, keepdims=True)
            if first:
                rest = dot_nt(k_ref[0:first, :], query_half)
                top = jnp.maximum(top, jnp.max(rest, axis=0, keepdims=True))
            diag = jnp.exp(diag - top)
            total = jnp.sum(diag, axis=0, keepdims=True)
            if first:
                rest = jnp.exp(rest - top)
                total = total + jnp.sum(rest, axis=0, keepdims=True)
            inverse = 1.0 / total
            result = dot_nn(values_t[rows, first:last], (diag * inverse).astype(BF16))
            if first:
                result = result + dot_nn(values_t[rows, 0:first], (rest * inverse).astype(BF16))
            outs.append(result)
            lse_ref[0, half : half + 1, first:last] = top + jnp.log(total)
        turned = jnp.concatenate(outs, axis=0)
        out_ref[first:last, :] = turned.T.astype(BF16)
        turned_ref[:, first:last] = turned.astype(BF16)


def attend_forward(qkv):
    length, width = qkv.shape
    pairs = width // (3 * PAIR)

    def lanes(part):
        return pl.BlockSpec((length, PAIR), lambda pair: (0, part * pairs + pair))

    return pl.pallas_call(
        attend_kernel,
        grid=(pairs,),
        in_specs=[lanes(0), lanes(1), lanes(2)],
        out_specs=[
            lanes(0),
            pl.BlockSpec((PAIR, length), lambda pair: (pair, 0)),
            pl.BlockSpec((1, 8, length), lambda pair: (pair, 0, 0)),
        ],
        out_shape=[
            jax.ShapeDtypeStruct((length, pairs * PAIR), BF16),
            jax.ShapeDtypeStruct((pairs * PAIR, length), BF16),
            jax.ShapeDtypeStruct((pairs, 8, length), F32),
        ],
        compiler_params=pltpu.CompilerParams(vmem_limit_bytes=40 * 2**20),
        cost_estimate=pl.CostEstimate(
            flops=pairs * 2 * 4 * length * length * HEAD_DIM,
            bytes_accessed=4 * length * pairs * PAIR * 2,
            transcendentals=pairs * length * length,
        ),
        name="attend_forward",
    )(qkv, qkv, qkv)


def attend_back_kernel(q_ref, k_ref, v_ref, go_ref, lse_ref, grad_ref, gk_sum, gv_sum):
    length = q_ref.shape[0]
    pairs = grad_ref.shape[1] // (3 * PAIR)
    block = min(QUERY_BLOCK, length)
    allowed = causal_block(block)
    keys_t = k_ref[...].T
    scaling = jnp.asarray(HEAD_DIM**-0.5, BF16)
    pair = pl.program_id(0)

    def lanes(part):
        return pl.ds(pl.multiple_of((part * pairs + pair) * PAIR, PAIR), PAIR)

    gk_sum[...] = jnp.zeros_like(gk_sum)
    gv_sum[...] = jnp.zeros_like(gv_sum)
    for first in range(0, length, block):
        last = first + block
        query = q_ref[first:last, :] * scaling
        grad_out = go_ref[first:last, :]
        outs = []
        for half in range(2):
            rows = slice(half * HEAD_DIM, (half + 1) * HEAD_DIM)
            pick = lane_pick(half)
            query_half = query * pick
            grad_half = grad_out * pick
            lse = lse_ref[0, half : half + 1, first:last]
            spans = [(first, last)] if first == 0 else [(0, first), (first, last)]
            probs, grads, inner = [], [], None
            for low, high in spans:
                scores = dot_nt(k_ref[low:high, :], query_half)
                if low == first:
                    scores = jnp.where(allowed, scores, -1e30)
                prob = jnp.exp(scores - lse)
                grad_prob = dot_nt(v_ref[low:high, :], grad_half)
                part = jnp.sum(prob * grad_prob, axis=0, keepdims=True)
                inner = part if inner is None else inner + part
                probs.append(prob)
                grads.append(grad_prob)
            result = None
            for (low, high), prob, grad_prob in zip(spans, probs, grads):
                grad_score = (prob * (grad_prob - inner)).astype(BF16)
                gk_sum[low:high, :] += dot_nn(grad_score, query_half)
                gv_sum[low:high, :] += dot_nn(prob.astype(BF16), grad_half)
                part = dot_nn(keys_t[rows, low:high], grad_score)
                result = part if result is None else result + part
            outs.append(result)
        grad_query = jnp.concatenate(outs, axis=0).T * (HEAD_DIM**-0.5)
        grad_ref[first:last, lanes(0)] = grad_query.astype(BF16)
    grad_ref[:, lanes(1)] = gk_sum[...].astype(BF16)
    grad_ref[:, lanes(2)] = gv_sum[...].astype(BF16)


def attend_backward(qkv, grad_heads, lse):
    length, width = qkv.shape
    pairs = width // (3 * PAIR)

    def lanes(part):
        return pl.BlockSpec((length, PAIR), lambda pair: (0, part * pairs + pair))

    return pl.pallas_call(
        attend_back_kernel,
        grid=(pairs,),
        in_specs=[
            lanes(0),
            lanes(1),
            lanes(2),
            lanes(0),
            pl.BlockSpec((1, 8, length), lambda pair: (pair, 0, 0)),
        ],
        out_specs=pl.BlockSpec((length, width), lambda pair: (0, 0)),
        out_shape=jax.ShapeDtypeStruct((length, width), BF16),
        scratch_shapes=[pltpu.VMEM((length, PAIR), F32), pltpu.VMEM((length, PAIR), F32)],
        compiler_params=pltpu.CompilerParams(vmem_limit_bytes=40 * 2**20),
        cost_estimate=pl.CostEstimate(
            flops=pairs * 2 * 10 * length * length * HEAD_DIM,
            bytes_accessed=7 * length * pairs * PAIR * 2,
            transcendentals=pairs * length * length,
        ),
        name="attend_backward",
    )(qkv, qkv, qkv, grad_heads, lse)


def rows_of(block, width):
    return pl.BlockSpec((block, width), lambda step: (step, 0))


def whole(shape):
    return pl.BlockSpec(shape, lambda *step: (0,) * len(shape))


def shaped(shape, dtype):
    return jax.ShapeDtypeStruct(shape, dtype)


def cost(flops, arrays):
    return pl.CostEstimate(flops=flops, bytes_accessed=arrays, transcendentals=0)


PARAMS = pltpu.CompilerParams(vmem_limit_bytes=48 * 2**20)


ANYWHERE = pl.BlockSpec(memory_space=pl.ANY)


def weight_copies(gathered, refs, held, sems):
    row = lax.axis_index("row")
    copies = ([], [])
    for number, (x, array, at, offset) in enumerate(gathered.table):
        if len(gathered.table) > 2:
            start = pl.multiple_of((row ^ offset) * gathered.rows, 16)
        else:
            start = 0
        target = held.at[x, pl.ds(start, gathered.rows), :]
        copies[x].append(
            pltpu.make_async_copy(refs[array].at[at], target, sems.at[number])
        )
    return copies


def weight_scratch(gathered):
    all_rows = len(gathered.table) // 2 * gathered.rows
    return [
        pltpu.VMEM((2, all_rows, gathered.cols), BF16),
        pltpu.SemaphoreType.DMA((len(gathered.table),)),
    ]


def start_all(copies):
    for copy in copies:
        copy.start()


def wait_all(copies):
    for copy in copies:
        copy.wait()


def store_parts(held, grid, refs, x, lanes):
    if len(refs) == 1:
        refs[0][x, :, lanes] = held[...]
        return
    row = lax.axis_index("row")
    rows = held.shape[0] // grid.row_count
    for index in range(grid.row_count):
        start = pl.multiple_of((row ^ index) * rows, 16)
        array, place = grid.part_of(x, index)
        refs[array][place + (slice(None), lanes)] = held[pl.ds(start, rows), :]


def parts_out(grid, width, cols):
    rows = width // grid.row_count
    if rows % 16:
        return [(2, width, cols)]
    return grid.part_shapes(rows, cols)


def turn(value):
    return value.T


def pick_half(here, mine_ref, other_ref):
    mine, other = mine_ref[...].astype(F32), other_ref[...].astype(F32)
    return jnp.where(here, mine, other)


def first_norm_kernel(gathered, cols, place_ref, mine_ref, other_ref, *refs):
    count = len(gathered.arrays)
    norm_ref, qkv_ref, tokens_ref, full_ref, out_w_ref, vec_ref, held, bias, sems = refs[count:]
    copies = weight_copies(gathered, refs[:count], held, sems)
    third = cols // 3
    step = pl.program_id(0)
    per_half = pl.num_programs(0) // 2

    @pl.when(step == 0)
    def _():
        start_all(copies[0] + copies[1])
        wait_all(copies[0] + copies[1])
        for x in range(2):
            out_w_ref[:, x * third : (x + 1) * third] = held[x, :, held.shape[2] - third :]
            for part in range(3):
                lanes = slice((2 * part + x) * third, (2 * part + x + 1) * third)
                full_ref[:, lanes] = held[x, :, part * third : (part + 1) * third]
        first = cols // 128 * 128
        rows = turn(held[0, :, first : first + 128].astype(F32))[cols - first :]
        vec_ref[...] = rows[: vec_ref.shape[0]]
        row_at = lax.broadcasted_iota(jnp.int32, (rows.shape[1], 2 * third), 0)
        lane_at = lax.broadcasted_iota(jnp.int32, (rows.shape[1], 2 * third), 1)
        wanted = jnp.where(
            lane_at < third, place_ref[1] + lane_at, place_ref[2] + lane_at - third
        )
        chosen = jnp.where(row_at == wanted, 1.0, 0.0).astype(BF16)
        picked = dot_nn(vec_ref[...].astype(BF16), chosen)
        bias[...] = jnp.zeros_like(bias)
        bias[0:1, : 2 * third] = picked[2:3]
        bias[0:1, 4 * third :] = picked[3:4]

    tokens = pick_half(step // per_half == place_ref[0], mine_ref, other_ref)
    tokens_ref[...] = tokens.astype(BF16)
    normed, _ = normalize_rows(tokens)
    first_in = (normed * vec_ref[0:1, :] + vec_ref[1:2, :]).astype(BF16)
    norm_ref[...] = first_in
    qkv_ref[...] = (dot_nn(first_in, full_ref[...]) + bias[0:1, :]).astype(BF16)


def first_norm(place, mine, other, gathered, width_loc):
    rows, width = mine.shape
    length = 2 * rows
    cols = 3 * width_loc
    steps = rows // ROW_BLOCK
    half = pl.BlockSpec((ROW_BLOCK, width), lambda step, place_ref: (step % steps, 0))

    def by_row(size):
        return pl.BlockSpec((ROW_BLOCK, size), lambda step, place_ref: (step, 0))

    return pl.pallas_call(
        functools.partial(first_norm_kernel, gathered, cols),
        grid_spec=pltpu.PrefetchScalarGridSpec(
            num_scalar_prefetch=1,
            grid=(2 * steps,),
            in_specs=[half, half] + [ANYWHERE] * len(gathered.arrays),
            out_specs=[
                by_row(width),
                by_row(2 * cols),
                by_row(width),
                whole((width, 2 * cols)),
                whole((width, 2 * width_loc)),
                whole((16, width)),
            ],
            scratch_shapes=weight_scratch(gathered)[:1]
            + [pltpu.VMEM((8, 2 * cols), F32)]
            + weight_scratch(gathered)[1:],
        ),
        out_shape=[
            shaped((length, width), BF16),
            shaped((length, 2 * cols), BF16),
            shaped((length, width), BF16),
            shaped((width, 2 * cols), BF16),
            shaped((width, 2 * width_loc), BF16),
            shaped((16, width), F32),
        ],
        compiler_params=PARAMS,
        cost_estimate=cost(4 * length * width * cols, 2 * length * (2 * width + cols)),
        name="first_norm",
    )(place, mine, other, *gathered.arrays)


def attended_kernel(
    place_ref, heads_ref, partner_ref, own_ref, other_ref, tokens_ref, vec_ref, first_ref,
    mine_ref, other_cot_ref, hidden_ref, norm_ref, norm_turned_ref, first_turned_ref,
    cot_turned_ref, cot_ref,
):
    attended = dot_nt(heads_ref[...], own_ref[...]) + dot_nt(partner_ref[...], other_ref[...])
    hidden = tokens_ref[...].astype(F32) + attended + vec_ref[4:5, :]
    hidden_ref[...] = hidden
    normed, _ = normalize_rows(hidden)
    second_in = (normed * vec_ref[5:6, :] + vec_ref[6:7, :]).astype(BF16)
    norm_ref[...] = second_in
    norm_turned_ref[...] = turn(second_in)
    first_turned_ref[...] = turn(first_ref[...])
    here = pl.program_id(0) // (pl.num_programs(0) // 2) == place_ref[0]
    cot = pick_half(here, mine_ref, other_cot_ref).astype(BF16)
    cot_ref[...] = cot
    cot_turned_ref[...] = turn(cot)


def attended_norm(place, heads, partner_heads, own_out, partner_out, tokens, vec_all, first_in, cots):
    length, width = tokens.shape
    cols = heads.shape[1]
    steps = length // ROW_BLOCK
    half = pl.BlockSpec((ROW_BLOCK, width), lambda step, place_ref: (step % (steps // 2), 0))
    turned = pl.BlockSpec((width, ROW_BLOCK), lambda step, place_ref: (0, step))

    def by_row(size):
        return pl.BlockSpec((ROW_BLOCK, size), lambda step, place_ref: (step, 0))

    full = by_row(width)
    return pl.pallas_call(
        attended_kernel,
        grid_spec=pltpu.PrefetchScalarGridSpec(
            num_scalar_prefetch=1,
            grid=(steps,),
            in_specs=[
                by_row(cols),
                by_row(cols),
                whole(own_out.shape),
                whole(partner_out.shape),
                full,
                whole(vec_all.shape),
                full,
                half,
                half,
            ],
            out_specs=[full, full, turned, turned, turned, full],
        ),
        out_shape=[shaped((length, width), F32), shaped((length, width), BF16)]
        + [shaped((width, length), BF16)] * 3
        + [shaped((length, width), BF16)],
        compiler_params=PARAMS,
        cost_estimate=cost(4 * length * width * cols, length * width * 20),
        name="attended_norm",
    )(place, heads, partner_heads, own_out, partner_out, tokens, vec_all, first_in, *cots)


def feed_kernel(gathered, norm_ref, cot_ref, bias_ref, *refs):
    count = len(gathered.arrays)
    act_ref, gup_ref, bias_sum_ref, out_ref, back_ref, back_low_ref, held, sems = refs[count:]
    copies = weight_copies(gathered, refs[:count], held, sems)
    step = pl.program_id(0)
    length = norm_ref.shape[0]
    curve, cubic = math.sqrt(2 / math.pi), 0.044715
    cols = held.shape[2] // 2
    x = step
    up_lanes, down_lanes = slice(0, cols), slice(cols, 2 * cols)

    @pl.when(step == 0)
    def _():
        start_all(copies[0] + copies[1])
        out_ref[...] = jnp.zeros_like(out_ref)
        back_ref[...] = jnp.zeros_like(back_ref)
        wait_all(copies[0])

    @pl.when(step == 1)
    def _():
        wait_all(copies[1])

    bias_sum = jnp.zeros(bias_ref.shape, F32)
    for first in range(0, length, ROW_BLOCK):
        rows = slice(first, first + ROW_BLOCK)
        up = dot_nn(norm_ref[rows, :], held[x, :, up_lanes]) + bias_ref[...]
        square = up * up
        tanh = jnp.tanh(curve * up * (1.0 + cubic * square))
        act = (0.5 * up * (1.0 + tanh)).astype(BF16)
        act_ref[rows, :] = act
        slope = 0.5 * (1.0 + tanh) + 0.5 * up * (1.0 - tanh * tanh) * (
            curve * (1.0 + 3.0 * cubic * square)
        )
        grad_up = (dot_nn(cot_ref[rows, :], held[x, :, down_lanes]) * slope).astype(BF16)
        gup_ref[rows, :] = grad_up
        bias_sum = bias_sum + jnp.sum(grad_up.astype(F32), axis=0, keepdims=True)
        out_ref[rows, :] += dot_nt(act, held[x, :, down_lanes])
        back_ref[rows, :] += dot_nt(grad_up, held[x, :, up_lanes])
    bias_sum_ref[...] = bias_sum

    @pl.when(step == pl.num_programs(0) - 1)
    def _():
        back_low_ref[...] = back_ref[...].astype(BF16)


def feed(norm, cot, bias, gathered):
    length, width = norm.shape
    hidden = bias.shape[1]
    block = hidden // 2
    tall = pl.BlockSpec((length, block), lambda step: (0, step))
    flat = pl.BlockSpec((1, block), lambda step: (0, step))
    full = whole((length, width))
    return pl.pallas_call(
        functools.partial(feed_kernel, gathered),
        grid=(hidden // block,),
        in_specs=[full, full, flat] + [ANYWHERE] * len(gathered.arrays),
        out_specs=[tall, tall, flat, full, full, full],
        out_shape=[
            shaped((length, hidden), BF16),
            shaped((length, hidden), BF16),
            shaped((1, hidden), F32),
            shaped((length, width), F32),
            shaped((length, width), F32),
            shaped((length, width), BF16),
        ],
        scratch_shapes=weight_scratch(gathered),
        compiler_params=PARAMS,
        cost_estimate=cost(8 * length * width * hidden, 4 * length * (width + hidden)),
        name="feed",
    )(norm, cot, bias, *gathered.arrays)


def feed_grads_kernel(grid, cot_ref, norm_ref, act_ref, gup_ref, *refs):
    kind, x_at = pl.program_id(0), pl.program_id(1)
    outs, held = refs[:-1], refs[-1]
    size = held.shape[1]

    @pl.when(kind == 0)
    def _():
        held[...] = dot_nn(cot_ref[...], act_ref[...]).astype(BF16)

    @pl.when(kind == 1)
    def _():
        held[...] = dot_nn(norm_ref[...], gup_ref[...]).astype(BF16)

    for index in range(2):
        for x in range(2):

            @pl.when((kind == index) & (x_at == x))
            def _():
                store_parts(held, grid, outs, x, slice((1 - index) * size, (2 - index) * size))


def feed_grads(cot_turned, norm_turned, act, grad_up, grid):
    width, length = cot_turned.shape
    hidden = act.shape[1]
    block = hidden // 2
    shapes = parts_out(grid, width, hidden)
    parts = pl.pallas_call(
        functools.partial(feed_grads_kernel, grid),
        grid=(2, 2),
        in_specs=[
            whole((width, length)),
            whole((width, length)),
            pl.BlockSpec((length, block), lambda kind, x: (0, jnp.where(kind == 0, x, 1))),
            pl.BlockSpec((length, block), lambda kind, x: (0, jnp.where(kind == 1, x, 0))),
        ],
        out_specs=[whole(shape) for shape in shapes],
        out_shape=[shaped(shape, BF16) for shape in shapes],
        scratch_shapes=[pltpu.VMEM((width, block), BF16)],
        compiler_params=PARAMS,
        cost_estimate=cost(4 * length * width * hidden, 4 * length * (width + hidden)),
        name="feed_grads",
    )(cot_turned, norm_turned, act, grad_up)
    return parts if len(parts) == 4 else grid.split(parts[0])


def second_back_kernel(
    part_ref, other_ref, hidden_ref, cot_ref, vec_ref, out_w_ref, turned_ref,
    grad_ref, heads_ref, sum_ref, out_grad_ref, total,
):
    step = pl.program_id(0)
    normed, inv_std = normalize_rows(hidden_ref[...])
    part = part_ref[...]
    cot = cot_ref[...].astype(F32)
    grad_second = part + other_ref[...].astype(F32)
    grad = cot + norm_back(grad_second * vec_ref[5:6, :], normed, inv_std)
    grad_ref[...] = grad
    low = grad.astype(BF16)
    heads_ref[...] = dot_nn(low, out_w_ref[...]).astype(BF16)

    @pl.when(step == 0)
    def _():
        sum_ref[...] = jnp.zeros_like(sum_ref)
        total[...] = jnp.zeros_like(total)

    total[...] += dot_nn(turned_ref[...], low)
    for row, value in enumerate((grad, part * normed, part, cot)):
        sum_ref[row : row + 1, :] += jnp.sum(value, axis=0, keepdims=True)

    @pl.when(step == pl.num_programs(0) - 1)
    def _():
        out_grad_ref[...] = total[...].T.astype(BF16)


def second_back(part, other, hidden, cot, vec_all, out_w, heads_turned):
    length, width = part.shape
    cols = out_w.shape[1]
    full = rows_of(ROW_BLOCK, width)
    return pl.pallas_call(
        second_back_kernel,
        grid=(length // ROW_BLOCK,),
        in_specs=[full, full, full, full, whole(vec_all.shape), whole(out_w.shape)]
        + [pl.BlockSpec((cols, ROW_BLOCK), lambda step: (0, step))],
        out_specs=[full, rows_of(ROW_BLOCK, cols), whole((8, width)), whole((width, cols))],
        out_shape=[
            shaped((length, width), F32),
            shaped((length, cols), BF16),
            shaped((8, width), F32),
            shaped((width, cols), BF16),
        ],
        scratch_shapes=[pltpu.VMEM((cols, width), F32)],
        compiler_params=PARAMS,
        cost_estimate=cost(4 * length * width * cols, length * width * 20),
        name="second_back",
    )(part, other, hidden, cot, vec_all, out_w, heads_turned)


def qkv_grads_kernel(grid, norm_ref, grad_ref, out_grad_ref, *refs):
    part = pl.program_id(0)
    outs, held = refs[:-1], refs[-1]
    half = held.shape[1]
    for index in range(4):

        @pl.when(part == index)
        def _():
            if index == 3:
                grads = out_grad_ref[...]
            else:
                grads = dot_nn(norm_ref[...], grad_ref[...]).astype(BF16)
            for x in range(2):
                held[...] = grads[:, x * half : (x + 1) * half]
                store_parts(held, grid, outs, x, slice(index * half, (index + 1) * half))


def qkv_grads(norm_turned, grad_qkv, out_grad, grid):
    width, length = norm_turned.shape
    cols = out_grad.shape[1]
    shapes = parts_out(grid, width, 2 * cols)
    parts = pl.pallas_call(
        functools.partial(qkv_grads_kernel, grid),
        grid=(4,),
        in_specs=[
            whole((width, length)),
            pl.BlockSpec((length, cols), lambda part: (0, jnp.minimum(part, 2))),
            whole((width, cols)),
        ],
        out_specs=[whole(shape) for shape in shapes],
        out_shape=[shaped(shape, BF16) for shape in shapes],
        scratch_shapes=[pltpu.VMEM((width, cols // 2), BF16)],
        compiler_params=PARAMS,
        cost_estimate=cost(6 * length * width * cols, 4 * length * (2 * width + 2 * cols)),
        name="qkv_grads",
    )(norm_turned, grad_qkv, out_grad)
    return parts if len(parts) == 4 else grid.split(parts[0])


def first_back_kernel(grad_ref, weight_ref, tokens_ref, after_ref, part_ref, sum_ref, bias_ref):
    part = dot_nt(grad_ref[...], weight_ref[...])
    part_ref[...] = part
    normed, _ = normalize_rows(tokens_ref[...].astype(F32))

    @pl.when(pl.program_id(0) == 0)
    def _():
        sum_ref[...] = jnp.zeros_like(sum_ref)
        bias_ref[...] = jnp.zeros_like(bias_ref)

    for row, value in enumerate((part * normed, part)):
        sum_ref[row : row + 1, :] += jnp.sum(value, axis=0, keepdims=True)
    bias_ref[0:1, :] += jnp.sum(grad_ref[...].astype(F32), axis=0, keepdims=True)


def first_back(grad_qkv, weight, tokens, after):
    length, width = tokens.shape
    cols = grad_qkv.shape[1]
    return pl.pallas_call(
        first_back_kernel,
        grid=(length // ROW_BLOCK,),
        in_specs=[
            rows_of(ROW_BLOCK, cols),
            whole(weight.shape),
            rows_of(ROW_BLOCK, width),
            ANYWHERE,
        ],
        out_specs=[rows_of(ROW_BLOCK, width), whole((8, width)), whole((8, cols))],
        out_shape=[
            shaped((length, width), F32),
            shaped((8, width), F32),
            shaped((8, cols), F32),
        ],
        compiler_params=PARAMS,
        cost_estimate=cost(2 * length * width * cols, length * (6 * width + 2 * cols)),
        name="first_back",
    )(grad_qkv, weight, tokens, after)


def token_back_kernel(core_ref, part_ref, other_ref, tokens_ref, grad_ref, vec_ref, out_ref):
    normed, inv_std = normalize_rows(tokens_ref[...].astype(F32))
    grad_first = part_ref[...] + other_ref[...].astype(F32)
    out_ref[...] = grad_ref[...] + norm_back(grad_first * vec_ref[0:1, :], normed, inv_std)


def token_back(core, part, other, tokens, grad_hidden, vec_all):
    rows, width = tokens.shape
    steps = rows // ROW_BLOCK
    own = pl.BlockSpec((ROW_BLOCK, width), lambda step, core_ref: (core_ref[0] * steps + step, 0))
    here = pl.BlockSpec((ROW_BLOCK, width), lambda step, core_ref: (step, 0))
    return pl.pallas_call(
        token_back_kernel,
        grid_spec=pltpu.PrefetchScalarGridSpec(
            num_scalar_prefetch=1,
            grid=(steps,),
            in_specs=[own, here, here, own, whole(vec_all.shape)],
            out_specs=here,
        ),
        out_shape=shaped((rows, width), F32),
        compiler_params=PARAMS,
        cost_estimate=cost(rows * width * 20, rows * width * 16),
        name="token_back",
    )(core.reshape(1), part, other, tokens, grad_hidden, vec_all)


def shards(
    tokens,
    cotangent,
    w_qkv,
    w_out,
    w_up,
    w_down,
    vectors,
    first_qkv,
    first_out,
    first_up,
    first_down,
    first_vectors,
    second_qkv,
    second_out,
    second_up,
    second_down,
    second_vectors,
):
    row_index = lax.axis_index("row")
    col_index = lax.axis_index("col")
    col_count = lax.axis_size("col")
    grid = Grid(lax.axis_size("row"))
    core_line = ("col", 1)
    core = col_index % 2
    other_col = col_index ^ 2
    rows_loc, width = tokens.shape
    width_loc = w_qkv.shape[2]
    width_core = 2 * width_loc
    hidden_loc = w_up.shape[1]
    shard_rows = w_up.shape[0]

    pad = -(3 * width_loc + VEC_ROWS) % 128
    pack_qkv = jnp.concatenate(
        [w_qkv[:, part].astype(BF16) for part in range(3)]
        + [vectors.T.astype(BF16), jnp.zeros((shard_rows, pad), BF16), w_out.T.astype(BF16)],
        axis=1,
    )
    pack_feed = jnp.concatenate([w_up.astype(BF16), w_down.T.astype(BF16)], axis=1)

    def own_rows(value):
        return lax.dynamic_slice_in_dim(value, core * rows_loc, rows_loc, 0)

    def partner_rows(value):
        return lax.dynamic_slice_in_dim(value, (1 - core) * rows_loc, rows_loc, 0)

    def rows_gathered(block):
        return lax.all_gather(block, "row", axis=0, tiled=True)[None]

    near_qkv = grid.gather_near(grid.gather_far(pack_qkv))
    near_feed = Gathered(
        [rows_gathered(pack_feed), rows_gathered(swap_over(pack_feed, grid.x_line))],
        [(0, 0, 0, 0), (1, 1, 0, 0)],
    )
    partner = swap_over(jnp.stack([tokens, cotangent]), core_line)
    place = jnp.stack([core, col_index * width_loc, other_col * width_loc]).astype(jnp.int32)

    def cat_blocks(vec_row, size):
        return jnp.concatenate(
            [
                lax.dynamic_slice_in_dim(vec_row, col_index * size, size, 0),
                lax.dynamic_slice_in_dim(vec_row, other_col * size, size, 0),
            ]
        )

    first_in, qkv, all_tokens, full_qkv, full_out, vec_all = first_norm(
        place, tokens, partner[0], near_qkv, width_loc
    )
    bias_up = cat_blocks(vec_all[8:VEC_ROWS].reshape(-1), hidden_loc)
    partner_out = swap_over(full_out, core_line)
    heads_low, heads_turned, lse = attend_forward(qkv)
    partner_heads = swap_over(heads_low, core_line)
    hidden_state, second_in, second_turned, first_turned, cot_turned, all_cot = attended_norm(
        place, heads_low, partner_heads, full_out, partner_out, all_tokens, vec_all, first_in,
        (cotangent, partner[1]),
    )
    activated, grad_upper, grad_bias_up, down_part, second_part, second_low = feed(
        second_in, all_cot, bias_up[None], near_feed
    )

    second_other = swap_over(second_low, core_line)
    parts_feed = feed_grads(cot_turned, second_turned, activated, grad_upper, grid)
    grad_hidden, grad_heads, second_sums, out_grad = second_back(
        second_part, second_other, hidden_state, all_cot, vec_all, full_out, heads_turned
    )
    down_other = swap_over(partner_rows(down_part).astype(BF16), core_line).astype(F32)
    mixed_out = own_rows(hidden_state) + own_rows(down_part) + down_other + vec_all[7]
    grad_qkv_low = attend_backward(qkv, grad_heads, lse)
    parts_qkv = qkv_grads(first_turned, grad_qkv_low, out_grad, grid)
    first_part, first_sums, bias_sums = first_back(
        grad_qkv_low, full_qkv, all_tokens, parts_qkv[1]
    )

    near_pack, arrived = grid.reduce_near(parts_qkv)
    owned_pack = grid.reduce_far(near_pack)
    owned_feed = grid.reduce_far(grid.reduce_near(parts_feed, parts_qkv[1])[0])
    owned_up, owned_down = owned_feed[:, :hidden_loc], owned_feed[:, hidden_loc:]
    first_part, first_sums, _ = lax.optimization_barrier((first_part, first_sums, arrived))
    first_other = swap_over(partner_rows(first_part).astype(BF16), core_line)
    token_grad = token_back(core, first_part, first_other, tokens, grad_hidden, vec_all)
    owned_qkv = jnp.stack(
        [owned_pack[:, part * width_loc : (part + 1) * width_loc] for part in range(3)], axis=1
    )
    owned_out = owned_pack[:, 3 * width_loc :]

    def placed(part_row, length):
        size = part_row.shape[0] // 2
        start = jnp.zeros((length,), F32)
        start = lax.dynamic_update_slice_in_dim(start, part_row[:size], col_index * size, 0)
        return lax.dynamic_update_slice_in_dim(start, part_row[size:], other_col * size, 0)

    front_rows = jnp.stack(
        [
            first_sums[0],
            first_sums[1],
            placed(bias_sums[0, :width_core], width),
            placed(bias_sums[0, 2 * width_core :], width),
            0.5 * second_sums[0],
            second_sums[1],
            second_sums[2],
            0.5 * second_sums[3],
        ]
    )
    up_rows = placed(grad_bias_up[0], hidden_loc * col_count).reshape(-1, width)
    grad_vec = sum_everywhere(jnp.concatenate([front_rows, up_rows], axis=0))
    owned_vec = lax.dynamic_slice_in_dim(grad_vec, row_index * shard_rows, shard_rows, 1)

    new_qkv, new_first_qkv, new_second_qkv = adamw(
        w_qkv, first_qkv, second_qkv, owned_qkv, RATE_MATRIX
    )
    new_out, new_first_out, new_second_out = adamw(
        w_out, first_out, second_out, owned_out.T, RATE_MATRIX
    )
    new_up, new_first_up, new_second_up = adamw(w_up, first_up, second_up, owned_up, RATE_MATRIX)
    new_down, new_first_down, new_second_down = adamw(
        w_down, first_down, second_down, owned_down.T, RATE_MATRIX
    )
    new_vectors, new_first_vectors, new_second_vectors = adamw(
        vectors, first_vectors, second_vectors, owned_vec, RATE_VECTOR
    )
    return (
        mixed_out,
        token_grad,
        new_qkv,
        new_out,
        new_up,
        new_down,
        new_vectors,
        new_first_qkv,
        new_first_out,
        new_first_up,
        new_first_down,
        new_first_vectors,
        new_second_qkv,
        new_second_out,
        new_second_up,
        new_second_down,
        new_second_vectors,
    )


def solution(mesh):
    by_token = P(("row", "col"), None)
    weights = (
        P("row", None, "col"),
        P("col", "row"),
        P("row", "col"),
        P("col", "row"),
        P(None, "row"),
    )
    return jax.shard_map(
        shards,
        mesh=mesh,
        in_specs=(by_token, by_token) + weights * 3,
        out_specs=(by_token, by_token) + weights * 3,
        check_vma=False,
    )
```

```python
import functools
import math

import jax
import jax.numpy as jnp
from jax import lax
from jax.experimental import pallas as pl
from jax.experimental.pallas import tpu as pltpu
from jax.sharding import PartitionSpec as P

HEAD_DIM = 64
LENGTH = 1024
STEP_NUMBER = 10
VEC_ROWS = 12
PAIR = 2 * HEAD_DIM
QUERY_BLOCK = 256
ROW_BLOCK = 256
VEC_LANES = 128
COST_SCALE = 2.3e8


EPS = 1e-05
BETA_ONE = 0.9
BETA_TWO = 0.999
ADAM_EPS = 1e-08
DECAY = 0.1
RATE_MATRIX = 0.04
RATE_VECTOR = 0.3

F32 = jnp.float32
BF16 = jnp.bfloat16


def normalize_rows(values_in):
    row_mean = jnp.mean(values_in, axis=-1, keepdims=True)
    centred = values_in - row_mean
    row_var = jnp.mean(centred * centred, axis=-1, keepdims=True)
    inv_std = lax.rsqrt(row_var + EPS)
    return (centred * inv_std, inv_std)


def norm_back(grad_in, normed, inv_std):
    mean_grad = jnp.mean(grad_in, axis=-1, keepdims=True)
    mean_cross = jnp.mean(grad_in * normed, axis=-1, keepdims=True)
    return inv_std * (grad_in - mean_grad - normed * mean_cross)


def adamw(weight, moment_one, moment_two, gradient, rate):
    first = BETA_ONE * moment_one + (1 - BETA_ONE) * gradient
    second = BETA_TWO * moment_two + (1 - BETA_TWO) * gradient * gradient
    first_hat = first / (1 - BETA_ONE**STEP_NUMBER)
    second_hat = second / (1 - BETA_TWO**STEP_NUMBER)
    updated = weight - rate * (first_hat / (jnp.sqrt(second_hat) + ADAM_EPS) + DECAY * weight)
    return (updated, first, second)


def swap_over(value, line):
    name, offset = line
    pairs = [(index, index ^ offset) for index in range(lax.axis_size(name))]
    return lax.ppermute(value, name, pairs)


def bit_offsets(low, high):
    offsets = []
    while low < high:
        offsets.append(low)
        low *= 2
    return offsets


def flip_order(blocks):
    count = blocks.shape[0]
    row = lax.axis_index("row")
    for offset in bit_offsets(1, count):
        cut = blocks.reshape((-1, 2, offset) + blocks.shape[1:])
        turned = jnp.where((row // offset) % 2 == 1, cut[:, ::-1], cut)
        blocks = turned.reshape(blocks.shape)
    return blocks


class Gathered:
    def __init__(self, arrays, table):
        self.arrays = arrays
        self.table = table
        self.rows = arrays[0].shape[1]
        self.cols = arrays[0].shape[2]
        if self.rows % 16:
            total = []
            for x in range(2):
                found = sorted((offset, array, at) for x_at, array, at, offset in table if x_at == x)
                blocks = jnp.stack([arrays[array][at] for _, array, at in found])
                total.append(flip_order(blocks).reshape(-1, self.cols))
            self.arrays = [jnp.stack(total)]
            self.table = [(0, 0, 0, 0), (1, 0, 1, 0)]
            self.rows = self.arrays[0].shape[1]


class Grid:
    def __init__(self, row_count):
        self.near_size = {8: 2, 64: 4}.get(row_count, 1)
        self.row_count = row_count
        self.far_count = row_count // self.near_size
        self.near = bit_offsets(1, self.near_size)
        self.x_line = ("col", 2)

    def gather_far(self, block):
        blocks = [block]
        for index in range(1, self.far_count):
            blocks.append(swap_over(block, ("row", index * self.near_size)))
        return blocks

    def gather_one(self, blocks):
        half = self.far_count // 2
        front, back = jnp.stack(blocks[:half]), jnp.stack(blocks[half:])
        step = self.near[0]
        return (front, back), (swap_over(front, ("row", step)), swap_over(back, self.x_line))

    def gather_two(self, kept, arrived):
        half = self.far_count // 2
        front = jnp.concatenate([kept[0], arrived[0]], axis=0)
        back = jnp.concatenate([kept[1], arrived[1]], axis=0)
        front_at = [index * self.near_size for index in range(half)]
        front_at = front_at + [at ^ self.near[0] for at in front_at]
        for offset in self.near[1:]:
            front = jnp.concatenate([front, swap_over(front, ("row", offset))], axis=0)
            front_at = front_at + [at ^ offset for at in front_at]
        return front, front_at, back

    def gather_three(self, front, front_at, back):
        half = self.far_count // 2
        back_at = [(x, (index + half) * self.near_size) for x in range(2) for index in range(half)]
        arrays = [front, swap_over(front, self.x_line), back]
        table = [(x, x, index, at) for x in range(2) for index, at in enumerate(front_at)]
        table += [(x, 2, index, at) for index, (x, at) in enumerate(back_at)]
        for offset in self.near:
            sent = back if len(arrays) == 3 else jnp.concatenate(arrays[2:], axis=0)
            arrays.append(swap_over(sent, ("row", offset)))
            moved = [(x, at ^ offset) for x, at in back_at]
            table += [(x, len(arrays) - 1, index, at) for index, (x, at) in enumerate(moved)]
            back_at = back_at + moved
        return Gathered(arrays, table)

    def split(self, pair):
        _, all_rows, cols = pair.shape
        blocks = jnp.moveaxis(pair.reshape(2, self.row_count, -1, cols), 1, 0)
        blocks = jnp.moveaxis(flip_order(blocks), 0, 1)
        rows = blocks.shape[2]
        half = self.row_count // 2
        back = blocks[:, half:].reshape(2, self.far_count // 2, 2, -1, rows, cols)
        return (
            blocks[0, :half],
            blocks[1, :half],
            back[:, :, 0].reshape(2, -1, rows, cols),
            back[:, :, 1].reshape(2, -1, rows, cols),
        )

    def part_of(self, x, index):
        far, near = index // self.near_size, index % self.near_size
        half, step = self.far_count // 2, self.near_size // 2
        if far < half:
            return x, (index,)
        if near < step:
            return 2, (x, (far - half) * step + near)
        return 3, (x, (far - half) * step + near - step)

    def part_shapes(self, rows, cols):
        count = self.row_count
        return [(count // 2, rows, cols)] * 2 + [(2, count // 4, rows, cols)] * 2

    def stage_one(self, parts):
        step = self.near_size // 2
        return swap_over(parts[1], self.x_line), swap_over(parts[3], ("row", step))

    def stage_two(self, parts, front_x, back_y):
        rows, cols = parts[0].shape[1:]
        half, step = self.far_count // 2, self.near_size // 2
        back = parts[2].astype(F32) + back_y.astype(F32)
        back = self.reduce_bits(back.reshape(2, half, step, rows, cols), 2)
        front = parts[0].astype(F32) + front_x.astype(F32)
        front = front.reshape(half, self.near_size, rows, cols)
        return (front[:, :step], back[0]), (front[:, step:].astype(BF16), back[1].astype(BF16))

    def stage_three(self, kept, sent):
        step = self.near_size // 2
        back = kept[1] + swap_over(sent[1], self.x_line).astype(F32)
        front = kept[0] + swap_over(sent[0], ("row", step)).astype(F32)
        front = self.reduce_bits(front, 1)
        rows, cols = front.shape[2:]
        return jnp.concatenate([front, back], axis=0).reshape(self.far_count, rows, cols)

    def reduce_bits(self, parts, dim):
        while parts.shape[dim] > 1:
            step = parts.shape[dim] // 2
            kept = lax.slice_in_dim(parts, 0, step, axis=dim)
            sent = lax.slice_in_dim(parts, step, 2 * step, axis=dim).astype(BF16)
            parts = kept + swap_over(sent, ("row", step)).astype(F32)
        return parts

    def reduce_chain(self, parts):
        offset = self.near_size
        while parts.shape[0] > 1:
            parts = parts[0::2] + swap_over(parts[1::2].astype(BF16), ("row", offset)).astype(F32)
            offset *= 2
        return parts[0]

    def reduce_direct(self, parts, hold):
        low = parts.astype(BF16)
        arrived = [
            swap_over(low[index], ("row", index * self.near_size))
            for index in range(1, self.far_count)
        ]
        arrived, hold = lax.optimization_barrier((arrived, hold))
        total = parts[0]
        for part in arrived:
            total = total + part.astype(F32)
        return total, hold


def dot_nt(left, right):
    return lax.dot_general(left, right, (((1,), (1,)), ((), ())), preferred_element_type=F32)


def dot_nn(left, right):
    return lax.dot_general(left, right, (((1,), (0,)), ((), ())), preferred_element_type=F32)


def lane_pick(half):
    lanes = lax.broadcasted_iota(jnp.int32, (1, PAIR), 1)
    return jnp.where((lanes // HEAD_DIM) == half, 1.0, 0.0).astype(BF16)


def causal_block(size):
    key_at = lax.broadcasted_iota(jnp.int32, (size, size), 0)
    query_at = lax.broadcasted_iota(jnp.int32, (size, size), 1)
    return key_at <= query_at


def cost(microseconds):
    return pl.CostEstimate(
        flops=int(microseconds * COST_SCALE), bytes_accessed=1024, transcendentals=0
    )


def attend_kernel(q_ref, k_ref, v_ref, out_ref, turned_ref, lse_ref):
    length = q_ref.shape[0]
    block = min(QUERY_BLOCK, length)
    allowed = causal_block(block)
    values_t = v_ref[...].T
    scaling = jnp.asarray(HEAD_DIM**-0.5, BF16)
    for first in range(0, length, block):
        last = first + block
        query = q_ref[first:last, :] * scaling
        outs = []
        for half in range(2):
            rows = slice(half * HEAD_DIM, (half + 1) * HEAD_DIM)
            query_half = query * lane_pick(half)
            diag = dot_nt(k_ref[first:last, :], query_half)
            diag = jnp.where(allowed, diag, -1e30)
            top = jnp.max(diag, axis=0, keepdims=True)
            if first:
                rest = dot_nt(k_ref[0:first, :], query_half)
                top = jnp.maximum(top, jnp.max(rest, axis=0, keepdims=True))
            diag = jnp.exp(diag - top)
            total = jnp.sum(diag, axis=0, keepdims=True)
            if first:
                rest = jnp.exp(rest - top)
                total = total + jnp.sum(rest, axis=0, keepdims=True)
            inverse = 1.0 / total
            result = dot_nn(values_t[rows, first:last], (diag * inverse).astype(BF16))
            if first:
                result = result + dot_nn(values_t[rows, 0:first], (rest * inverse).astype(BF16))
            outs.append(result)
            lse_ref[0, half : half + 1, first:last] = top + jnp.log(total)
        turned = jnp.concatenate(outs, axis=0)
        out_ref[first:last, :] = turned.T.astype(BF16)
        turned_ref[:, first:last] = turned.astype(BF16)


def pair_lanes(length, first, part):
    return pl.BlockSpec((length, PAIR), lambda pair: (0, 3 * (first + pair) + part))


def attend_forward(qkv, first, pairs, after):
    length = qkv.shape[0]
    return pl.pallas_call(
        lambda q, k, v, *refs: attend_kernel(q, k, v, *refs[len(after) :]),
        grid=(pairs,),
        in_specs=[pair_lanes(length, first, part) for part in range(3)]
        + [pl.BlockSpec(memory_space=pl.ANY)] * len(after),
        out_specs=[
            pl.BlockSpec((length, PAIR), lambda pair: (0, pair)),
            pl.BlockSpec((PAIR, length), lambda pair: (pair, 0)),
            pl.BlockSpec((1, 8, length), lambda pair: (pair, 0, 0)),
        ],
        out_shape=[
            jax.ShapeDtypeStruct((length, pairs * PAIR), BF16),
            jax.ShapeDtypeStruct((pairs * PAIR, length), BF16),
            jax.ShapeDtypeStruct((pairs, 8, length), F32),
        ],
        compiler_params=pltpu.CompilerParams(vmem_limit_bytes=40 * 2**20),
        cost_estimate=cost(4.2 * pairs),
        name="attend_forward",
    )(qkv, qkv, qkv, *after)


def attend_back_kernel(q_ref, k_ref, v_ref, go_ref, lse_ref, grad_ref, gk_sum, gv_sum):
    length = q_ref.shape[0]
    block = min(QUERY_BLOCK, length)
    allowed = causal_block(block)
    keys_t = k_ref[...].T
    scaling = jnp.asarray(HEAD_DIM**-0.5, BF16)
    pair = pl.program_id(0)

    def lanes(part):
        return pl.ds(pl.multiple_of((3 * pair + part) * PAIR, PAIR), PAIR)

    gk_sum[...] = jnp.zeros_like(gk_sum)
    gv_sum[...] = jnp.zeros_like(gv_sum)
    for first in range(0, length, block):
        last = first + block
        query = q_ref[first:last, :] * scaling
        grad_out = go_ref[first:last, :]
        outs = []
        for half in range(2):
            rows = slice(half * HEAD_DIM, (half + 1) * HEAD_DIM)
            pick = lane_pick(half)
            query_half = query * pick
            grad_half = grad_out * pick
            lse = lse_ref[0, half : half + 1, first:last]
            spans = [(first, last)] if first == 0 else [(0, first), (first, last)]
            probs, grads, inner = [], [], None
            for low, high in spans:
                scores = dot_nt(k_ref[low:high, :], query_half)
                if low == first:
                    scores = jnp.where(allowed, scores, -1e30)
                prob = jnp.exp(scores - lse)
                grad_prob = dot_nt(v_ref[low:high, :], grad_half)
                part = jnp.sum(prob * grad_prob, axis=0, keepdims=True)
                inner = part if inner is None else inner + part
                probs.append(prob)
                grads.append(grad_prob)
            result = None
            for (low, high), prob, grad_prob in zip(spans, probs, grads):
                grad_score = (prob * (grad_prob - inner)).astype(BF16)
                gk_sum[low:high, :] += dot_nn(grad_score, query_half)
                gv_sum[low:high, :] += dot_nn(prob.astype(BF16), grad_half)
                part = dot_nn(keys_t[rows, low:high], grad_score)
                result = part if result is None else result + part
            outs.append(result)
        grad_query = jnp.concatenate(outs, axis=0).T * (HEAD_DIM**-0.5)
        grad_ref[first:last, lanes(0)] = grad_query.astype(BF16)
    grad_ref[:, lanes(1)] = gk_sum[...].astype(BF16)
    grad_ref[:, lanes(2)] = gv_sum[...].astype(BF16)


def attend_backward(qkv, grad_heads, lse, first, after):
    length = qkv.shape[0]
    pairs = lse.shape[0]
    width = 3 * PAIR * pairs
    return pl.pallas_call(
        lambda q, k, v, go, lse_at, *refs: attend_back_kernel(
            q, k, v, go, lse_at, *refs[len(after) :]
        ),
        grid=(pairs,),
        in_specs=[pair_lanes(length, first, part) for part in range(3)]
        + [
            pl.BlockSpec((length, PAIR), lambda pair: (0, first + pair)),
            pl.BlockSpec((1, 8, length), lambda pair: (pair, 0, 0)),
        ]
        + [pl.BlockSpec(memory_space=pl.ANY)] * len(after),
        out_specs=pl.BlockSpec((length, width), lambda pair: (0, 0)),
        out_shape=jax.ShapeDtypeStruct((length, width), BF16),
        scratch_shapes=[pltpu.VMEM((length, PAIR), F32), pltpu.VMEM((length, PAIR), F32)],
        compiler_params=pltpu.CompilerParams(vmem_limit_bytes=40 * 2**20),
        cost_estimate=cost(1.5 * pairs),
        name="attend_backward",
    )(qkv, qkv, qkv, grad_heads, lse, *after)


def rows_of(block, width):
    return pl.BlockSpec((block, width), lambda step: (step, 0))


def whole(shape):
    return pl.BlockSpec(shape, lambda *step: (0,) * len(shape))


def shaped(shape, dtype):
    return jax.ShapeDtypeStruct(shape, dtype)


PARAMS = pltpu.CompilerParams(vmem_limit_bytes=48 * 2**20)


ANYWHERE = pl.BlockSpec(memory_space=pl.ANY)


def weight_copies(gathered, refs, held, sems):
    row = lax.axis_index("row")
    copies = ([], [])
    for number, (x, array, at, offset) in enumerate(gathered.table):
        if len(gathered.table) > 2:
            start = pl.multiple_of((row ^ offset) * gathered.rows, 16)
        else:
            start = 0
        target = held.at[x, pl.ds(start, gathered.rows), :]
        copies[x].append(
            pltpu.make_async_copy(refs[array].at[at], target, sems.at[number])
        )
    return copies


def weight_scratch(gathered):
    all_rows = len(gathered.table) // 2 * gathered.rows
    return [
        pltpu.VMEM((2, all_rows, gathered.cols), BF16),
        pltpu.SemaphoreType.DMA((len(gathered.table),)),
    ]


def start_all(copies):
    for copy in copies:
        copy.start()


def wait_all(copies):
    for copy in copies:
        copy.wait()


def store_parts(held, grid, refs, x, source, lanes):
    if len(refs) == 1:
        refs[0][x, :, lanes] = held[:, source]
        return
    row = lax.axis_index("row")
    rows = held.shape[0] // grid.row_count
    for index in range(grid.row_count):
        start = pl.multiple_of((row ^ index) * rows, 16)
        array, place = grid.part_of(x, index)
        refs[array][place + (slice(None), lanes)] = held[pl.ds(start, rows), source]


def segments(pair, third):
    low, high, found = pair * PAIR, (pair + 1) * PAIR, []
    while low < high:
        x = low // third
        end = min(high, (x + 1) * third)
        found.append((x, low - x * third, end - x * third, low - pair * PAIR))
        low = end
    return found


def parts_out(grid, width, cols):
    rows = width // grid.row_count
    if rows % 16:
        return [(2, width, cols)]
    return grid.part_shapes(rows, cols)


def turn(value):
    return value.T


def pick_half(here, mine_ref, other_ref):
    mine, other = mine_ref[...].astype(F32), other_ref[...].astype(F32)
    return jnp.where(here, mine, other)


def first_norm_kernel(gathered, cols, place_ref, mine_ref, other_ref, *refs):
    count = len(gathered.arrays)
    norm_ref, qkv_ref, tokens_ref, full_ref, out_w_ref, vec_ref, held, bias, sems = refs[count:]
    copies = weight_copies(gathered, refs[:count], held, sems)
    third = cols // 3
    step = pl.program_id(0)
    per_half = pl.num_programs(0) // 2

    @pl.when(step == 0)
    def _():
        start_all(copies[0] + copies[1])
        wait_all(copies[0] + copies[1])
        for x in range(2):
            out_w_ref[:, x * third : (x + 1) * third] = held[x, :, held.shape[2] - third :]
        for pair in range(2 * third // PAIR):
            for part in range(3):
                for x, low, high, lane in segments(pair, third):
                    at = (3 * pair + part) * PAIR + lane
                    source = slice(part * third + low, part * third + high)
                    full_ref[:, at : at + high - low] = held[x, :, source]
        first = cols // 128 * 128
        rows = turn(held[0, :, first : first + 128].astype(F32))[cols - first :]
        vec_ref[...] = rows[: vec_ref.shape[0]]
        row_at = lax.broadcasted_iota(jnp.int32, (rows.shape[1], 2 * third), 0)
        lane_at = lax.broadcasted_iota(jnp.int32, (rows.shape[1], 2 * third), 1)
        wanted = jnp.where(
            lane_at < third, place_ref[1] + lane_at, place_ref[2] + lane_at - third
        )
        chosen = jnp.where(row_at == wanted, 1.0, 0.0).astype(BF16)
        picked = dot_nn(vec_ref[...].astype(BF16), chosen)
        bias[...] = jnp.zeros_like(bias)
        for pair in range(2 * third // PAIR):
            lanes = slice(pair * PAIR, (pair + 1) * PAIR)
            at = 3 * pair * PAIR
            bias[0:1, at : at + PAIR] = picked[2:3, lanes]
            bias[0:1, at + 2 * PAIR : at + 3 * PAIR] = picked[3:4, lanes]

    tokens = pick_half(step // per_half == place_ref[0], mine_ref, other_ref)
    tokens_ref[...] = tokens.astype(BF16)
    normed, _ = normalize_rows(tokens)
    first_in = (normed * vec_ref[0:1, :] + vec_ref[1:2, :]).astype(BF16)
    norm_ref[...] = first_in
    qkv_ref[...] = (dot_nn(first_in, full_ref[...]) + bias[0:1, :]).astype(BF16)


def first_norm(place, mine, other, gathered, width_loc):
    rows, width = mine.shape
    length = 2 * rows
    cols = 3 * width_loc
    steps = rows // ROW_BLOCK
    half = pl.BlockSpec((ROW_BLOCK, width), lambda step, place_ref: (step % steps, 0))

    def by_row(size):
        return pl.BlockSpec((ROW_BLOCK, size), lambda step, place_ref: (step, 0))

    return pl.pallas_call(
        functools.partial(first_norm_kernel, gathered, cols),
        grid_spec=pltpu.PrefetchScalarGridSpec(
            num_scalar_prefetch=1,
            grid=(2 * steps,),
            in_specs=[half, half] + [ANYWHERE] * len(gathered.arrays),
            out_specs=[
                by_row(width),
                by_row(2 * cols),
                by_row(width),
                whole((width, 2 * cols)),
                whole((width, 2 * width_loc)),
                whole((16, width)),
            ],
            scratch_shapes=weight_scratch(gathered)[:1]
            + [pltpu.VMEM((8, 2 * cols), F32)]
            + weight_scratch(gathered)[1:],
        ),
        out_shape=[
            shaped((length, width), BF16),
            shaped((length, 2 * cols), BF16),
            shaped((length, width), BF16),
            shaped((width, 2 * cols), BF16),
            shaped((width, 2 * width_loc), BF16),
            shaped((16, width), F32),
        ],
        compiler_params=PARAMS,
        cost_estimate=cost(8),
        name="first_norm",
    )(place, mine, other, *gathered.arrays)


def attended_kernel(
    place_ref, heads_ref, heads_two_ref, partner_ref, partner_two_ref, own_ref, other_ref, tokens_ref, vec_ref, first_ref,
    mine_ref, other_cot_ref, hidden_ref, norm_ref, norm_turned_ref, first_turned_ref,
    cot_turned_ref, cot_ref,
):
    heads = jnp.concatenate([heads_ref[...], heads_two_ref[...]], axis=1)
    partner = jnp.concatenate([partner_ref[...], partner_two_ref[...]], axis=1)
    attended = dot_nt(heads, own_ref[...]) + dot_nt(partner, other_ref[...])
    hidden = tokens_ref[...].astype(F32) + attended + vec_ref[4:5, :]
    hidden_ref[...] = hidden
    normed, _ = normalize_rows(hidden)
    second_in = (normed * vec_ref[5:6, :] + vec_ref[6:7, :]).astype(BF16)
    norm_ref[...] = second_in
    norm_turned_ref[...] = turn(second_in)
    first_turned_ref[...] = turn(first_ref[...])
    here = pl.program_id(0) // (pl.num_programs(0) // 2) == place_ref[0]
    cot = pick_half(here, mine_ref, other_cot_ref).astype(BF16)
    cot_ref[...] = cot
    cot_turned_ref[...] = turn(cot)


def attended_norm(place, heads, partner_heads, own_out, partner_out, tokens, vec_all, first_in, cots):
    length, width = tokens.shape
    cols = own_out.shape[1]
    steps = length // ROW_BLOCK
    half = pl.BlockSpec((ROW_BLOCK, width), lambda step, place_ref: (step % (steps // 2), 0))
    turned = pl.BlockSpec((width, ROW_BLOCK), lambda step, place_ref: (0, step))

    def by_row(size):
        return pl.BlockSpec((ROW_BLOCK, size), lambda step, place_ref: (step, 0))

    full = by_row(width)
    return pl.pallas_call(
        attended_kernel,
        grid_spec=pltpu.PrefetchScalarGridSpec(
            num_scalar_prefetch=1,
            grid=(steps,),
            in_specs=[
                *[by_row(part.shape[1]) for part in (*heads, *partner_heads)],
                whole(own_out.shape),
                whole(partner_out.shape),
                full,
                whole(vec_all.shape),
                full,
                half,
                half,
            ],
            out_specs=[full, full, turned, turned, turned, full],
        ),
        out_shape=[shaped((length, width), F32), shaped((length, width), BF16)]
        + [shaped((width, length), BF16)] * 3
        + [shaped((length, width), BF16)],
        compiler_params=PARAMS,
        cost_estimate=cost(8),
        name="attended_norm",
    )(place, *heads, *partner_heads, own_out, partner_out, tokens, vec_all, first_in, *cots)


def feed_kernel(gathered, norm_ref, cot_ref, bias_ref, *refs):
    count = len(gathered.arrays)
    act_ref, gup_ref, bias_sum_ref, out_ref, back_ref, back_low_ref, held, sems = refs[count:]
    copies = weight_copies(gathered, refs[:count], held, sems)
    step = pl.program_id(0)
    length = norm_ref.shape[0]
    curve, cubic = math.sqrt(2 / math.pi), 0.044715
    cols = held.shape[2] // 2
    x = step
    up_lanes, down_lanes = slice(0, cols), slice(cols, 2 * cols)

    @pl.when(step == 0)
    def _():
        start_all(copies[0] + copies[1])
        out_ref[...] = jnp.zeros_like(out_ref)
        back_ref[...] = jnp.zeros_like(back_ref)
        wait_all(copies[0])

    @pl.when(step == 1)
    def _():
        wait_all(copies[1])

    bias_sum = jnp.zeros(bias_ref.shape, F32)
    for first in range(0, length, ROW_BLOCK):
        rows = slice(first, first + ROW_BLOCK)
        up = dot_nn(norm_ref[rows, :], held[x, :, up_lanes]) + bias_ref[...]
        square = up * up
        tanh = jnp.tanh(curve * up * (1.0 + cubic * square))
        act = (0.5 * up * (1.0 + tanh)).astype(BF16)
        act_ref[rows, :] = act
        slope = 0.5 * (1.0 + tanh) + 0.5 * up * (1.0 - tanh * tanh) * (
            curve * (1.0 + 3.0 * cubic * square)
        )
        grad_up = (dot_nn(cot_ref[rows, :], held[x, :, down_lanes]) * slope).astype(BF16)
        gup_ref[rows, :] = grad_up
        bias_sum = bias_sum + jnp.sum(grad_up.astype(F32), axis=0, keepdims=True)
        out_ref[rows, :] += dot_nt(act, held[x, :, down_lanes])
        back_ref[rows, :] += dot_nt(grad_up, held[x, :, up_lanes])
    bias_sum_ref[...] = bias_sum

    @pl.when(step == pl.num_programs(0) - 1)
    def _():
        back_low_ref[...] = back_ref[...].astype(BF16)


def feed(norm, cot, bias, gathered):
    length, width = norm.shape
    hidden = bias.shape[1]
    block = hidden // 2
    tall = pl.BlockSpec((length, block), lambda step: (0, step))
    flat = pl.BlockSpec((1, block), lambda step: (0, step))
    full = whole((length, width))
    return pl.pallas_call(
        functools.partial(feed_kernel, gathered),
        grid=(hidden // block,),
        in_specs=[full, full, flat] + [ANYWHERE] * len(gathered.arrays),
        out_specs=[tall, tall, flat, full, full, full],
        out_shape=[
            shaped((length, hidden), BF16),
            shaped((length, hidden), BF16),
            shaped((1, hidden), F32),
            shaped((length, width), F32),
            shaped((length, width), F32),
            shaped((length, width), BF16),
        ],
        scratch_shapes=weight_scratch(gathered),
        compiler_params=PARAMS,
        cost_estimate=cost(18),
        name="feed",
    )(norm, cot, bias, *gathered.arrays)


def feed_grads_kernel(grid, cot_ref, norm_ref, act_ref, gup_ref, *refs):
    kind, x_at = pl.program_id(0), pl.program_id(1)
    outs, held = refs[:-1], refs[-1]
    size = held.shape[1]

    @pl.when(kind == 0)
    def _():
        held[...] = dot_nn(cot_ref[...], act_ref[...]).astype(BF16)

    @pl.when(kind == 1)
    def _():
        held[...] = dot_nn(norm_ref[...], gup_ref[...]).astype(BF16)

    for index in range(2):
        for x in range(2):

            @pl.when((kind == index) & (x_at == x))
            def _():
                lanes = slice((1 - index) * size, (2 - index) * size)
                store_parts(held, grid, outs, x, slice(None), lanes)


def feed_grads(cot_turned, norm_turned, act, grad_up, grid):
    width, length = cot_turned.shape
    hidden = act.shape[1]
    block = hidden // 2
    shapes = parts_out(grid, width, hidden)
    parts = pl.pallas_call(
        functools.partial(feed_grads_kernel, grid),
        grid=(2, 2),
        in_specs=[
            whole((width, length)),
            whole((width, length)),
            pl.BlockSpec((length, block), lambda kind, x: (0, jnp.where(kind == 0, x, 1))),
            pl.BlockSpec((length, block), lambda kind, x: (0, jnp.where(kind == 1, x, 0))),
        ],
        out_specs=[whole(shape) for shape in shapes],
        out_shape=[shaped(shape, BF16) for shape in shapes],
        scratch_shapes=[pltpu.VMEM((width, block), BF16)],
        compiler_params=PARAMS,
        cost_estimate=cost(10),
        name="feed_grads",
    )(cot_turned, norm_turned, act, grad_up)
    return parts if len(parts) == 4 else grid.split(parts[0])


def second_back_kernel(
    part_ref, other_ref, hidden_ref, cot_ref, vec_ref, out_w_ref, turned_ref,
    turned_two_ref, grad_ref, heads_ref, sum_ref, out_grad_ref, total,
):
    step = pl.program_id(0)
    normed, inv_std = normalize_rows(hidden_ref[...])
    part = part_ref[...]
    cot = cot_ref[...].astype(F32)
    grad_second = part + other_ref[...].astype(F32)
    grad = cot + norm_back(grad_second * vec_ref[5:6, :], normed, inv_std)
    grad_ref[...] = grad
    low = grad.astype(BF16)
    heads_ref[...] = dot_nn(low, out_w_ref[...]).astype(BF16)

    @pl.when(step == 0)
    def _():
        sum_ref[...] = jnp.zeros_like(sum_ref)
        total[...] = jnp.zeros_like(total)

    turned = jnp.concatenate([turned_ref[...], turned_two_ref[...]], axis=0)
    total[...] += dot_nn(turned, low)
    for row, value in enumerate((grad, part * normed, part, cot)):
        sum_ref[row : row + 1, :] += jnp.sum(value, axis=0, keepdims=True)

    @pl.when(step == pl.num_programs(0) - 1)
    def _():
        out_grad_ref[...] = total[...].T.astype(BF16)


def second_back(part, other, hidden, cot, vec_all, out_w, heads_turned):
    length, width = part.shape
    cols = out_w.shape[1]
    full = rows_of(ROW_BLOCK, width)
    return pl.pallas_call(
        second_back_kernel,
        grid=(length // ROW_BLOCK,),
        in_specs=[full, full, full, full, whole(vec_all.shape), whole(out_w.shape)]
        + [pl.BlockSpec((part.shape[0], ROW_BLOCK), lambda step: (0, step)) for part in heads_turned],
        out_specs=[full, rows_of(ROW_BLOCK, cols), whole((8, width)), whole((width, cols))],
        out_shape=[
            shaped((length, width), F32),
            shaped((length, cols), BF16),
            shaped((8, width), F32),
            shaped((width, cols), BF16),
        ],
        scratch_shapes=[pltpu.VMEM((cols, width), F32)],
        compiler_params=PARAMS,
        cost_estimate=cost(8.6),
        name="second_back",
    )(part, other, hidden, cot, vec_all, out_w, *heads_turned)


def qkv_grads_kernel(grid, norm_ref, grad_ref, grad_two_ref, out_grad_ref, vec_ref, *refs):
    step = pl.program_id(0)
    outs, held = refs[:-1], refs[-1]
    third = held.shape[1] // 2
    pairs = 2 * third // PAIR
    for index in range(pairs + 1):

        @pl.when(step == index)
        def _():
            if index == pairs:
                held[...] = out_grad_ref[...]
                for x in range(2):
                    source = slice(x * third, (x + 1) * third)
                    store_parts(held, grid, outs, x, source, slice(3 * third, 4 * third))
                rows = vec_ref[...]
                blank = jnp.zeros((VEC_LANES - rows.shape[0], rows.shape[1]), F32)
                held[:, :VEC_LANES] = jnp.concatenate([rows, blank], axis=0).T.astype(BF16)
                for x in range(2):
                    lanes = slice(4 * third, 4 * third + VEC_LANES)
                    store_parts(held, grid, outs, x, slice(0, VEC_LANES), lanes)
                return
            right = grad_two_ref if index == pairs - 1 else grad_ref
            held[...] = dot_nn(norm_ref[...], right[...]).astype(BF16)
            for part in range(3):
                for x, low, high, lane in segments(index, third):
                    at = part * PAIR + lane
                    lanes = slice(part * third + low, part * third + high)
                    store_parts(held, grid, outs, x, slice(at, at + high - low), lanes)


def qkv_grads(norm_turned, grads, out_grad, grid, grad_vec):
    width, length = norm_turned.shape
    cols = out_grad.shape[1]
    pairs = cols // PAIR
    shapes = parts_out(grid, width, 2 * cols + VEC_LANES)
    parts = pl.pallas_call(
        functools.partial(qkv_grads_kernel, grid),
        grid=(pairs + 1,),
        in_specs=[
            whole((width, length)),
            pl.BlockSpec((length, cols), lambda step: (0, jnp.minimum(step, pairs - 2))),
            whole((length, cols)),
            whole((width, cols)),
            whole(grad_vec.shape),
        ],
        out_specs=[whole(shape) for shape in shapes],
        out_shape=[shaped(shape, BF16) for shape in shapes],
        scratch_shapes=[pltpu.VMEM((width, cols), BF16)],
        compiler_params=PARAMS,
        cost_estimate=cost(1.5),
        name="qkv_grads",
    )(norm_turned, *grads, out_grad, grad_vec)
    return parts if len(parts) == 4 else grid.split(parts[0])


def first_back_kernel(
    place_ref, grad_ref, grad_two_ref, weight_ref, tokens_ref, second_ref, up_ref,
    part_ref, vec_ref, bias,
):
    grads = jnp.concatenate([grad_ref[...], grad_two_ref[...]], axis=1)
    part = dot_nt(grads, weight_ref[...])
    part_ref[...] = part
    normed, _ = normalize_rows(tokens_ref[...].astype(F32))

    @pl.when(pl.program_id(0) == 0)
    def _():
        vec_ref[...] = jnp.zeros_like(vec_ref)
        bias[...] = jnp.zeros_like(bias)

    for row, value in enumerate((part * normed, part)):
        vec_ref[row : row + 1, :] += jnp.sum(value, axis=0, keepdims=True)
    bias[0:1, :] += jnp.sum(grads.astype(F32), axis=0, keepdims=True)

    @pl.when(pl.program_id(0) == pl.num_programs(0) - 1)
    def _():
        width = vec_ref.shape[1]
        pairs = bias.shape[1] // (3 * PAIR)
        third = pairs * PAIR // 2
        for row, part_at in ((2, 0), (3, 2)):
            lanes = [
                bias[:, (3 * pair + part_at) * PAIR : (3 * pair + part_at + 1) * PAIR]
                for pair in range(pairs)
            ]
            joined = jnp.concatenate(lanes, axis=1)
            blank = jnp.zeros((joined.shape[0], width - third), F32)
            for x in range(2):
                block = jnp.concatenate([joined[:, x * third : (x + 1) * third], blank], axis=1)
                vec_ref[row : row + 1, :] += pltpu.roll(block, place_ref[1 + x], 1)[0:1]
        vec_ref[4:5, :] = 0.5 * second_ref[0:1, :]
        vec_ref[5:7, :] = second_ref[1:3, :]
        vec_ref[7:8, :] = 0.5 * second_ref[3:4, :]
        row_at = lax.broadcasted_iota(jnp.int32, (8, width), 0)
        vec_ref[8:16, :] = jnp.where(row_at == place_ref[3], up_ref[0:1, :width], 0.0) + jnp.where(
            row_at == place_ref[4], up_ref[0:1, width:], 0.0
        )


def first_back(place, grads, weight, tokens, second_sums, up_sums):
    length, width = tokens.shape
    cols = weight.shape[1]

    def by_row(size):
        return pl.BlockSpec((ROW_BLOCK, size), lambda step, place_ref: (step, 0))

    return pl.pallas_call(
        first_back_kernel,
        grid_spec=pltpu.PrefetchScalarGridSpec(
            num_scalar_prefetch=1,
            grid=(length // ROW_BLOCK,),
            in_specs=[
                by_row(grads[0].shape[1]),
                by_row(grads[1].shape[1]),
                whole(weight.shape),
                by_row(width),
                whole(second_sums.shape),
                whole(up_sums.shape),
            ],
            out_specs=[by_row(width), whole((16, width))],
            scratch_shapes=[pltpu.VMEM((8, cols), F32)],
        ),
        out_shape=[shaped((length, width), F32), shaped((16, width), F32)],
        compiler_params=PARAMS,
        cost_estimate=cost(1.5),
        name="first_back",
    )(place, *grads, weight, tokens, second_sums, up_sums)


def token_back_kernel(core_ref, part_ref, other_ref, tokens_ref, grad_ref, vec_ref, out_ref):
    normed, inv_std = normalize_rows(tokens_ref[...].astype(F32))
    grad_first = part_ref[...] + other_ref[...].astype(F32)
    out_ref[...] = grad_ref[...] + norm_back(grad_first * vec_ref[0:1, :], normed, inv_std)


def token_back(core, part, other, tokens, grad_hidden, vec_all):
    rows, width = tokens.shape
    steps = rows // ROW_BLOCK
    own = pl.BlockSpec((ROW_BLOCK, width), lambda step, core_ref: (core_ref[0] * steps + step, 0))
    here = pl.BlockSpec((ROW_BLOCK, width), lambda step, core_ref: (step, 0))
    return pl.pallas_call(
        token_back_kernel,
        grid_spec=pltpu.PrefetchScalarGridSpec(
            num_scalar_prefetch=1,
            grid=(steps,),
            in_specs=[own, here, here, own, whole(vec_all.shape)],
            out_specs=here,
        ),
        out_shape=shaped((rows, width), F32),
        compiler_params=PARAMS,
        cost_estimate=cost(3.2),
        name="token_back",
    )(core.reshape(1), part, other, tokens, grad_hidden, vec_all)


def out_step_kernel(grad_ref, weight_ref, first_ref, second_ref, new_ref, new_first_ref, new_second_ref):
    grads = grad_ref[...].T
    results = adamw(weight_ref[...], first_ref[...], second_ref[...], grads, RATE_MATRIX)
    new_ref[...], new_first_ref[...], new_second_ref[...] = results


def out_step(weight, first, second, grads):
    return pl.pallas_call(
        out_step_kernel,
        out_shape=[shaped(weight.shape, F32)] * 3,
        compiler_params=PARAMS,
        name="out_step",
    )(grads, weight, first, second)


def shards(
    tokens,
    cotangent,
    w_qkv,
    w_out,
    w_up,
    w_down,
    vectors,
    first_qkv,
    first_out,
    first_up,
    first_down,
    first_vectors,
    second_qkv,
    second_out,
    second_up,
    second_down,
    second_vectors,
):
    col_index = lax.axis_index("col")
    grid = Grid(lax.axis_size("row"))
    core_line = ("col", 1)
    core = col_index % 2
    other_col = col_index ^ 2
    rows_loc, width = tokens.shape
    width_loc = w_qkv.shape[2]
    hidden_loc = w_up.shape[1]
    shard_rows = w_up.shape[0]

    pad = -(3 * width_loc + VEC_ROWS) % 128
    pack_qkv = jnp.concatenate(
        [w_qkv[:, part].astype(BF16) for part in range(3)]
        + [vectors.T.astype(BF16), jnp.zeros((shard_rows, pad), BF16), w_out.T.astype(BF16)],
        axis=1,
    )
    pack_feed = jnp.concatenate([w_up.astype(BF16), w_down.T.astype(BF16)], axis=1)

    def own_rows(value):
        return lax.dynamic_slice_in_dim(value, core * rows_loc, rows_loc, 0)

    def partner_rows(value):
        return lax.dynamic_slice_in_dim(value, (1 - core) * rows_loc, rows_loc, 0)

    place = jnp.stack(
        [core, col_index * width_loc, other_col * width_loc, col_index, other_col]
    ).astype(jnp.int32)

    far_qkv = grid.gather_far(pack_qkv)
    partner = swap_over(jnp.stack([tokens, cotangent]), core_line)
    far_qkv, partner, pack_feed = lax.optimization_barrier((far_qkv, partner, pack_feed))
    one_qkv = grid.gather_one(far_qkv)
    far_feed = grid.gather_far(pack_feed)
    near_qkv = grid.gather_three(*grid.gather_two(*one_qkv))
    one_feed = grid.gather_one(far_feed)

    def cat_blocks(vec_row, size):
        return jnp.concatenate(
            [
                lax.dynamic_slice_in_dim(vec_row, col_index * size, size, 0),
                lax.dynamic_slice_in_dim(vec_row, other_col * size, size, 0),
            ]
        )

    first_in, qkv, all_tokens, full_qkv, full_out, vec_all = first_norm(
        place, tokens, partner[0], near_qkv, width_loc
    )
    bias_up = cat_blocks(vec_all[8:VEC_ROWS].reshape(-1), hidden_loc)
    partner_out = swap_over(full_out, core_line)
    pairs = 2 * width_loc // PAIR
    heads_one, turned_one, lse_one = attend_forward(qkv, 0, pairs - 1, ())
    kept, arrived = one_feed
    arrived, heads_one = lax.optimization_barrier((arrived, heads_one))
    front, front_at, back = grid.gather_two(kept, arrived)
    heads_two, turned_two, lse_two = attend_forward(qkv, pairs - 1, 1, (front, back))
    near_feed = grid.gather_three(front, front_at, back)
    heads = (heads_one, heads_two)
    partner_heads = [swap_over(part, core_line) for part in heads]
    hidden_state, second_in, second_turned, first_turned, cot_turned, all_cot = attended_norm(
        place, heads, partner_heads, full_out, partner_out, all_tokens, vec_all, first_in,
        (cotangent, partner[1]),
    )
    activated, grad_upper, grad_bias_up, down_part, second_part, second_low = feed(
        second_in, all_cot, bias_up[None], near_feed
    )

    second_other = swap_over(second_low, core_line)
    parts_feed = feed_grads(cot_turned, second_turned, activated, grad_upper, grid)
    arrived_feed = grid.stage_one(parts_feed)
    grad_hidden, grad_heads, second_sums, out_grad = second_back(
        second_part, second_other, hidden_state, all_cot, vec_all, full_out,
        (turned_one, turned_two),
    )
    grad_one = attend_backward(qkv, grad_heads, lse_one, 0, ())
    arrived_feed, grad_one = lax.optimization_barrier((arrived_feed, grad_one))
    kept_feed, sent_feed = grid.stage_two(parts_feed, *arrived_feed)
    grad_two = attend_backward(qkv, grad_heads, lse_two, pairs - 1, sent_feed)
    grads_qkv = (grad_one, grad_two)
    first_part, grad_vec = first_back(
        place, grads_qkv, full_qkv, all_tokens, second_sums, grad_bias_up
    )
    parts_qkv = qkv_grads(first_turned, grads_qkv, out_grad, grid, grad_vec)
    arrived_pack = grid.stage_one(parts_qkv)
    owned_feed = grid.reduce_chain(grid.stage_three(kept_feed, sent_feed))
    owned_up, owned_down = owned_feed[:, :hidden_loc], owned_feed[:, hidden_loc:]

    kept_pack, sent_pack = grid.stage_two(parts_qkv, *arrived_pack)
    sent_pack, first_part, down_part = lax.optimization_barrier(
        (sent_pack, first_part, down_part)
    )
    near_pack = grid.stage_three(kept_pack, sent_pack)
    first_other = swap_over(partner_rows(first_part).astype(BF16), core_line)
    down_other = swap_over(partner_rows(down_part).astype(BF16), core_line).astype(F32)
    mixed_out = own_rows(hidden_state) + own_rows(down_part) + down_other + vec_all[7]
    token_grad = token_back(core, first_part, first_other, tokens, grad_hidden, vec_all)
    owned_pack, (mixed_out, token_grad) = grid.reduce_direct(near_pack, (mixed_out, token_grad))
    part_vec = owned_pack[:, 4 * width_loc :]
    owned_vec = (part_vec + swap_over(part_vec, core_line))[:, :VEC_ROWS].T
    owned_qkv = jnp.stack(
        [owned_pack[:, part * width_loc : (part + 1) * width_loc] for part in range(3)], axis=1
    )
    owned_out = owned_pack[:, 3 * width_loc : 4 * width_loc]

    new_qkv, new_first_qkv, new_second_qkv = adamw(
        w_qkv, first_qkv, second_qkv, owned_qkv, RATE_MATRIX
    )
    new_out, new_first_out, new_second_out = out_step(w_out, first_out, second_out, owned_out)
    new_up, new_first_up, new_second_up = adamw(w_up, first_up, second_up, owned_up, RATE_MATRIX)
    new_down, new_first_down, new_second_down = adamw(
        w_down, first_down, second_down, owned_down.T, RATE_MATRIX
    )
    new_vectors, new_first_vectors, new_second_vectors = adamw(
        vectors, first_vectors, second_vectors, owned_vec, RATE_VECTOR
    )
    return (
        mixed_out,
        token_grad,
        new_qkv,
        new_out,
        new_up,
        new_down,
        new_vectors,
        new_first_qkv,
        new_first_out,
        new_first_up,
        new_first_down,
        new_first_vectors,
        new_second_qkv,
        new_second_out,
        new_second_up,
        new_second_down,
        new_second_vectors,
    )


def solution(mesh):
    by_token = P(("row", "col"), None)
    weights = (
        P("row", None, "col"),
        P("col", "row"),
        P("row", "col"),
        P("col", "row"),
        P(None, "row"),
    )
    return jax.shard_map(
        shards,
        mesh=mesh,
        in_specs=(by_token, by_token) + weights * 3,
        out_specs=(by_token, by_token) + weights * 3,
        check_vma=False,
    )
```

```python
import functools
import math

import jax
import jax.numpy as jnp
from jax import lax
from jax.experimental import pallas as pl
from jax.experimental.pallas import tpu as pltpu
from jax.sharding import PartitionSpec as P

HEAD_DIM = 64
LENGTH = 1024
STEP_NUMBER = 10
VEC_ROWS = 12
PAIR = 2 * HEAD_DIM
QUERY_BLOCK = 256
ROW_BLOCK = 256
VEC_LANES = 128
COST_SCALE = 2.3e8


EPS = 1e-05
BETA_ONE = 0.9
BETA_TWO = 0.999
ADAM_EPS = 1e-08
DECAY = 0.1
RATE_MATRIX = 0.04
RATE_VECTOR = 0.3

F32 = jnp.float32
BF16 = jnp.bfloat16


def normalize_rows(values_in):
    row_mean = jnp.mean(values_in, axis=-1, keepdims=True)
    centred = values_in - row_mean
    row_var = jnp.mean(centred * centred, axis=-1, keepdims=True)
    inv_std = lax.rsqrt(row_var + EPS)
    return (centred * inv_std, inv_std)


def norm_back(grad_in, normed, inv_std):
    mean_grad = jnp.mean(grad_in, axis=-1, keepdims=True)
    mean_cross = jnp.mean(grad_in * normed, axis=-1, keepdims=True)
    return inv_std * (grad_in - mean_grad - normed * mean_cross)


def adamw(weight, moment_one, moment_two, gradient, rate):
    first = BETA_ONE * moment_one + (1 - BETA_ONE) * gradient
    second = BETA_TWO * moment_two + (1 - BETA_TWO) * gradient * gradient
    first_hat = first / (1 - BETA_ONE**STEP_NUMBER)
    second_hat = second / (1 - BETA_TWO**STEP_NUMBER)
    updated = weight - rate * (first_hat / (jnp.sqrt(second_hat) + ADAM_EPS) + DECAY * weight)
    return (updated, first, second)


def swap_over(value, line):
    name, offset = line
    pairs = [(index, index ^ offset) for index in range(lax.axis_size(name))]
    return lax.ppermute(value, name, pairs)


def bit_offsets(low, high):
    offsets = []
    while low < high:
        offsets.append(low)
        low *= 2
    return offsets


def flip_order(blocks):
    count = blocks.shape[0]
    row = lax.axis_index("row")
    for offset in bit_offsets(1, count):
        cut = blocks.reshape((-1, 2, offset) + blocks.shape[1:])
        turned = jnp.where((row // offset) % 2 == 1, cut[:, ::-1], cut)
        blocks = turned.reshape(blocks.shape)
    return blocks


class Gathered:
    def __init__(self, arrays, table):
        self.arrays = arrays
        self.table = table
        self.rows = arrays[0].shape[1]
        self.cols = arrays[0].shape[2]
        if self.rows % 16:
            total = []
            for x in range(2):
                found = sorted((offset, array, at) for x_at, array, at, offset in table if x_at == x)
                blocks = jnp.stack([arrays[array][at] for _, array, at in found])
                total.append(flip_order(blocks).reshape(-1, self.cols))
            self.arrays = [jnp.stack(total)]
            self.table = [(0, 0, 0, 0), (1, 0, 1, 0)]
            self.rows = self.arrays[0].shape[1]


class Grid:
    def __init__(self, row_count):
        self.near_size = {8: 2, 64: 4}.get(row_count, 1)
        self.row_count = row_count
        self.far_count = row_count // self.near_size
        self.near = bit_offsets(1, self.near_size)
        self.x_line = ("col", 2)

    def gather_far(self, block):
        blocks = [block]
        for index in range(1, self.far_count):
            blocks.append(swap_over(block, ("row", index * self.near_size)))
        return blocks

    def gather_ready(self, blocks):
        half = self.far_count // 2
        return jnp.stack(blocks[:half]), jnp.stack(blocks[half:])

    def gather_one(self, sent):
        return swap_over(sent[0], ("row", self.near[0])), swap_over(sent[1], self.x_line)

    def gather_two(self, kept, arrived):
        half = self.far_count // 2
        front = jnp.concatenate([kept[0], arrived[0]], axis=0)
        back = jnp.concatenate([kept[1], arrived[1]], axis=0)
        front_at = [index * self.near_size for index in range(half)]
        front_at = front_at + [at ^ self.near[0] for at in front_at]
        for offset in self.near[1:]:
            front = jnp.concatenate([front, swap_over(front, ("row", offset))], axis=0)
            front_at = front_at + [at ^ offset for at in front_at]
        return front, front_at, back

    def gather_three(self, front, front_at, back):
        half = self.far_count // 2
        back_at = [(x, (index + half) * self.near_size) for x in range(2) for index in range(half)]
        arrays = [front, swap_over(front, self.x_line), back]
        table = [(x, x, index, at) for x in range(2) for index, at in enumerate(front_at)]
        table += [(x, 2, index, at) for index, (x, at) in enumerate(back_at)]
        for offset in self.near:
            sent = back if len(arrays) == 3 else jnp.concatenate(arrays[2:], axis=0)
            arrays.append(swap_over(sent, ("row", offset)))
            moved = [(x, at ^ offset) for x, at in back_at]
            table += [(x, len(arrays) - 1, index, at) for index, (x, at) in enumerate(moved)]
            back_at = back_at + moved
        return Gathered(arrays, table)

    def split(self, pair):
        _, all_rows, cols = pair.shape
        blocks = jnp.moveaxis(pair.reshape(2, self.row_count, -1, cols), 1, 0)
        blocks = jnp.moveaxis(flip_order(blocks), 0, 1)
        rows = blocks.shape[2]
        half = self.row_count // 2
        back = blocks[:, half:].reshape(2, self.far_count // 2, 2, -1, rows, cols)
        return (
            blocks[0, :half],
            blocks[1, :half],
            back[:, :, 0].reshape(2, -1, rows, cols),
            back[:, :, 1].reshape(2, -1, rows, cols),
        )

    def part_of(self, x, index):
        far, near = index // self.near_size, index % self.near_size
        half, step = self.far_count // 2, self.near_size // 2
        if far < half:
            return x, (index,)
        if near < step:
            return 2, (x, (far - half) * step + near)
        return 3, (x, (far - half) * step + near - step)

    def part_shapes(self, rows, cols):
        count = self.row_count
        return [(count // 2, rows, cols)] * 2 + [(2, count // 4, rows, cols)] * 2

    def stage_one(self, parts):
        step = self.near_size // 2
        return swap_over(parts[1], self.x_line), swap_over(parts[3], ("row", step))

    def stage_two(self, parts, front_x, back_y):
        rows, cols = parts[0].shape[1:]
        half, step = self.far_count // 2, self.near_size // 2
        back = parts[2].astype(F32) + back_y.astype(F32)
        back = self.reduce_bits(back.reshape(2, half, step, rows, cols), 2)
        front = parts[0].astype(F32) + front_x.astype(F32)
        front = front.reshape(half, self.near_size, rows, cols)
        return (front[:, :step], back[0]), (front[:, step:].astype(BF16), back[1].astype(BF16))

    def stage_three(self, kept, sent, hold=None):
        step = self.near_size // 2
        front, back = swap_over(sent[0], ("row", step)), swap_over(sent[1], self.x_line)
        if hold is not None:
            front, back, _ = lax.optimization_barrier((front, back, hold))
        back = kept[1] + back.astype(F32)
        front = kept[0] + front.astype(F32)
        front = self.reduce_bits(front, 1)
        rows, cols = front.shape[2:]
        return jnp.concatenate([front, back], axis=0).reshape(self.far_count, rows, cols)

    def reduce_bits(self, parts, dim):
        while parts.shape[dim] > 1:
            step = parts.shape[dim] // 2
            kept = lax.slice_in_dim(parts, 0, step, axis=dim)
            sent = lax.slice_in_dim(parts, step, 2 * step, axis=dim).astype(BF16)
            parts = kept + swap_over(sent, ("row", step)).astype(F32)
        return parts

    def chain_send(self, parts):
        return parts[0::2], parts[1::2].astype(BF16)

    def reduce_chain(self, kept, sent):
        offset = self.near_size
        parts = kept + swap_over(sent, ("row", offset)).astype(F32)
        while parts.shape[0] > 1:
            offset *= 2
            kept, sent = self.chain_send(parts)
            parts = kept + swap_over(sent, ("row", offset)).astype(F32)
        return parts[0]

    def reduce_direct(self, parts, hold):
        low = parts.astype(BF16)
        arrived = [
            swap_over(low[index], ("row", index * self.near_size))
            for index in range(1, self.far_count)
        ]
        arrived, hold = lax.optimization_barrier((arrived, hold))
        total = parts[0]
        for part in arrived:
            total = total + part.astype(F32)
        return total, hold


def dot_nt(left, right):
    return lax.dot_general(left, right, (((1,), (1,)), ((), ())), preferred_element_type=F32)


def dot_nn(left, right):
    return lax.dot_general(left, right, (((1,), (0,)), ((), ())), preferred_element_type=F32)


def lane_pick(half):
    lanes = lax.broadcasted_iota(jnp.int32, (1, PAIR), 1)
    return jnp.where((lanes // HEAD_DIM) == half, 1.0, 0.0).astype(BF16)


def causal_block(size):
    key_at = lax.broadcasted_iota(jnp.int32, (size, size), 0)
    query_at = lax.broadcasted_iota(jnp.int32, (size, size), 1)
    return key_at <= query_at


def cost(microseconds):
    return pl.CostEstimate(
        flops=int(microseconds * COST_SCALE), bytes_accessed=1024, transcendentals=0
    )


def attend_kernel(q_ref, k_ref, v_ref, out_ref, turned_ref, lse_ref):
    length = q_ref.shape[0]
    block = min(QUERY_BLOCK, length)
    allowed = causal_block(block)
    values_t = v_ref[...].T
    scaling = jnp.asarray(HEAD_DIM**-0.5, BF16)
    for first in range(0, length, block):
        last = first + block
        query = q_ref[first:last, :] * scaling
        outs = []
        for half in range(2):
            rows = slice(half * HEAD_DIM, (half + 1) * HEAD_DIM)
            query_half = query * lane_pick(half)
            diag = dot_nt(k_ref[first:last, :], query_half)
            diag = jnp.where(allowed, diag, -1e30)
            top = jnp.max(diag, axis=0, keepdims=True)
            if first:
                rest = dot_nt(k_ref[0:first, :], query_half)
                top = jnp.maximum(top, jnp.max(rest, axis=0, keepdims=True))
            diag = jnp.exp(diag - top)
            total = jnp.sum(diag, axis=0, keepdims=True)
            if first:
                rest = jnp.exp(rest - top)
                total = total + jnp.sum(rest, axis=0, keepdims=True)
            inverse = 1.0 / total
            result = dot_nn(values_t[rows, first:last], (diag * inverse).astype(BF16))
            if first:
                result = result + dot_nn(values_t[rows, 0:first], (rest * inverse).astype(BF16))
            outs.append(result)
            lse_ref[0, half : half + 1, first:last] = top + jnp.log(total)
        turned = jnp.concatenate(outs, axis=0)
        out_ref[first:last, :] = turned.T.astype(BF16)
        turned_ref[:, first:last] = turned.astype(BF16)


def pair_lanes(length, first, part):
    return pl.BlockSpec((length, PAIR), lambda pair: (0, 3 * (first + pair) + part))


def attend_forward(qkv, after):
    length = qkv.shape[0]
    pairs = qkv.shape[1] // (3 * PAIR)
    return pl.pallas_call(
        lambda q, k, v, *refs: attend_kernel(q, k, v, *refs[len(after) :]),
        grid=(pairs,),
        in_specs=[pair_lanes(length, 0, part) for part in range(3)]
        + [pl.BlockSpec(memory_space=pl.ANY)] * len(after),
        out_specs=[
            pl.BlockSpec((length, PAIR), lambda pair: (0, pair)),
            pl.BlockSpec((PAIR, length), lambda pair: (pair, 0)),
            pl.BlockSpec((1, 8, length), lambda pair: (pair, 0, 0)),
        ],
        out_shape=[
            jax.ShapeDtypeStruct((length, pairs * PAIR), BF16),
            jax.ShapeDtypeStruct((pairs * PAIR, length), BF16),
            jax.ShapeDtypeStruct((pairs, 8, length), F32),
        ],
        compiler_params=pltpu.CompilerParams(vmem_limit_bytes=40 * 2**20),
        cost_estimate=cost(4.2 * pairs),
        name="attend_forward",
    )(qkv, qkv, qkv, *after)


def attend_back_kernel(q_ref, k_ref, v_ref, go_ref, lse_ref, grad_ref, gk_sum, gv_sum):
    length = q_ref.shape[0]
    block = min(QUERY_BLOCK, length)
    allowed = causal_block(block)
    keys_t = k_ref[...].T
    scaling = jnp.asarray(HEAD_DIM**-0.5, BF16)
    pair = pl.program_id(0)

    def lanes(part):
        return pl.ds(pl.multiple_of((3 * pair + part) * PAIR, PAIR), PAIR)

    gk_sum[...] = jnp.zeros_like(gk_sum)
    gv_sum[...] = jnp.zeros_like(gv_sum)
    for first in range(0, length, block):
        last = first + block
        query = q_ref[first:last, :] * scaling
        grad_out = go_ref[first:last, :]
        outs = []
        for half in range(2):
            rows = slice(half * HEAD_DIM, (half + 1) * HEAD_DIM)
            pick = lane_pick(half)
            query_half = query * pick
            grad_half = grad_out * pick
            lse = lse_ref[0, half : half + 1, first:last]
            spans = [(first, last)] if first == 0 else [(0, first), (first, last)]
            probs, grads, inner = [], [], None
            for low, high in spans:
                scores = dot_nt(k_ref[low:high, :], query_half)
                if low == first:
                    scores = jnp.where(allowed, scores, -1e30)
                prob = jnp.exp(scores - lse)
                grad_prob = dot_nt(v_ref[low:high, :], grad_half)
                part = jnp.sum(prob * grad_prob, axis=0, keepdims=True)
                inner = part if inner is None else inner + part
                probs.append(prob)
                grads.append(grad_prob)
            result = None
            for (low, high), prob, grad_prob in zip(spans, probs, grads):
                grad_score = (prob * (grad_prob - inner)).astype(BF16)
                gk_sum[low:high, :] += dot_nn(grad_score, query_half)
                gv_sum[low:high, :] += dot_nn(prob.astype(BF16), grad_half)
                part = dot_nn(keys_t[rows, low:high], grad_score)
                result = part if result is None else result + part
            outs.append(result)
        grad_query = jnp.concatenate(outs, axis=0).T * (HEAD_DIM**-0.5)
        grad_ref[first:last, lanes(0)] = grad_query.astype(BF16)
    grad_ref[:, lanes(1)] = gk_sum[...].astype(BF16)
    grad_ref[:, lanes(2)] = gv_sum[...].astype(BF16)


def attend_backward(qkv, grad_heads, lse, first, pairs, after):
    length = qkv.shape[0]
    width = 3 * PAIR * pairs
    return pl.pallas_call(
        lambda q, k, v, go, lse_at, *refs: attend_back_kernel(
            q, k, v, go, lse_at, *refs[len(after) :]
        ),
        grid=(pairs,),
        in_specs=[pair_lanes(length, first, part) for part in range(3)]
        + [
            pl.BlockSpec((length, PAIR), lambda pair: (0, first + pair)),
            pl.BlockSpec((1, 8, length), lambda pair: (first + pair, 0, 0)),
        ]
        + [pl.BlockSpec(memory_space=pl.ANY)] * len(after),
        out_specs=pl.BlockSpec((length, width), lambda pair: (0, 0)),
        out_shape=jax.ShapeDtypeStruct((length, width), BF16),
        scratch_shapes=[pltpu.VMEM((length, PAIR), F32), pltpu.VMEM((length, PAIR), F32)],
        compiler_params=pltpu.CompilerParams(vmem_limit_bytes=40 * 2**20),
        cost_estimate=cost(1.5 * pairs),
        name="attend_backward",
    )(qkv, qkv, qkv, grad_heads, lse, *after)


def rows_of(block, width):
    return pl.BlockSpec((block, width), lambda step: (step, 0))


def whole(shape):
    return pl.BlockSpec(shape, lambda *step: (0,) * len(shape))


def shaped(shape, dtype):
    return jax.ShapeDtypeStruct(shape, dtype)


PARAMS = pltpu.CompilerParams(vmem_limit_bytes=48 * 2**20)


ANYWHERE = pl.BlockSpec(memory_space=pl.ANY)


def weight_copies(gathered, refs, held, sems):
    row = lax.axis_index("row")
    copies = ([], [])
    for number, (x, array, at, offset) in enumerate(gathered.table):
        if len(gathered.table) > 2:
            start = pl.multiple_of((row ^ offset) * gathered.rows, 16)
        else:
            start = 0
        target = held.at[x, pl.ds(start, gathered.rows), :]
        copies[x].append(
            pltpu.make_async_copy(refs[array].at[at], target, sems.at[number])
        )
    return copies


def weight_scratch(gathered):
    all_rows = len(gathered.table) // 2 * gathered.rows
    return [
        pltpu.VMEM((2, all_rows, gathered.cols), BF16),
        pltpu.SemaphoreType.DMA((len(gathered.table),)),
    ]


def start_all(copies):
    for copy in copies:
        copy.start()


def wait_all(copies):
    for copy in copies:
        copy.wait()


def store_parts(held, grid, refs, x, source, lanes):
    if len(refs) == 1:
        refs[0][x, :, lanes] = held[:, source]
        return
    row = lax.axis_index("row")
    rows = held.shape[0] // grid.row_count
    for index in range(grid.row_count):
        start = pl.multiple_of((row ^ index) * rows, 16)
        array, place = grid.part_of(x, index)
        refs[array][place + (slice(None), lanes)] = held[pl.ds(start, rows), source]


def segments(pair, third):
    low, high, found = pair * PAIR, (pair + 1) * PAIR, []
    while low < high:
        x = low // third
        end = min(high, (x + 1) * third)
        found.append((x, low - x * third, end - x * third, low - pair * PAIR))
        low = end
    return found


def parts_out(grid, width, cols):
    rows = width // grid.row_count
    if rows % 16:
        return [(2, width, cols)]
    return grid.part_shapes(rows, cols)


def turn(value):
    return value.T


def pick_half(here, mine_ref, other_ref):
    mine, other = mine_ref[...].astype(F32), other_ref[...].astype(F32)
    return jnp.where(here, mine, other)


def first_norm_kernel(gathered, cols, place_ref, mine_ref, other_ref, after_ref, *refs):
    count = len(gathered.arrays)
    norm_ref, qkv_ref, tokens_ref, full_ref, out_w_ref, vec_ref, held, bias, sems = refs[count:]
    copies = weight_copies(gathered, refs[:count], held, sems)
    third = cols // 3
    step = pl.program_id(0)
    per_half = pl.num_programs(0) // 2

    @pl.when(step == 0)
    def _():
        start_all(copies[0] + copies[1])
        wait_all(copies[0] + copies[1])
        for x in range(2):
            out_w_ref[:, x * third : (x + 1) * third] = held[x, :, held.shape[2] - third :]
        for pair in range(2 * third // PAIR):
            for part in range(3):
                for x, low, high, lane in segments(pair, third):
                    at = (3 * pair + part) * PAIR + lane
                    source = slice(part * third + low, part * third + high)
                    full_ref[:, at : at + high - low] = held[x, :, source]
        first = cols // 128 * 128
        rows = turn(held[0, :, first : first + 128].astype(F32))[cols - first :]
        vec_ref[...] = rows[: vec_ref.shape[0]]
        row_at = lax.broadcasted_iota(jnp.int32, (rows.shape[1], 2 * third), 0)
        lane_at = lax.broadcasted_iota(jnp.int32, (rows.shape[1], 2 * third), 1)
        wanted = jnp.where(
            lane_at < third, place_ref[1] + lane_at, place_ref[2] + lane_at - third
        )
        chosen = jnp.where(row_at == wanted, 1.0, 0.0).astype(BF16)
        picked = dot_nn(vec_ref[...].astype(BF16), chosen)
        bias[...] = jnp.zeros_like(bias)
        for pair in range(2 * third // PAIR):
            lanes = slice(pair * PAIR, (pair + 1) * PAIR)
            at = 3 * pair * PAIR
            bias[0:1, at : at + PAIR] = picked[2:3, lanes]
            bias[0:1, at + 2 * PAIR : at + 3 * PAIR] = picked[3:4, lanes]

    tokens = pick_half(step // per_half == place_ref[0], mine_ref, other_ref)
    tokens_ref[...] = tokens.astype(BF16)
    normed, _ = normalize_rows(tokens)
    first_in = (normed * vec_ref[0:1, :] + vec_ref[1:2, :]).astype(BF16)
    norm_ref[...] = first_in
    qkv_ref[...] = (dot_nn(first_in, full_ref[...]) + bias[0:1, :]).astype(BF16)


def first_norm(place, mine, other, gathered, width_loc, after):
    rows, width = mine.shape
    length = 2 * rows
    cols = 3 * width_loc
    steps = rows // ROW_BLOCK
    half = pl.BlockSpec((ROW_BLOCK, width), lambda step, place_ref: (step % steps, 0))

    def by_row(size):
        return pl.BlockSpec((ROW_BLOCK, size), lambda step, place_ref: (step, 0))

    return pl.pallas_call(
        functools.partial(first_norm_kernel, gathered, cols),
        grid_spec=pltpu.PrefetchScalarGridSpec(
            num_scalar_prefetch=1,
            grid=(2 * steps,),
            in_specs=[half, half, ANYWHERE] + [ANYWHERE] * len(gathered.arrays),
            out_specs=[
                by_row(width),
                by_row(2 * cols),
                by_row(width),
                whole((width, 2 * cols)),
                whole((width, 2 * width_loc)),
                whole((16, width)),
            ],
            scratch_shapes=weight_scratch(gathered)[:1]
            + [pltpu.VMEM((8, 2 * cols), F32)]
            + weight_scratch(gathered)[1:],
        ),
        out_shape=[
            shaped((length, width), BF16),
            shaped((length, 2 * cols), BF16),
            shaped((length, width), BF16),
            shaped((width, 2 * cols), BF16),
            shaped((width, 2 * width_loc), BF16),
            shaped((16, width), F32),
        ],
        compiler_params=PARAMS,
        cost_estimate=cost(8),
        name="first_norm",
    )(place, mine, other, after, *gathered.arrays)


def attended_kernel(
    heads_ref, partner_ref, own_ref, other_ref, tokens_ref, vec_ref, first_ref,
    hidden_ref, norm_ref, norm_turned_ref, first_turned_ref,
):
    attended = dot_nt(heads_ref[...], own_ref[...]) + dot_nt(partner_ref[...], other_ref[...])
    hidden = tokens_ref[...].astype(F32) + attended + vec_ref[4:5, :]
    hidden_ref[...] = hidden
    normed, _ = normalize_rows(hidden)
    second_in = (normed * vec_ref[5:6, :] + vec_ref[6:7, :]).astype(BF16)
    norm_ref[...] = second_in
    norm_turned_ref[...] = turn(second_in)
    first_turned_ref[...] = turn(first_ref[...])


def attended_norm(heads, partner_heads, own_out, partner_out, tokens, vec_all, first_in):
    length, width = tokens.shape
    cols = own_out.shape[1]
    full, part = rows_of(ROW_BLOCK, width), rows_of(ROW_BLOCK, cols)
    turned = pl.BlockSpec((width, ROW_BLOCK), lambda step: (0, step))
    return pl.pallas_call(
        attended_kernel,
        grid=(length // ROW_BLOCK,),
        in_specs=[
            part,
            part,
            whole(own_out.shape),
            whole(partner_out.shape),
            full,
            whole(vec_all.shape),
            full,
        ],
        out_specs=[full, full, turned, turned],
        out_shape=[shaped((length, width), F32), shaped((length, width), BF16)]
        + [shaped((width, length), BF16)] * 2,
        compiler_params=PARAMS,
        cost_estimate=cost(8),
        name="attended_norm",
    )(heads, partner_heads, own_out, partner_out, tokens, vec_all, first_in)


def join_kernel(place_ref, mine_ref, other_ref, joined_ref, turned_ref):
    here = pl.program_id(0) // (pl.num_programs(0) // 2) == place_ref[0]
    joined = pick_half(here, mine_ref, other_ref).astype(BF16)
    joined_ref[...] = joined
    turned_ref[...] = turn(joined)


def join_halves(place, mine, other):
    rows, width = mine.shape
    steps = rows // ROW_BLOCK
    half = pl.BlockSpec((ROW_BLOCK, width), lambda step, place_ref: (step % steps, 0))
    return pl.pallas_call(
        join_kernel,
        grid_spec=pltpu.PrefetchScalarGridSpec(
            num_scalar_prefetch=1,
            grid=(2 * steps,),
            in_specs=[half, half],
            out_specs=[
                pl.BlockSpec((ROW_BLOCK, width), lambda step, place_ref: (step, 0)),
                pl.BlockSpec((width, ROW_BLOCK), lambda step, place_ref: (0, step)),
            ],
        ),
        out_shape=[shaped((2 * rows, width), BF16), shaped((width, 2 * rows), BF16)],
        compiler_params=PARAMS,
        cost_estimate=cost(4),
        name="join_halves",
    )(place, mine, other)


def feed_kernel(gathered, place_ref, norm_ref, cot_ref, vec_ref, *refs):
    count = len(gathered.arrays)
    act_ref, gup_ref, bias_sum_ref, out_ref, back_ref, back_low_ref, held, sems = refs[count:]
    copies = weight_copies(gathered, refs[:count], held, sems)
    step = pl.program_id(0)
    length = norm_ref.shape[0]
    curve, cubic = math.sqrt(2 / math.pi), 0.044715
    cols = held.shape[2] // 2
    x = step
    up_lanes, down_lanes = slice(0, cols), slice(cols, 2 * cols)
    bias = vec_ref[pl.ds(8 + place_ref[3 + x], 1), :]

    @pl.when(step == 0)
    def _():
        start_all(copies[0] + copies[1])
        out_ref[...] = jnp.zeros_like(out_ref)
        back_ref[...] = jnp.zeros_like(back_ref)
        wait_all(copies[0])

    @pl.when(step == 1)
    def _():
        wait_all(copies[1])

    bias_sum = jnp.zeros(bias.shape, F32)
    for first in range(0, length, ROW_BLOCK):
        rows = slice(first, first + ROW_BLOCK)
        up = dot_nn(norm_ref[rows, :], held[x, :, up_lanes]) + bias
        square = up * up
        tanh = jnp.tanh(curve * up * (1.0 + cubic * square))
        act = (0.5 * up * (1.0 + tanh)).astype(BF16)
        act_ref[rows, :] = act
        slope = 0.5 * (1.0 + tanh) + 0.5 * up * (1.0 - tanh * tanh) * (
            curve * (1.0 + 3.0 * cubic * square)
        )
        grad_up = (dot_nn(cot_ref[rows, :], held[x, :, down_lanes]) * slope).astype(BF16)
        gup_ref[rows, :] = grad_up
        bias_sum = bias_sum + jnp.sum(grad_up.astype(F32), axis=0, keepdims=True)
        out_ref[rows, :] += dot_nt(act, held[x, :, down_lanes])
        back_ref[rows, :] += dot_nt(grad_up, held[x, :, up_lanes])
    bias_sum_ref[...] = bias_sum

    @pl.when(step == pl.num_programs(0) - 1)
    def _():
        back_low_ref[...] = back_ref[...].astype(BF16)


def feed(place, norm, cot, vec_all, gathered):
    length, width = norm.shape
    block = gathered.cols // 2
    hidden = 2 * block
    tall = pl.BlockSpec((length, block), lambda step, place_ref: (0, step))
    flat = pl.BlockSpec((1, block), lambda step, place_ref: (0, step))
    full = whole((length, width))
    return pl.pallas_call(
        functools.partial(feed_kernel, gathered),
        grid_spec=pltpu.PrefetchScalarGridSpec(
            num_scalar_prefetch=1,
            grid=(2,),
            in_specs=[full, full, whole(vec_all.shape)] + [ANYWHERE] * len(gathered.arrays),
            out_specs=[tall, tall, flat, full, full, full],
            scratch_shapes=weight_scratch(gathered),
        ),
        out_shape=[
            shaped((length, hidden), BF16),
            shaped((length, hidden), BF16),
            shaped((1, hidden), F32),
            shaped((length, width), F32),
            shaped((length, width), F32),
            shaped((length, width), BF16),
        ],
        compiler_params=PARAMS,
        cost_estimate=cost(18),
        name="feed",
    )(place, norm, cot, vec_all, *gathered.arrays)


def feed_grads_kernel(grid, cot_ref, norm_ref, act_ref, gup_ref, *refs):
    kind, x_at = pl.program_id(0), pl.program_id(1)
    outs, held = refs[:-1], refs[-1]
    size = held.shape[1]

    @pl.when(kind == 0)
    def _():
        held[...] = dot_nn(cot_ref[...], act_ref[...]).astype(BF16)

    @pl.when(kind == 1)
    def _():
        held[...] = dot_nn(norm_ref[...], gup_ref[...]).astype(BF16)

    for index in range(2):
        for x in range(2):

            @pl.when((kind == index) & (x_at == x))
            def _():
                lanes = slice((1 - index) * size, (2 - index) * size)
                store_parts(held, grid, outs, x, slice(None), lanes)


def feed_grads(cot_turned, norm_turned, act, grad_up, grid):
    width, length = cot_turned.shape
    hidden = act.shape[1]
    block = hidden // 2
    shapes = parts_out(grid, width, hidden)
    parts = pl.pallas_call(
        functools.partial(feed_grads_kernel, grid),
        grid=(2, 2),
        in_specs=[
            whole((width, length)),
            whole((width, length)),
            pl.BlockSpec((length, block), lambda kind, x: (0, jnp.where(kind == 0, x, 1))),
            pl.BlockSpec((length, block), lambda kind, x: (0, jnp.where(kind == 1, x, 0))),
        ],
        out_specs=[whole(shape) for shape in shapes],
        out_shape=[shaped(shape, BF16) for shape in shapes],
        scratch_shapes=[pltpu.VMEM((width, block), BF16)],
        compiler_params=PARAMS,
        cost_estimate=cost(10),
        name="feed_grads",
    )(cot_turned, norm_turned, act, grad_up)
    return parts if len(parts) == 4 else grid.split(parts[0])


def second_back_kernel(
    part_ref, other_ref, hidden_ref, cot_ref, vec_ref, out_w_ref, turned_ref,
    grad_ref, heads_ref, sum_ref, out_grad_ref, total,
):
    step = pl.program_id(0)
    normed, inv_std = normalize_rows(hidden_ref[...])
    part = part_ref[...]
    cot = cot_ref[...].astype(F32)
    grad_second = part + other_ref[...].astype(F32)
    grad = cot + norm_back(grad_second * vec_ref[5:6, :], normed, inv_std)
    grad_ref[...] = grad
    low = grad.astype(BF16)
    heads_ref[...] = dot_nn(low, out_w_ref[...]).astype(BF16)

    @pl.when(step == 0)
    def _():
        sum_ref[...] = jnp.zeros_like(sum_ref)
        total[...] = jnp.zeros_like(total)

    total[...] += dot_nn(turned_ref[...], low)
    for row, value in enumerate((grad, part * normed, part, cot)):
        sum_ref[row : row + 1, :] += jnp.sum(value, axis=0, keepdims=True)

    @pl.when(step == pl.num_programs(0) - 1)
    def _():
        out_grad_ref[...] = total[...].T.astype(BF16)


def second_back(part, other, hidden, cot, vec_all, out_w, heads_turned):
    length, width = part.shape
    cols = out_w.shape[1]
    full = rows_of(ROW_BLOCK, width)
    return pl.pallas_call(
        second_back_kernel,
        grid=(length // ROW_BLOCK,),
        in_specs=[full, full, full, full, whole(vec_all.shape), whole(out_w.shape)]
        + [pl.BlockSpec((cols, ROW_BLOCK), lambda step: (0, step))],
        out_specs=[full, rows_of(ROW_BLOCK, cols), whole((8, width)), whole((width, cols))],
        out_shape=[
            shaped((length, width), F32),
            shaped((length, cols), BF16),
            shaped((8, width), F32),
            shaped((width, cols), BF16),
        ],
        scratch_shapes=[pltpu.VMEM((cols, width), F32)],
        compiler_params=PARAMS,
        cost_estimate=cost(8.6),
        name="second_back",
    )(part, other, hidden, cot, vec_all, out_w, heads_turned)


def qkv_grads_kernel(grid, norm_ref, grad_ref, grad_two_ref, out_grad_ref, vec_ref, after_ref, *refs):
    step = pl.program_id(0)
    outs, held = refs[:-1], refs[-1]
    third = held.shape[1] // 2
    pairs = 2 * third // PAIR
    for index in range(pairs + 1):

        @pl.when(step == index)
        def _():
            if index == pairs:
                held[...] = out_grad_ref[...]
                for x in range(2):
                    source = slice(x * third, (x + 1) * third)
                    store_parts(held, grid, outs, x, source, slice(3 * third, 4 * third))
                rows = vec_ref[...]
                blank = jnp.zeros((VEC_LANES - rows.shape[0], rows.shape[1]), F32)
                held[:, :VEC_LANES] = jnp.concatenate([rows, blank], axis=0).T.astype(BF16)
                for x in range(2):
                    lanes = slice(4 * third, 4 * third + VEC_LANES)
                    store_parts(held, grid, outs, x, slice(0, VEC_LANES), lanes)
                return
            right = grad_two_ref if index == pairs - 1 else grad_ref
            held[...] = dot_nn(norm_ref[...], right[...]).astype(BF16)
            for part in range(3):
                for x, low, high, lane in segments(index, third):
                    at = part * PAIR + lane
                    lanes = slice(part * third + low, part * third + high)
                    store_parts(held, grid, outs, x, slice(at, at + high - low), lanes)


def qkv_grads(norm_turned, grads, out_grad, grid, grad_vec, after):
    width, length = norm_turned.shape
    cols = out_grad.shape[1]
    pairs = cols // PAIR
    shapes = parts_out(grid, width, 2 * cols + VEC_LANES)
    parts = pl.pallas_call(
        functools.partial(qkv_grads_kernel, grid),
        grid=(pairs + 1,),
        in_specs=[
            whole((width, length)),
            pl.BlockSpec((length, cols), lambda step: (0, jnp.minimum(step, pairs - 2))),
            whole((length, cols)),
            whole((width, cols)),
            whole(grad_vec.shape),
            ANYWHERE,
        ],
        out_specs=[whole(shape) for shape in shapes],
        out_shape=[shaped(shape, BF16) for shape in shapes],
        scratch_shapes=[pltpu.VMEM((width, cols), BF16)],
        compiler_params=PARAMS,
        cost_estimate=cost(1.5),
        name="qkv_grads",
    )(norm_turned, *grads, out_grad, grad_vec, after)
    return parts if len(parts) == 4 else grid.split(parts[0])


def first_back_kernel(
    place_ref, grad_ref, grad_two_ref, weight_ref, tokens_ref, second_ref, up_ref,
    part_ref, vec_ref, bias,
):
    grads = jnp.concatenate([grad_ref[...], grad_two_ref[...]], axis=1)
    part = dot_nt(grads, weight_ref[...])
    part_ref[...] = part
    normed, _ = normalize_rows(tokens_ref[...].astype(F32))

    @pl.when(pl.program_id(0) == 0)
    def _():
        vec_ref[...] = jnp.zeros_like(vec_ref)
        bias[...] = jnp.zeros_like(bias)

    for row, value in enumerate((part * normed, part)):
        vec_ref[row : row + 1, :] += jnp.sum(value, axis=0, keepdims=True)
    bias[0:1, :] += jnp.sum(grads.astype(F32), axis=0, keepdims=True)

    @pl.when(pl.program_id(0) == pl.num_programs(0) - 1)
    def _():
        width = vec_ref.shape[1]
        pairs = bias.shape[1] // (3 * PAIR)
        third = pairs * PAIR // 2
        for row, part_at in ((2, 0), (3, 2)):
            lanes = [
                bias[:, (3 * pair + part_at) * PAIR : (3 * pair + part_at + 1) * PAIR]
                for pair in range(pairs)
            ]
            joined = jnp.concatenate(lanes, axis=1)
            blank = jnp.zeros((joined.shape[0], width - third), F32)
            for x in range(2):
                block = jnp.concatenate([joined[:, x * third : (x + 1) * third], blank], axis=1)
                vec_ref[row : row + 1, :] += pltpu.roll(block, place_ref[1 + x], 1)[0:1]
        vec_ref[4:5, :] = 0.5 * second_ref[0:1, :]
        vec_ref[5:7, :] = second_ref[1:3, :]
        vec_ref[7:8, :] = 0.5 * second_ref[3:4, :]
        row_at = lax.broadcasted_iota(jnp.int32, (8, width), 0)
        vec_ref[8:16, :] = jnp.where(row_at == place_ref[3], up_ref[0:1, :width], 0.0) + jnp.where(
            row_at == place_ref[4], up_ref[0:1, width:], 0.0
        )


def first_back(place, grads, weight, tokens, second_sums, up_sums):
    length, width = tokens.shape
    cols = weight.shape[1]

    def by_row(size):
        return pl.BlockSpec((ROW_BLOCK, size), lambda step, place_ref: (step, 0))

    return pl.pallas_call(
        first_back_kernel,
        grid_spec=pltpu.PrefetchScalarGridSpec(
            num_scalar_prefetch=1,
            grid=(length // ROW_BLOCK,),
            in_specs=[
                by_row(grads[0].shape[1]),
                by_row(grads[1].shape[1]),
                whole(weight.shape),
                by_row(width),
                whole(second_sums.shape),
                whole(up_sums.shape),
            ],
            out_specs=[by_row(width), whole((16, width))],
            scratch_shapes=[pltpu.VMEM((8, cols), F32)],
        ),
        out_shape=[shaped((length, width), F32), shaped((16, width), F32)],
        compiler_params=PARAMS,
        cost_estimate=cost(1.5),
        name="first_back",
    )(place, *grads, weight, tokens, second_sums, up_sums)


def token_back_kernel(core_ref, part_ref, other_ref, tokens_ref, grad_ref, vec_ref, out_ref):
    normed, inv_std = normalize_rows(tokens_ref[...].astype(F32))
    grad_first = part_ref[...] + other_ref[...].astype(F32)
    out_ref[...] = grad_ref[...] + norm_back(grad_first * vec_ref[0:1, :], normed, inv_std)


def token_back(core, part, other, tokens, grad_hidden, vec_all):
    rows, width = tokens.shape
    steps = rows // ROW_BLOCK
    own = pl.BlockSpec((ROW_BLOCK, width), lambda step, core_ref: (core_ref[0] * steps + step, 0))
    here = pl.BlockSpec((ROW_BLOCK, width), lambda step, core_ref: (step, 0))
    return pl.pallas_call(
        token_back_kernel,
        grid_spec=pltpu.PrefetchScalarGridSpec(
            num_scalar_prefetch=1,
            grid=(steps,),
            in_specs=[own, here, here, own, whole(vec_all.shape)],
            out_specs=here,
        ),
        out_shape=shaped((rows, width), F32),
        compiler_params=PARAMS,
        cost_estimate=cost(3.2),
        name="token_back",
    )(core.reshape(1), part, other, tokens, grad_hidden, vec_all)


def out_step_kernel(grad_ref, weight_ref, first_ref, second_ref, new_ref, new_first_ref, new_second_ref):
    grads = grad_ref[...].T
    results = adamw(weight_ref[...], first_ref[...], second_ref[...], grads, RATE_MATRIX)
    new_ref[...], new_first_ref[...], new_second_ref[...] = results


def out_step(weight, first, second, grads):
    return pl.pallas_call(
        out_step_kernel,
        out_shape=[shaped(weight.shape, F32)] * 3,
        compiler_params=PARAMS,
        name="out_step",
    )(grads, weight, first, second)


def vector_step_kernel(
    part_ref, other_ref, weight_ref, first_ref, second_ref, new_ref, new_first_ref, new_second_ref
):
    grads = (part_ref[...] + other_ref[...]).T[: weight_ref.shape[0]]
    results = adamw(weight_ref[...], first_ref[...], second_ref[...], grads, RATE_VECTOR)
    new_ref[...], new_first_ref[...], new_second_ref[...] = results


def vector_step(weight, first, second, part, other):
    return pl.pallas_call(
        vector_step_kernel,
        out_shape=[shaped(weight.shape, F32)] * 3,
        compiler_params=PARAMS,
        name="vector_step",
    )(part, other, weight, first, second)


def shards(
    tokens,
    cotangent,
    w_qkv,
    w_out,
    w_up,
    w_down,
    vectors,
    first_qkv,
    first_out,
    first_up,
    first_down,
    first_vectors,
    second_qkv,
    second_out,
    second_up,
    second_down,
    second_vectors,
):
    col_index = lax.axis_index("col")
    grid = Grid(lax.axis_size("row"))
    core_line = ("col", 1)
    core = col_index % 2
    other_col = col_index ^ 2
    rows_loc, width = tokens.shape
    width_loc = w_qkv.shape[2]
    hidden_loc = w_up.shape[1]
    shard_rows = w_up.shape[0]

    pad = -(3 * width_loc + VEC_ROWS) % 128
    pack_qkv = jnp.concatenate(
        [w_qkv[:, part].astype(BF16) for part in range(3)]
        + [vectors.T.astype(BF16), jnp.zeros((shard_rows, pad), BF16), w_out.T.astype(BF16)],
        axis=1,
    )
    pack_feed = jnp.concatenate([w_up.astype(BF16), w_down.T.astype(BF16)], axis=1)

    def own_rows(value):
        return lax.dynamic_slice_in_dim(value, core * rows_loc, rows_loc, 0)

    def partner_rows(value):
        return lax.dynamic_slice_in_dim(value, (1 - core) * rows_loc, rows_loc, 0)

    place = jnp.stack(
        [core, col_index * width_loc, other_col * width_loc, col_index, other_col]
    ).astype(jnp.int32)

    far_qkv = grid.gather_far(pack_qkv)
    partner = [swap_over(tokens, core_line), swap_over(cotangent, core_line)]
    far_qkv, partner = lax.optimization_barrier((far_qkv, partner))
    sent_qkv = grid.gather_ready(far_qkv)
    pack_feed, _ = lax.optimization_barrier((pack_feed, sent_qkv))
    arrived_qkv = grid.gather_one(sent_qkv)
    far_feed = grid.gather_far(pack_feed)
    two_qkv = grid.gather_two(sent_qkv, arrived_qkv)
    near_qkv = grid.gather_three(*two_qkv)
    far_feed, _ = lax.optimization_barrier((far_feed, (two_qkv[0], two_qkv[2])))
    sent_feed = grid.gather_ready(far_feed)
    arrived_feed = grid.gather_one(sent_feed)

    all_cot, cot_turned = join_halves(place, cotangent, partner[1])
    first_in, qkv, all_tokens, full_qkv, full_out, vec_all = first_norm(
        place, tokens, partner[0], near_qkv, width_loc, all_cot
    )
    partner_out = swap_over(full_out, core_line)
    pairs = 2 * width_loc // PAIR
    arrived_feed, _ = lax.optimization_barrier((arrived_feed, qkv))
    front, front_at, back = grid.gather_two(sent_feed, arrived_feed)
    near_feed = grid.gather_three(front, front_at, back)
    heads_low, heads_turned, lse = attend_forward(qkv, (front, back))
    partner_heads = swap_over(heads_low, core_line)
    hidden_state, second_in, second_turned, first_turned = attended_norm(
        heads_low, partner_heads, full_out, partner_out, all_tokens, vec_all, first_in
    )
    activated, grad_upper, grad_bias_up, down_part, second_part, second_low = feed(
        place, second_in, all_cot, vec_all, near_feed
    )

    second_other = swap_over(second_low, core_line)
    parts_feed = feed_grads(cot_turned, second_turned, activated, grad_upper, grid)
    arrived_feed = grid.stage_one(parts_feed)
    grad_hidden, grad_heads, second_sums, out_grad = second_back(
        second_part, second_other, hidden_state, all_cot, vec_all, full_out, heads_turned
    )
    grad_one = attend_backward(qkv, grad_heads, lse, 0, pairs - 1, ())
    arrived_feed, grad_one = lax.optimization_barrier((arrived_feed, grad_one))
    kept_feed, sent_feed = grid.stage_two(parts_feed, *arrived_feed)
    grad_two = attend_backward(qkv, grad_heads, lse, pairs - 1, 1, sent_feed)
    grads_qkv = (grad_one, grad_two)
    first_part, grad_vec = first_back(
        place, grads_qkv, full_qkv, all_tokens, second_sums, grad_bias_up
    )
    chain_feed = grid.chain_send(grid.stage_three(kept_feed, sent_feed, grad_vec))
    parts_qkv = qkv_grads(first_turned, grads_qkv, out_grad, grid, grad_vec, chain_feed[1])
    arrived_pack = grid.stage_one(parts_qkv)
    owned_feed = grid.reduce_chain(*chain_feed)
    owned_up, owned_down = owned_feed[:, :hidden_loc], owned_feed[:, hidden_loc:]

    kept_pack, sent_pack = grid.stage_two(parts_qkv, *arrived_pack)
    sent_pack, first_part, down_part = lax.optimization_barrier(
        (sent_pack, first_part, down_part)
    )
    near_pack = grid.stage_three(kept_pack, sent_pack)
    first_other = swap_over(partner_rows(first_part).astype(BF16), core_line)
    down_other = swap_over(partner_rows(down_part).astype(BF16), core_line).astype(F32)
    mixed_out = own_rows(hidden_state) + own_rows(down_part) + down_other + vec_all[7]
    token_grad = token_back(core, first_part, first_other, tokens, grad_hidden, vec_all)
    owned_pack, (mixed_out, token_grad) = grid.reduce_direct(near_pack, (mixed_out, token_grad))
    part_vec = owned_pack[:, 4 * width_loc :]
    other_vec = swap_over(part_vec, core_line)
    owned_qkv = jnp.stack(
        [owned_pack[:, part * width_loc : (part + 1) * width_loc] for part in range(3)], axis=1
    )
    owned_out = owned_pack[:, 3 * width_loc : 4 * width_loc]

    new_qkv, new_first_qkv, new_second_qkv = adamw(
        w_qkv, first_qkv, second_qkv, owned_qkv, RATE_MATRIX
    )
    new_out, new_first_out, new_second_out = out_step(w_out, first_out, second_out, owned_out)
    new_up, new_first_up, new_second_up = adamw(w_up, first_up, second_up, owned_up, RATE_MATRIX)
    new_down, new_first_down, new_second_down = adamw(
        w_down, first_down, second_down, owned_down.T, RATE_MATRIX
    )
    new_vectors, new_first_vectors, new_second_vectors = vector_step(
        vectors, first_vectors, second_vectors, part_vec, other_vec
    )
    return (
        mixed_out,
        token_grad,
        new_qkv,
        new_out,
        new_up,
        new_down,
        new_vectors,
        new_first_qkv,
        new_first_out,
        new_first_up,
        new_first_down,
        new_first_vectors,
        new_second_qkv,
        new_second_out,
        new_second_up,
        new_second_down,
        new_second_vectors,
    )


def solution(mesh):
    by_token = P(("row", "col"), None)
    weights = (
        P("row", None, "col"),
        P("col", "row"),
        P("row", "col"),
        P("col", "row"),
        P(None, "row"),
    )
    return jax.shard_map(
        shards,
        mesh=mesh,
        in_specs=(by_token, by_token) + weights * 3,
        out_specs=(by_token, by_token) + weights * 3,
        check_vma=False,
    )
```

```python
import functools
import math

import jax
import jax.numpy as jnp
from jax import lax
from jax.experimental import pallas as pl
from jax.experimental.pallas import tpu as pltpu
from jax.sharding import PartitionSpec as P

HEAD_DIM = 64
LENGTH = 1024
STEP_NUMBER = 10
VEC_ROWS = 12
PAIR = 2 * HEAD_DIM
QUERY_BLOCK = 256
ROW_BLOCK = 512
VEC_LANES = 128
COST_SCALE = 2.3e8


EPS = 1e-05
BETA_ONE = 0.9
BETA_TWO = 0.999
ADAM_EPS = 1e-08
DECAY = 0.1
RATE_MATRIX = 0.04
RATE_VECTOR = 0.3

F32 = jnp.float32
BF16 = jnp.bfloat16


def normalize_rows(values_in):
    row_mean = jnp.mean(values_in, axis=-1, keepdims=True)
    centred = values_in - row_mean
    row_var = jnp.mean(centred * centred, axis=-1, keepdims=True)
    inv_std = lax.rsqrt(row_var + EPS)
    return (centred * inv_std, inv_std)


def norm_back(grad_in, normed, inv_std):
    mean_grad = jnp.mean(grad_in, axis=-1, keepdims=True)
    mean_cross = jnp.mean(grad_in * normed, axis=-1, keepdims=True)
    return inv_std * (grad_in - mean_grad - normed * mean_cross)


def adamw(weight, moment_one, moment_two, gradient, rate):
    first = BETA_ONE * moment_one + (1 - BETA_ONE) * gradient
    second = BETA_TWO * moment_two + (1 - BETA_TWO) * gradient * gradient
    first_hat = first / (1 - BETA_ONE**STEP_NUMBER)
    second_hat = second / (1 - BETA_TWO**STEP_NUMBER)
    updated = weight - rate * (first_hat / (jnp.sqrt(second_hat) + ADAM_EPS) + DECAY * weight)
    return (updated, first, second)


def swap_over(value, line):
    name, offset = line
    pairs = [(index, index ^ offset) for index in range(lax.axis_size(name))]
    return lax.ppermute(value, name, pairs)


def bit_offsets(low, high):
    offsets = []
    while low < high:
        offsets.append(low)
        low *= 2
    return offsets


def flip_order(blocks):
    count = blocks.shape[0]
    row = lax.axis_index("row")
    for offset in bit_offsets(1, count):
        cut = blocks.reshape((-1, 2, offset) + blocks.shape[1:])
        turned = jnp.where((row // offset) % 2 == 1, cut[:, ::-1], cut)
        blocks = turned.reshape(blocks.shape)
    return blocks


class Gathered:
    def __init__(self, arrays, table):
        self.arrays = arrays
        self.table = table
        self.rows = arrays[0].shape[1]
        self.cols = arrays[0].shape[2]
        if self.rows % 16:
            total = []
            for x in range(2):
                found = sorted((offset, array, at) for x_at, array, at, offset in table if x_at == x)
                blocks = jnp.stack([arrays[array][at] for _, array, at in found])
                total.append(flip_order(blocks).reshape(-1, self.cols))
            self.arrays = [jnp.stack(total)]
            self.table = [(0, 0, 0, 0), (1, 0, 1, 0)]
            self.rows = self.arrays[0].shape[1]


class Grid:
    def __init__(self, row_count):
        self.row_count = row_count
        self.far_count = row_count // 2
        self.half = self.far_count // 2
        self.x_line = ("col", 2)
        self.near_line = ("row", 1)

    def far_line(self, index):
        return ("row", 2 * index)

    def gather_far(self, block):
        return [block] + [
            swap_over(block, self.far_line(index)) for index in range(1, self.far_count)
        ]

    def gather_one(self, sent):
        return swap_over(sent, self.x_line), swap_over(sent, self.near_line)

    def gather_ready(self, arrived):
        return arrived[1][: self.half], arrived[0][self.half :]

    def gather_two(self, own, arrived, sent):
        by_x, by_near = swap_over(sent[0], self.x_line), swap_over(sent[1], self.near_line)
        arrays = [own, arrived[0], arrived[1], by_x, by_near]
        far = range(self.far_count)
        table = [(0, 0, index, 2 * index) for index in far]
        table += [(1, 1, index, 2 * index) for index in far]
        table += [(0, 2, index, 2 * index + 1) for index in far]
        table += [(1, 3, index, 2 * index + 1) for index in far[: self.half]]
        table += [(1, 4, index - self.half, 2 * index + 1) for index in far[self.half :]]
        return Gathered(arrays, table)

    def split(self, pair):
        _, all_rows, cols = pair.shape
        blocks = jnp.moveaxis(pair.reshape(2, self.row_count, -1, cols), 1, 0)
        blocks = jnp.moveaxis(flip_order(blocks), 0, 1)
        blocks = blocks.reshape(2, self.far_count, 2, -1, cols)
        last = blocks[1, :, 1]
        return (
            blocks[0, :, 0],
            blocks[1, :, 0],
            blocks[0, :, 1],
            last[: self.half],
            last[self.half :],
        )

    def part_of(self, x, index):
        far, near = index // 2, index % 2
        if not (x and near):
            return x + 2 * near, far
        return (3, far) if far < self.half else (4, far - self.half)

    def part_shapes(self, rows, cols):
        return [(self.far_count, rows, cols)] * 3 + [(self.half, rows, cols)] * 2

    def stage_one(self, parts):
        return swap_over(parts[3], self.x_line), swap_over(parts[4], self.near_line)

    def stage_two(self, parts, by_x, by_near):
        over_x, over_near = parts[1].astype(F32), parts[2].astype(F32)
        half = self.half
        over_x = jnp.concatenate([over_x[:half], over_x[half:] + by_near.astype(F32)], axis=0)
        over_near = jnp.concatenate([over_near[:half] + by_x.astype(F32), over_near[half:]], axis=0)
        return over_x.astype(BF16), over_near.astype(BF16)

    def stage_three(self, parts, sent, hold=None):
        by_x, by_near = swap_over(sent[0], self.x_line), swap_over(sent[1], self.near_line)
        if hold is not None:
            by_x, by_near, _ = lax.optimization_barrier((by_x, by_near, hold))
        return parts[0].astype(F32) + by_x.astype(F32) + by_near.astype(F32)

    def chain_send(self, parts):
        return parts[0::2], parts[1::2].astype(BF16)

    def reduce_chain(self, kept, sent):
        index = 1
        parts = kept + swap_over(sent, self.far_line(index)).astype(F32)
        while parts.shape[0] > 1:
            index *= 2
            kept, sent = self.chain_send(parts)
            parts = kept + swap_over(sent, self.far_line(index)).astype(F32)
        return parts[0]

    def reduce_direct(self, parts, hold):
        low = parts.astype(BF16)
        arrived = [
            swap_over(low[index], self.far_line(index))
            for index in range(1, self.far_count)
        ]
        arrived, hold = lax.optimization_barrier((arrived, hold))
        total = parts[0]
        for part in arrived:
            total = total + part.astype(F32)
        return total, hold


def dot_nt(left, right):
    return lax.dot_general(left, right, (((1,), (1,)), ((), ())), preferred_element_type=F32)


def dot_nn(left, right):
    return lax.dot_general(left, right, (((1,), (0,)), ((), ())), preferred_element_type=F32)


def lane_pick(half):
    lanes = lax.broadcasted_iota(jnp.int32, (1, PAIR), 1)
    return jnp.where((lanes // HEAD_DIM) == half, 1.0, 0.0).astype(BF16)


def causal_block(size):
    key_at = lax.broadcasted_iota(jnp.int32, (size, size), 0)
    query_at = lax.broadcasted_iota(jnp.int32, (size, size), 1)
    return key_at <= query_at


def cost(microseconds):
    return pl.CostEstimate(
        flops=int(microseconds * COST_SCALE), bytes_accessed=1024, transcendentals=0
    )


def attend_kernel(q_ref, k_ref, v_ref, out_ref, turned_ref, lse_ref):
    length = q_ref.shape[0]
    block = min(QUERY_BLOCK, length)
    allowed = causal_block(block)
    values_t = v_ref[...].T
    scaling = jnp.asarray(HEAD_DIM**-0.5, BF16)
    for first in range(0, length, block):
        last = first + block
        query = q_ref[first:last, :] * scaling
        outs = []
        for half in range(2):
            rows = slice(half * HEAD_DIM, (half + 1) * HEAD_DIM)
            query_half = query * lane_pick(half)
            diag = dot_nt(k_ref[first:last, :], query_half)
            diag = jnp.where(allowed, diag, -1e30)
            top = jnp.max(diag, axis=0, keepdims=True)
            if first:
                rest = dot_nt(k_ref[0:first, :], query_half)
                top = jnp.maximum(top, jnp.max(rest, axis=0, keepdims=True))
            diag = jnp.exp(diag - top)
            total = jnp.sum(diag, axis=0, keepdims=True)
            if first:
                rest = jnp.exp(rest - top)
                total = total + jnp.sum(rest, axis=0, keepdims=True)
            inverse = 1.0 / total
            result = dot_nn(values_t[rows, first:last], (diag * inverse).astype(BF16))
            if first:
                result = result + dot_nn(values_t[rows, 0:first], (rest * inverse).astype(BF16))
            outs.append(result)
            lse_ref[0, half : half + 1, first:last] = top + jnp.log(total)
        turned = jnp.concatenate(outs, axis=0)
        out_ref[first:last, :] = turned.T.astype(BF16)
        turned_ref[:, first:last] = turned.astype(BF16)


def pair_lanes(length, first, part):
    return pl.BlockSpec((length, PAIR), lambda pair: (0, 3 * (first + pair) + part))


def attend_forward(qkv, after):
    length = qkv.shape[0]
    pairs = qkv.shape[1] // (3 * PAIR)
    return pl.pallas_call(
        lambda q, k, v, *refs: attend_kernel(q, k, v, *refs[len(after) :]),
        grid=(pairs,),
        in_specs=[pair_lanes(length, 0, part) for part in range(3)]
        + [pl.BlockSpec(memory_space=pl.ANY)] * len(after),
        out_specs=[
            pl.BlockSpec((length, PAIR), lambda pair: (0, pair)),
            pl.BlockSpec((PAIR, length), lambda pair: (pair, 0)),
            pl.BlockSpec((1, 8, length), lambda pair: (pair, 0, 0)),
        ],
        out_shape=[
            jax.ShapeDtypeStruct((length, pairs * PAIR), BF16),
            jax.ShapeDtypeStruct((pairs * PAIR, length), BF16),
            jax.ShapeDtypeStruct((pairs, 8, length), F32),
        ],
        compiler_params=pltpu.CompilerParams(vmem_limit_bytes=40 * 2**20),
        cost_estimate=cost(4.2 * pairs),
        name="attend_forward",
    )(qkv, qkv, qkv, *after)


def attend_back_kernel(q_ref, k_ref, v_ref, go_ref, lse_ref, grad_ref, gk_sum, gv_sum):
    length = q_ref.shape[0]
    block = min(QUERY_BLOCK, length)
    allowed = causal_block(block)
    keys_t = k_ref[...].T
    scaling = jnp.asarray(HEAD_DIM**-0.5, BF16)
    pair = pl.program_id(0)

    def lanes(part):
        return pl.ds(pl.multiple_of((3 * pair + part) * PAIR, PAIR), PAIR)

    gk_sum[...] = jnp.zeros_like(gk_sum)
    gv_sum[...] = jnp.zeros_like(gv_sum)
    for first in range(0, length, block):
        last = first + block
        query = q_ref[first:last, :] * scaling
        grad_out = go_ref[first:last, :]
        outs = []
        for half in range(2):
            rows = slice(half * HEAD_DIM, (half + 1) * HEAD_DIM)
            pick = lane_pick(half)
            query_half = query * pick
            grad_half = grad_out * pick
            lse = lse_ref[0, half : half + 1, first:last]
            spans = [(first, last)] if first == 0 else [(0, first), (first, last)]
            probs, grads, inner = [], [], None
            for low, high in spans:
                scores = dot_nt(k_ref[low:high, :], query_half)
                if low == first:
                    scores = jnp.where(allowed, scores, -1e30)
                prob = jnp.exp(scores - lse)
                grad_prob = dot_nt(v_ref[low:high, :], grad_half)
                part = jnp.sum(prob * grad_prob, axis=0, keepdims=True)
                inner = part if inner is None else inner + part
                probs.append(prob)
                grads.append(grad_prob)
            result = None
            for (low, high), prob, grad_prob in zip(spans, probs, grads):
                grad_score = (prob * (grad_prob - inner)).astype(BF16)
                gk_sum[low:high, :] += dot_nn(grad_score, query_half)
                gv_sum[low:high, :] += dot_nn(prob.astype(BF16), grad_half)
                part = dot_nn(keys_t[rows, low:high], grad_score)
                result = part if result is None else result + part
            outs.append(result)
        grad_query = jnp.concatenate(outs, axis=0).T * (HEAD_DIM**-0.5)
        grad_ref[first:last, lanes(0)] = grad_query.astype(BF16)
    grad_ref[:, lanes(1)] = gk_sum[...].astype(BF16)
    grad_ref[:, lanes(2)] = gv_sum[...].astype(BF16)


def attend_backward(qkv, grad_heads, lse, first, pairs, after):
    length = qkv.shape[0]
    width = 3 * PAIR * pairs
    return pl.pallas_call(
        lambda q, k, v, go, lse_at, *refs: attend_back_kernel(
            q, k, v, go, lse_at, *refs[len(after) :]
        ),
        grid=(pairs,),
        in_specs=[pair_lanes(length, first, part) for part in range(3)]
        + [
            pl.BlockSpec((length, PAIR), lambda pair: (0, first + pair)),
            pl.BlockSpec((1, 8, length), lambda pair: (first + pair, 0, 0)),
        ]
        + [pl.BlockSpec(memory_space=pl.ANY)] * len(after),
        out_specs=pl.BlockSpec((length, width), lambda pair: (0, 0)),
        out_shape=jax.ShapeDtypeStruct((length, width), BF16),
        scratch_shapes=[pltpu.VMEM((length, PAIR), F32), pltpu.VMEM((length, PAIR), F32)],
        compiler_params=pltpu.CompilerParams(vmem_limit_bytes=40 * 2**20),
        cost_estimate=cost(1.5 * pairs),
        name="attend_backward",
    )(qkv, qkv, qkv, grad_heads, lse, *after)


def rows_of(block, width):
    return pl.BlockSpec((block, width), lambda step: (step, 0))


def whole(shape):
    return pl.BlockSpec(shape, lambda *step: (0,) * len(shape))


def shaped(shape, dtype):
    return jax.ShapeDtypeStruct(shape, dtype)


PARAMS = pltpu.CompilerParams(vmem_limit_bytes=48 * 2**20)


ANYWHERE = pl.BlockSpec(memory_space=pl.ANY)


def weight_copies(gathered, refs, held, sems):
    row = lax.axis_index("row")
    copies = ([], [])
    for number, (x, array, at, offset) in enumerate(gathered.table):
        if len(gathered.table) > 2:
            start = pl.multiple_of((row ^ offset) * gathered.rows, 16)
        else:
            start = 0
        target = held.at[x, pl.ds(start, gathered.rows), :]
        copies[x].append(
            pltpu.make_async_copy(refs[array].at[at], target, sems.at[number])
        )
    return copies


def weight_scratch(gathered):
    all_rows = len(gathered.table) // 2 * gathered.rows
    return [
        pltpu.VMEM((2, all_rows, gathered.cols), BF16),
        pltpu.SemaphoreType.DMA((len(gathered.table),)),
    ]


def start_all(copies):
    for copy in copies:
        copy.start()


def wait_all(copies):
    for copy in copies:
        copy.wait()


def store_parts(held, grid, refs, x, source, lanes):
    if len(refs) == 1:
        refs[0][x, :, lanes] = held[:, source]
        return
    row = lax.axis_index("row")
    rows = held.shape[0] // grid.row_count
    for index in range(grid.row_count):
        start = pl.multiple_of((row ^ index) * rows, 16)
        array, place = grid.part_of(x, index)
        refs[array][place, :, lanes] = held[pl.ds(start, rows), source]


def segments(pair, third):
    low, high, found = pair * PAIR, (pair + 1) * PAIR, []
    while low < high:
        x = low // third
        end = min(high, (x + 1) * third)
        found.append((x, low - x * third, end - x * third, low - pair * PAIR))
        low = end
    return found


def parts_out(grid, width, cols):
    rows = width // grid.row_count
    if rows % 16:
        return [(2, width, cols)]
    return grid.part_shapes(rows, cols)


def turn(value):
    return value.T


def pick_half(here, mine_ref, other_ref):
    mine, other = mine_ref[...].astype(F32), other_ref[...].astype(F32)
    return jnp.where(here, mine, other)


def first_norm_kernel(gathered, cols, place_ref, mine_ref, other_ref, after_ref, *refs):
    count = len(gathered.arrays)
    norm_ref, qkv_ref, tokens_ref, full_ref, out_w_ref, vec_ref, held, bias, sems = refs[count:]
    copies = weight_copies(gathered, refs[:count], held, sems)
    third = cols // 3
    step = pl.program_id(0)
    per_half = pl.num_programs(0) // 2

    @pl.when(step == 0)
    def _():
        start_all(copies[0] + copies[1])
        wait_all(copies[0] + copies[1])
        for x in range(2):
            out_w_ref[:, x * third : (x + 1) * third] = held[x, :, held.shape[2] - third :]
        for pair in range(2 * third // PAIR):
            for part in range(3):
                for x, low, high, lane in segments(pair, third):
                    at = (3 * pair + part) * PAIR + lane
                    source = slice(part * third + low, part * third + high)
                    full_ref[:, at : at + high - low] = held[x, :, source]
        first = cols // 128 * 128
        rows = turn(held[0, :, first : first + 128].astype(F32))[cols - first :]
        vec_ref[...] = rows[: vec_ref.shape[0]]
        row_at = lax.broadcasted_iota(jnp.int32, (rows.shape[1], 2 * third), 0)
        lane_at = lax.broadcasted_iota(jnp.int32, (rows.shape[1], 2 * third), 1)
        wanted = jnp.where(
            lane_at < third, place_ref[1] + lane_at, place_ref[2] + lane_at - third
        )
        chosen = jnp.where(row_at == wanted, 1.0, 0.0).astype(BF16)
        picked = dot_nn(vec_ref[...].astype(BF16), chosen)
        bias[...] = jnp.zeros_like(bias)
        for pair in range(2 * third // PAIR):
            lanes = slice(pair * PAIR, (pair + 1) * PAIR)
            at = 3 * pair * PAIR
            bias[0:1, at : at + PAIR] = picked[2:3, lanes]
            bias[0:1, at + 2 * PAIR : at + 3 * PAIR] = picked[3:4, lanes]

    tokens = pick_half(step // per_half == place_ref[0], mine_ref, other_ref)
    tokens_ref[...] = tokens.astype(BF16)
    normed, _ = normalize_rows(tokens)
    first_in = (normed * vec_ref[0:1, :] + vec_ref[1:2, :]).astype(BF16)
    norm_ref[...] = first_in
    qkv_ref[...] = (dot_nn(first_in, full_ref[...]) + bias[0:1, :]).astype(BF16)


def first_norm(place, mine, other, gathered, width_loc, after):
    rows, width = mine.shape
    length = 2 * rows
    cols = 3 * width_loc
    steps = rows // ROW_BLOCK
    half = pl.BlockSpec((ROW_BLOCK, width), lambda step, place_ref: (step % steps, 0))

    def by_row(size):
        return pl.BlockSpec((ROW_BLOCK, size), lambda step, place_ref: (step, 0))

    return pl.pallas_call(
        functools.partial(first_norm_kernel, gathered, cols),
        grid_spec=pltpu.PrefetchScalarGridSpec(
            num_scalar_prefetch=1,
            grid=(2 * steps,),
            in_specs=[half, half, ANYWHERE] + [ANYWHERE] * len(gathered.arrays),
            out_specs=[
                by_row(width),
                by_row(2 * cols),
                by_row(width),
                whole((width, 2 * cols)),
                whole((width, 2 * width_loc)),
                whole((16, width)),
            ],
            scratch_shapes=weight_scratch(gathered)[:1]
            + [pltpu.VMEM((8, 2 * cols), F32)]
            + weight_scratch(gathered)[1:],
        ),
        out_shape=[
            shaped((length, width), BF16),
            shaped((length, 2 * cols), BF16),
            shaped((length, width), BF16),
            shaped((width, 2 * cols), BF16),
            shaped((width, 2 * width_loc), BF16),
            shaped((16, width), F32),
        ],
        compiler_params=PARAMS,
        cost_estimate=cost(8),
        name="first_norm",
    )(place, mine, other, after, *gathered.arrays)


def attended_kernel(
    heads_ref, partner_ref, own_ref, other_ref, tokens_ref, vec_ref, first_ref,
    hidden_ref, norm_ref, norm_turned_ref, first_turned_ref,
):
    attended = dot_nt(heads_ref[...], own_ref[...]) + dot_nt(partner_ref[...], other_ref[...])
    hidden = tokens_ref[...].astype(F32) + attended + vec_ref[4:5, :]
    hidden_ref[...] = hidden
    normed, _ = normalize_rows(hidden)
    second_in = (normed * vec_ref[5:6, :] + vec_ref[6:7, :]).astype(BF16)
    norm_ref[...] = second_in
    norm_turned_ref[...] = turn(second_in)
    first_turned_ref[...] = turn(first_ref[...])


def attended_norm(heads, partner_heads, own_out, partner_out, tokens, vec_all, first_in):
    length, width = tokens.shape
    cols = own_out.shape[1]
    full, part = rows_of(ROW_BLOCK, width), rows_of(ROW_BLOCK, cols)
    turned = pl.BlockSpec((width, ROW_BLOCK), lambda step: (0, step))
    return pl.pallas_call(
        attended_kernel,
        grid=(length // ROW_BLOCK,),
        in_specs=[
            part,
            part,
            whole(own_out.shape),
            whole(partner_out.shape),
            full,
            whole(vec_all.shape),
            full,
        ],
        out_specs=[full, full, turned, turned],
        out_shape=[shaped((length, width), F32), shaped((length, width), BF16)]
        + [shaped((width, length), BF16)] * 2,
        compiler_params=PARAMS,
        cost_estimate=cost(8),
        name="attended_norm",
    )(heads, partner_heads, own_out, partner_out, tokens, vec_all, first_in)


def join_kernel(place_ref, mine_ref, other_ref, joined_ref, turned_ref):
    here = pl.program_id(0) // (pl.num_programs(0) // 2) == place_ref[0]
    joined = pick_half(here, mine_ref, other_ref).astype(BF16)
    joined_ref[...] = joined
    turned_ref[...] = turn(joined)


def join_halves(place, mine, other):
    rows, width = mine.shape
    steps = rows // ROW_BLOCK
    half = pl.BlockSpec((ROW_BLOCK, width), lambda step, place_ref: (step % steps, 0))
    return pl.pallas_call(
        join_kernel,
        grid_spec=pltpu.PrefetchScalarGridSpec(
            num_scalar_prefetch=1,
            grid=(2 * steps,),
            in_specs=[half, half],
            out_specs=[
                pl.BlockSpec((ROW_BLOCK, width), lambda step, place_ref: (step, 0)),
                pl.BlockSpec((width, ROW_BLOCK), lambda step, place_ref: (0, step)),
            ],
        ),
        out_shape=[shaped((2 * rows, width), BF16), shaped((width, 2 * rows), BF16)],
        compiler_params=PARAMS,
        cost_estimate=cost(0.1),
        name="join_halves",
    )(place, mine, other)


def feed_kernel(gathered, place_ref, norm_ref, cot_ref, vec_ref, *refs):
    count = len(gathered.arrays)
    act_ref, gup_ref, bias_sum_ref, out_ref, back_ref, back_low_ref, held, sems = refs[count:]
    copies = weight_copies(gathered, refs[:count], held, sems)
    step = pl.program_id(0)
    length = norm_ref.shape[0]
    curve, cubic = math.sqrt(2 / math.pi), 0.044715
    cols = held.shape[2] // 2
    x = step
    up_lanes, down_lanes = slice(0, cols), slice(cols, 2 * cols)
    bias = vec_ref[pl.ds(8 + place_ref[3 + x], 1), :]

    @pl.when(step == 0)
    def _():
        start_all(copies[0] + copies[1])
        out_ref[...] = jnp.zeros_like(out_ref)
        back_ref[...] = jnp.zeros_like(back_ref)
        wait_all(copies[0])

    @pl.when(step == 1)
    def _():
        wait_all(copies[1])

    bias_sum = jnp.zeros(bias.shape, F32)
    for first in range(0, length, ROW_BLOCK):
        rows = slice(first, first + ROW_BLOCK)
        up = dot_nn(norm_ref[rows, :], held[x, :, up_lanes]) + bias
        cubed = up * up * (curve * cubic)
        tanh = jnp.tanh(up * (curve + cubed))
        halved = 0.5 * up
        act_ref[rows, :] = (halved + halved * tanh).astype(BF16)
        slope = 0.5 + 0.5 * tanh + halved * (1.0 - tanh * tanh) * (curve + 3.0 * cubed)
        grad_up = (dot_nn(cot_ref[rows, :], held[x, :, down_lanes]) * slope).astype(BF16)
        gup_ref[rows, :] = grad_up
        bias_sum = bias_sum + jnp.sum(grad_up.astype(F32), axis=0, keepdims=True)
    back_ref[...] += dot_nt(gup_ref[...], held[x, :, up_lanes])
    out_ref[...] += dot_nt(act_ref[...], held[x, :, down_lanes])
    bias_sum_ref[...] = bias_sum

    @pl.when(step == pl.num_programs(0) - 1)
    def _():
        back_low_ref[...] = back_ref[...].astype(BF16)


def feed(place, norm, cot, vec_all, gathered):
    length, width = norm.shape
    block = gathered.cols // 2
    hidden = 2 * block
    tall = pl.BlockSpec((length, block), lambda step, place_ref: (0, step))
    flat = pl.BlockSpec((1, block), lambda step, place_ref: (0, step))
    full = whole((length, width))
    return pl.pallas_call(
        functools.partial(feed_kernel, gathered),
        grid_spec=pltpu.PrefetchScalarGridSpec(
            num_scalar_prefetch=1,
            grid=(2,),
            in_specs=[full, full, whole(vec_all.shape)] + [ANYWHERE] * len(gathered.arrays),
            out_specs=[tall, tall, flat, full, full, full],
            scratch_shapes=weight_scratch(gathered),
        ),
        out_shape=[
            shaped((length, hidden), BF16),
            shaped((length, hidden), BF16),
            shaped((1, hidden), F32),
            shaped((length, width), F32),
            shaped((length, width), F32),
            shaped((length, width), BF16),
        ],
        compiler_params=PARAMS,
        cost_estimate=cost(18),
        name="feed",
    )(place, norm, cot, vec_all, *gathered.arrays)


def feed_grads_kernel(grid, cot_ref, norm_ref, act_ref, gup_ref, *refs):
    kind, x_at = pl.program_id(0), pl.program_id(1)
    outs, held = refs[:-1], refs[-1]
    size = held.shape[1]

    @pl.when(kind == 0)
    def _():
        held[...] = dot_nn(cot_ref[...], act_ref[...]).astype(BF16)

    @pl.when(kind == 1)
    def _():
        held[...] = dot_nn(norm_ref[...], gup_ref[...]).astype(BF16)

    for index in range(2):
        for x in range(2):

            @pl.when((kind == index) & (x_at == x))
            def _():
                lanes = slice((1 - index) * size, (2 - index) * size)
                store_parts(held, grid, outs, x, slice(None), lanes)


def feed_grads(cot_turned, norm_turned, act, grad_up, grid):
    width, length = cot_turned.shape
    hidden = act.shape[1]
    block = hidden // 2
    shapes = parts_out(grid, width, hidden)
    parts = pl.pallas_call(
        functools.partial(feed_grads_kernel, grid),
        grid=(2, 2),
        in_specs=[
            whole((width, length)),
            whole((width, length)),
            pl.BlockSpec((length, block), lambda kind, x: (0, jnp.where(kind == 0, x, 1))),
            pl.BlockSpec((length, block), lambda kind, x: (0, jnp.where(kind == 1, x, 0))),
        ],
        out_specs=[whole(shape) for shape in shapes],
        out_shape=[shaped(shape, BF16) for shape in shapes],
        scratch_shapes=[pltpu.VMEM((width, block), BF16)],
        compiler_params=PARAMS,
        cost_estimate=cost(10),
        name="feed_grads",
    )(cot_turned, norm_turned, act, grad_up)
    return parts if len(parts) == 5 else grid.split(parts[0])


def second_back_kernel(
    part_ref, other_ref, hidden_ref, cot_ref, vec_ref, out_w_ref, turned_ref,
    grad_ref, heads_ref, sum_ref, out_grad_ref, total,
):
    step = pl.program_id(0)
    normed, inv_std = normalize_rows(hidden_ref[...])
    part = part_ref[...]
    cot = cot_ref[...].astype(F32)
    grad_second = part + other_ref[...].astype(F32)
    grad = cot + norm_back(grad_second * vec_ref[5:6, :], normed, inv_std)
    grad_ref[...] = grad
    low = grad.astype(BF16)
    heads_ref[...] = dot_nn(low, out_w_ref[...]).astype(BF16)

    @pl.when(step == 0)
    def _():
        sum_ref[...] = jnp.zeros_like(sum_ref)
        total[...] = jnp.zeros_like(total)

    total[...] += dot_nn(turned_ref[...], low)
    for row, value in enumerate((grad, part * normed, part, cot)):
        sum_ref[row : row + 1, :] += jnp.sum(value, axis=0, keepdims=True)

    @pl.when(step == pl.num_programs(0) - 1)
    def _():
        out_grad_ref[...] = total[...].T.astype(BF16)


def second_back(part, other, hidden, cot, vec_all, out_w, heads_turned):
    length, width = part.shape
    cols = out_w.shape[1]
    full = rows_of(ROW_BLOCK, width)
    return pl.pallas_call(
        second_back_kernel,
        grid=(length // ROW_BLOCK,),
        in_specs=[full, full, full, full, whole(vec_all.shape), whole(out_w.shape)]
        + [pl.BlockSpec((cols, ROW_BLOCK), lambda step: (0, step))],
        out_specs=[full, rows_of(ROW_BLOCK, cols), whole((8, width)), whole((width, cols))],
        out_shape=[
            shaped((length, width), F32),
            shaped((length, cols), BF16),
            shaped((8, width), F32),
            shaped((width, cols), BF16),
        ],
        scratch_shapes=[pltpu.VMEM((cols, width), F32)],
        compiler_params=PARAMS,
        cost_estimate=cost(8.6),
        name="second_back",
    )(part, other, hidden, cot, vec_all, out_w, heads_turned)


def qkv_grads_kernel(grid, norm_ref, grad_ref, grad_two_ref, out_grad_ref, vec_ref, after_ref, *refs):
    step = pl.program_id(0)
    outs, held = refs[:-1], refs[-1]
    third = held.shape[1] // 2
    pairs = 2 * third // PAIR
    for index in range(pairs + 1):

        @pl.when(step == index)
        def _():
            if index == pairs:
                held[...] = out_grad_ref[...]
                for x in range(2):
                    source = slice(x * third, (x + 1) * third)
                    store_parts(held, grid, outs, x, source, slice(3 * third, 4 * third))
                rows = vec_ref[...]
                blank = jnp.zeros((VEC_LANES - rows.shape[0], rows.shape[1]), F32)
                held[:, :VEC_LANES] = jnp.concatenate([rows, blank], axis=0).T.astype(BF16)
                for x in range(2):
                    lanes = slice(4 * third, 4 * third + VEC_LANES)
                    store_parts(held, grid, outs, x, slice(0, VEC_LANES), lanes)
                return
            right = grad_two_ref if index == pairs - 1 else grad_ref
            held[...] = dot_nn(norm_ref[...], right[...]).astype(BF16)
            for part in range(3):
                for x, low, high, lane in segments(index, third):
                    at = part * PAIR + lane
                    lanes = slice(part * third + low, part * third + high)
                    store_parts(held, grid, outs, x, slice(at, at + high - low), lanes)


def qkv_grads(norm_turned, grads, out_grad, grid, grad_vec, after):
    width, length = norm_turned.shape
    cols = out_grad.shape[1]
    pairs = cols // PAIR
    shapes = parts_out(grid, width, 2 * cols + VEC_LANES)
    parts = pl.pallas_call(
        functools.partial(qkv_grads_kernel, grid),
        grid=(pairs + 1,),
        in_specs=[
            whole((width, length)),
            pl.BlockSpec((length, cols), lambda step: (0, jnp.minimum(step, pairs - 2))),
            whole((length, cols)),
            whole((width, cols)),
            whole(grad_vec.shape),
            ANYWHERE,
        ],
        out_specs=[whole(shape) for shape in shapes],
        out_shape=[shaped(shape, BF16) for shape in shapes],
        scratch_shapes=[pltpu.VMEM((width, cols), BF16)],
        compiler_params=PARAMS,
        cost_estimate=cost(1.5),
        name="qkv_grads",
    )(norm_turned, *grads, out_grad, grad_vec, after)
    return parts if len(parts) == 5 else grid.split(parts[0])


def first_back_kernel(
    place_ref, grad_ref, grad_two_ref, weight_ref, tokens_ref, second_ref, up_ref,
    part_ref, vec_ref, bias,
):
    grads = jnp.concatenate([grad_ref[...], grad_two_ref[...]], axis=1)
    part = dot_nt(grads, weight_ref[...])
    part_ref[...] = part
    normed, _ = normalize_rows(tokens_ref[...].astype(F32))

    @pl.when(pl.program_id(0) == 0)
    def _():
        vec_ref[...] = jnp.zeros_like(vec_ref)
        bias[...] = jnp.zeros_like(bias)

    for row, value in enumerate((part * normed, part)):
        vec_ref[row : row + 1, :] += jnp.sum(value, axis=0, keepdims=True)
    bias[0:1, :] += jnp.sum(grads.astype(F32), axis=0, keepdims=True)

    @pl.when(pl.program_id(0) == pl.num_programs(0) - 1)
    def _():
        width = vec_ref.shape[1]
        pairs = bias.shape[1] // (3 * PAIR)
        third = pairs * PAIR // 2
        for row, part_at in ((2, 0), (3, 2)):
            lanes = [
                bias[:, (3 * pair + part_at) * PAIR : (3 * pair + part_at + 1) * PAIR]
                for pair in range(pairs)
            ]
            joined = jnp.concatenate(lanes, axis=1)
            blank = jnp.zeros((joined.shape[0], width - third), F32)
            for x in range(2):
                block = jnp.concatenate([joined[:, x * third : (x + 1) * third], blank], axis=1)
                vec_ref[row : row + 1, :] += pltpu.roll(block, place_ref[1 + x], 1)[0:1]
        vec_ref[4:5, :] = 0.5 * second_ref[0:1, :]
        vec_ref[5:7, :] = second_ref[1:3, :]
        vec_ref[7:8, :] = 0.5 * second_ref[3:4, :]
        row_at = lax.broadcasted_iota(jnp.int32, (8, width), 0)
        vec_ref[8:16, :] = jnp.where(row_at == place_ref[3], up_ref[0:1, :width], 0.0) + jnp.where(
            row_at == place_ref[4], up_ref[0:1, width:], 0.0
        )


def first_back(place, grads, weight, tokens, second_sums, up_sums):
    length, width = tokens.shape
    cols = weight.shape[1]

    def by_row(size):
        return pl.BlockSpec((ROW_BLOCK, size), lambda step, place_ref: (step, 0))

    return pl.pallas_call(
        first_back_kernel,
        grid_spec=pltpu.PrefetchScalarGridSpec(
            num_scalar_prefetch=1,
            grid=(length // ROW_BLOCK,),
            in_specs=[
                by_row(grads[0].shape[1]),
                by_row(grads[1].shape[1]),
                whole(weight.shape),
                by_row(width),
                whole(second_sums.shape),
                whole(up_sums.shape),
            ],
            out_specs=[by_row(width), whole((16, width))],
            scratch_shapes=[pltpu.VMEM((8, cols), F32)],
        ),
        out_shape=[shaped((length, width), F32), shaped((16, width), F32)],
        compiler_params=PARAMS,
        cost_estimate=cost(1.5),
        name="first_back",
    )(place, *grads, weight, tokens, second_sums, up_sums)


def token_back_kernel(core_ref, part_ref, other_ref, tokens_ref, grad_ref, vec_ref, out_ref):
    normed, inv_std = normalize_rows(tokens_ref[...].astype(F32))
    grad_first = part_ref[...] + other_ref[...].astype(F32)
    out_ref[...] = grad_ref[...] + norm_back(grad_first * vec_ref[0:1, :], normed, inv_std)


def token_back(core, part, other, tokens, grad_hidden, vec_all):
    rows, width = tokens.shape
    steps = rows // ROW_BLOCK
    own = pl.BlockSpec((ROW_BLOCK, width), lambda step, core_ref: (core_ref[0] * steps + step, 0))
    here = pl.BlockSpec((ROW_BLOCK, width), lambda step, core_ref: (step, 0))
    return pl.pallas_call(
        token_back_kernel,
        grid_spec=pltpu.PrefetchScalarGridSpec(
            num_scalar_prefetch=1,
            grid=(steps,),
            in_specs=[own, here, here, own, whole(vec_all.shape)],
            out_specs=here,
        ),
        out_shape=shaped((rows, width), F32),
        compiler_params=PARAMS,
        cost_estimate=cost(3.2),
        name="token_back",
    )(core.reshape(1), part, other, tokens, grad_hidden, vec_all)


def out_step_kernel(grad_ref, weight_ref, first_ref, second_ref, new_ref, new_first_ref, new_second_ref):
    grads = grad_ref[...].T
    results = adamw(weight_ref[...], first_ref[...], second_ref[...], grads, RATE_MATRIX)
    new_ref[...], new_first_ref[...], new_second_ref[...] = results


def out_step(weight, first, second, grads):
    return pl.pallas_call(
        out_step_kernel,
        out_shape=[shaped(weight.shape, F32)] * 3,
        compiler_params=PARAMS,
        name="out_step",
    )(grads, weight, first, second)


def vector_step_kernel(
    part_ref, other_ref, weight_ref, first_ref, second_ref, new_ref, new_first_ref, new_second_ref
):
    grads = (part_ref[...] + other_ref[...]).T[: weight_ref.shape[0]]
    results = adamw(weight_ref[...], first_ref[...], second_ref[...], grads, RATE_VECTOR)
    new_ref[...], new_first_ref[...], new_second_ref[...] = results


def vector_step(weight, first, second, part, other):
    return pl.pallas_call(
        vector_step_kernel,
        out_shape=[shaped(weight.shape, F32)] * 3,
        compiler_params=PARAMS,
        name="vector_step",
    )(part, other, weight, first, second)


def shards(
    tokens,
    cotangent,
    w_qkv,
    w_out,
    w_up,
    w_down,
    vectors,
    first_qkv,
    first_out,
    first_up,
    first_down,
    first_vectors,
    second_qkv,
    second_out,
    second_up,
    second_down,
    second_vectors,
):
    col_index = lax.axis_index("col")
    grid = Grid(lax.axis_size("row"))
    core_line = ("col", 1)
    core = col_index % 2
    other_col = col_index ^ 2
    rows_loc, width = tokens.shape
    width_loc = w_qkv.shape[2]
    hidden_loc = w_up.shape[1]
    shard_rows = w_up.shape[0]

    pad = -(3 * width_loc + VEC_ROWS) % 128
    pack_qkv = jnp.concatenate(
        [w_qkv[:, part].astype(BF16) for part in range(3)]
        + [vectors.T.astype(BF16), jnp.zeros((shard_rows, pad), BF16), w_out.T.astype(BF16)],
        axis=1,
    )
    pack_feed = jnp.concatenate([w_up.astype(BF16), w_down.T.astype(BF16)], axis=1)

    def own_rows(value):
        return lax.dynamic_slice_in_dim(value, core * rows_loc, rows_loc, 0)

    def partner_rows(value):
        return lax.dynamic_slice_in_dim(value, (1 - core) * rows_loc, rows_loc, 0)

    place = jnp.stack(
        [core, col_index * width_loc, other_col * width_loc, col_index, other_col]
    ).astype(jnp.int32)

    far_qkv = grid.gather_far(pack_qkv)
    partner = [swap_over(tokens, core_line), swap_over(cotangent, core_line)]
    far_qkv, partner = lax.optimization_barrier((far_qkv, partner))
    own_qkv = jnp.stack(far_qkv)
    pack_feed, _ = lax.optimization_barrier((pack_feed, own_qkv))
    arrived_qkv = grid.gather_one(own_qkv)
    far_feed = grid.gather_far(pack_feed)
    arrived_qkv, _ = lax.optimization_barrier((arrived_qkv, far_feed[grid.half]))
    sent_qkv = grid.gather_ready(arrived_qkv)
    near_qkv = grid.gather_two(own_qkv, arrived_qkv, sent_qkv)
    all_cot, cot_turned = join_halves(place, cotangent, partner[1])
    far_feed, _ = lax.optimization_barrier(
        (far_feed, (near_qkv.arrays[-2:], all_cot))
    )
    own_feed = jnp.stack(far_feed)
    arrived_feed = grid.gather_one(own_feed)

    first_in, qkv, all_tokens, full_qkv, full_out, vec_all = first_norm(
        place, tokens, partner[0], near_qkv, width_loc, all_cot
    )
    partner_out = swap_over(full_out, core_line)
    pairs = 2 * width_loc // PAIR
    heads_low, heads_turned, lse = attend_forward(qkv, ())
    arrived_feed, _ = lax.optimization_barrier((arrived_feed, heads_low))
    near_feed = grid.gather_two(own_feed, arrived_feed, grid.gather_ready(arrived_feed))
    partner_heads = swap_over(heads_low, core_line)
    hidden_state, second_in, second_turned, first_turned = attended_norm(
        heads_low, partner_heads, full_out, partner_out, all_tokens, vec_all, first_in
    )
    activated, grad_upper, grad_bias_up, down_part, second_part, second_low = feed(
        place, second_in, all_cot, vec_all, near_feed
    )

    second_other = swap_over(second_low, core_line)
    parts_feed = feed_grads(cot_turned, second_turned, activated, grad_upper, grid)
    arrived_feed = grid.stage_one(parts_feed)
    grad_hidden, grad_heads, second_sums, out_grad = second_back(
        second_part, second_other, hidden_state, all_cot, vec_all, full_out, heads_turned
    )
    grad_one = attend_backward(qkv, grad_heads, lse, 0, pairs - 1, ())
    arrived_feed, grad_one = lax.optimization_barrier((arrived_feed, grad_one))
    sent_feed = grid.stage_two(parts_feed, *arrived_feed)
    grad_two = attend_backward(qkv, grad_heads, lse, pairs - 1, 1, sent_feed)
    grads_qkv = (grad_one, grad_two)
    first_part, grad_vec = first_back(
        place, grads_qkv, full_qkv, all_tokens, second_sums, grad_bias_up
    )
    chain_feed = grid.chain_send(grid.stage_three(parts_feed, sent_feed, grad_vec))
    parts_qkv = qkv_grads(first_turned, grads_qkv, out_grad, grid, grad_vec, chain_feed[1])
    arrived_pack = grid.stage_one(parts_qkv)
    owned_feed = grid.reduce_chain(*chain_feed)
    owned_up, owned_down = owned_feed[:, :hidden_loc], owned_feed[:, hidden_loc:]

    sent_pack = grid.stage_two(parts_qkv, *arrived_pack)
    sent_pack, first_part, down_part = lax.optimization_barrier(
        (sent_pack, first_part, down_part)
    )
    near_pack = grid.stage_three(parts_qkv, sent_pack)
    first_other = swap_over(partner_rows(first_part).astype(BF16), core_line)
    down_other = swap_over(partner_rows(down_part).astype(BF16), core_line).astype(F32)
    mixed_out = own_rows(hidden_state) + own_rows(down_part) + down_other + vec_all[7]
    token_grad = token_back(core, first_part, first_other, tokens, grad_hidden, vec_all)
    owned_pack, (mixed_out, token_grad) = grid.reduce_direct(near_pack, (mixed_out, token_grad))
    part_vec = owned_pack[:, 4 * width_loc :]
    other_vec = swap_over(part_vec, core_line)
    owned_qkv = jnp.stack(
        [owned_pack[:, part * width_loc : (part + 1) * width_loc] for part in range(3)], axis=1
    )
    owned_out = owned_pack[:, 3 * width_loc : 4 * width_loc]

    new_qkv, new_first_qkv, new_second_qkv = adamw(
        w_qkv, first_qkv, second_qkv, owned_qkv, RATE_MATRIX
    )
    new_out, new_first_out, new_second_out = out_step(w_out, first_out, second_out, owned_out)
    new_up, new_first_up, new_second_up = adamw(w_up, first_up, second_up, owned_up, RATE_MATRIX)
    new_down, new_first_down, new_second_down = adamw(
        w_down, first_down, second_down, owned_down.T, RATE_MATRIX
    )
    new_vectors, new_first_vectors, new_second_vectors = vector_step(
        vectors, first_vectors, second_vectors, part_vec, other_vec
    )
    return (
        mixed_out,
        token_grad,
        new_qkv,
        new_out,
        new_up,
        new_down,
        new_vectors,
        new_first_qkv,
        new_first_out,
        new_first_up,
        new_first_down,
        new_first_vectors,
        new_second_qkv,
        new_second_out,
        new_second_up,
        new_second_down,
        new_second_vectors,
    )


def solution(mesh):
    by_token = P(("row", "col"), None)
    weights = (
        P("row", None, "col"),
        P("col", "row"),
        P("row", "col"),
        P("col", "row"),
        P(None, "row"),
    )
    return jax.shard_map(
        shards,
        mesh=mesh,
        in_specs=(by_token, by_token) + weights * 3,
        out_specs=(by_token, by_token) + weights * 3,
        check_vma=False,
    )
```

```python
import functools
import math

import jax
import jax.numpy as jnp
from jax import lax
from jax.experimental import pallas as pl
from jax.experimental.pallas import tpu as pltpu
from jax.sharding import PartitionSpec as P

HEAD_DIM = 64
LENGTH = 1024
STEP_NUMBER = 10
VEC_ROWS = 12
PAIR = 2 * HEAD_DIM
QUERY_BLOCK = 256
ROW_BLOCK = 512
VEC_LANES = 128
COST_SCALE = 2.3e8


EPS = 1e-05
BETA_ONE = 0.9
BETA_TWO = 0.999
ADAM_EPS = 1e-08
DECAY = 0.1
RATE_MATRIX = 0.04
RATE_VECTOR = 0.3

F32 = jnp.float32
BF16 = jnp.bfloat16


def normalize_rows(values_in):
    row_mean = jnp.mean(values_in, axis=-1, keepdims=True)
    centred = values_in - row_mean
    row_var = jnp.mean(centred * centred, axis=-1, keepdims=True)
    inv_std = lax.rsqrt(row_var + EPS)
    return (centred * inv_std, inv_std)


def norm_back(grad_in, normed, inv_std):
    mean_grad = jnp.mean(grad_in, axis=-1, keepdims=True)
    mean_cross = jnp.mean(grad_in * normed, axis=-1, keepdims=True)
    return inv_std * (grad_in - mean_grad - normed * mean_cross)


def adamw(weight, moment_one, moment_two, gradient, rate):
    first = BETA_ONE * moment_one + (1 - BETA_ONE) * gradient
    second = BETA_TWO * moment_two + (1 - BETA_TWO) * gradient * gradient
    first_hat = first / (1 - BETA_ONE**STEP_NUMBER)
    second_hat = second / (1 - BETA_TWO**STEP_NUMBER)
    updated = weight - rate * (first_hat / (jnp.sqrt(second_hat) + ADAM_EPS) + DECAY * weight)
    return (updated, first, second)


def swap_over(value, line):
    name, offset = line
    pairs = [(index, index ^ offset) for index in range(lax.axis_size(name))]
    return lax.ppermute(value, name, pairs)


def bit_offsets(low, high):
    offsets = []
    while low < high:
        offsets.append(low)
        low *= 2
    return offsets


def flip_order(blocks):
    count = blocks.shape[0]
    row = lax.axis_index("row")
    for offset in bit_offsets(1, count):
        cut = blocks.reshape((-1, 2, offset) + blocks.shape[1:])
        turned = jnp.where((row // offset) % 2 == 1, cut[:, ::-1], cut)
        blocks = turned.reshape(blocks.shape)
    return blocks


class Gathered:
    def __init__(self, arrays, table):
        self.arrays = arrays
        self.table = table
        self.rows = arrays[0].shape[1]
        self.cols = arrays[0].shape[2]
        if self.rows % 16:
            total = []
            for x in range(2):
                found = sorted((offset, array, at) for x_at, array, at, offset in table if x_at == x)
                blocks = jnp.stack([arrays[array][at] for _, array, at in found])
                total.append(flip_order(blocks).reshape(-1, self.cols))
            self.arrays = [jnp.stack(total)]
            self.table = [(0, 0, 0, 0), (1, 0, 1, 0)]
            self.rows = self.arrays[0].shape[1]


class Grid:
    def __init__(self, row_count):
        self.row_count = row_count
        self.far_count = row_count // 2
        self.half = self.far_count // 2
        self.x_line = ("col", 2)
        self.near_line = ("row", 1)

    def far_line(self, index):
        return ("row", 2 * index)

    def gather_far(self, block):
        return [block] + [
            swap_over(block, self.far_line(index)) for index in range(1, self.far_count)
        ]

    def gather_ready(self, blocks):
        return jnp.stack(blocks[: self.half]), jnp.stack(blocks[self.half :])

    def gather_one(self, sent):
        return swap_over(sent[0], self.near_line), swap_over(sent[1], self.x_line)

    def gather_two(self, sent, arrived):
        front = jnp.concatenate([sent[0], arrived[0]], axis=0)
        back = jnp.concatenate([sent[1], arrived[1]], axis=0)
        return front, back

    def gather_three(self, front, back):
        arrays = [front, swap_over(front, self.x_line), back, swap_over(back, self.near_line)]
        table = []
        for index in range(self.half):
            for x in range(2):
                table.append((x, x, index, 2 * index))
                table.append((x, x, index + self.half, 2 * index + 1))
                table.append((x, 2, index + x * self.half, 2 * (index + self.half)))
                table.append((x, 3, index + x * self.half, 2 * (index + self.half) + 1))
        return Gathered(arrays, table)

    def split(self, pair):
        _, all_rows, cols = pair.shape
        blocks = jnp.moveaxis(pair.reshape(2, self.row_count, -1, cols), 1, 0)
        blocks = jnp.moveaxis(flip_order(blocks), 0, 1)
        blocks = blocks.reshape(2, self.far_count, 2, -1, cols)
        last = blocks[1, :, 1]
        return (
            blocks[0, :, 0],
            blocks[1, :, 0],
            blocks[0, :, 1],
            last[: self.half],
            last[self.half :],
        )

    def part_of(self, x, index):
        far, near = index // 2, index % 2
        if not (x and near):
            return x + 2 * near, far
        return (3, far) if far < self.half else (4, far - self.half)

    def part_shapes(self, rows, cols):
        return [(self.far_count, rows, cols)] * 3 + [(self.half, rows, cols)] * 2

    def stage_one(self, parts):
        return swap_over(parts[3], self.x_line), swap_over(parts[4], self.near_line)

    def stage_two(self, parts, by_x, by_near):
        over_x, over_near = parts[1].astype(F32), parts[2].astype(F32)
        half = self.half
        over_x = jnp.concatenate([over_x[:half], over_x[half:] + by_near.astype(F32)], axis=0)
        over_near = jnp.concatenate([over_near[:half] + by_x.astype(F32), over_near[half:]], axis=0)
        return over_x.astype(BF16), over_near.astype(BF16)

    def stage_three(self, parts, sent, hold=None):
        by_x, by_near = swap_over(sent[0], self.x_line), swap_over(sent[1], self.near_line)
        if hold is not None:
            by_x, by_near, _ = lax.optimization_barrier((by_x, by_near, hold))
        return parts[0].astype(F32) + by_x.astype(F32) + by_near.astype(F32)

    def chain_send(self, parts):
        return parts[0::2], parts[1::2].astype(BF16)

    def reduce_chain(self, kept, sent):
        index = 1
        parts = kept + swap_over(sent, self.far_line(index)).astype(F32)
        while parts.shape[0] > 1:
            index *= 2
            kept, sent = self.chain_send(parts)
            parts = kept + swap_over(sent, self.far_line(index)).astype(F32)
        return parts[0]

    def reduce_direct(self, parts, hold):
        low = parts.astype(BF16)
        arrived = [
            swap_over(low[index], self.far_line(index))
            for index in range(1, self.far_count)
        ]
        arrived, hold = lax.optimization_barrier((arrived, hold))
        total = parts[0]
        for part in arrived:
            total = total + part.astype(F32)
        return total, hold


def dot_nt(left, right):
    return lax.dot_general(left, right, (((1,), (1,)), ((), ())), preferred_element_type=F32)


def dot_nn(left, right):
    return lax.dot_general(left, right, (((1,), (0,)), ((), ())), preferred_element_type=F32)


def lane_pick(half):
    lanes = lax.broadcasted_iota(jnp.int32, (1, PAIR), 1)
    return jnp.where((lanes // HEAD_DIM) == half, 1.0, 0.0).astype(BF16)


def causal_block(size):
    key_at = lax.broadcasted_iota(jnp.int32, (size, size), 0)
    query_at = lax.broadcasted_iota(jnp.int32, (size, size), 1)
    return key_at <= query_at


def cost(microseconds):
    return pl.CostEstimate(
        flops=int(microseconds * COST_SCALE), bytes_accessed=1024, transcendentals=0
    )


def attend_kernel(q_ref, k_ref, v_ref, out_ref, turned_ref, lse_ref):
    length = q_ref.shape[0]
    block = min(QUERY_BLOCK, length)
    allowed = causal_block(block)
    values_t = v_ref[...].T
    scaling = jnp.asarray(HEAD_DIM**-0.5, BF16)
    for first in range(0, length, block):
        last = first + block
        query = q_ref[first:last, :] * scaling
        outs = []
        for half in range(2):
            rows = slice(half * HEAD_DIM, (half + 1) * HEAD_DIM)
            query_half = query * lane_pick(half)
            diag = dot_nt(k_ref[first:last, :], query_half)
            diag = jnp.where(allowed, diag, -1e30)
            top = jnp.max(diag, axis=0, keepdims=True)
            if first:
                rest = dot_nt(k_ref[0:first, :], query_half)
                top = jnp.maximum(top, jnp.max(rest, axis=0, keepdims=True))
            diag = jnp.exp(diag - top)
            total = jnp.sum(diag, axis=0, keepdims=True)
            if first:
                rest = jnp.exp(rest - top)
                total = total + jnp.sum(rest, axis=0, keepdims=True)
            inverse = 1.0 / total
            result = dot_nn(values_t[rows, first:last], (diag * inverse).astype(BF16))
            if first:
                result = result + dot_nn(values_t[rows, 0:first], (rest * inverse).astype(BF16))
            outs.append(result)
            lse_ref[0, half : half + 1, first:last] = top + jnp.log(total)
        turned = jnp.concatenate(outs, axis=0)
        out_ref[first:last, :] = turned.T.astype(BF16)
        turned_ref[:, first:last] = turned.astype(BF16)


def pair_lanes(length, first, part):
    return pl.BlockSpec((length, PAIR), lambda pair: (0, 3 * (first + pair) + part))


def attend_forward(qkv, after):
    length = qkv.shape[0]
    pairs = qkv.shape[1] // (3 * PAIR)
    return pl.pallas_call(
        lambda q, k, v, *refs: attend_kernel(q, k, v, *refs[len(after) :]),
        grid=(pairs,),
        in_specs=[pair_lanes(length, 0, part) for part in range(3)]
        + [pl.BlockSpec(memory_space=pl.ANY)] * len(after),
        out_specs=[
            pl.BlockSpec((length, PAIR), lambda pair: (0, pair)),
            pl.BlockSpec((PAIR, length), lambda pair: (pair, 0)),
            pl.BlockSpec((1, 8, length), lambda pair: (pair, 0, 0)),
        ],
        out_shape=[
            jax.ShapeDtypeStruct((length, pairs * PAIR), BF16),
            jax.ShapeDtypeStruct((pairs * PAIR, length), BF16),
            jax.ShapeDtypeStruct((pairs, 8, length), F32),
        ],
        compiler_params=pltpu.CompilerParams(vmem_limit_bytes=40 * 2**20),
        cost_estimate=cost(4.2 * pairs),
        name="attend_forward",
    )(qkv, qkv, qkv, *after)


def attend_back_kernel(q_ref, k_ref, v_ref, go_ref, lse_ref, grad_ref, gk_sum, gv_sum):
    length = q_ref.shape[0]
    block = min(QUERY_BLOCK, length)
    allowed = causal_block(block)
    keys_t = k_ref[...].T
    scaling = jnp.asarray(HEAD_DIM**-0.5, BF16)
    pair = pl.program_id(0)

    def lanes(part):
        return pl.ds(pl.multiple_of((3 * pair + part) * PAIR, PAIR), PAIR)

    gk_sum[...] = jnp.zeros_like(gk_sum)
    gv_sum[...] = jnp.zeros_like(gv_sum)
    for first in range(0, length, block):
        last = first + block
        query = q_ref[first:last, :] * scaling
        grad_out = go_ref[first:last, :]
        outs = []
        for half in range(2):
            rows = slice(half * HEAD_DIM, (half + 1) * HEAD_DIM)
            pick = lane_pick(half)
            query_half = query * pick
            grad_half = grad_out * pick
            lse = lse_ref[0, half : half + 1, first:last]
            spans = [(first, last)] if first == 0 else [(0, first), (first, last)]
            probs, grads, inner = [], [], None
            for low, high in spans:
                scores = dot_nt(k_ref[low:high, :], query_half)
                if low == first:
                    scores = jnp.where(allowed, scores, -1e30)
                prob = jnp.exp(scores - lse)
                grad_prob = dot_nt(v_ref[low:high, :], grad_half)
                part = jnp.sum(prob * grad_prob, axis=0, keepdims=True)
                inner = part if inner is None else inner + part
                probs.append(prob)
                grads.append(grad_prob)
            result = None
            for (low, high), prob, grad_prob in zip(spans, probs, grads):
                grad_score = (prob * (grad_prob - inner)).astype(BF16)
                gk_sum[low:high, :] += dot_nn(grad_score, query_half)
                gv_sum[low:high, :] += dot_nn(prob.astype(BF16), grad_half)
                part = dot_nn(keys_t[rows, low:high], grad_score)
                result = part if result is None else result + part
            outs.append(result)
        grad_query = jnp.concatenate(outs, axis=0).T * (HEAD_DIM**-0.5)
        grad_ref[first:last, lanes(0)] = grad_query.astype(BF16)
    grad_ref[:, lanes(1)] = gk_sum[...].astype(BF16)
    grad_ref[:, lanes(2)] = gv_sum[...].astype(BF16)


def attend_backward(qkv, grad_heads, lse, first, pairs, after):
    length = qkv.shape[0]
    width = 3 * PAIR * pairs
    return pl.pallas_call(
        lambda q, k, v, go, lse_at, *refs: attend_back_kernel(
            q, k, v, go, lse_at, *refs[len(after) :]
        ),
        grid=(pairs,),
        in_specs=[pair_lanes(length, first, part) for part in range(3)]
        + [
            pl.BlockSpec((length, PAIR), lambda pair: (0, first + pair)),
            pl.BlockSpec((1, 8, length), lambda pair: (first + pair, 0, 0)),
        ]
        + [pl.BlockSpec(memory_space=pl.ANY)] * len(after),
        out_specs=pl.BlockSpec((length, width), lambda pair: (0, 0)),
        out_shape=jax.ShapeDtypeStruct((length, width), BF16),
        scratch_shapes=[pltpu.VMEM((length, PAIR), F32), pltpu.VMEM((length, PAIR), F32)],
        compiler_params=pltpu.CompilerParams(vmem_limit_bytes=40 * 2**20),
        cost_estimate=cost(0.5 * pairs),
        name="attend_backward",
    )(qkv, qkv, qkv, grad_heads, lse, *after)


def rows_of(block, width):
    return pl.BlockSpec((block, width), lambda step: (step, 0))


def whole(shape):
    return pl.BlockSpec(shape, lambda *step: (0,) * len(shape))


def shaped(shape, dtype):
    return jax.ShapeDtypeStruct(shape, dtype)


PARAMS = pltpu.CompilerParams(vmem_limit_bytes=48 * 2**20)


ANYWHERE = pl.BlockSpec(memory_space=pl.ANY)


def weight_copies(gathered, refs, held, sems):
    row = lax.axis_index("row")
    copies = ([], [])
    for number, (x, array, at, offset) in enumerate(gathered.table):
        if len(gathered.table) > 2:
            start = pl.multiple_of((row ^ offset) * gathered.rows, 16)
        else:
            start = 0
        target = held.at[x, pl.ds(start, gathered.rows), :]
        copies[x].append(
            pltpu.make_async_copy(refs[array].at[at], target, sems.at[number])
        )
    return copies


def weight_scratch(gathered):
    all_rows = len(gathered.table) // 2 * gathered.rows
    return [
        pltpu.VMEM((2, all_rows, gathered.cols), BF16),
        pltpu.SemaphoreType.DMA((len(gathered.table),)),
    ]


def start_all(copies):
    for copy in copies:
        copy.start()


def wait_all(copies):
    for copy in copies:
        copy.wait()


def store_parts(held, grid, refs, x, source, lanes):
    if len(refs) == 1:
        refs[0][x, :, lanes] = held[:, source]
        return
    row = lax.axis_index("row")
    rows = held.shape[0] // grid.row_count
    for index in range(grid.row_count):
        start = pl.multiple_of((row ^ index) * rows, 16)
        array, place = grid.part_of(x, index)
        refs[array][place, :, lanes] = held[pl.ds(start, rows), source]


def segments(pair, third):
    low, high, found = pair * PAIR, (pair + 1) * PAIR, []
    while low < high:
        x = low // third
        end = min(high, (x + 1) * third)
        found.append((x, low - x * third, end - x * third, low - pair * PAIR))
        low = end
    return found


def parts_out(grid, width, cols):
    rows = width // grid.row_count
    if rows % 16:
        return [(2, width, cols)]
    return grid.part_shapes(rows, cols)


def turn(value):
    return value.T


def pick_half(here, mine_ref, other_ref):
    mine, other = mine_ref[...].astype(F32), other_ref[...].astype(F32)
    return jnp.where(here, mine, other)


def first_norm_kernel(gathered, cols, place_ref, mine_ref, other_ref, after_ref, *refs):
    count = len(gathered.arrays)
    norm_ref, qkv_ref, tokens_ref, full_ref, out_w_ref, vec_ref, held, bias, sems = refs[count:]
    copies = weight_copies(gathered, refs[:count], held, sems)
    third = cols // 3
    step = pl.program_id(0)
    per_half = pl.num_programs(0) // 2

    @pl.when(step == 0)
    def _():
        start_all(copies[0] + copies[1])
        wait_all(copies[0] + copies[1])
        for x in range(2):
            out_w_ref[:, x * third : (x + 1) * third] = held[x, :, held.shape[2] - third :]
        for pair in range(2 * third // PAIR):
            for part in range(3):
                for x, low, high, lane in segments(pair, third):
                    at = (3 * pair + part) * PAIR + lane
                    source = slice(part * third + low, part * third + high)
                    full_ref[:, at : at + high - low] = held[x, :, source]
        first = cols // 128 * 128
        rows = turn(held[0, :, first : first + 128].astype(F32))[cols - first :]
        vec_ref[...] = rows[: vec_ref.shape[0]]
        row_at = lax.broadcasted_iota(jnp.int32, (rows.shape[1], 2 * third), 0)
        lane_at = lax.broadcasted_iota(jnp.int32, (rows.shape[1], 2 * third), 1)
        wanted = jnp.where(
            lane_at < third, place_ref[1] + lane_at, place_ref[2] + lane_at - third
        )
        chosen = jnp.where(row_at == wanted, 1.0, 0.0).astype(BF16)
        picked = dot_nn(vec_ref[...].astype(BF16), chosen)
        bias[...] = jnp.zeros_like(bias)
        for pair in range(2 * third // PAIR):
            lanes = slice(pair * PAIR, (pair + 1) * PAIR)
            at = 3 * pair * PAIR
            bias[0:1, at : at + PAIR] = picked[2:3, lanes]
            bias[0:1, at + 2 * PAIR : at + 3 * PAIR] = picked[3:4, lanes]

    tokens = pick_half(step // per_half == place_ref[0], mine_ref, other_ref)
    tokens_ref[...] = tokens.astype(BF16)
    normed, _ = normalize_rows(tokens)
    first_in = (normed * vec_ref[0:1, :] + vec_ref[1:2, :]).astype(BF16)
    norm_ref[...] = first_in
    qkv_ref[...] = (dot_nn(first_in, full_ref[...]) + bias[0:1, :]).astype(BF16)


def first_norm(place, mine, other, gathered, width_loc, after):
    rows, width = mine.shape
    length = 2 * rows
    cols = 3 * width_loc
    steps = rows // ROW_BLOCK
    half = pl.BlockSpec((ROW_BLOCK, width), lambda step, place_ref: (step % steps, 0))

    def by_row(size):
        return pl.BlockSpec((ROW_BLOCK, size), lambda step, place_ref: (step, 0))

    return pl.pallas_call(
        functools.partial(first_norm_kernel, gathered, cols),
        grid_spec=pltpu.PrefetchScalarGridSpec(
            num_scalar_prefetch=1,
            grid=(2 * steps,),
            in_specs=[half, half, ANYWHERE] + [ANYWHERE] * len(gathered.arrays),
            out_specs=[
                by_row(width),
                by_row(2 * cols),
                by_row(width),
                whole((width, 2 * cols)),
                whole((width, 2 * width_loc)),
                whole((16, width)),
            ],
            scratch_shapes=weight_scratch(gathered)[:1]
            + [pltpu.VMEM((8, 2 * cols), F32)]
            + weight_scratch(gathered)[1:],
        ),
        out_shape=[
            shaped((length, width), BF16),
            shaped((length, 2 * cols), BF16),
            shaped((length, width), BF16),
            shaped((width, 2 * cols), BF16),
            shaped((width, 2 * width_loc), BF16),
            shaped((16, width), F32),
        ],
        compiler_params=PARAMS,
        cost_estimate=cost(8),
        name="first_norm",
    )(place, mine, other, after, *gathered.arrays)


def attended_kernel(
    heads_ref, partner_ref, own_ref, other_ref, tokens_ref, vec_ref, first_ref,
    hidden_ref, norm_ref, norm_turned_ref, first_turned_ref,
):
    attended = dot_nt(heads_ref[...], own_ref[...]) + dot_nt(partner_ref[...], other_ref[...])
    hidden = tokens_ref[...].astype(F32) + attended + vec_ref[4:5, :]
    hidden_ref[...] = hidden
    normed, _ = normalize_rows(hidden)
    second_in = (normed * vec_ref[5:6, :] + vec_ref[6:7, :]).astype(BF16)
    norm_ref[...] = second_in
    norm_turned_ref[...] = turn(second_in)
    first_turned_ref[...] = turn(first_ref[...])


def attended_norm(heads, partner_heads, own_out, partner_out, tokens, vec_all, first_in):
    length, width = tokens.shape
    cols = own_out.shape[1]
    full, part = rows_of(ROW_BLOCK, width), rows_of(ROW_BLOCK, cols)
    turned = pl.BlockSpec((width, ROW_BLOCK), lambda step: (0, step))
    return pl.pallas_call(
        attended_kernel,
        grid=(length // ROW_BLOCK,),
        in_specs=[
            part,
            part,
            whole(own_out.shape),
            whole(partner_out.shape),
            full,
            whole(vec_all.shape),
            full,
        ],
        out_specs=[full, full, turned, turned],
        out_shape=[shaped((length, width), F32), shaped((length, width), BF16)]
        + [shaped((width, length), BF16)] * 2,
        compiler_params=PARAMS,
        cost_estimate=cost(8),
        name="attended_norm",
    )(heads, partner_heads, own_out, partner_out, tokens, vec_all, first_in)


def join_kernel(place_ref, mine_ref, other_ref, joined_ref, turned_ref):
    here = pl.program_id(0) // (pl.num_programs(0) // 2) == place_ref[0]
    joined = pick_half(here, mine_ref, other_ref).astype(BF16)
    joined_ref[...] = joined
    turned_ref[...] = turn(joined)


def join_halves(place, mine, other):
    rows, width = mine.shape
    steps = rows // ROW_BLOCK
    half = pl.BlockSpec((ROW_BLOCK, width), lambda step, place_ref: (step % steps, 0))
    return pl.pallas_call(
        join_kernel,
        grid_spec=pltpu.PrefetchScalarGridSpec(
            num_scalar_prefetch=1,
            grid=(2 * steps,),
            in_specs=[half, half],
            out_specs=[
                pl.BlockSpec((ROW_BLOCK, width), lambda step, place_ref: (step, 0)),
                pl.BlockSpec((width, ROW_BLOCK), lambda step, place_ref: (0, step)),
            ],
        ),
        out_shape=[shaped((2 * rows, width), BF16), shaped((width, 2 * rows), BF16)],
        compiler_params=PARAMS,
        cost_estimate=cost(0.1),
        name="join_halves",
    )(place, mine, other)


def feed_kernel(gathered, place_ref, norm_ref, cot_ref, vec_ref, *refs):
    count = len(gathered.arrays)
    act_ref, gup_ref, bias_sum_ref, out_low_ref, back_low_ref, out_ref, back_ref, held, sems = refs[count:]
    copies = weight_copies(gathered, refs[:count], held, sems)
    step = pl.program_id(0)
    length = norm_ref.shape[0]
    curve, cubic = math.sqrt(2 / math.pi), 0.044715
    cols = held.shape[2] // 2
    x = step
    up_lanes, down_lanes = slice(0, cols), slice(cols, 2 * cols)
    bias = vec_ref[pl.ds(8 + place_ref[3 + x], 1), :]

    @pl.when(step == 0)
    def _():
        start_all(copies[0] + copies[1])
        out_ref[...] = jnp.zeros_like(out_ref)
        back_ref[...] = jnp.zeros_like(back_ref)
        wait_all(copies[0])

    @pl.when(step == 1)
    def _():
        wait_all(copies[1])

    bias_sum = jnp.zeros(bias.shape, F32)
    for first in range(0, length, ROW_BLOCK):
        rows = slice(first, first + ROW_BLOCK)
        up = dot_nn(norm_ref[rows, :], held[x, :, up_lanes]) + bias
        cubed = up * up * (curve * cubic)
        tanh = jnp.tanh(up * (curve + cubed))
        halved = 0.5 * up
        act_ref[rows, :] = (halved + halved * tanh).astype(BF16)
        slope = 0.5 + 0.5 * tanh + halved * (1.0 - tanh * tanh) * (curve + 3.0 * cubed)
        grad_up = (dot_nn(cot_ref[rows, :], held[x, :, down_lanes]) * slope).astype(BF16)
        gup_ref[rows, :] = grad_up
        bias_sum = bias_sum + jnp.sum(grad_up.astype(F32), axis=0, keepdims=True)
    back_ref[...] += dot_nt(gup_ref[...], held[x, :, up_lanes])
    out_ref[...] += dot_nt(act_ref[...], held[x, :, down_lanes])
    bias_sum_ref[...] = bias_sum

    @pl.when(step == pl.num_programs(0) - 1)
    def _():
        back_low_ref[...] = back_ref[...].astype(BF16)
        out_low_ref[...] = out_ref[...].astype(BF16)


def feed(place, norm, cot, vec_all, gathered):
    length, width = norm.shape
    block = gathered.cols // 2
    hidden = 2 * block
    tall = pl.BlockSpec((length, block), lambda step, place_ref: (0, step))
    flat = pl.BlockSpec((1, block), lambda step, place_ref: (0, step))
    full = whole((length, width))
    return pl.pallas_call(
        functools.partial(feed_kernel, gathered),
        grid_spec=pltpu.PrefetchScalarGridSpec(
            num_scalar_prefetch=1,
            grid=(2,),
            in_specs=[full, full, whole(vec_all.shape)] + [ANYWHERE] * len(gathered.arrays),
            out_specs=[tall, tall, flat, full, full],
            scratch_shapes=[pltpu.VMEM((length, width), F32)] * 2 + weight_scratch(gathered),
        ),
        out_shape=[
            shaped((length, hidden), BF16),
            shaped((length, hidden), BF16),
            shaped((1, hidden), F32),
            shaped((length, width), BF16),
            shaped((length, width), BF16),
        ],
        compiler_params=PARAMS,
        cost_estimate=cost(18),
        name="feed",
    )(place, norm, cot, vec_all, *gathered.arrays)


def feed_grads_kernel(grid, cot_ref, norm_ref, act_ref, gup_ref, *refs):
    kind, x_at = pl.program_id(0), pl.program_id(1)
    outs, held = refs[:-1], refs[-1]
    size = held.shape[1]

    @pl.when(kind == 0)
    def _():
        held[...] = dot_nn(cot_ref[...], act_ref[...]).astype(BF16)

    @pl.when(kind == 1)
    def _():
        held[...] = dot_nn(norm_ref[...], gup_ref[...]).astype(BF16)

    for index in range(2):
        for x in range(2):

            @pl.when((kind == index) & (x_at == x))
            def _():
                lanes = slice((1 - index) * size, (2 - index) * size)
                store_parts(held, grid, outs, x, slice(None), lanes)


def feed_grads(cot_turned, norm_turned, act, grad_up, grid):
    width, length = cot_turned.shape
    hidden = act.shape[1]
    block = hidden // 2
    shapes = parts_out(grid, width, hidden)
    parts = pl.pallas_call(
        functools.partial(feed_grads_kernel, grid),
        grid=(2, 2),
        in_specs=[
            whole((width, length)),
            whole((width, length)),
            pl.BlockSpec((length, block), lambda kind, x: (0, jnp.where(kind == 0, x, 1))),
            pl.BlockSpec((length, block), lambda kind, x: (0, jnp.where(kind == 1, x, 0))),
        ],
        out_specs=[whole(shape) for shape in shapes],
        out_shape=[shaped(shape, BF16) for shape in shapes],
        scratch_shapes=[pltpu.VMEM((width, block), BF16)],
        compiler_params=PARAMS,
        cost_estimate=cost(10),
        name="feed_grads",
    )(cot_turned, norm_turned, act, grad_up)
    return parts if len(parts) == 5 else grid.split(parts[0])


def second_back_kernel(
    part_ref, other_ref, hidden_ref, cot_ref, vec_ref, out_w_ref, turned_ref,
    grad_ref, heads_ref, sum_ref, out_grad_ref, total,
):
    step = pl.program_id(0)
    normed, inv_std = normalize_rows(hidden_ref[...])
    part = part_ref[...].astype(F32)
    cot = cot_ref[...].astype(F32)
    grad_second = part + other_ref[...].astype(F32)
    grad = cot + norm_back(grad_second * vec_ref[5:6, :], normed, inv_std)
    grad_ref[...] = grad
    low = grad.astype(BF16)
    heads_ref[...] = dot_nn(low, out_w_ref[...]).astype(BF16)

    @pl.when(step == 0)
    def _():
        sum_ref[...] = jnp.zeros_like(sum_ref)
        total[...] = jnp.zeros_like(total)

    total[...] += dot_nn(turned_ref[...], low)
    for row, value in enumerate((grad, part * normed, part, cot)):
        sum_ref[row : row + 1, :] += jnp.sum(value, axis=0, keepdims=True)

    @pl.when(step == pl.num_programs(0) - 1)
    def _():
        out_grad_ref[...] = total[...].T.astype(BF16)


def second_back(part, other, hidden, cot, vec_all, out_w, heads_turned):
    length, width = part.shape
    cols = out_w.shape[1]
    full = rows_of(ROW_BLOCK, width)
    return pl.pallas_call(
        second_back_kernel,
        grid=(length // ROW_BLOCK,),
        in_specs=[full, full, full, full, whole(vec_all.shape), whole(out_w.shape)]
        + [pl.BlockSpec((cols, ROW_BLOCK), lambda step: (0, step))],
        out_specs=[full, rows_of(ROW_BLOCK, cols), whole((8, width)), whole((width, cols))],
        out_shape=[
            shaped((length, width), F32),
            shaped((length, cols), BF16),
            shaped((8, width), F32),
            shaped((width, cols), BF16),
        ],
        scratch_shapes=[pltpu.VMEM((cols, width), F32)],
        compiler_params=PARAMS,
        cost_estimate=cost(8.6),
        name="second_back",
    )(part, other, hidden, cot, vec_all, out_w, heads_turned)


def qkv_grads_kernel(grid, norm_ref, grad_ref, grad_two_ref, out_grad_ref, vec_ref, *refs):
    step = pl.program_id(0)
    outs, held = refs[:-1], refs[-1]
    third = held.shape[1] // 2
    pairs = 2 * third // PAIR
    for index in range(pairs + 1):

        @pl.when(step == index)
        def _():
            if index == pairs:
                held[...] = out_grad_ref[...]
                for x in range(2):
                    source = slice(x * third, (x + 1) * third)
                    store_parts(held, grid, outs, x, source, slice(3 * third, 4 * third))
                rows = vec_ref[...]
                blank = jnp.zeros((VEC_LANES - rows.shape[0], rows.shape[1]), F32)
                held[:, :VEC_LANES] = jnp.concatenate([rows, blank], axis=0).T.astype(BF16)
                for x in range(2):
                    lanes = slice(4 * third, 4 * third + VEC_LANES)
                    store_parts(held, grid, outs, x, slice(0, VEC_LANES), lanes)
                return
            right = grad_two_ref if index == pairs - 1 else grad_ref
            held[...] = dot_nn(norm_ref[...], right[...]).astype(BF16)
            for part in range(3):
                for x, low, high, lane in segments(index, third):
                    at = part * PAIR + lane
                    lanes = slice(part * third + low, part * third + high)
                    store_parts(held, grid, outs, x, slice(at, at + high - low), lanes)


def qkv_grads(norm_turned, grads, out_grad, grid, grad_vec):
    width, length = norm_turned.shape
    cols = out_grad.shape[1]
    pairs = cols // PAIR
    shapes = parts_out(grid, width, 2 * cols + VEC_LANES)
    parts = pl.pallas_call(
        functools.partial(qkv_grads_kernel, grid),
        grid=(pairs + 1,),
        in_specs=[
            whole((width, length)),
            pl.BlockSpec((length, cols), lambda step: (0, jnp.minimum(step, pairs - 2))),
            whole((length, cols)),
            whole((width, cols)),
            whole(grad_vec.shape),
        ],
        out_specs=[whole(shape) for shape in shapes],
        out_shape=[shaped(shape, BF16) for shape in shapes],
        scratch_shapes=[pltpu.VMEM((width, cols), BF16)],
        compiler_params=PARAMS,
        cost_estimate=cost(0.3),
        name="qkv_grads",
    )(norm_turned, *grads, out_grad, grad_vec)
    return parts if len(parts) == 5 else grid.split(parts[0])


def first_back_kernel(
    place_ref, grad_ref, grad_two_ref, weight_ref, tokens_ref, second_ref, up_ref,
    part_ref, vec_ref, bias,
):
    grads = jnp.concatenate([grad_ref[...], grad_two_ref[...]], axis=1)
    part = dot_nt(grads, weight_ref[...])
    part_ref[...] = part.astype(BF16)
    normed, _ = normalize_rows(tokens_ref[...].astype(F32))

    @pl.when(pl.program_id(0) == 0)
    def _():
        vec_ref[...] = jnp.zeros_like(vec_ref)
        bias[...] = jnp.zeros_like(bias)

    for row, value in enumerate((part * normed, part)):
        vec_ref[row : row + 1, :] += jnp.sum(value, axis=0, keepdims=True)
    bias[0:1, :] += jnp.sum(grads.astype(F32), axis=0, keepdims=True)

    @pl.when(pl.program_id(0) == pl.num_programs(0) - 1)
    def _():
        width = vec_ref.shape[1]
        pairs = bias.shape[1] // (3 * PAIR)
        third = pairs * PAIR // 2
        for row, part_at in ((2, 0), (3, 2)):
            lanes = [
                bias[:, (3 * pair + part_at) * PAIR : (3 * pair + part_at + 1) * PAIR]
                for pair in range(pairs)
            ]
            joined = jnp.concatenate(lanes, axis=1)
            blank = jnp.zeros((joined.shape[0], width - third), F32)
            for x in range(2):
                block = jnp.concatenate([joined[:, x * third : (x + 1) * third], blank], axis=1)
                vec_ref[row : row + 1, :] += pltpu.roll(block, place_ref[1 + x], 1)[0:1]
        vec_ref[4:5, :] = 0.5 * second_ref[0:1, :]
        vec_ref[5:7, :] = second_ref[1:3, :]
        vec_ref[7:8, :] = 0.5 * second_ref[3:4, :]
        row_at = lax.broadcasted_iota(jnp.int32, (8, width), 0)
        vec_ref[8:16, :] = jnp.where(row_at == place_ref[3], up_ref[0:1, :width], 0.0) + jnp.where(
            row_at == place_ref[4], up_ref[0:1, width:], 0.0
        )


def first_back(place, grads, weight, tokens, second_sums, up_sums):
    length, width = tokens.shape
    cols = weight.shape[1]

    def by_row(size):
        return pl.BlockSpec((ROW_BLOCK, size), lambda step, place_ref: (step, 0))

    return pl.pallas_call(
        first_back_kernel,
        grid_spec=pltpu.PrefetchScalarGridSpec(
            num_scalar_prefetch=1,
            grid=(length // ROW_BLOCK,),
            in_specs=[
                by_row(grads[0].shape[1]),
                by_row(grads[1].shape[1]),
                whole(weight.shape),
                by_row(width),
                whole(second_sums.shape),
                whole(up_sums.shape),
            ],
            out_specs=[by_row(width), whole((16, width))],
            scratch_shapes=[pltpu.VMEM((8, cols), F32)],
        ),
        out_shape=[shaped((length, width), BF16), shaped((16, width), F32)],
        compiler_params=PARAMS,
        cost_estimate=cost(0.3),
        name="first_back",
    )(place, *grads, weight, tokens, second_sums, up_sums)


def token_back_kernel(core_ref, part_ref, other_ref, tokens_ref, grad_ref, vec_ref, out_ref):
    normed, inv_std = normalize_rows(tokens_ref[...].astype(F32))
    grad_first = part_ref[...].astype(F32) + other_ref[...].astype(F32)
    out_ref[...] = grad_ref[...] + norm_back(grad_first * vec_ref[0:1, :], normed, inv_std)


def token_back(core, part, other, tokens, grad_hidden, vec_all):
    rows, width = tokens.shape
    steps = rows // ROW_BLOCK
    own = pl.BlockSpec((ROW_BLOCK, width), lambda step, core_ref: (core_ref[0] * steps + step, 0))
    here = pl.BlockSpec((ROW_BLOCK, width), lambda step, core_ref: (step, 0))
    return pl.pallas_call(
        token_back_kernel,
        grid_spec=pltpu.PrefetchScalarGridSpec(
            num_scalar_prefetch=1,
            grid=(steps,),
            in_specs=[own, here, here, own, whole(vec_all.shape)],
            out_specs=here,
        ),
        out_shape=shaped((rows, width), F32),
        compiler_params=PARAMS,
        cost_estimate=cost(3.2),
        name="token_back",
    )(core.reshape(1), part, other, tokens, grad_hidden, vec_all)


def out_step_kernel(grad_ref, weight_ref, first_ref, second_ref, new_ref, new_first_ref, new_second_ref):
    grads = grad_ref[...].T
    results = adamw(weight_ref[...], first_ref[...], second_ref[...], grads, RATE_MATRIX)
    new_ref[...], new_first_ref[...], new_second_ref[...] = results


def out_step(weight, first, second, grads):
    return pl.pallas_call(
        out_step_kernel,
        out_shape=[shaped(weight.shape, F32)] * 3,
        compiler_params=PARAMS,
        name="out_step",
    )(grads, weight, first, second)


def vector_step_kernel(
    part_ref, other_ref, weight_ref, first_ref, second_ref, new_ref, new_first_ref, new_second_ref
):
    grads = (part_ref[...] + other_ref[...]).T[: weight_ref.shape[0]]
    results = adamw(weight_ref[...], first_ref[...], second_ref[...], grads, RATE_VECTOR)
    new_ref[...], new_first_ref[...], new_second_ref[...] = results


def vector_step(weight, first, second, part, other):
    return pl.pallas_call(
        vector_step_kernel,
        out_shape=[shaped(weight.shape, F32)] * 3,
        compiler_params=PARAMS,
        name="vector_step",
    )(part, other, weight, first, second)


def shards(
    tokens,
    cotangent,
    w_qkv,
    w_out,
    w_up,
    w_down,
    vectors,
    first_qkv,
    first_out,
    first_up,
    first_down,
    first_vectors,
    second_qkv,
    second_out,
    second_up,
    second_down,
    second_vectors,
):
    col_index = lax.axis_index("col")
    grid = Grid(lax.axis_size("row"))
    core_line = ("col", 1)
    core = col_index % 2
    other_col = col_index ^ 2
    rows_loc, width = tokens.shape
    width_loc = w_qkv.shape[2]
    hidden_loc = w_up.shape[1]
    shard_rows = w_up.shape[0]

    pad = -(3 * width_loc + VEC_ROWS) % 128
    pack_qkv = jnp.concatenate(
        [w_qkv[:, part].astype(BF16) for part in range(3)]
        + [vectors.T.astype(BF16), jnp.zeros((shard_rows, pad), BF16), w_out.T.astype(BF16)],
        axis=1,
    )
    pack_feed = jnp.concatenate([w_up.astype(BF16), w_down.T.astype(BF16)], axis=1)

    def own_rows(value):
        return lax.dynamic_slice_in_dim(value, core * rows_loc, rows_loc, 0)

    def partner_rows(value):
        return lax.dynamic_slice_in_dim(value, (1 - core) * rows_loc, rows_loc, 0)

    place = jnp.stack(
        [core, col_index * width_loc, other_col * width_loc, col_index, other_col]
    ).astype(jnp.int32)

    far_qkv = grid.gather_far(pack_qkv)
    partner = [swap_over(tokens, core_line), swap_over(cotangent, core_line)]
    far_qkv, partner = lax.optimization_barrier((far_qkv, partner))
    sent_qkv = grid.gather_ready(far_qkv)
    pack_feed, _ = lax.optimization_barrier((pack_feed, sent_qkv))
    arrived_qkv = grid.gather_one(sent_qkv)
    far_feed = grid.gather_far(pack_feed)
    two_qkv = grid.gather_two(sent_qkv, arrived_qkv)
    near_qkv = grid.gather_three(*two_qkv)
    all_cot, cot_turned = join_halves(place, cotangent, partner[1])
    far_feed, _ = lax.optimization_barrier((far_feed, (two_qkv, all_cot)))
    sent_feed = grid.gather_ready(far_feed)
    arrived_feed = grid.gather_one(sent_feed)

    first_in, qkv, all_tokens, full_qkv, full_out, vec_all = first_norm(
        place, tokens, partner[0], near_qkv, width_loc, all_cot
    )
    partner_out = swap_over(full_out, core_line)
    pairs = 2 * width_loc // PAIR
    arrived_feed, _ = lax.optimization_barrier((arrived_feed, qkv))
    two_feed = grid.gather_two(sent_feed, arrived_feed)
    near_feed = grid.gather_three(*two_feed)
    heads_low, heads_turned, lse = attend_forward(qkv, two_feed)
    partner_heads = swap_over(heads_low, core_line)
    hidden_state, second_in, second_turned, first_turned = attended_norm(
        heads_low, partner_heads, full_out, partner_out, all_tokens, vec_all, first_in
    )
    activated, grad_upper, grad_bias_up, down_part, second_part = feed(
        place, second_in, all_cot, vec_all, near_feed
    )

    second_other = swap_over(second_part, core_line)
    parts_feed = feed_grads(cot_turned, second_turned, activated, grad_upper, grid)
    arrived_feed = grid.stage_one(parts_feed)
    grad_hidden, grad_heads, second_sums, out_grad = second_back(
        second_part, second_other, hidden_state, all_cot, vec_all, full_out, heads_turned
    )
    grad_one = attend_backward(qkv, grad_heads, lse, 0, pairs - 1, ())
    arrived_feed, grad_one = lax.optimization_barrier((arrived_feed, grad_one))
    sent_feed = grid.stage_two(parts_feed, *arrived_feed)
    grad_two = attend_backward(qkv, grad_heads, lse, pairs - 1, 1, sent_feed)
    grads_qkv = (grad_one, grad_two)
    first_part, grad_vec = first_back(
        place, grads_qkv, full_qkv, all_tokens, second_sums, grad_bias_up
    )
    parts_qkv = qkv_grads(first_turned, grads_qkv, out_grad, grid, grad_vec)
    arrived_pack = grid.stage_one(parts_qkv)
    chain_feed = grid.chain_send(grid.stage_three(parts_feed, sent_feed, parts_qkv[0]))
    arrived_pack, _ = lax.optimization_barrier((arrived_pack, chain_feed[1]))
    owned_feed = grid.reduce_chain(*chain_feed)
    owned_up, owned_down = owned_feed[:, :hidden_loc], owned_feed[:, hidden_loc:]

    sent_pack = grid.stage_two(parts_qkv, *arrived_pack)
    sent_pack, first_part, down_part = lax.optimization_barrier(
        (sent_pack, first_part, down_part)
    )
    near_pack = grid.stage_three(parts_qkv, sent_pack)
    first_other = swap_over(partner_rows(first_part), core_line)
    down_other = swap_over(partner_rows(down_part), core_line).astype(F32)
    mixed_out = own_rows(hidden_state) + own_rows(down_part).astype(F32) + down_other + vec_all[7]
    token_grad = token_back(core, first_part, first_other, tokens, grad_hidden, vec_all)
    owned_pack, (mixed_out, token_grad) = grid.reduce_direct(near_pack, (mixed_out, token_grad))
    part_vec = owned_pack[:, 4 * width_loc :]
    other_vec = swap_over(part_vec, core_line)
    owned_qkv = jnp.stack(
        [owned_pack[:, part * width_loc : (part + 1) * width_loc] for part in range(3)], axis=1
    )
    owned_out = owned_pack[:, 3 * width_loc : 4 * width_loc]

    new_qkv, new_first_qkv, new_second_qkv = adamw(
        w_qkv, first_qkv, second_qkv, owned_qkv, RATE_MATRIX
    )
    new_out, new_first_out, new_second_out = out_step(w_out, first_out, second_out, owned_out)
    new_up, new_first_up, new_second_up = adamw(w_up, first_up, second_up, owned_up, RATE_MATRIX)
    new_down, new_first_down, new_second_down = adamw(
        w_down, first_down, second_down, owned_down.T, RATE_MATRIX
    )
    new_vectors, new_first_vectors, new_second_vectors = vector_step(
        vectors, first_vectors, second_vectors, part_vec, other_vec
    )
    return (
        mixed_out,
        token_grad,
        new_qkv,
        new_out,
        new_up,
        new_down,
        new_vectors,
        new_first_qkv,
        new_first_out,
        new_first_up,
        new_first_down,
        new_first_vectors,
        new_second_qkv,
        new_second_out,
        new_second_up,
        new_second_down,
        new_second_vectors,
    )


def solution(mesh):
    by_token = P(("row", "col"), None)
    weights = (
        P("row", None, "col"),
        P("col", "row"),
        P("row", "col"),
        P("col", "row"),
        P(None, "row"),
    )
    return jax.shard_map(
        shards,
        mesh=mesh,
        in_specs=(by_token, by_token) + weights * 3,
        out_specs=(by_token, by_token) + weights * 3,
        check_vma=False,
    )
```

```python
import functools
import math

import jax
import jax.numpy as jnp
from jax import lax
from jax.experimental import pallas as pl
from jax.experimental.pallas import tpu as pltpu
from jax.sharding import PartitionSpec as P

HEAD_DIM = 64
LENGTH = 1024
STEP_NUMBER = 10
VEC_ROWS = 12
PAIR = 2 * HEAD_DIM
QUERY_BLOCK = 256
ROW_BLOCK = 512
VEC_LANES = 128
COST_SCALE = 2.3e8


EPS = 1e-05
BETA_ONE = 0.9
BETA_TWO = 0.999
ADAM_EPS = 1e-08
DECAY = 0.1
RATE_MATRIX = 0.04
RATE_VECTOR = 0.3

F32 = jnp.float32
BF16 = jnp.bfloat16


def normalize_rows(values_in):
    row_mean = jnp.mean(values_in, axis=-1, keepdims=True)
    centred = values_in - row_mean
    row_var = jnp.mean(centred * centred, axis=-1, keepdims=True)
    inv_std = lax.rsqrt(row_var + EPS)
    return (centred * inv_std, inv_std)


def norm_back(grad_in, normed, inv_std):
    mean_grad = jnp.mean(grad_in, axis=-1, keepdims=True)
    mean_cross = jnp.mean(grad_in * normed, axis=-1, keepdims=True)
    return inv_std * (grad_in - mean_grad - normed * mean_cross)


def adamw(weight, moment_one, moment_two, gradient, rate):
    first = BETA_ONE * moment_one + (1 - BETA_ONE) * gradient
    second = BETA_TWO * moment_two + (1 - BETA_TWO) * gradient * gradient
    first_hat = first / (1 - BETA_ONE**STEP_NUMBER)
    second_hat = second / (1 - BETA_TWO**STEP_NUMBER)
    updated = weight - rate * (first_hat / (jnp.sqrt(second_hat) + ADAM_EPS) + DECAY * weight)
    return (updated, first, second)


def swap_over(value, line):
    name, offset = line
    pairs = [(index, index ^ offset) for index in range(lax.axis_size(name))]
    return lax.ppermute(value, name, pairs)


def bit_offsets(low, high):
    offsets = []
    while low < high:
        offsets.append(low)
        low *= 2
    return offsets


def flip_order(blocks):
    count = blocks.shape[0]
    row = lax.axis_index("row")
    for offset in bit_offsets(1, count):
        cut = blocks.reshape((-1, 2, offset) + blocks.shape[1:])
        turned = jnp.where((row // offset) % 2 == 1, cut[:, ::-1], cut)
        blocks = turned.reshape(blocks.shape)
    return blocks


class Gathered:
    def __init__(self, arrays, table):
        self.arrays = arrays
        self.table = table
        self.rows = arrays[0].shape[1]
        self.cols = arrays[0].shape[2]
        if self.rows % 16:
            total = []
            for x in range(2):
                found = sorted((offset, array, at) for x_at, array, at, offset in table if x_at == x)
                blocks = jnp.stack([arrays[array][at] for _, array, at in found])
                total.append(flip_order(blocks).reshape(-1, self.cols))
            self.arrays = [jnp.stack(total)]
            self.table = [(0, 0, 0, 0), (1, 0, 1, 0)]
            self.rows = self.arrays[0].shape[1]


class Grid:
    def __init__(self, row_count):
        self.row_count = row_count
        self.far_count = row_count // 2
        self.half = self.far_count // 2
        self.x_line = ("col", 2)
        self.near_line = ("row", 1)

    def far_line(self, index):
        return ("row", 2 * index)

    def gather_far(self, block):
        return [block] + [
            swap_over(block, self.far_line(index)) for index in range(1, self.far_count)
        ]

    def gather_ready(self, blocks):
        return jnp.stack(blocks[: self.half]), jnp.stack(blocks[self.half :])

    def gather_one(self, sent):
        return swap_over(sent[0], self.near_line), swap_over(sent[1], self.x_line)

    def gather_two(self, sent, arrived):
        front = jnp.concatenate([sent[0], arrived[0]], axis=0)
        back = jnp.concatenate([sent[1], arrived[1]], axis=0)
        return front, back

    def gather_three(self, front, back):
        arrays = [front, swap_over(front, self.x_line), back, swap_over(back, self.near_line)]
        table = []
        for index in range(self.half):
            for x in range(2):
                table.append((x, x, index, 2 * index))
                table.append((x, x, index + self.half, 2 * index + 1))
                table.append((x, 2, index + x * self.half, 2 * (index + self.half)))
                table.append((x, 3, index + x * self.half, 2 * (index + self.half) + 1))
        return Gathered(arrays, table)

    def split(self, pair):
        _, all_rows, cols = pair.shape
        blocks = jnp.moveaxis(pair.reshape(2, self.row_count, -1, cols), 1, 0)
        blocks = jnp.moveaxis(flip_order(blocks), 0, 1)
        blocks = blocks.reshape(2, self.far_count, 2, -1, cols)
        last = blocks[1, :, 1]
        return (
            blocks[0, :, 0],
            blocks[1, :, 0],
            blocks[0, :, 1],
            last[: self.half],
            last[self.half :],
        )

    def part_of(self, x, index):
        far, near = index // 2, index % 2
        if not (x and near):
            return x + 2 * near, far
        return (3, far) if far < self.half else (4, far - self.half)

    def part_shapes(self, rows, cols):
        return [(self.far_count, rows, cols)] * 3 + [(self.half, rows, cols)] * 2

    def stage_one(self, parts):
        return swap_over(parts[3], self.x_line), swap_over(parts[4], self.near_line)

    def stage_two(self, parts, by_x, by_near):
        over_x, over_near = parts[1].astype(F32), parts[2].astype(F32)
        half = self.half
        over_x = jnp.concatenate([over_x[:half], over_x[half:] + by_near.astype(F32)], axis=0)
        over_near = jnp.concatenate([over_near[:half] + by_x.astype(F32), over_near[half:]], axis=0)
        return over_x.astype(BF16), over_near.astype(BF16)

    def stage_three(self, parts, sent, hold=None):
        by_x, by_near = swap_over(sent[0], self.x_line), swap_over(sent[1], self.near_line)
        if hold is not None:
            by_x, by_near, _ = lax.optimization_barrier((by_x, by_near, hold))
        return parts[0].astype(F32) + by_x.astype(F32) + by_near.astype(F32)

    def reduce_direct(self, parts, hold):
        low = parts.astype(BF16)
        arrived = [
            swap_over(low[index], self.far_line(index))
            for index in range(1, self.far_count)
        ]
        arrived, hold = lax.optimization_barrier((arrived, hold))
        total = parts[0]
        for part in arrived:
            total = total + part.astype(F32)
        return total, hold


def dot_nt(left, right):
    return lax.dot_general(left, right, (((1,), (1,)), ((), ())), preferred_element_type=F32)


def dot_nn(left, right):
    return lax.dot_general(left, right, (((1,), (0,)), ((), ())), preferred_element_type=F32)


def lane_pick(half):
    lanes = lax.broadcasted_iota(jnp.int32, (1, PAIR), 1)
    return jnp.where((lanes // HEAD_DIM) == half, 1.0, 0.0).astype(BF16)


def causal_block(size):
    key_at = lax.broadcasted_iota(jnp.int32, (size, size), 0)
    query_at = lax.broadcasted_iota(jnp.int32, (size, size), 1)
    return key_at <= query_at


def cost(microseconds):
    return pl.CostEstimate(
        flops=int(microseconds * COST_SCALE), bytes_accessed=1024, transcendentals=0
    )


def attend_kernel(q_ref, k_ref, v_ref, out_ref, turned_ref, lse_ref):
    length = q_ref.shape[0]
    block = min(QUERY_BLOCK, length)
    allowed = causal_block(block)
    values_t = v_ref[...].T
    scaling = jnp.asarray(HEAD_DIM**-0.5, BF16)
    for first in range(0, length, block):
        last = first + block
        query = q_ref[first:last, :] * scaling
        outs = []
        for half in range(2):
            rows = slice(half * HEAD_DIM, (half + 1) * HEAD_DIM)
            query_half = query * lane_pick(half)
            diag = dot_nt(k_ref[first:last, :], query_half)
            diag = jnp.where(allowed, diag, -1e30)
            top = jnp.max(diag, axis=0, keepdims=True)
            if first:
                rest = dot_nt(k_ref[0:first, :], query_half)
                top = jnp.maximum(top, jnp.max(rest, axis=0, keepdims=True))
            diag = jnp.exp(diag - top)
            total = jnp.sum(diag, axis=0, keepdims=True)
            if first:
                rest = jnp.exp(rest - top)
                total = total + jnp.sum(rest, axis=0, keepdims=True)
            inverse = 1.0 / total
            result = dot_nn(values_t[rows, first:last], (diag * inverse).astype(BF16))
            if first:
                result = result + dot_nn(values_t[rows, 0:first], (rest * inverse).astype(BF16))
            outs.append(result)
            lse_ref[0, half : half + 1, first:last] = top + jnp.log(total)
        turned = jnp.concatenate(outs, axis=0)
        out_ref[first:last, :] = turned.T.astype(BF16)
        turned_ref[:, first:last] = turned.astype(BF16)


def pair_lanes(length, part):
    return pl.BlockSpec((length, PAIR), lambda pair: (0, 3 * pair + part))


def attend_forward(qkv, after):
    length = qkv.shape[0]
    pairs = qkv.shape[1] // (3 * PAIR)
    return pl.pallas_call(
        lambda q, k, v, *refs: attend_kernel(q, k, v, *refs[len(after) :]),
        grid=(pairs,),
        in_specs=[pair_lanes(length, part) for part in range(3)]
        + [pl.BlockSpec(memory_space=pl.ANY)] * len(after),
        out_specs=[
            pl.BlockSpec((length, PAIR), lambda pair: (0, pair)),
            pl.BlockSpec((PAIR, length), lambda pair: (pair, 0)),
            pl.BlockSpec((1, 8, length), lambda pair: (pair, 0, 0)),
        ],
        out_shape=[
            jax.ShapeDtypeStruct((length, pairs * PAIR), BF16),
            jax.ShapeDtypeStruct((pairs * PAIR, length), BF16),
            jax.ShapeDtypeStruct((pairs, 8, length), F32),
        ],
        compiler_params=pltpu.CompilerParams(vmem_limit_bytes=40 * 2**20),
        cost_estimate=cost(4.2 * pairs),
        name="attend_forward",
    )(qkv, qkv, qkv, *after)


def attend_back_kernel(q_ref, k_ref, v_ref, go_ref, lse_ref, grad_ref, gk_sum, gv_sum):
    length = q_ref.shape[0]
    block = min(QUERY_BLOCK, length)
    allowed = causal_block(block)
    keys_t = k_ref[...].T
    scaling = jnp.asarray(HEAD_DIM**-0.5, BF16)
    pair = pl.program_id(0)

    def lanes(part):
        return pl.ds(pl.multiple_of((3 * pair + part) * PAIR, PAIR), PAIR)

    gk_sum[...] = jnp.zeros_like(gk_sum)
    gv_sum[...] = jnp.zeros_like(gv_sum)
    for first in range(0, length, block):
        last = first + block
        query = q_ref[first:last, :] * scaling
        grad_out = go_ref[first:last, :]
        outs = []
        for half in range(2):
            rows = slice(half * HEAD_DIM, (half + 1) * HEAD_DIM)
            pick = lane_pick(half)
            query_half = query * pick
            grad_half = grad_out * pick
            lse = lse_ref[0, half : half + 1, first:last]
            spans = [(first, last)] if first == 0 else [(0, first), (first, last)]
            probs, grads, inner = [], [], None
            for low, high in spans:
                scores = dot_nt(k_ref[low:high, :], query_half)
                if low == first:
                    scores = jnp.where(allowed, scores, -1e30)
                prob = jnp.exp(scores - lse)
                grad_prob = dot_nt(v_ref[low:high, :], grad_half)
                part = jnp.sum(prob * grad_prob, axis=0, keepdims=True)
                inner = part if inner is None else inner + part
                probs.append(prob)
                grads.append(grad_prob)
            result = None
            for (low, high), prob, grad_prob in zip(spans, probs, grads):
                grad_score = (prob * (grad_prob - inner)).astype(BF16)
                gk_sum[low:high, :] += dot_nn(grad_score, query_half)
                gv_sum[low:high, :] += dot_nn(prob.astype(BF16), grad_half)
                part = dot_nn(keys_t[rows, low:high], grad_score)
                result = part if result is None else result + part
            outs.append(result)
        grad_query = jnp.concatenate(outs, axis=0).T * (HEAD_DIM**-0.5)
        grad_ref[first:last, lanes(0)] = grad_query.astype(BF16)
    grad_ref[:, lanes(1)] = gk_sum[...].astype(BF16)
    grad_ref[:, lanes(2)] = gv_sum[...].astype(BF16)


def attend_backward(qkv, grad_heads, lse, after):
    length, width = qkv.shape
    pairs = width // (3 * PAIR)
    return pl.pallas_call(
        lambda q, k, v, go, lse_at, *refs: attend_back_kernel(
            q, k, v, go, lse_at, *refs[len(after) :]
        ),
        grid=(pairs,),
        in_specs=[pair_lanes(length, part) for part in range(3)]
        + [
            pl.BlockSpec((length, PAIR), lambda pair: (0, pair)),
            pl.BlockSpec((1, 8, length), lambda pair: (pair, 0, 0)),
        ]
        + [pl.BlockSpec(memory_space=pl.ANY)] * len(after),
        out_specs=pl.BlockSpec((length, width), lambda pair: (0, 0)),
        out_shape=jax.ShapeDtypeStruct((length, width), BF16),
        scratch_shapes=[pltpu.VMEM((length, PAIR), F32), pltpu.VMEM((length, PAIR), F32)],
        compiler_params=pltpu.CompilerParams(vmem_limit_bytes=40 * 2**20),
        cost_estimate=cost(0.5 * pairs),
        name="attend_backward",
    )(qkv, qkv, qkv, grad_heads, lse, *after)


def rows_of(block, width):
    return pl.BlockSpec((block, width), lambda step: (step, 0))


def whole(shape):
    return pl.BlockSpec(shape, lambda *step: (0,) * len(shape))


def shaped(shape, dtype):
    return jax.ShapeDtypeStruct(shape, dtype)


PARAMS = pltpu.CompilerParams(vmem_limit_bytes=48 * 2**20)


ANYWHERE = pl.BlockSpec(memory_space=pl.ANY)


def weight_copies(gathered, refs, held, sems):
    row = lax.axis_index("row")
    copies = ([], [])
    for number, (x, array, at, offset) in enumerate(gathered.table):
        if len(gathered.table) > 2:
            start = pl.multiple_of((row ^ offset) * gathered.rows, 16)
        else:
            start = 0
        target = held.at[x, pl.ds(start, gathered.rows), :]
        copies[x].append(
            pltpu.make_async_copy(refs[array].at[at], target, sems.at[number])
        )
    return copies


def weight_scratch(gathered):
    all_rows = len(gathered.table) // 2 * gathered.rows
    return [
        pltpu.VMEM((2, all_rows, gathered.cols), BF16),
        pltpu.SemaphoreType.DMA((len(gathered.table),)),
    ]


def start_all(copies):
    for copy in copies:
        copy.start()


def wait_all(copies):
    for copy in copies:
        copy.wait()


def store_parts(held, grid, refs, x, source, lanes):
    if len(refs) == 1:
        refs[0][x, :, lanes] = held[:, source]
        return
    row = lax.axis_index("row")
    rows = held.shape[0] // grid.row_count
    for index in range(grid.row_count):
        start = pl.multiple_of((row ^ index) * rows, 16)
        array, place = grid.part_of(x, index)
        refs[array][place, :, lanes] = held[pl.ds(start, rows), source]


def segments(pair, third):
    low, high, found = pair * PAIR, (pair + 1) * PAIR, []
    while low < high:
        x = low // third
        end = min(high, (x + 1) * third)
        found.append((x, low - x * third, end - x * third, low - pair * PAIR))
        low = end
    return found


def parts_out(grid, width, cols):
    rows = width // grid.row_count
    if rows % 16:
        return [(2, width, cols)]
    return grid.part_shapes(rows, cols)


def turn(value):
    return value.T


def pick_half(here, mine_ref, other_ref):
    mine, other = mine_ref[...].astype(F32), other_ref[...].astype(F32)
    return jnp.where(here, mine, other)


def first_norm_kernel(gathered, cols, place_ref, mine_ref, other_ref, after_ref, *refs):
    count = len(gathered.arrays)
    norm_ref, qkv_ref, tokens_ref, full_ref, out_w_ref, vec_ref, held, bias, sems = refs[count:]
    copies = weight_copies(gathered, refs[:count], held, sems)
    third = cols // 3
    step = pl.program_id(0)
    per_half = pl.num_programs(0) // 2

    @pl.when(step == 0)
    def _():
        start_all(copies[0] + copies[1])
        wait_all(copies[0] + copies[1])
        for x in range(2):
            out_w_ref[:, x * third : (x + 1) * third] = held[x, :, held.shape[2] - third :]
        for pair in range(2 * third // PAIR):
            for part in range(3):
                for x, low, high, lane in segments(pair, third):
                    at = (3 * pair + part) * PAIR + lane
                    source = slice(part * third + low, part * third + high)
                    full_ref[:, at : at + high - low] = held[x, :, source]
        first = cols // 128 * 128
        rows = turn(held[0, :, first : first + 128].astype(F32))[cols - first :]
        vec_ref[...] = rows[: vec_ref.shape[0]]
        row_at = lax.broadcasted_iota(jnp.int32, (rows.shape[1], 2 * third), 0)
        lane_at = lax.broadcasted_iota(jnp.int32, (rows.shape[1], 2 * third), 1)
        wanted = jnp.where(
            lane_at < third, place_ref[1] + lane_at, place_ref[2] + lane_at - third
        )
        chosen = jnp.where(row_at == wanted, 1.0, 0.0).astype(BF16)
        picked = dot_nn(vec_ref[...].astype(BF16), chosen)
        bias[...] = jnp.zeros_like(bias)
        for pair in range(2 * third // PAIR):
            lanes = slice(pair * PAIR, (pair + 1) * PAIR)
            at = 3 * pair * PAIR
            bias[0:1, at : at + PAIR] = picked[2:3, lanes]
            bias[0:1, at + 2 * PAIR : at + 3 * PAIR] = picked[3:4, lanes]

    tokens = pick_half(step // per_half == place_ref[0], mine_ref, other_ref)
    tokens_ref[...] = tokens.astype(BF16)
    normed, _ = normalize_rows(tokens)
    first_in = (normed * vec_ref[0:1, :] + vec_ref[1:2, :]).astype(BF16)
    norm_ref[...] = first_in
    qkv_ref[...] = (dot_nn(first_in, full_ref[...]) + bias[0:1, :]).astype(BF16)


def first_norm(place, mine, other, gathered, width_loc, after):
    rows, width = mine.shape
    length = 2 * rows
    cols = 3 * width_loc
    steps = rows // ROW_BLOCK
    half = pl.BlockSpec((ROW_BLOCK, width), lambda step, place_ref: (step % steps, 0))

    def by_row(size):
        return pl.BlockSpec((ROW_BLOCK, size), lambda step, place_ref: (step, 0))

    return pl.pallas_call(
        functools.partial(first_norm_kernel, gathered, cols),
        grid_spec=pltpu.PrefetchScalarGridSpec(
            num_scalar_prefetch=1,
            grid=(2 * steps,),
            in_specs=[half, half, ANYWHERE] + [ANYWHERE] * len(gathered.arrays),
            out_specs=[
                by_row(width),
                by_row(2 * cols),
                by_row(width),
                whole((width, 2 * cols)),
                whole((width, 2 * width_loc)),
                whole((16, width)),
            ],
            scratch_shapes=weight_scratch(gathered)[:1]
            + [pltpu.VMEM((8, 2 * cols), F32)]
            + weight_scratch(gathered)[1:],
        ),
        out_shape=[
            shaped((length, width), BF16),
            shaped((length, 2 * cols), BF16),
            shaped((length, width), BF16),
            shaped((width, 2 * cols), BF16),
            shaped((width, 2 * width_loc), BF16),
            shaped((16, width), F32),
        ],
        compiler_params=PARAMS,
        cost_estimate=cost(8),
        name="first_norm",
    )(place, mine, other, after, *gathered.arrays)


def attended_kernel(
    heads_ref, partner_ref, own_ref, other_ref, tokens_ref, vec_ref, first_ref,
    hidden_ref, norm_ref, norm_turned_ref, first_turned_ref,
):
    attended = dot_nt(heads_ref[...], own_ref[...]) + dot_nt(partner_ref[...], other_ref[...])
    hidden = tokens_ref[...].astype(F32) + attended + vec_ref[4:5, :]
    hidden_ref[...] = hidden
    normed, _ = normalize_rows(hidden)
    second_in = (normed * vec_ref[5:6, :] + vec_ref[6:7, :]).astype(BF16)
    norm_ref[...] = second_in
    norm_turned_ref[...] = turn(second_in)
    first_turned_ref[...] = turn(first_ref[...])


def attended_norm(heads, partner_heads, own_out, partner_out, tokens, vec_all, first_in):
    length, width = tokens.shape
    cols = own_out.shape[1]
    full, part = rows_of(ROW_BLOCK, width), rows_of(ROW_BLOCK, cols)
    turned = pl.BlockSpec((width, ROW_BLOCK), lambda step: (0, step))
    return pl.pallas_call(
        attended_kernel,
        grid=(length // ROW_BLOCK,),
        in_specs=[
            part,
            part,
            whole(own_out.shape),
            whole(partner_out.shape),
            full,
            whole(vec_all.shape),
            full,
        ],
        out_specs=[full, full, turned, turned],
        out_shape=[shaped((length, width), F32), shaped((length, width), BF16)]
        + [shaped((width, length), BF16)] * 2,
        compiler_params=PARAMS,
        cost_estimate=cost(8),
        name="attended_norm",
    )(heads, partner_heads, own_out, partner_out, tokens, vec_all, first_in)


def join_kernel(place_ref, mine_ref, other_ref, joined_ref, turned_ref):
    here = pl.program_id(0) // (pl.num_programs(0) // 2) == place_ref[0]
    joined = pick_half(here, mine_ref, other_ref).astype(BF16)
    joined_ref[...] = joined
    turned_ref[...] = turn(joined)


def join_halves(place, mine, other):
    rows, width = mine.shape
    steps = rows // ROW_BLOCK
    half = pl.BlockSpec((ROW_BLOCK, width), lambda step, place_ref: (step % steps, 0))
    return pl.pallas_call(
        join_kernel,
        grid_spec=pltpu.PrefetchScalarGridSpec(
            num_scalar_prefetch=1,
            grid=(2 * steps,),
            in_specs=[half, half],
            out_specs=[
                pl.BlockSpec((ROW_BLOCK, width), lambda step, place_ref: (step, 0)),
                pl.BlockSpec((width, ROW_BLOCK), lambda step, place_ref: (0, step)),
            ],
        ),
        out_shape=[shaped((2 * rows, width), BF16), shaped((width, 2 * rows), BF16)],
        compiler_params=PARAMS,
        cost_estimate=cost(0.1),
        name="join_halves",
    )(place, mine, other)


def feed_kernel(gathered, place_ref, norm_ref, cot_ref, vec_ref, *refs):
    count = len(gathered.arrays)
    act_ref, gup_ref, bias_sum_ref, out_low_ref, back_low_ref, out_ref, back_ref, held, sems = refs[count:]
    copies = weight_copies(gathered, refs[:count], held, sems)
    step = pl.program_id(0)
    length = norm_ref.shape[0]
    curve, cubic = math.sqrt(2 / math.pi), 0.044715
    cols = held.shape[2] // 2
    x = step
    up_lanes, down_lanes = slice(0, cols), slice(cols, 2 * cols)
    bias = vec_ref[pl.ds(8 + place_ref[3 + x], 1), :]

    @pl.when(step == 0)
    def _():
        start_all(copies[0] + copies[1])
        out_ref[...] = jnp.zeros_like(out_ref)
        back_ref[...] = jnp.zeros_like(back_ref)
        wait_all(copies[0])

    @pl.when(step == 1)
    def _():
        wait_all(copies[1])

    bias_sum = jnp.zeros(bias.shape, F32)
    for first in range(0, length, ROW_BLOCK):
        rows = slice(first, first + ROW_BLOCK)
        up = dot_nn(norm_ref[rows, :], held[x, :, up_lanes]) + bias
        cubed = up * up * (curve * cubic)
        tanh = jnp.tanh(up * (curve + cubed))
        halved = 0.5 * up
        act_ref[rows, :] = (halved + halved * tanh).astype(BF16)
        slope = 0.5 + 0.5 * tanh + halved * (1.0 - tanh * tanh) * (curve + 3.0 * cubed)
        grad_up = (dot_nn(cot_ref[rows, :], held[x, :, down_lanes]) * slope).astype(BF16)
        gup_ref[rows, :] = grad_up
        bias_sum = bias_sum + jnp.sum(grad_up.astype(F32), axis=0, keepdims=True)
    back_ref[...] += dot_nt(gup_ref[...], held[x, :, up_lanes])
    out_ref[...] += dot_nt(act_ref[...], held[x, :, down_lanes])
    bias_sum_ref[...] = bias_sum

    @pl.when(step == pl.num_programs(0) - 1)
    def _():
        back_low_ref[...] = back_ref[...].astype(BF16)
        out_low_ref[...] = out_ref[...].astype(BF16)


def feed(place, norm, cot, vec_all, gathered):
    length, width = norm.shape
    block = gathered.cols // 2
    hidden = 2 * block
    tall = pl.BlockSpec((length, block), lambda step, place_ref: (0, step))
    flat = pl.BlockSpec((1, block), lambda step, place_ref: (0, step))
    full = whole((length, width))
    return pl.pallas_call(
        functools.partial(feed_kernel, gathered),
        grid_spec=pltpu.PrefetchScalarGridSpec(
            num_scalar_prefetch=1,
            grid=(2,),
            in_specs=[full, full, whole(vec_all.shape)] + [ANYWHERE] * len(gathered.arrays),
            out_specs=[tall, tall, flat, full, full],
            scratch_shapes=[pltpu.VMEM((length, width), F32)] * 2 + weight_scratch(gathered),
        ),
        out_shape=[
            shaped((length, hidden), BF16),
            shaped((length, hidden), BF16),
            shaped((1, hidden), F32),
            shaped((length, width), BF16),
            shaped((length, width), BF16),
        ],
        compiler_params=PARAMS,
        cost_estimate=cost(18),
        name="feed",
    )(place, norm, cot, vec_all, *gathered.arrays)


def feed_grads_kernel(grid, cot_ref, norm_ref, act_ref, gup_ref, *refs):
    kind, x_at = pl.program_id(0), pl.program_id(1)
    outs, held = refs[:-1], refs[-1]
    size = held.shape[1]

    @pl.when(kind == 0)
    def _():
        held[...] = dot_nn(cot_ref[...], act_ref[...]).astype(BF16)

    @pl.when(kind == 1)
    def _():
        held[...] = dot_nn(norm_ref[...], gup_ref[...]).astype(BF16)

    for index in range(2):
        for x in range(2):

            @pl.when((kind == index) & (x_at == x))
            def _():
                lanes = slice((1 - index) * size, (2 - index) * size)
                store_parts(held, grid, outs, x, slice(None), lanes)


def feed_grads(cot_turned, norm_turned, act, grad_up, grid):
    width, length = cot_turned.shape
    hidden = act.shape[1]
    block = hidden // 2
    shapes = parts_out(grid, width, hidden)
    parts = pl.pallas_call(
        functools.partial(feed_grads_kernel, grid),
        grid=(2, 2),
        in_specs=[
            whole((width, length)),
            whole((width, length)),
            pl.BlockSpec((length, block), lambda kind, x: (0, jnp.where(kind == 0, x, 1))),
            pl.BlockSpec((length, block), lambda kind, x: (0, jnp.where(kind == 1, x, 0))),
        ],
        out_specs=[whole(shape) for shape in shapes],
        out_shape=[shaped(shape, BF16) for shape in shapes],
        scratch_shapes=[pltpu.VMEM((width, block), BF16)],
        compiler_params=PARAMS,
        cost_estimate=cost(10),
        name="feed_grads",
    )(cot_turned, norm_turned, act, grad_up)
    return parts if len(parts) == 5 else grid.split(parts[0])


def second_back_kernel(
    part_ref, other_ref, hidden_ref, cot_ref, vec_ref, out_w_ref, turned_ref,
    grad_ref, heads_ref, sum_ref, out_grad_ref, total,
):
    step = pl.program_id(0)
    normed, inv_std = normalize_rows(hidden_ref[...])
    part = part_ref[...].astype(F32)
    cot = cot_ref[...].astype(F32)
    grad_second = part + other_ref[...].astype(F32)
    grad = cot + norm_back(grad_second * vec_ref[5:6, :], normed, inv_std)
    grad_ref[...] = grad
    low = grad.astype(BF16)
    heads_ref[...] = dot_nn(low, out_w_ref[...]).astype(BF16)

    @pl.when(step == 0)
    def _():
        sum_ref[...] = jnp.zeros_like(sum_ref)
        total[...] = jnp.zeros_like(total)

    total[...] += dot_nn(turned_ref[...], low)
    for row, value in enumerate((grad, part * normed, part, cot)):
        sum_ref[row : row + 1, :] += jnp.sum(value, axis=0, keepdims=True)

    @pl.when(step == pl.num_programs(0) - 1)
    def _():
        out_grad_ref[...] = total[...].T.astype(BF16)


def second_back(part, other, hidden, cot, vec_all, out_w, heads_turned):
    length, width = part.shape
    cols = out_w.shape[1]
    full = rows_of(ROW_BLOCK, width)
    return pl.pallas_call(
        second_back_kernel,
        grid=(length // ROW_BLOCK,),
        in_specs=[full, full, full, full, whole(vec_all.shape), whole(out_w.shape)]
        + [pl.BlockSpec((cols, ROW_BLOCK), lambda step: (0, step))],
        out_specs=[full, rows_of(ROW_BLOCK, cols), whole((8, width)), whole((width, cols))],
        out_shape=[
            shaped((length, width), F32),
            shaped((length, cols), BF16),
            shaped((8, width), F32),
            shaped((width, cols), BF16),
        ],
        scratch_shapes=[pltpu.VMEM((cols, width), F32)],
        compiler_params=PARAMS,
        cost_estimate=cost(8.6),
        name="second_back",
    )(part, other, hidden, cot, vec_all, out_w, heads_turned)


def qkv_grads_kernel(grid, norm_ref, grad_ref, out_grad_ref, vec_ref, *refs):
    step = pl.program_id(0)
    outs, held = refs[:-1], refs[-1]
    third = held.shape[1] // 2
    pairs = 2 * third // PAIR
    for index in range(pairs + 1):

        @pl.when(step == index)
        def _():
            if index == pairs:
                held[...] = out_grad_ref[...]
                for x in range(2):
                    source = slice(x * third, (x + 1) * third)
                    store_parts(held, grid, outs, x, source, slice(3 * third, 4 * third))
                rows = vec_ref[...]
                blank = jnp.zeros((VEC_LANES - rows.shape[0], rows.shape[1]), F32)
                held[:, :VEC_LANES] = jnp.concatenate([rows, blank], axis=0).T.astype(BF16)
                for x in range(2):
                    lanes = slice(4 * third, 4 * third + VEC_LANES)
                    store_parts(held, grid, outs, x, slice(0, VEC_LANES), lanes)
                return
            held[...] = dot_nn(norm_ref[...], grad_ref[...]).astype(BF16)
            for part in range(3):
                for x, low, high, lane in segments(index, third):
                    at = part * PAIR + lane
                    lanes = slice(part * third + low, part * third + high)
                    store_parts(held, grid, outs, x, slice(at, at + high - low), lanes)


def qkv_grads(norm_turned, grads, out_grad, grid, grad_vec):
    width, length = norm_turned.shape
    cols = out_grad.shape[1]
    pairs = cols // PAIR
    shapes = parts_out(grid, width, 2 * cols + VEC_LANES)
    parts = pl.pallas_call(
        functools.partial(qkv_grads_kernel, grid),
        grid=(pairs + 1,),
        in_specs=[
            whole((width, length)),
            pl.BlockSpec((length, cols), lambda step: (0, jnp.minimum(step, pairs - 1))),
            whole((width, cols)),
            whole(grad_vec.shape),
        ],
        out_specs=[whole(shape) for shape in shapes],
        out_shape=[shaped(shape, BF16) for shape in shapes],
        scratch_shapes=[pltpu.VMEM((width, cols), BF16)],
        compiler_params=PARAMS,
        cost_estimate=cost(0.3),
        name="qkv_grads",
    )(norm_turned, grads, out_grad, grad_vec)
    return parts if len(parts) == 5 else grid.split(parts[0])


def first_back_kernel(
    place_ref, grad_ref, weight_ref, tokens_ref, second_ref, up_ref,
    part_ref, vec_ref, bias,
):
    grads = grad_ref[...]
    part = dot_nt(grads, weight_ref[...])
    part_ref[...] = part.astype(BF16)
    normed, _ = normalize_rows(tokens_ref[...].astype(F32))

    @pl.when(pl.program_id(0) == 0)
    def _():
        vec_ref[...] = jnp.zeros_like(vec_ref)
        bias[...] = jnp.zeros_like(bias)

    for row, value in enumerate((part * normed, part)):
        vec_ref[row : row + 1, :] += jnp.sum(value, axis=0, keepdims=True)
    bias[0:1, :] += jnp.sum(grads.astype(F32), axis=0, keepdims=True)

    @pl.when(pl.program_id(0) == pl.num_programs(0) - 1)
    def _():
        width = vec_ref.shape[1]
        pairs = bias.shape[1] // (3 * PAIR)
        third = pairs * PAIR // 2
        for row, part_at in ((2, 0), (3, 2)):
            lanes = [
                bias[:, (3 * pair + part_at) * PAIR : (3 * pair + part_at + 1) * PAIR]
                for pair in range(pairs)
            ]
            joined = jnp.concatenate(lanes, axis=1)
            blank = jnp.zeros((joined.shape[0], width - third), F32)
            for x in range(2):
                block = jnp.concatenate([joined[:, x * third : (x + 1) * third], blank], axis=1)
                vec_ref[row : row + 1, :] += pltpu.roll(block, place_ref[1 + x], 1)[0:1]
        vec_ref[4:5, :] = 0.5 * second_ref[0:1, :]
        vec_ref[5:7, :] = second_ref[1:3, :]
        vec_ref[7:8, :] = 0.5 * second_ref[3:4, :]
        row_at = lax.broadcasted_iota(jnp.int32, (8, width), 0)
        vec_ref[8:16, :] = jnp.where(row_at == place_ref[3], up_ref[0:1, :width], 0.0) + jnp.where(
            row_at == place_ref[4], up_ref[0:1, width:], 0.0
        )


def first_back(place, grads, weight, tokens, second_sums, up_sums):
    length, width = tokens.shape
    cols = weight.shape[1]

    def by_row(size):
        return pl.BlockSpec((ROW_BLOCK, size), lambda step, place_ref: (step, 0))

    return pl.pallas_call(
        first_back_kernel,
        grid_spec=pltpu.PrefetchScalarGridSpec(
            num_scalar_prefetch=1,
            grid=(length // ROW_BLOCK,),
            in_specs=[
                by_row(cols),
                whole(weight.shape),
                by_row(width),
                whole(second_sums.shape),
                whole(up_sums.shape),
            ],
            out_specs=[by_row(width), whole((16, width))],
            scratch_shapes=[pltpu.VMEM((8, cols), F32)],
        ),
        out_shape=[shaped((length, width), BF16), shaped((16, width), F32)],
        compiler_params=PARAMS,
        cost_estimate=cost(0.3),
        name="first_back",
    )(place, grads, weight, tokens, second_sums, up_sums)


def token_back_kernel(core_ref, part_ref, other_ref, tokens_ref, grad_ref, vec_ref, out_ref):
    normed, inv_std = normalize_rows(tokens_ref[...].astype(F32))
    grad_first = part_ref[...].astype(F32) + other_ref[...].astype(F32)
    out_ref[...] = grad_ref[...] + norm_back(grad_first * vec_ref[0:1, :], normed, inv_std)


def token_back(core, part, other, tokens, grad_hidden, vec_all):
    rows, width = tokens.shape
    steps = rows // ROW_BLOCK
    own = pl.BlockSpec((ROW_BLOCK, width), lambda step, core_ref: (core_ref[0] * steps + step, 0))
    here = pl.BlockSpec((ROW_BLOCK, width), lambda step, core_ref: (step, 0))
    return pl.pallas_call(
        token_back_kernel,
        grid_spec=pltpu.PrefetchScalarGridSpec(
            num_scalar_prefetch=1,
            grid=(steps,),
            in_specs=[own, here, here, own, whole(vec_all.shape)],
            out_specs=here,
        ),
        out_shape=shaped((rows, width), F32),
        compiler_params=PARAMS,
        cost_estimate=cost(3.2),
        name="token_back",
    )(core.reshape(1), part, other, tokens, grad_hidden, vec_all)


def out_step_kernel(grad_ref, weight_ref, first_ref, second_ref, new_ref, new_first_ref, new_second_ref):
    grads = grad_ref[...].T
    results = adamw(weight_ref[...], first_ref[...], second_ref[...], grads, RATE_MATRIX)
    new_ref[...], new_first_ref[...], new_second_ref[...] = results


def out_step(weight, first, second, grads):
    return pl.pallas_call(
        out_step_kernel,
        out_shape=[shaped(weight.shape, F32)] * 3,
        compiler_params=PARAMS,
        name="out_step",
    )(grads, weight, first, second)


def vector_step_kernel(
    part_ref, other_ref, weight_ref, first_ref, second_ref, new_ref, new_first_ref, new_second_ref
):
    grads = (part_ref[...] + other_ref[...]).T[: weight_ref.shape[0]]
    results = adamw(weight_ref[...], first_ref[...], second_ref[...], grads, RATE_VECTOR)
    new_ref[...], new_first_ref[...], new_second_ref[...] = results


def vector_step(weight, first, second, part, other):
    return pl.pallas_call(
        vector_step_kernel,
        out_shape=[shaped(weight.shape, F32)] * 3,
        compiler_params=PARAMS,
        name="vector_step",
    )(part, other, weight, first, second)


def shards(
    tokens,
    cotangent,
    w_qkv,
    w_out,
    w_up,
    w_down,
    vectors,
    first_qkv,
    first_out,
    first_up,
    first_down,
    first_vectors,
    second_qkv,
    second_out,
    second_up,
    second_down,
    second_vectors,
):
    col_index = lax.axis_index("col")
    grid = Grid(lax.axis_size("row"))
    core_line = ("col", 1)
    core = col_index % 2
    other_col = col_index ^ 2
    rows_loc, width = tokens.shape
    width_loc = w_qkv.shape[2]
    hidden_loc = w_up.shape[1]
    shard_rows = w_up.shape[0]

    pad = -(3 * width_loc + VEC_ROWS) % 128
    pack_qkv = jnp.concatenate(
        [w_qkv[:, part].astype(BF16) for part in range(3)]
        + [vectors.T.astype(BF16), jnp.zeros((shard_rows, pad), BF16), w_out.T.astype(BF16)],
        axis=1,
    )
    pack_feed = jnp.concatenate([w_up.astype(BF16), w_down.T.astype(BF16)], axis=1)

    def own_rows(value):
        return lax.dynamic_slice_in_dim(value, core * rows_loc, rows_loc, 0)

    def partner_rows(value):
        return lax.dynamic_slice_in_dim(value, (1 - core) * rows_loc, rows_loc, 0)

    place = jnp.stack(
        [core, col_index * width_loc, other_col * width_loc, col_index, other_col]
    ).astype(jnp.int32)

    far_qkv = grid.gather_far(pack_qkv)
    partner = [swap_over(tokens, core_line), swap_over(cotangent, core_line)]
    far_qkv, partner = lax.optimization_barrier((far_qkv, partner))
    sent_qkv = grid.gather_ready(far_qkv)
    pack_feed, _ = lax.optimization_barrier((pack_feed, sent_qkv))
    arrived_qkv = grid.gather_one(sent_qkv)
    far_feed = grid.gather_far(pack_feed)
    two_qkv = grid.gather_two(sent_qkv, arrived_qkv)
    near_qkv = grid.gather_three(*two_qkv)
    all_cot, cot_turned = join_halves(place, cotangent, partner[1])
    far_feed, _ = lax.optimization_barrier((far_feed, (two_qkv, all_cot)))
    sent_feed = grid.gather_ready(far_feed)
    arrived_feed = grid.gather_one(sent_feed)

    first_in, qkv, all_tokens, full_qkv, full_out, vec_all = first_norm(
        place, tokens, partner[0], near_qkv, width_loc, all_cot
    )
    partner_out = swap_over(full_out, core_line)
    arrived_feed, _ = lax.optimization_barrier((arrived_feed, qkv))
    two_feed = grid.gather_two(sent_feed, arrived_feed)
    near_feed = grid.gather_three(*two_feed)
    heads_low, heads_turned, lse = attend_forward(qkv, two_feed)
    partner_heads = swap_over(heads_low, core_line)
    hidden_state, second_in, second_turned, first_turned = attended_norm(
        heads_low, partner_heads, full_out, partner_out, all_tokens, vec_all, first_in
    )
    activated, grad_upper, grad_bias_up, down_part, second_part = feed(
        place, second_in, all_cot, vec_all, near_feed
    )

    second_other = swap_over(second_part, core_line)
    parts_feed = feed_grads(cot_turned, second_turned, activated, grad_upper, grid)
    arrived_feed = grid.stage_one(parts_feed)
    grad_hidden, grad_heads, second_sums, out_grad = second_back(
        second_part, second_other, hidden_state, all_cot, vec_all, full_out, heads_turned
    )
    arrived_feed, _ = lax.optimization_barrier((arrived_feed, grad_heads))
    sent_feed = grid.stage_two(parts_feed, *arrived_feed)
    grads_qkv = attend_backward(qkv, grad_heads, lse, sent_feed)
    first_part, grad_vec = first_back(
        place, grads_qkv, full_qkv, all_tokens, second_sums, grad_bias_up
    )
    parts_qkv = qkv_grads(first_turned, grads_qkv, out_grad, grid, grad_vec)
    far_feed_grads = grid.stage_three(parts_feed, sent_feed, parts_qkv[0])
    far_sent = far_feed_grads[1:].astype(BF16)
    last_parts, far_sent = lax.optimization_barrier((parts_qkv[3:], far_sent))
    parts_qkv = [*parts_qkv[:3], *last_parts]
    arrived_pack = grid.stage_one(parts_qkv)
    owned_feed = far_feed_grads[0]
    for index in range(1, grid.far_count):
        owned_feed = owned_feed + swap_over(far_sent[index - 1], grid.far_line(index)).astype(F32)
    owned_up, owned_down = owned_feed[:, :hidden_loc], owned_feed[:, hidden_loc:]

    sent_pack = grid.stage_two(parts_qkv, *arrived_pack)
    first_other = swap_over(partner_rows(first_part), core_line)
    down_other = swap_over(partner_rows(down_part), core_line)
    sent_pack, first_other, down_other = lax.optimization_barrier(
        (sent_pack, first_other, down_other)
    )
    near_pack = grid.stage_three(parts_qkv, sent_pack)
    down_other = down_other.astype(F32)
    mixed_out = own_rows(hidden_state) + own_rows(down_part).astype(F32) + down_other + vec_all[7]
    token_grad = token_back(core, first_part, first_other, tokens, grad_hidden, vec_all)
    owned_pack, (mixed_out, token_grad) = grid.reduce_direct(near_pack, (mixed_out, token_grad))
    part_vec = owned_pack[:, 4 * width_loc :]
    other_vec = swap_over(part_vec, core_line)
    owned_qkv = jnp.stack(
        [owned_pack[:, part * width_loc : (part + 1) * width_loc] for part in range(3)], axis=1
    )
    owned_out = owned_pack[:, 3 * width_loc : 4 * width_loc]

    new_qkv, new_first_qkv, new_second_qkv = adamw(
        w_qkv, first_qkv, second_qkv, owned_qkv, RATE_MATRIX
    )
    new_out, new_first_out, new_second_out = out_step(w_out, first_out, second_out, owned_out)
    new_up, new_first_up, new_second_up = adamw(w_up, first_up, second_up, owned_up, RATE_MATRIX)
    new_down, new_first_down, new_second_down = adamw(
        w_down, first_down, second_down, owned_down.T, RATE_MATRIX
    )
    new_vectors, new_first_vectors, new_second_vectors = vector_step(
        vectors, first_vectors, second_vectors, part_vec, other_vec
    )
    return (
        mixed_out,
        token_grad,
        new_qkv,
        new_out,
        new_up,
        new_down,
        new_vectors,
        new_first_qkv,
        new_first_out,
        new_first_up,
        new_first_down,
        new_first_vectors,
        new_second_qkv,
        new_second_out,
        new_second_up,
        new_second_down,
        new_second_vectors,
    )


def solution(mesh):
    by_token = P(("row", "col"), None)
    weights = (
        P("row", None, "col"),
        P("col", "row"),
        P("row", "col"),
        P("col", "row"),
        P(None, "row"),
    )
    return jax.shard_map(
        shards,
        mesh=mesh,
        in_specs=(by_token, by_token) + weights * 3,
        out_specs=(by_token, by_token) + weights * 3,
        check_vma=False,
    )
```

```python
import functools
import math

import jax
import jax.numpy as jnp
from jax import lax
from jax.experimental import pallas as pl
from jax.experimental.pallas import tpu as pltpu
from jax.sharding import PartitionSpec as P

HEAD_DIM = 64
LENGTH = 1024
STEP_NUMBER = 10
VEC_ROWS = 12
PAIR = 2 * HEAD_DIM
QUERY_BLOCK = 256
ROW_BLOCK = 512
VEC_LANES = 128
COST_SCALE = 2.3e8


EPS = 1e-05
BETA_ONE = 0.9
BETA_TWO = 0.999
ADAM_EPS = 1e-08
DECAY = 0.1
RATE_MATRIX = 0.04
RATE_VECTOR = 0.3

F32 = jnp.float32
BF16 = jnp.bfloat16


def normalize_rows(values_in):
    row_mean = jnp.mean(values_in, axis=-1, keepdims=True)
    centred = values_in - row_mean
    row_var = jnp.mean(centred * centred, axis=-1, keepdims=True)
    inv_std = lax.rsqrt(row_var + EPS)
    return (centred * inv_std, inv_std)


def norm_back(grad_in, normed, inv_std):
    mean_grad = jnp.mean(grad_in, axis=-1, keepdims=True)
    mean_cross = jnp.mean(grad_in * normed, axis=-1, keepdims=True)
    return inv_std * (grad_in - mean_grad - normed * mean_cross)


def adamw(weight, moment_one, moment_two, gradient, rate):
    first = BETA_ONE * moment_one + (1 - BETA_ONE) * gradient
    second = BETA_TWO * moment_two + (1 - BETA_TWO) * gradient * gradient
    first_hat = first / (1 - BETA_ONE**STEP_NUMBER)
    second_hat = second / (1 - BETA_TWO**STEP_NUMBER)
    updated = weight - rate * (first_hat / (jnp.sqrt(second_hat) + ADAM_EPS) + DECAY * weight)
    return (updated, first, second)


def swap_over(value, line):
    name, offset = line
    pairs = [(index, index ^ offset) for index in range(lax.axis_size(name))]
    return lax.ppermute(value, name, pairs)


def bit_offsets(low, high):
    offsets = []
    while low < high:
        offsets.append(low)
        low *= 2
    return offsets


def flip_order(blocks):
    count = blocks.shape[0]
    row = lax.axis_index("row")
    for offset in bit_offsets(1, count):
        cut = blocks.reshape((-1, 2, offset) + blocks.shape[1:])
        turned = jnp.where((row // offset) % 2 == 1, cut[:, ::-1], cut)
        blocks = turned.reshape(blocks.shape)
    return blocks


class Gathered:
    def __init__(self, arrays, table):
        self.arrays = arrays
        self.table = table
        self.rows = arrays[0].shape[1]
        self.cols = arrays[0].shape[2]
        if self.rows % 16:
            total = []
            for x in range(2):
                found = sorted((offset, array, at) for x_at, array, at, offset in table if x_at == x)
                blocks = jnp.stack([arrays[array][at] for _, array, at in found])
                total.append(flip_order(blocks).reshape(-1, self.cols))
            self.arrays = [jnp.stack(total)]
            self.table = [(0, 0, 0, 0), (1, 0, 1, 0)]
            self.rows = self.arrays[0].shape[1]


class Grid:
    def __init__(self, row_count):
        self.row_count = row_count
        self.far_count = row_count // 2
        self.half = self.far_count // 2
        self.x_line = ("col", 2)
        self.near_line = ("row", 1)

    def far_line(self, index):
        return ("row", 2 * index)

    def gather_far(self, block):
        return [block] + [
            swap_over(block, self.far_line(index)) for index in range(1, self.far_count)
        ]

    def gather_ready(self, blocks):
        return jnp.stack(blocks[: self.half]), jnp.stack(blocks[self.half :])

    def gather_one(self, sent):
        return swap_over(sent[0], self.near_line), swap_over(sent[1], self.x_line)

    def gather_two(self, sent, arrived):
        front = jnp.concatenate([sent[0], arrived[0]], axis=0)
        back = jnp.concatenate([sent[1], arrived[1]], axis=0)
        return front, back

    def gather_three(self, front, back):
        arrays = [front, swap_over(front, self.x_line), back, swap_over(back, self.near_line)]
        table = []
        for index in range(self.half):
            for x in range(2):
                table.append((x, x, index, 2 * index))
                table.append((x, x, index + self.half, 2 * index + 1))
                table.append((x, 2, index + x * self.half, 2 * (index + self.half)))
                table.append((x, 3, index + x * self.half, 2 * (index + self.half) + 1))
        return Gathered(arrays, table)

    def split(self, pair):
        _, all_rows, cols = pair.shape
        blocks = jnp.moveaxis(pair.reshape(2, self.row_count, -1, cols), 1, 0)
        blocks = jnp.moveaxis(flip_order(blocks), 0, 1)
        blocks = blocks.reshape(2, self.far_count, 2, -1, cols)
        last = blocks[1, :, 1]
        return (
            blocks[0, :, 0],
            blocks[1, :, 0],
            blocks[0, :, 1],
            last[: self.half],
            last[self.half :],
        )

    def part_of(self, x, index):
        far, near = index // 2, index % 2
        if not (x and near):
            return x + 2 * near, far
        return (3, far) if far < self.half else (4, far - self.half)

    def part_shapes(self, rows, cols):
        return [(self.far_count, rows, cols)] * 3 + [(self.half, rows, cols)] * 2

    def stage_one(self, parts):
        return swap_over(parts[3], self.x_line), swap_over(parts[4], self.near_line)

    def stage_two(self, parts, by_x, by_near):
        half = self.half

        def added(blocks, first, other):
            kept = lax.slice_in_dim(blocks, first, first + half, axis=0)
            total = (kept.astype(F32) + other.astype(F32)).astype(BF16)
            return lax.dynamic_update_slice_in_dim(blocks, total, first, 0)

        return added(parts[1], half, by_near), added(parts[2], 0, by_x)

    def stage_three(self, parts, sent, hold=None):
        by_x, by_near = swap_over(sent[0], self.x_line), swap_over(sent[1], self.near_line)
        if hold is not None:
            by_x, by_near, _ = lax.optimization_barrier((by_x, by_near, hold))
        return parts[0].astype(F32) + by_x.astype(F32) + by_near.astype(F32)

    def chain_send(self, parts):
        return parts[0::2], parts[1::2].astype(BF16)

    def reduce_chain(self, kept, sent):
        index = 1
        parts = kept + swap_over(sent, self.far_line(index)).astype(F32)
        while parts.shape[0] > 1:
            index *= 2
            kept, sent = self.chain_send(parts)
            parts = kept + swap_over(sent, self.far_line(index)).astype(F32)
        return parts[0]

    def reduce_direct(self, parts, hold):
        low = parts.astype(BF16)
        arrived = [
            swap_over(low[index], self.far_line(index))
            for index in range(1, self.far_count)
        ]
        arrived, hold = lax.optimization_barrier((arrived, hold))
        total = parts[0]
        for part in arrived:
            total = total + part.astype(F32)
        return total, hold


def dot_nt(left, right):
    return lax.dot_general(left, right, (((1,), (1,)), ((), ())), preferred_element_type=F32)


def dot_nn(left, right):
    return lax.dot_general(left, right, (((1,), (0,)), ((), ())), preferred_element_type=F32)


def lane_pick(half):
    lanes = lax.broadcasted_iota(jnp.int32, (1, PAIR), 1)
    return jnp.where((lanes // HEAD_DIM) == half, 1.0, 0.0).astype(BF16)


def causal_block(size):
    key_at = lax.broadcasted_iota(jnp.int32, (size, size), 0)
    query_at = lax.broadcasted_iota(jnp.int32, (size, size), 1)
    return key_at <= query_at


def cost(microseconds):
    return pl.CostEstimate(
        flops=int(microseconds * COST_SCALE), bytes_accessed=1024, transcendentals=0
    )


def attend_kernel(q_ref, k_ref, v_ref, out_ref, turned_ref, lse_ref):
    length = q_ref.shape[0]
    block = min(QUERY_BLOCK, length)
    allowed = causal_block(block)
    values_t = v_ref[...].T
    scaling = jnp.asarray(HEAD_DIM**-0.5, BF16)
    for first in range(0, length, block):
        last = first + block
        query = q_ref[first:last, :] * scaling
        outs = []
        for half in range(2):
            rows = slice(half * HEAD_DIM, (half + 1) * HEAD_DIM)
            query_half = query * lane_pick(half)
            diag = dot_nt(k_ref[first:last, :], query_half)
            diag = jnp.where(allowed, diag, -1e30)
            top = jnp.max(diag, axis=0, keepdims=True)
            if first:
                rest = dot_nt(k_ref[0:first, :], query_half)
                top = jnp.maximum(top, jnp.max(rest, axis=0, keepdims=True))
            diag = jnp.exp(diag - top)
            total = jnp.sum(diag, axis=0, keepdims=True)
            if first:
                rest = jnp.exp(rest - top)
                total = total + jnp.sum(rest, axis=0, keepdims=True)
            inverse = 1.0 / total
            result = dot_nn(values_t[rows, first:last], (diag * inverse).astype(BF16))
            if first:
                result = result + dot_nn(values_t[rows, 0:first], (rest * inverse).astype(BF16))
            outs.append(result)
            lse_ref[0, half : half + 1, first:last] = top + jnp.log(total)
        turned = jnp.concatenate(outs, axis=0)
        out_ref[first:last, :] = turned.T.astype(BF16)
        turned_ref[:, first:last] = turned.astype(BF16)


def pair_lanes(length, first, part):
    return pl.BlockSpec((length, PAIR), lambda pair: (0, 3 * (first + pair) + part))


def attend_forward(qkv, after):
    length = qkv.shape[0]
    pairs = qkv.shape[1] // (3 * PAIR)
    return pl.pallas_call(
        lambda q, k, v, *refs: attend_kernel(q, k, v, *refs[len(after) :]),
        grid=(pairs,),
        in_specs=[pair_lanes(length, 0, part) for part in range(3)]
        + [pl.BlockSpec(memory_space=pl.ANY)] * len(after),
        out_specs=[
            pl.BlockSpec((length, PAIR), lambda pair: (0, pair)),
            pl.BlockSpec((PAIR, length), lambda pair: (pair, 0)),
            pl.BlockSpec((1, 8, length), lambda pair: (pair, 0, 0)),
        ],
        out_shape=[
            jax.ShapeDtypeStruct((length, pairs * PAIR), BF16),
            jax.ShapeDtypeStruct((pairs * PAIR, length), BF16),
            jax.ShapeDtypeStruct((pairs, 8, length), F32),
        ],
        compiler_params=pltpu.CompilerParams(vmem_limit_bytes=40 * 2**20),
        cost_estimate=cost(4.2 * pairs),
        name="attend_forward",
    )(qkv, qkv, qkv, *after)


def attend_back_kernel(q_ref, k_ref, v_ref, go_ref, lse_ref, grad_ref, gk_sum, gv_sum):
    length = q_ref.shape[0]
    block = min(QUERY_BLOCK, length)
    allowed = causal_block(block)
    keys_t = k_ref[...].T
    scaling = jnp.asarray(HEAD_DIM**-0.5, BF16)
    pair = pl.program_id(0)

    def lanes(part):
        return pl.ds(pl.multiple_of((3 * pair + part) * PAIR, PAIR), PAIR)

    gk_sum[...] = jnp.zeros_like(gk_sum)
    gv_sum[...] = jnp.zeros_like(gv_sum)
    for first in range(0, length, block):
        last = first + block
        query = q_ref[first:last, :] * scaling
        grad_out = go_ref[first:last, :]
        outs = []
        for half in range(2):
            rows = slice(half * HEAD_DIM, (half + 1) * HEAD_DIM)
            pick = lane_pick(half)
            query_half = query * pick
            grad_half = grad_out * pick
            lse = lse_ref[0, half : half + 1, first:last]
            spans = [(first, last)] if first == 0 else [(0, first), (first, last)]
            probs, grads, inner = [], [], None
            for low, high in spans:
                scores = dot_nt(k_ref[low:high, :], query_half)
                if low == first:
                    scores = jnp.where(allowed, scores, -1e30)
                prob = jnp.exp(scores - lse)
                grad_prob = dot_nt(v_ref[low:high, :], grad_half)
                part = jnp.sum(prob * grad_prob, axis=0, keepdims=True)
                inner = part if inner is None else inner + part
                probs.append(prob)
                grads.append(grad_prob)
            result = None
            for (low, high), prob, grad_prob in zip(spans, probs, grads):
                grad_score = (prob * (grad_prob - inner)).astype(BF16)
                gk_sum[low:high, :] += dot_nn(grad_score, query_half)
                gv_sum[low:high, :] += dot_nn(prob.astype(BF16), grad_half)
                part = dot_nn(keys_t[rows, low:high], grad_score)
                result = part if result is None else result + part
            outs.append(result)
        grad_query = jnp.concatenate(outs, axis=0).T * (HEAD_DIM**-0.5)
        grad_ref[first:last, lanes(0)] = grad_query.astype(BF16)
    grad_ref[:, lanes(1)] = gk_sum[...].astype(BF16)
    grad_ref[:, lanes(2)] = gv_sum[...].astype(BF16)


def attend_backward(qkv, grad_heads, lse, first, pairs, after):
    length = qkv.shape[0]
    width = 3 * PAIR * pairs
    return pl.pallas_call(
        lambda q, k, v, go, lse_at, *refs: attend_back_kernel(
            q, k, v, go, lse_at, *refs[len(after) :]
        ),
        grid=(pairs,),
        in_specs=[pair_lanes(length, first, part) for part in range(3)]
        + [
            pl.BlockSpec((length, PAIR), lambda pair: (0, first + pair)),
            pl.BlockSpec((1, 8, length), lambda pair: (first + pair, 0, 0)),
        ]
        + [pl.BlockSpec(memory_space=pl.ANY)] * len(after),
        out_specs=pl.BlockSpec((length, width), lambda pair: (0, 0)),
        out_shape=jax.ShapeDtypeStruct((length, width), BF16),
        scratch_shapes=[pltpu.VMEM((length, PAIR), F32), pltpu.VMEM((length, PAIR), F32)],
        compiler_params=pltpu.CompilerParams(vmem_limit_bytes=40 * 2**20),
        cost_estimate=cost(0.5 * pairs),
        name="attend_backward",
    )(qkv, qkv, qkv, grad_heads, lse, *after)


def rows_of(block, width):
    return pl.BlockSpec((block, width), lambda step: (step, 0))


def whole(shape):
    return pl.BlockSpec(shape, lambda *step: (0,) * len(shape))


def shaped(shape, dtype):
    return jax.ShapeDtypeStruct(shape, dtype)


PARAMS = pltpu.CompilerParams(vmem_limit_bytes=48 * 2**20)


ANYWHERE = pl.BlockSpec(memory_space=pl.ANY)


def weight_copies(gathered, refs, held, sems):
    row = lax.axis_index("row")
    copies = ([], [])
    for number, (x, array, at, offset) in enumerate(gathered.table):
        if len(gathered.table) > 2:
            start = pl.multiple_of((row ^ offset) * gathered.rows, 16)
        else:
            start = 0
        target = held.at[x, pl.ds(start, gathered.rows), :]
        copies[x].append(
            pltpu.make_async_copy(refs[array].at[at], target, sems.at[number])
        )
    return copies


def weight_scratch(gathered):
    all_rows = len(gathered.table) // 2 * gathered.rows
    return [
        pltpu.VMEM((2, all_rows, gathered.cols), BF16),
        pltpu.SemaphoreType.DMA((len(gathered.table),)),
    ]


def start_all(copies):
    for copy in copies:
        copy.start()


def wait_all(copies):
    for copy in copies:
        copy.wait()


def store_parts(held, grid, refs, x, source, lanes):
    if len(refs) == 1:
        refs[0][x, :, lanes] = held[:, source]
        return
    row = lax.axis_index("row")
    rows = held.shape[0] // grid.row_count
    for index in range(grid.row_count):
        start = pl.multiple_of((row ^ index) * rows, 16)
        array, place = grid.part_of(x, index)
        refs[array][place, :, lanes] = held[pl.ds(start, rows), source]


def segments(pair, third):
    low, high, found = pair * PAIR, (pair + 1) * PAIR, []
    while low < high:
        x = low // third
        end = min(high, (x + 1) * third)
        found.append((x, low - x * third, end - x * third, low - pair * PAIR))
        low = end
    return found


def parts_out(grid, width, cols):
    rows = width // grid.row_count
    if rows % 16:
        return [(2, width, cols)]
    return grid.part_shapes(rows, cols)


def turn(value):
    return value.T


def pick_half(here, mine_ref, other_ref):
    mine, other = mine_ref[...].astype(F32), other_ref[...].astype(F32)
    return jnp.where(here, mine, other)


def first_norm_kernel(gathered, cols, place_ref, mine_ref, other_ref, after_ref, *refs):
    count = len(gathered.arrays)
    norm_ref, qkv_ref, tokens_ref, full_ref, out_w_ref, vec_ref, held, bias, sems = refs[count:]
    copies = weight_copies(gathered, refs[:count], held, sems)
    third = cols // 3
    step = pl.program_id(0)
    per_half = pl.num_programs(0) // 2

    @pl.when(step == 0)
    def _():
        start_all(copies[0] + copies[1])
        wait_all(copies[0] + copies[1])
        for x in range(2):
            out_w_ref[:, x * third : (x + 1) * third] = held[x, :, held.shape[2] - third :]
        for pair in range(2 * third // PAIR):
            for part in range(3):
                for x, low, high, lane in segments(pair, third):
                    at = (3 * pair + part) * PAIR + lane
                    source = slice(part * third + low, part * third + high)
                    full_ref[:, at : at + high - low] = held[x, :, source]
        first = cols // 128 * 128
        rows = turn(held[0, :, first : first + 128].astype(F32))[cols - first :]
        vec_ref[...] = rows[: vec_ref.shape[0]]
        row_at = lax.broadcasted_iota(jnp.int32, (rows.shape[1], 2 * third), 0)
        lane_at = lax.broadcasted_iota(jnp.int32, (rows.shape[1], 2 * third), 1)
        wanted = jnp.where(
            lane_at < third, place_ref[1] + lane_at, place_ref[2] + lane_at - third
        )
        chosen = jnp.where(row_at == wanted, 1.0, 0.0).astype(BF16)
        picked = dot_nn(vec_ref[...].astype(BF16), chosen)
        bias[...] = jnp.zeros_like(bias)
        for pair in range(2 * third // PAIR):
            lanes = slice(pair * PAIR, (pair + 1) * PAIR)
            at = 3 * pair * PAIR
            bias[0:1, at : at + PAIR] = picked[2:3, lanes]
            bias[0:1, at + 2 * PAIR : at + 3 * PAIR] = picked[3:4, lanes]

    tokens = pick_half(step // per_half == place_ref[0], mine_ref, other_ref)
    tokens_ref[...] = tokens.astype(BF16)
    normed, _ = normalize_rows(tokens)
    first_in = (normed * vec_ref[0:1, :] + vec_ref[1:2, :]).astype(BF16)
    norm_ref[...] = first_in
    qkv_ref[...] = (dot_nn(first_in, full_ref[...]) + bias[0:1, :]).astype(BF16)


def first_norm(place, mine, other, gathered, width_loc, after):
    rows, width = mine.shape
    length = 2 * rows
    cols = 3 * width_loc
    steps = rows // ROW_BLOCK
    half = pl.BlockSpec((ROW_BLOCK, width), lambda step, place_ref: (step % steps, 0))

    def by_row(size):
        return pl.BlockSpec((ROW_BLOCK, size), lambda step, place_ref: (step, 0))

    return pl.pallas_call(
        functools.partial(first_norm_kernel, gathered, cols),
        grid_spec=pltpu.PrefetchScalarGridSpec(
            num_scalar_prefetch=1,
            grid=(2 * steps,),
            in_specs=[half, half, ANYWHERE] + [ANYWHERE] * len(gathered.arrays),
            out_specs=[
                by_row(width),
                by_row(2 * cols),
                by_row(width),
                whole((width, 2 * cols)),
                whole((width, 2 * width_loc)),
                whole((16, width)),
            ],
            scratch_shapes=weight_scratch(gathered)[:1]
            + [pltpu.VMEM((8, 2 * cols), F32)]
            + weight_scratch(gathered)[1:],
        ),
        out_shape=[
            shaped((length, width), BF16),
            shaped((length, 2 * cols), BF16),
            shaped((length, width), BF16),
            shaped((width, 2 * cols), BF16),
            shaped((width, 2 * width_loc), BF16),
            shaped((16, width), F32),
        ],
        compiler_params=PARAMS,
        cost_estimate=cost(8),
        name="first_norm",
    )(place, mine, other, after, *gathered.arrays)


def attended_kernel(
    heads_ref, partner_ref, own_ref, other_ref, tokens_ref, vec_ref, first_ref,
    hidden_ref, norm_ref, norm_turned_ref, first_turned_ref,
):
    attended = dot_nt(heads_ref[...], own_ref[...]) + dot_nt(partner_ref[...], other_ref[...])
    hidden = tokens_ref[...].astype(F32) + attended + vec_ref[4:5, :]
    hidden_ref[...] = hidden
    normed, _ = normalize_rows(hidden)
    second_in = (normed * vec_ref[5:6, :] + vec_ref[6:7, :]).astype(BF16)
    norm_ref[...] = second_in
    norm_turned_ref[...] = turn(second_in)
    first_turned_ref[...] = turn(first_ref[...])


def attended_norm(heads, partner_heads, own_out, partner_out, tokens, vec_all, first_in):
    length, width = tokens.shape
    cols = own_out.shape[1]
    full, part = rows_of(ROW_BLOCK, width), rows_of(ROW_BLOCK, cols)
    turned = pl.BlockSpec((width, ROW_BLOCK), lambda step: (0, step))
    return pl.pallas_call(
        attended_kernel,
        grid=(length // ROW_BLOCK,),
        in_specs=[
            part,
            part,
            whole(own_out.shape),
            whole(partner_out.shape),
            full,
            whole(vec_all.shape),
            full,
        ],
        out_specs=[full, full, turned, turned],
        out_shape=[shaped((length, width), F32), shaped((length, width), BF16)]
        + [shaped((width, length), BF16)] * 2,
        compiler_params=PARAMS,
        cost_estimate=cost(8),
        name="attended_norm",
    )(heads, partner_heads, own_out, partner_out, tokens, vec_all, first_in)


def join_kernel(place_ref, mine_ref, other_ref, joined_ref, turned_ref):
    here = pl.program_id(0) // (pl.num_programs(0) // 2) == place_ref[0]
    joined = pick_half(here, mine_ref, other_ref).astype(BF16)
    joined_ref[...] = joined
    turned_ref[...] = turn(joined)


def join_halves(place, mine, other):
    rows, width = mine.shape
    steps = rows // ROW_BLOCK
    half = pl.BlockSpec((ROW_BLOCK, width), lambda step, place_ref: (step % steps, 0))
    return pl.pallas_call(
        join_kernel,
        grid_spec=pltpu.PrefetchScalarGridSpec(
            num_scalar_prefetch=1,
            grid=(2 * steps,),
            in_specs=[half, half],
            out_specs=[
                pl.BlockSpec((ROW_BLOCK, width), lambda step, place_ref: (step, 0)),
                pl.BlockSpec((width, ROW_BLOCK), lambda step, place_ref: (0, step)),
            ],
        ),
        out_shape=[shaped((2 * rows, width), BF16), shaped((width, 2 * rows), BF16)],
        compiler_params=PARAMS,
        cost_estimate=cost(0.1),
        name="join_halves",
    )(place, mine, other)


def feed_kernel(gathered, place_ref, norm_ref, cot_ref, vec_ref, *refs):
    count = len(gathered.arrays)
    act_ref, gup_ref, bias_sum_ref, out_low_ref, back_low_ref, out_ref, back_ref, held, sems = refs[count:]
    copies = weight_copies(gathered, refs[:count], held, sems)
    step = pl.program_id(0)
    length = norm_ref.shape[0]
    curve, cubic = math.sqrt(2 / math.pi), 0.044715
    cols = held.shape[2] // 2
    x = step
    up_lanes, down_lanes = slice(0, cols), slice(cols, 2 * cols)
    bias = vec_ref[pl.ds(8 + place_ref[3 + x], 1), :]

    @pl.when(step == 0)
    def _():
        start_all(copies[0] + copies[1])
        out_ref[...] = jnp.zeros_like(out_ref)
        back_ref[...] = jnp.zeros_like(back_ref)
        wait_all(copies[0])

    @pl.when(step == 1)
    def _():
        wait_all(copies[1])

    bias_sum = jnp.zeros(bias.shape, F32)
    for first in range(0, length, ROW_BLOCK):
        rows = slice(first, first + ROW_BLOCK)
        up = dot_nn(norm_ref[rows, :], held[x, :, up_lanes]) + bias
        cubed = up * up * (curve * cubic)
        tanh = jnp.tanh(up * (curve + cubed))
        halved = 0.5 * up
        act_ref[rows, :] = (halved + halved * tanh).astype(BF16)
        slope = 0.5 + 0.5 * tanh + halved * (1.0 - tanh * tanh) * (curve + 3.0 * cubed)
        grad_up = (dot_nn(cot_ref[rows, :], held[x, :, down_lanes]) * slope).astype(BF16)
        gup_ref[rows, :] = grad_up
        bias_sum = bias_sum + jnp.sum(grad_up.astype(F32), axis=0, keepdims=True)
    back_ref[...] += dot_nt(gup_ref[...], held[x, :, up_lanes])
    out_ref[...] += dot_nt(act_ref[...], held[x, :, down_lanes])
    bias_sum_ref[...] = bias_sum

    @pl.when(step == pl.num_programs(0) - 1)
    def _():
        back_low_ref[...] = back_ref[...].astype(BF16)
        out_low_ref[...] = out_ref[...].astype(BF16)


def feed(place, norm, cot, vec_all, gathered):
    length, width = norm.shape
    block = gathered.cols // 2
    hidden = 2 * block
    tall = pl.BlockSpec((length, block), lambda step, place_ref: (0, step))
    flat = pl.BlockSpec((1, block), lambda step, place_ref: (0, step))
    full = whole((length, width))
    return pl.pallas_call(
        functools.partial(feed_kernel, gathered),
        grid_spec=pltpu.PrefetchScalarGridSpec(
            num_scalar_prefetch=1,
            grid=(2,),
            in_specs=[full, full, whole(vec_all.shape)] + [ANYWHERE] * len(gathered.arrays),
            out_specs=[tall, tall, flat, full, full],
            scratch_shapes=[pltpu.VMEM((length, width), F32)] * 2 + weight_scratch(gathered),
        ),
        out_shape=[
            shaped((length, hidden), BF16),
            shaped((length, hidden), BF16),
            shaped((1, hidden), F32),
            shaped((length, width), BF16),
            shaped((length, width), BF16),
        ],
        compiler_params=PARAMS,
        cost_estimate=cost(18),
        name="feed",
    )(place, norm, cot, vec_all, *gathered.arrays)


def feed_grads_kernel(grid, cot_ref, norm_ref, act_ref, gup_ref, *refs):
    kind, x_at = pl.program_id(0), pl.program_id(1)
    outs, held = refs[:-1], refs[-1]
    size = held.shape[1]

    @pl.when(kind == 0)
    def _():
        held[...] = dot_nn(cot_ref[...], act_ref[...]).astype(BF16)

    @pl.when(kind == 1)
    def _():
        held[...] = dot_nn(norm_ref[...], gup_ref[...]).astype(BF16)

    for index in range(2):
        for x in range(2):

            @pl.when((kind == index) & (x_at == x))
            def _():
                lanes = slice((1 - index) * size, (2 - index) * size)
                store_parts(held, grid, outs, x, slice(None), lanes)


def feed_grads(cot_turned, norm_turned, act, grad_up, grid):
    width, length = cot_turned.shape
    hidden = act.shape[1]
    block = hidden // 2
    shapes = parts_out(grid, width, hidden)
    parts = pl.pallas_call(
        functools.partial(feed_grads_kernel, grid),
        grid=(2, 2),
        in_specs=[
            whole((width, length)),
            whole((width, length)),
            pl.BlockSpec((length, block), lambda kind, x: (0, jnp.where(kind == 0, x, 1))),
            pl.BlockSpec((length, block), lambda kind, x: (0, jnp.where(kind == 1, x, 0))),
        ],
        out_specs=[whole(shape) for shape in shapes],
        out_shape=[shaped(shape, BF16) for shape in shapes],
        scratch_shapes=[pltpu.VMEM((width, block), BF16)],
        compiler_params=PARAMS,
        cost_estimate=cost(10),
        name="feed_grads",
    )(cot_turned, norm_turned, act, grad_up)
    return parts if len(parts) == 5 else grid.split(parts[0])


def second_back_kernel(
    part_ref, other_ref, hidden_ref, cot_ref, vec_ref, out_w_ref, turned_ref,
    grad_ref, heads_ref, sum_ref, out_grad_ref, total,
):
    step = pl.program_id(0)
    normed, inv_std = normalize_rows(hidden_ref[...])
    part = part_ref[...].astype(F32)
    cot = cot_ref[...].astype(F32)
    grad_second = part + other_ref[...].astype(F32)
    grad = cot + norm_back(grad_second * vec_ref[5:6, :], normed, inv_std)
    grad_ref[...] = grad
    low = grad.astype(BF16)
    heads_ref[...] = dot_nn(low, out_w_ref[...]).astype(BF16)

    @pl.when(step == 0)
    def _():
        sum_ref[...] = jnp.zeros_like(sum_ref)
        total[...] = jnp.zeros_like(total)

    total[...] += dot_nn(turned_ref[...], low)
    for row, value in enumerate((grad, part * normed, part, cot)):
        sum_ref[row : row + 1, :] += jnp.sum(value, axis=0, keepdims=True)

    @pl.when(step == pl.num_programs(0) - 1)
    def _():
        out_grad_ref[...] = total[...].T.astype(BF16)


def second_back(part, other, hidden, cot, vec_all, out_w, heads_turned):
    length, width = part.shape
    cols = out_w.shape[1]
    full = rows_of(ROW_BLOCK, width)
    return pl.pallas_call(
        second_back_kernel,
        grid=(length // ROW_BLOCK,),
        in_specs=[full, full, full, full, whole(vec_all.shape), whole(out_w.shape)]
        + [pl.BlockSpec((cols, ROW_BLOCK), lambda step: (0, step))],
        out_specs=[full, rows_of(ROW_BLOCK, cols), whole((8, width)), whole((width, cols))],
        out_shape=[
            shaped((length, width), F32),
            shaped((length, cols), BF16),
            shaped((8, width), F32),
            shaped((width, cols), BF16),
        ],
        scratch_shapes=[pltpu.VMEM((cols, width), F32)],
        compiler_params=PARAMS,
        cost_estimate=cost(8.6),
        name="second_back",
    )(part, other, hidden, cot, vec_all, out_w, heads_turned)


def qkv_grads_kernel(grid, norm_ref, grad_ref, grad_two_ref, out_grad_ref, vec_ref, *refs):
    step = pl.program_id(0)
    outs, held = refs[:-1], refs[-1]
    third = held.shape[1] // 2
    pairs = 2 * third // PAIR
    for index in range(pairs + 1):

        @pl.when(step == index)
        def _():
            if index == pairs:
                held[...] = out_grad_ref[...]
                for x in range(2):
                    source = slice(x * third, (x + 1) * third)
                    store_parts(held, grid, outs, x, source, slice(3 * third, 4 * third))
                rows = vec_ref[...]
                blank = jnp.zeros((VEC_LANES - rows.shape[0], rows.shape[1]), F32)
                held[:, :VEC_LANES] = jnp.concatenate([rows, blank], axis=0).T.astype(BF16)
                for x in range(2):
                    lanes = slice(4 * third, 4 * third + VEC_LANES)
                    store_parts(held, grid, outs, x, slice(0, VEC_LANES), lanes)
                return
            right = grad_two_ref if index == pairs - 1 else grad_ref
            held[...] = dot_nn(norm_ref[...], right[...]).astype(BF16)
            for part in range(3):
                for x, low, high, lane in segments(index, third):
                    at = part * PAIR + lane
                    lanes = slice(part * third + low, part * third + high)
                    store_parts(held, grid, outs, x, slice(at, at + high - low), lanes)


def qkv_grads(norm_turned, grads, out_grad, grid, grad_vec):
    width, length = norm_turned.shape
    cols = out_grad.shape[1]
    pairs = cols // PAIR
    shapes = parts_out(grid, width, 2 * cols + VEC_LANES)
    parts = pl.pallas_call(
        functools.partial(qkv_grads_kernel, grid),
        grid=(pairs + 1,),
        in_specs=[
            whole((width, length)),
            pl.BlockSpec((length, cols), lambda step: (0, jnp.minimum(step, pairs - 2))),
            whole((length, cols)),
            whole((width, cols)),
            whole(grad_vec.shape),
        ],
        out_specs=[whole(shape) for shape in shapes],
        out_shape=[shaped(shape, BF16) for shape in shapes],
        scratch_shapes=[pltpu.VMEM((width, cols), BF16)],
        compiler_params=PARAMS,
        cost_estimate=cost(0.3),
        name="qkv_grads",
    )(norm_turned, *grads, out_grad, grad_vec)
    return parts if len(parts) == 5 else grid.split(parts[0])


def first_back_kernel(
    place_ref, grad_ref, grad_two_ref, weight_ref, tokens_ref, second_ref, up_ref,
    part_ref, vec_ref, bias,
):
    grads = jnp.concatenate([grad_ref[...], grad_two_ref[...]], axis=1)
    part = dot_nt(grads, weight_ref[...])
    part_ref[...] = part.astype(BF16)
    normed, _ = normalize_rows(tokens_ref[...].astype(F32))

    @pl.when(pl.program_id(0) == 0)
    def _():
        vec_ref[...] = jnp.zeros_like(vec_ref)
        bias[...] = jnp.zeros_like(bias)

    for row, value in enumerate((part * normed, part)):
        vec_ref[row : row + 1, :] += jnp.sum(value, axis=0, keepdims=True)
    bias[0:1, :] += jnp.sum(grads.astype(F32), axis=0, keepdims=True)

    @pl.when(pl.program_id(0) == pl.num_programs(0) - 1)
    def _():
        width = vec_ref.shape[1]
        pairs = bias.shape[1] // (3 * PAIR)
        third = pairs * PAIR // 2
        for row, part_at in ((2, 0), (3, 2)):
            lanes = [
                bias[:, (3 * pair + part_at) * PAIR : (3 * pair + part_at + 1) * PAIR]
                for pair in range(pairs)
            ]
            joined = jnp.concatenate(lanes, axis=1)
            blank = jnp.zeros((joined.shape[0], width - third), F32)
            for x in range(2):
                block = jnp.concatenate([joined[:, x * third : (x + 1) * third], blank], axis=1)
                vec_ref[row : row + 1, :] += pltpu.roll(block, place_ref[1 + x], 1)[0:1]
        vec_ref[4:5, :] = 0.5 * second_ref[0:1, :]
        vec_ref[5:7, :] = second_ref[1:3, :]
        vec_ref[7:8, :] = 0.5 * second_ref[3:4, :]
        row_at = lax.broadcasted_iota(jnp.int32, (8, width), 0)
        vec_ref[8:16, :] = jnp.where(row_at == place_ref[3], up_ref[0:1, :width], 0.0) + jnp.where(
            row_at == place_ref[4], up_ref[0:1, width:], 0.0
        )


def first_back(place, grads, weight, tokens, second_sums, up_sums):
    length, width = tokens.shape
    cols = weight.shape[1]

    def by_row(size):
        return pl.BlockSpec((ROW_BLOCK, size), lambda step, place_ref: (step, 0))

    return pl.pallas_call(
        first_back_kernel,
        grid_spec=pltpu.PrefetchScalarGridSpec(
            num_scalar_prefetch=1,
            grid=(length // ROW_BLOCK,),
            in_specs=[
                by_row(grads[0].shape[1]),
                by_row(grads[1].shape[1]),
                whole(weight.shape),
                by_row(width),
                whole(second_sums.shape),
                whole(up_sums.shape),
            ],
            out_specs=[by_row(width), whole((16, width))],
            scratch_shapes=[pltpu.VMEM((8, cols), F32)],
        ),
        out_shape=[shaped((length, width), BF16), shaped((16, width), F32)],
        compiler_params=PARAMS,
        cost_estimate=cost(0.3),
        name="first_back",
    )(place, *grads, weight, tokens, second_sums, up_sums)


def token_back_kernel(core_ref, part_ref, other_ref, tokens_ref, grad_ref, vec_ref, out_ref):
    normed, inv_std = normalize_rows(tokens_ref[...].astype(F32))
    grad_first = part_ref[...].astype(F32) + other_ref[...].astype(F32)
    out_ref[...] = grad_ref[...] + norm_back(grad_first * vec_ref[0:1, :], normed, inv_std)


def token_back(core, part, other, tokens, grad_hidden, vec_all):
    rows, width = tokens.shape
    steps = rows // ROW_BLOCK
    own = pl.BlockSpec((ROW_BLOCK, width), lambda step, core_ref: (core_ref[0] * steps + step, 0))
    here = pl.BlockSpec((ROW_BLOCK, width), lambda step, core_ref: (step, 0))
    return pl.pallas_call(
        token_back_kernel,
        grid_spec=pltpu.PrefetchScalarGridSpec(
            num_scalar_prefetch=1,
            grid=(steps,),
            in_specs=[own, here, here, own, whole(vec_all.shape)],
            out_specs=here,
        ),
        out_shape=shaped((rows, width), F32),
        compiler_params=PARAMS,
        cost_estimate=cost(3.2),
        name="token_back",
    )(core.reshape(1), part, other, tokens, grad_hidden, vec_all)


def out_step_kernel(grad_ref, weight_ref, first_ref, second_ref, new_ref, new_first_ref, new_second_ref):
    grads = grad_ref[...].T
    results = adamw(weight_ref[...], first_ref[...], second_ref[...], grads, RATE_MATRIX)
    new_ref[...], new_first_ref[...], new_second_ref[...] = results


def out_step(weight, first, second, grads):
    return pl.pallas_call(
        out_step_kernel,
        out_shape=[shaped(weight.shape, F32)] * 3,
        compiler_params=PARAMS,
        name="out_step",
    )(grads, weight, first, second)


def vector_step_kernel(
    part_ref, other_ref, weight_ref, first_ref, second_ref, new_ref, new_first_ref, new_second_ref
):
    grads = (part_ref[...] + other_ref[...]).T[: weight_ref.shape[0]]
    results = adamw(weight_ref[...], first_ref[...], second_ref[...], grads, RATE_VECTOR)
    new_ref[...], new_first_ref[...], new_second_ref[...] = results


def vector_step(weight, first, second, part, other):
    return pl.pallas_call(
        vector_step_kernel,
        out_shape=[shaped(weight.shape, F32)] * 3,
        compiler_params=PARAMS,
        name="vector_step",
    )(part, other, weight, first, second)


def shards(
    tokens,
    cotangent,
    w_qkv,
    w_out,
    w_up,
    w_down,
    vectors,
    first_qkv,
    first_out,
    first_up,
    first_down,
    first_vectors,
    second_qkv,
    second_out,
    second_up,
    second_down,
    second_vectors,
):
    col_index = lax.axis_index("col")
    grid = Grid(lax.axis_size("row"))
    core_line = ("col", 1)
    core = col_index % 2
    other_col = col_index ^ 2
    rows_loc, width = tokens.shape
    width_loc = w_qkv.shape[2]
    hidden_loc = w_up.shape[1]
    shard_rows = w_up.shape[0]

    pad = -(3 * width_loc + VEC_ROWS) % 128
    pack_qkv = jnp.concatenate(
        [w_qkv[:, part].astype(BF16) for part in range(3)]
        + [vectors.T.astype(BF16), jnp.zeros((shard_rows, pad), BF16), w_out.T.astype(BF16)],
        axis=1,
    )
    pack_feed = jnp.concatenate([w_up.astype(BF16), w_down.T.astype(BF16)], axis=1)

    def own_rows(value):
        return lax.dynamic_slice_in_dim(value, core * rows_loc, rows_loc, 0)

    def partner_rows(value):
        return lax.dynamic_slice_in_dim(value, (1 - core) * rows_loc, rows_loc, 0)

    place = jnp.stack(
        [core, col_index * width_loc, other_col * width_loc, col_index, other_col]
    ).astype(jnp.int32)

    far_qkv = grid.gather_far(pack_qkv)
    partner = [swap_over(tokens, core_line), swap_over(cotangent, core_line)]
    far_qkv, partner = lax.optimization_barrier((far_qkv, partner))
    sent_qkv = grid.gather_ready(far_qkv)
    pack_feed, _ = lax.optimization_barrier((pack_feed, sent_qkv))
    arrived_qkv = grid.gather_one(sent_qkv)
    far_feed = grid.gather_far(pack_feed)
    two_qkv = grid.gather_two(sent_qkv, arrived_qkv)
    near_qkv = grid.gather_three(*two_qkv)
    all_cot, cot_turned = join_halves(place, cotangent, partner[1])
    far_feed, _ = lax.optimization_barrier((far_feed, (two_qkv, all_cot)))
    sent_feed = grid.gather_ready(far_feed)
    arrived_feed = grid.gather_one(sent_feed)

    first_in, qkv, all_tokens, full_qkv, full_out, vec_all = first_norm(
        place, tokens, partner[0], near_qkv, width_loc, all_cot
    )
    partner_out = swap_over(full_out, core_line)
    pairs = 2 * width_loc // PAIR
    arrived_feed, _ = lax.optimization_barrier((arrived_feed, qkv))
    two_feed = grid.gather_two(sent_feed, arrived_feed)
    near_feed = grid.gather_three(*two_feed)
    heads_low, heads_turned, lse = attend_forward(qkv, two_feed)
    partner_heads = swap_over(heads_low, core_line)
    hidden_state, second_in, second_turned, first_turned = attended_norm(
        heads_low, partner_heads, full_out, partner_out, all_tokens, vec_all, first_in
    )
    activated, grad_upper, grad_bias_up, down_part, second_part = feed(
        place, second_in, all_cot, vec_all, near_feed
    )

    second_other = swap_over(second_part, core_line)
    parts_feed = feed_grads(cot_turned, second_turned, activated, grad_upper, grid)
    arrived_feed = grid.stage_one(parts_feed)
    grad_hidden, grad_heads, second_sums, out_grad = second_back(
        second_part, second_other, hidden_state, all_cot, vec_all, full_out, heads_turned
    )
    grad_one = attend_backward(qkv, grad_heads, lse, 0, pairs - 1, ())
    arrived_feed, grad_one = lax.optimization_barrier((arrived_feed, grad_one))
    sent_feed = grid.stage_two(parts_feed, *arrived_feed)
    grad_two = attend_backward(qkv, grad_heads, lse, pairs - 1, 1, sent_feed)
    grads_qkv = (grad_one, grad_two)
    first_part, grad_vec = first_back(
        place, grads_qkv, full_qkv, all_tokens, second_sums, grad_bias_up
    )
    parts_qkv = qkv_grads(first_turned, grads_qkv, out_grad, grid, grad_vec)
    arrived_pack = grid.stage_one(parts_qkv)
    chain_feed = grid.chain_send(grid.stage_three(parts_feed, sent_feed, parts_qkv[0]))
    arrived_pack, _ = lax.optimization_barrier((arrived_pack, chain_feed[1]))
    owned_feed = grid.reduce_chain(*chain_feed)
    owned_up, owned_down = owned_feed[:, :hidden_loc], owned_feed[:, hidden_loc:]

    sent_pack = grid.stage_two(parts_qkv, *arrived_pack)
    sent_pack, first_part, down_part = lax.optimization_barrier(
        (sent_pack, first_part, down_part)
    )
    near_pack = grid.stage_three(parts_qkv, sent_pack)
    first_other = swap_over(partner_rows(first_part), core_line)
    down_other = swap_over(partner_rows(down_part), core_line).astype(F32)
    mixed_out = own_rows(hidden_state) + own_rows(down_part).astype(F32) + down_other + vec_all[7]
    token_grad = token_back(core, first_part, first_other, tokens, grad_hidden, vec_all)
    owned_pack, (mixed_out, token_grad) = grid.reduce_direct(near_pack, (mixed_out, token_grad))
    part_vec = owned_pack[:, 4 * width_loc :]
    other_vec = swap_over(part_vec, core_line)
    owned_qkv = jnp.stack(
        [owned_pack[:, part * width_loc : (part + 1) * width_loc] for part in range(3)], axis=1
    )
    owned_out = owned_pack[:, 3 * width_loc : 4 * width_loc]

    new_qkv, new_first_qkv, new_second_qkv = adamw(
        w_qkv, first_qkv, second_qkv, owned_qkv, RATE_MATRIX
    )
    new_out, new_first_out, new_second_out = out_step(w_out, first_out, second_out, owned_out)
    new_up, new_first_up, new_second_up = adamw(w_up, first_up, second_up, owned_up, RATE_MATRIX)
    new_down, new_first_down, new_second_down = adamw(
        w_down, first_down, second_down, owned_down.T, RATE_MATRIX
    )
    new_vectors, new_first_vectors, new_second_vectors = vector_step(
        vectors, first_vectors, second_vectors, part_vec, other_vec
    )
    return (
        mixed_out,
        token_grad,
        new_qkv,
        new_out,
        new_up,
        new_down,
        new_vectors,
        new_first_qkv,
        new_first_out,
        new_first_up,
        new_first_down,
        new_first_vectors,
        new_second_qkv,
        new_second_out,
        new_second_up,
        new_second_down,
        new_second_vectors,
    )


def solution(mesh):
    by_token = P(("row", "col"), None)
    weights = (
        P("row", None, "col"),
        P("col", "row"),
        P("row", "col"),
        P("col", "row"),
        P(None, "row"),
    )
    return jax.shard_map(
        shards,
        mesh=mesh,
        in_specs=(by_token, by_token) + weights * 3,
        out_specs=(by_token, by_token) + weights * 3,
        check_vma=False,
    )
```
